32 devices in a mesh: ha: 8 (over z, y), ta: 2 (over x), col: 2 (over core).
Axes of the slice: x: 2, y: 2, z: 4, core: 2. Of those that a mesh axis runs over, the one named last changes fastest.
Arguments:
- tokens: bfloat16 [16, 224, 28, 128], P(('col', 'ta'), 'ha'), parts along dimension 0, may hold values from -6 to 6
- regions_one: int32 [16, 224, 28], P(('col', 'ta'), 'ha'), parts along dimension 0, may hold values from 0 to 2
- regions_three: int32 [16, 56, 7], P(('col', 'ta'), 'ha'), parts along dimension 0, may hold values from 0 to 2
- gain_one: float32 [128], replicated, may hold values from 0.25 to 1.75
- projection_one: bfloat16 [128, 384], replicated, may hold values from -0.5 to 0.5
- outward_one: bfloat16 [128, 128], replicated, may hold values from -0.5 to 0.5
- table_one: float32 [1183, 4], replicated, may hold values from -4 to 303
- merge_gain_one: float32 [512], replicated, may hold values from 0.25 to 1.75
- merge_weight_one: bfloat16 [512, 256], replicated, may hold values from -0.25 to 0.25
- merge_gain_two: float32 [1024], replicated, may hold values from 0.25 to 1.75
- merge_weight_two: bfloat16 [1024, 512], replicated, may hold values from -0.1875 to 0.1875
- gain_three: float32 [512], replicated, may hold values from 0.25 to 1.75
- projection_three: bfloat16 [512, 1536], replicated, may hold values from -0.25 to 0.25
- outward_three: bfloat16 [512, 512], replicated, may hold values from -0.25 to 0.25
- table_three: float32 [1183, 16], replicated, may hold values from -4 to 303
- cotangent: bfloat16 [16, 56, 7, 512], P(('col', 'ta'), 'ha'), parts along dimension 0, may hold values from -6 to 6
Outputs:
- section_three: bfloat16 [16, 56, 7, 512], P(('col', 'ta'), 'ha'), parts along dimension 0
- grad_tokens: bfloat16 [16, 224, 28, 128], P(('col', 'ta'), 'ha'), parts along dimension 0
The draws below stay inside these ranges and needn't reach their ends.
There are 2 independent parts, one for each index of `col`. The reference program is written for one: setup_inputs(seed, part) draws one part's arguments, and reference() takes and returns one part's arrays. A program takes and returns all parts, laid end to end along the dimension named above; an argument that names none is the same for every part. Nothing has to cross between parts.
Inputs may be any that keep to these rules, and one draw needn't show every extreme that they name: `regions_one`: region ids are free for each position. `regions_three`: region ids are free for each position.
All inputs are finite; a program needn't handle non-finite values.
Results may differ from the reference program's by a relative error of at most 0.03.
Values may be sent and summed in bfloat16 or wider, within the bound.
No kernel may reach another device: no remote copies, remote signals or barrier semaphores. Data moves between devices by JAX's collectives and lax.ppermute only.
A program may use at most 192 MiB of HBM per device.

```python
import jax
import jax.numpy as jnp
from jax import lax

C1 = 128
C2 = 256
C3 = 512
HEADS1 = 4
HEADS3 = 16
WT = 4
WS = 7
ST = 2
SS = 3
WIDTH = 28
FRAMES = 8
HEIGHT = 224
NREL = 1183


def hot_table(key, head_count):
    normal_key, choose_key = jax.random.split(key)
    baseline = jnp.clip(jax.random.normal(normal_key, (NREL, head_count), jnp.float32), -4.0, 4.0)
    pair_count = (NREL + 1) // 2
    chosen = (jax.random.uniform(choose_key, (pair_count, head_count), jnp.float32) < 0.005).astype(jnp.float32)
    chosen = jnp.repeat(chosen, 2, axis=0)[:NREL]
    parity = (jnp.arange(NREL) % 2).astype(jnp.float32)[:, None]
    raised = 0.25 * baseline + 2.0 * parity
    return jnp.where(chosen > 0.5, raised, baseline)


def draw_table_one(key, part):
    key = jax.random.fold_in(key, 1)
    return hot_table(key, HEADS1)


def draw_table_three(key, part):
    key = jax.random.fold_in(key, 2)
    return hot_table(key, HEADS3)


def set_ends(result, own_key, least, top_value):
    place = [jax.random.randint(jax.random.fold_in(own_key, axis), (), 0, length) for axis, length in enumerate(result.shape)]
    widest = result.shape.index(max(result.shape))
    neighbour = place[:widest] + [(place[widest] + 1) % result.shape[widest]] + place[widest + 1:]
    return result.at[tuple(place)].set(least).at[tuple(neighbour)].set(top_value)


def steps_of(stream_key, shape, cuts, low, high):
    def one(axis_at, blocks):
        steps = jax.random.uniform(jax.random.fold_in(jax.random.fold_in(stream_key, 6), axis_at), (blocks,), jnp.float32, low / len(cuts), high / len(cuts))
        return jnp.repeat(jnp.exp(steps), shape[axis_at] // blocks).reshape((-1,) + (1,) * (len(shape) - axis_at - 1))

    level = one(*cuts[0])
    for cut in cuts[1:]:
        level = level * one(*cut)
    return level


def scatter_about(key, shape, deviation, most, shards=(), kind=jnp.bfloat16):
    level = steps_of(key, shape, shards, -0.22, 0.18) if shards else 1.0
    values = jax.random.normal(key, shape, jnp.float32) * deviation * level
    return jnp.minimum(jnp.maximum(values, -most), most).astype(kind)


def setup_inputs(seed: int = 0, part: int = 0) -> dict:
    arg_keys = jax.random.split(jax.random.key(seed), 17)
    own_keys = jax.random.split(jax.random.fold_in(arg_keys[16], part), 17)
    return {
        "tokens": scatter_about(own_keys[0], (FRAMES, HEIGHT, WIDTH, C1), 1.0, 6.0, ((0, 2), (1, 8))),
        "regions_one": set_ends(jax.random.randint(own_keys[1], (FRAMES, HEIGHT, WIDTH), 0, 3), jax.random.fold_in(own_keys[1], 1), 0, 2).astype(jnp.int32),
        "regions_three": set_ends(jax.random.randint(own_keys[2], (FRAMES, HEIGHT // 4, WIDTH // 4), 0, 3), jax.random.fold_in(own_keys[2], 1), 0, 2).astype(jnp.int32),
        "gain_one": jnp.clip(1.0 + 0.15 * jax.random.normal(arg_keys[3], (C1,), jnp.float32), 0.25, 1.75),
        "projection_one": scatter_about(arg_keys[4], (C1, 3 * C1), C1 ** -0.5, 0.5),
        "outward_one": scatter_about(arg_keys[5], (C1, C1), C1 ** -0.5, 0.5),
        "table_one": draw_table_one(jax.random.fold_in(arg_keys[16], 71), part),
        "merge_gain_one": jnp.clip(1.0 + 0.15 * jax.random.normal(arg_keys[7], (4 * C1,), jnp.float32), 0.25, 1.75),
        "merge_weight_one": scatter_about(arg_keys[8], (4 * C1, C2), (4 * C1) ** -0.5, 0.25),
        "merge_gain_two": jnp.clip(1.0 + 0.15 * jax.random.normal(arg_keys[9], (4 * C2,), jnp.float32), 0.25, 1.75),
        "merge_weight_two": scatter_about(arg_keys[10], (4 * C2, C3), (4 * C2) ** -0.5, 0.1875),
        "gain_three": jnp.clip(1.0 + 0.15 * jax.random.normal(arg_keys[11], (C3,), jnp.float32), 0.25, 1.75),
        "projection_three": scatter_about(arg_keys[12], (C3, 3 * C3), C3 ** -0.5, 0.25),
        "outward_three": scatter_about(arg_keys[13], (C3, C3), C3 ** -0.5, 0.25),
        "table_three": draw_table_three(jax.random.fold_in(arg_keys[16], 71), part),
        "cotangent": scatter_about(own_keys[15], (FRAMES, HEIGHT // 4, WIDTH // 4, C3), 1.0, 6.0, ((0, 2), (1, 8))),
    }


EPSILON = 1e-05

def layer_norm(values, gain_row):
    widened = values.astype(jnp.float32)
    centred = widened - lax.optimization_barrier(jnp.mean(widened, -1, keepdims=True))
    spread = lax.optimization_barrier(jnp.mean(centred * centred, -1, keepdims=True))
    return (centred * lax.rsqrt(spread + EPSILON) * gain_row).astype(jnp.bfloat16)

def relative_bias(bias_table, window_time, window_side):
    token_count = window_time * window_side * window_side
    positions = jnp.arange(token_count, dtype=jnp.int32)
    time_place = positions // (window_side * window_side)
    row_place = positions // window_side % window_side
    column_place = positions % window_side
    extent = 2 * window_side - 1
    table_index = (time_place[:, None] - time_place[None, :] + window_time - 1) * extent * extent
    table_index = table_index + (row_place[:, None] - row_place[None, :] + window_side - 1) * extent
    table_index = table_index + (column_place[:, None] - column_place[None, :] + window_side - 1)
    picked = jnp.take(jnp.transpose(bias_table), table_index.reshape(-1).astype(jnp.int32), axis=1)
    return picked.reshape(bias_table.shape[1], token_count, token_count)

def to_windows(values, window_time, window_side):
    frames, height, width_cells = values.shape[:3]
    trailing = values.shape[3:]
    blocked = values.reshape((frames // window_time, window_time, height // window_side, window_side, width_cells // window_side, window_side) + trailing)
    extra_dims = tuple(range(6, 6 + len(trailing)))
    blocked = jnp.transpose(blocked, (0, 2, 4, 1, 3, 5) + extra_dims)
    return blocked.reshape((-1, window_time * window_side * window_side) + trailing)

def from_windows(windows, frames, height, width_cells, window_time, window_side):
    trailing = windows.shape[2:]
    blocked = windows.reshape((frames // window_time, height // window_side, width_cells // window_side, window_time, window_side, window_side) + trailing)
    extra_dims = tuple(range(6, 6 + len(trailing)))
    blocked = jnp.transpose(blocked, (0, 3, 1, 4, 2, 5) + extra_dims)
    return blocked.reshape((frames, height, width_cells) + trailing)

def window_attention(inputs, region_ids, projection, outward, bias_block, head_count):
    token_count, channels = inputs.shape
    head_size = channels // head_count
    packed = jnp.dot(inputs, projection, preferred_element_type=jnp.float32).astype(jnp.bfloat16)
    queries = packed[:, :channels].reshape(token_count, head_count, head_size).astype(jnp.float32)
    key_rows = packed[:, channels:2 * channels].reshape(token_count, head_count, head_size).astype(jnp.float32)
    value_rows = packed[:, 2 * channels:].reshape(token_count, head_count, head_size).astype(jnp.float32)
    scores = jnp.einsum('qhd,khd->hqk', queries, key_rows) * head_size ** (-0.5) + bias_block
    same_region = region_ids[:, None] == region_ids[None, :]
    scores = jnp.where(same_region[None], scores, -jnp.inf)
    row_peak = lax.stop_gradient(lax.optimization_barrier(jnp.max(scores, -1, keepdims=True)))
    raised = jnp.exp(scores - row_peak)
    probabilities = (raised / lax.optimization_barrier(jnp.sum(raised, -1, keepdims=True))).astype(jnp.bfloat16)
    attended = jnp.einsum('hqk,khd->qhd', probabilities.astype(jnp.float32), value_rows).astype(jnp.bfloat16)
    return jnp.dot(attended.reshape(token_count, channels), outward, preferred_element_type=jnp.float32).astype(jnp.bfloat16)

def attend(rolled, region_ids, projection, outward, bias_table, head_count):
    frames, height, width_cells, channels = rolled.shape
    bias_block = relative_bias(bias_table, WT, WS)
    windows = to_windows(rolled, WT, WS)
    window_ids = to_windows(region_ids, WT, WS)

    def per_window(operands):
        return window_attention(operands[0], operands[1], projection, outward, bias_block, head_count)
    results = lax.map(jax.checkpoint(per_window), (windows, window_ids))
    return from_windows(results, frames, height, width_cells, WT, WS)

def shifted_attention(normed, region_ids, projection, outward, bias_table, head_count):
    rolled = jnp.roll(normed, (-ST, -SS, -SS), (0, 1, 2))
    mixed_heads = attend(rolled, region_ids, projection, outward, bias_table, head_count)
    return jnp.roll(mixed_heads, (ST, SS, SS), (0, 1, 2))

def merge_patches(values, gain_row, weight):
    frames, height, width_cells, channels = values.shape
    grouped = values.reshape(frames, height // 2, 2, width_cells // 2, 2, channels)
    grouped = jnp.transpose(grouped, (0, 1, 3, 4, 2, 5)).reshape(frames, height // 2, width_cells // 2, 4 * channels)
    return jnp.dot(layer_norm(grouped, gain_row), weight, preferred_element_type=jnp.float32).astype(jnp.bfloat16)

def reference(tokens, regions_one, regions_three, gain_one, projection_one, outward_one, table_one, merge_gain_one, merge_weight_one, merge_gain_two, merge_weight_two, gain_three, projection_three, outward_three, table_three, cotangent):

    def forward(inputs):
        normed_one = layer_norm(inputs, gain_one)
        mixed_one = shifted_attention(normed_one, regions_one, projection_one, outward_one, table_one, HEADS1)
        residual_one = (inputs.astype(jnp.float32) + mixed_one.astype(jnp.float32)).astype(jnp.bfloat16)
        merged_one = merge_patches(residual_one, merge_gain_one, merge_weight_one)
        merged_two = merge_patches(merged_one, merge_gain_two, merge_weight_two)
        normed_three = layer_norm(merged_two, gain_three)
        mixed_three = shifted_attention(normed_three, regions_three, projection_three, outward_three, table_three, HEADS3)
        return (merged_two.astype(jnp.float32) + mixed_three.astype(jnp.float32)).astype(jnp.bfloat16)
    section_three, pullback = jax.vjp(forward, tokens)
    grad_tokens = pullback(cotangent)[0]
    return (section_three, grad_tokens)
```

```python
import functools

import jax
import jax.numpy as jnp
import numpy as np
from jax import lax
from jax.experimental import pallas as pl
from jax.experimental.pallas import tpu as pltpu
from jax.sharding import PartitionSpec as P

HEADS1 = 4
HEADS3 = 16
WT = 4
WS = 7
ST = 2
SS = 3
EPSILON = 1e-05
LOG2E = 1.4426950408889634
HEAD = 32
SCALE = HEAD**-0.5
ROWS = WT * WS * 8
LANES = 256
SPAN = 1280
GONE = -1e30
BF = jnp.bfloat16
F32 = jnp.float32


def dot(a, b):
    return jnp.dot(a, b, preferred_element_type=F32)


def dot_nt(a, b):
    return lax.dot_general(a, b, (((1,), (1,)), ((), ())), preferred_element_type=F32)


def params(limit=48):
    return pltpu.CompilerParams(vmem_limit_bytes=limit * 1024 * 1024)


def normalise(x):
    centred = x - jnp.mean(x, -1, keepdims=True)
    rstd = lax.rsqrt(jnp.mean(centred * centred, -1, keepdims=True) + EPSILON)
    return centred * rstd, rstd


def normalise_back(grad, xhat, rstd):
    return rstd * (
        grad
        - jnp.mean(grad, -1, keepdims=True)
        - xhat * jnp.mean(grad * xhat, -1, keepdims=True)
    )


def only_head(rows, h):
    parts = []
    if h:
        parts.append(jnp.zeros((HEAD * h, LANES), rows.dtype))
    parts.append(rows)
    if h < 3:
        parts.append(jnp.zeros((HEAD * (3 - h), LANES), rows.dtype))
    return jnp.concatenate(parts, 0)


def lengthen(x):
    return jnp.concatenate([x, jnp.zeros((LANES - ROWS, x.shape[1]), x.dtype)], 0)


def region_mask(column, row):
    return jnp.where(column == row, 0.0, GONE).astype(F32)


def attend_four(k, qT, vT, mask, bias_at, keep_probs):
    outs, inverses = [], []
    for h in range(4):
        mine = slice(HEAD * h, HEAD * (h + 1))
        scores = dot(k, only_head(qT[mine], h)) + (bias_at(h) + mask)
        peak = jnp.max(scores, 0, keepdims=True)
        probs = jnp.exp2(scores - peak).astype(BF)
        keep_probs(h, probs)
        extended = jnp.concatenate([vT[mine, :ROWS], jnp.ones((16, ROWS), BF)], 0)
        out = dot(extended, probs)
        inverse = 1.0 / out[HEAD : HEAD + 1]
        outs.append(out[:HEAD] * inverse)
        inverses.append(inverse)
    return jnp.concatenate(outs, 0), inverses


def attend_four_back(v, qT, kT, oT, doT, inverse_at, probs_at):
    dk = dv = None
    dqs = []
    for h in range(4):
        mine = slice(HEAD * h, HEAD * (h + 1))
        scaled = doT[mine] * inverse_at(h)
        delta = jnp.sum(scaled * oT[mine], 0, keepdims=True)
        scaled = only_head(scaled.astype(BF), h)
        probs = probs_at(h)
        dprobs = dot(v, scaled)
        dscores = (probs.astype(F32) * (dprobs - delta)).astype(BF)
        dv_h = dot_nt(probs, scaled)
        dk_h = dot_nt(dscores, only_head(qT[mine], h))
        dv = dv_h if dv is None else dv + dv_h
        dk = dk_h if dk is None else dk + dk_h
        dqs.append(dot(kT[mine, :ROWS], dscores))
    dq = jnp.concatenate(dqs, 0).T[:ROWS] * SCALE
    return dq, dk * (1.0 / LOG2E), dv


def bias_kernel(x1_ref, x3_ref, s1_ref, s3_ref, o1_ref, o3_ref):
    for x_ref, s_ref, o_ref, heads in (
        (x1_ref, s1_ref, o1_ref, HEADS1),
        (x3_ref, s3_ref, o3_ref, HEADS3),
    ):
        chosen = s_ref[...]
        for tj in range(WT):
            rows = []
            for hj in range(WS):
                slabs = []
                for ti in range(WT):
                    start = (ti - tj + 3) * 169 + (6 - hj) * 13 + 6
                    low = start // 128 * 128
                    pair = x_ref[:, low : low + 256]
                    turn = start - low
                    slabs.append(pltpu.roll(pair, 256 - turn, 1)[:, :128] if turn else pair[:, :128])
                rows.append(jnp.concatenate(slabs, 1))
            left = jnp.concatenate(rows, 0)
            first = left.astype(BF)
            rest = left - first.astype(F32)
            second = rest.astype(BF)
            third = (rest - second.astype(F32)).astype(BF)
            got = dot(first, chosen) + dot(second, chosen) + dot(third, chosen)
            for hj in range(WS):
                for head in range(heads):
                    at = (hj * heads + head) * 8
                    o_ref[head, (tj * WS + hj) * 8 : (tj * WS + hj) * 8 + 8, :] = got[at : at + 8]


def column_order(section):
    return [(c + 4) % 7 if section == 3 else c for c in range(7)]


def chooser(section):
    chosen = np.zeros((WT * 128, LANES), np.float32)
    for ti in range(WT):
        for hi in range(WS):
            for c, wi in enumerate(column_order(section)):
                chosen[ti * 128 + 13 * hi + wi, ti * 56 + hi * 8 + c] = 1.0
    return jnp.asarray(chosen, BF)


def spread_table(table, section):
    flat = jnp.transpose(table) * LOG2E
    shifts = column_order(section) + [0]
    layers = [jnp.pad(flat, ((0, 0), (s, SPAN - flat.shape[1] - s))) for s in shifts]
    return jnp.stack(layers, 1).reshape(-1, SPAN)


def build_biases(table_one, table_three):
    return pl.pallas_call(
        bias_kernel,
        out_shape=(
            jax.ShapeDtypeStruct((HEADS1, ROWS, LANES), F32),
            jax.ShapeDtypeStruct((HEADS3, ROWS, LANES), F32),
        ),
        compiler_params=params(),
    )(spread_table(table_one, 1), spread_table(table_three, 3), chooser(1), chooser(3))


def put_rows(stage, frames, rows, values):
    values = values.astype(F32)
    stage[frames, rows, 0:28, :] = values
    stage[frames, rows, 28:36, :] = values[:, :, 0:8, :]


def cut_windows(stage, win):
    for hw in range(2):
        for ww in range(4):
            win[hw * 4 + ww] = stage[:, 7 * hw : 7 * hw + 7, 3 + 7 * ww : 11 + 7 * ww, :].reshape(
                ROWS, 128
            )


def join_windows(win, stage):
    for hw in range(2):
        for ww in range(4):
            stage[:, 7 * hw : 7 * hw + 7, 3 + 7 * ww : 11 + 7 * ww, :] = win[hw * 4 + ww].reshape(
                WT, WS, 8, 128
            )
    stage[:, :, 0:3, :] = stage[:, :, 28:31, :]


def front_kernel(late, *refs):
    n_in = 4 if late else 2
    pieces, refs = refs[:n_in], refs[n_in:]
    gain_ref, proj_ref, projT_ref, outw_ref, bias_ref, row_ref, col_ref = refs[:7]
    refs = refs[7:]
    n_out = 1 if late else 2
    outs, refs = refs[:n_out], refs[n_out:]
    xw_ref, kv_ref, t_ref, p_ref, o_ref, inv_ref, stage, win = refs
    step = pl.program_id(0)

    @pl.when(step == 0)
    def _():
        own = pieces[0]
        if late:
            put_rows(stage, slice(0, 2), slice(0, 11), own[2:4, 17:28])
            put_rows(stage, slice(2, 4), slice(0, 11), pieces[1][...])
            put_rows(stage, slice(0, 2), slice(11, 14), pieces[2][...])
            put_rows(stage, slice(2, 4), slice(11, 14), pieces[3][...])
        else:
            put_rows(stage, slice(0, 2), slice(0, 14), own[2:4, 3:17])
            put_rows(stage, slice(2, 4), slice(0, 14), pieces[1][...])
        cut_windows(stage, win)

    x = win[step]
    xw_ref[0] = x.astype(BF)
    xhat, _ = normalise(x)
    n = (xhat * gain_ref[...]).astype(BF)
    kv = dot(n, proj_ref[:, 128:]).astype(BF)
    kv_ref[0] = kv
    t = dot_nt(projT_ref[...], lengthen(n))
    qT = (t[:128] * (SCALE * LOG2E)).astype(BF)
    rest = t[128:].astype(BF)
    t_ref[0, :128] = qT
    t_ref[0, 128:] = rest[:128]
    mask = region_mask(col_ref[0], row_ref[0])

    def keep(h, probs):
        p_ref[0, h] = probs

    oT, inverses = attend_four(
        kv[:, :128], qT, rest[128:], mask, lambda h: bias_ref[h], keep
    )
    o_ref[0] = oT.astype(BF)
    inv_ref[0] = jnp.concatenate(inverses + inverses, 0)
    att = oT.T[:ROWS].astype(BF)
    mixed = dot(att, outw_ref[...]).astype(BF).astype(F32)
    win[step] = x + mixed

    @pl.when(step == 7)
    def _():
        join_windows(win, stage)
        if late:
            outs[0][...] = stage[:, :, 0:28, :].astype(BF)
        else:
            outs[0][...] = stage[:, 0:9, 0:28, :].astype(BF)
            outs[1][...] = stage[:, 9:14, 0:28, :].astype(BF)


def whole(shape):
    return pl.BlockSpec(shape, lambda i: (0,) * len(shape))


def each(shape):
    return pl.BlockSpec((1,) + shape, lambda i: (i,) + (0,) * len(shape))


SAVED = (
    ((ROWS, 128), BF),
    ((ROWS, 256), BF),
    ((256, LANES), BF),
    ((4, ROWS, LANES), BF),
    ((128, LANES), BF),
    ((8, LANES), F32),
)


def front(late, pieces, gain, proj, projT, outw, bias, row, col):
    consts = (gain, proj, projT, outw, bias)
    shapes = [(4, 14, 28, 128)] if late else [(4, 9, 28, 128), (4, 5, 28, 128)]
    out = pl.pallas_call(
        functools.partial(front_kernel, late),
        grid=(8,),
        in_specs=[whole(a.shape) for a in tuple(pieces) + consts]
        + [each((1, LANES)), each((ROWS, 1))],
        out_specs=[whole(s) for s in shapes] + [each(s) for s, _ in SAVED],
        out_shape=[jax.ShapeDtypeStruct(s, BF) for s in shapes]
        + [jax.ShapeDtypeStruct((8,) + s, d) for s, d in SAVED],
        scratch_shapes=[
            pltpu.VMEM((4, 14, 40, 128), F32),
            pltpu.VMEM((8, ROWS, 128), F32),
        ],
        compiler_params=params(),
    )(*pieces, *consts, row, col)
    return out[: len(shapes)], out[len(shapes) :]


def back_kernel(late, *refs):
    n_in = 1 if late else 2
    pieces, refs = refs[:n_in], refs[n_in:]
    gain_ref, proj_ref, outw_ref = refs[:3]
    xw_ref, kv_ref, t_ref, p_ref, o_ref, inv_ref = refs[3:9]
    refs = refs[9:]
    n_out = 4 if late else 2
    outs, refs = refs[:n_out], refs[n_out:]
    stage, win = refs
    step = pl.program_id(0)

    @pl.when(step == 0)
    def _():
        if late:
            put_rows(stage, slice(0, 4), slice(0, 14), pieces[0][...])
        else:
            put_rows(stage, slice(0, 4), slice(0, 9), pieces[0][...])
            put_rows(stage, slice(0, 4), slice(9, 14), pieces[1][...])
        cut_windows(stage, win)

    dr = win[step]
    doT = dot_nt(outw_ref[...], lengthen(dr.astype(BF)))
    dq, dk, dv = attend_four_back(
        kv_ref[0, :, 128:],
        t_ref[0, :128],
        t_ref[0, 128:],
        o_ref[0].astype(F32),
        doT,
        lambda h: inv_ref[0, h : h + 1],
        lambda h: p_ref[0, h],
    )
    dpacked = jnp.concatenate([dq.astype(BF), dk.astype(BF), dv.astype(BF)], 1)
    dn = dot_nt(dpacked, proj_ref[...])
    xhat, rstd = normalise(xw_ref[0].astype(F32))
    win[step] = dr + normalise_back(dn * gain_ref[...], xhat, rstd)

    @pl.when(step == 7)
    def _():
        join_windows(win, stage)
        if late:
            outs[0][...] = stage[0:2, 0:11, 0:28, :].astype(BF)
            outs[1][...] = stage[2:4, 0:11, 0:28, :].astype(BF)
            outs[2][...] = stage[0:2, 11:14, 0:28, :].astype(BF)
            outs[3][...] = stage[2:4, 11:14, 0:28, :].astype(BF)
        else:
            outs[0][...] = stage[0:2, :, 0:28, :].astype(BF)
            outs[1][...] = stage[2:4, :, 0:28, :].astype(BF)


def back(late, pieces, gain, proj, outw, saved):
    consts = (gain, proj, outw)
    if late:
        shapes = [(2, 11, 28, 128), (2, 11, 28, 128), (2, 3, 28, 128), (2, 3, 28, 128)]
    else:
        shapes = [(2, 14, 28, 128), (2, 14, 28, 128)]
    return pl.pallas_call(
        functools.partial(back_kernel, late),
        grid=(8,),
        in_specs=[whole(a.shape) for a in tuple(pieces) + consts] + [each(s) for s, _ in SAVED],
        out_specs=[whole(s) for s in shapes],
        out_shape=[jax.ShapeDtypeStruct(s, BF) for s in shapes],
        scratch_shapes=[
            pltpu.VMEM((4, 14, 40, 128), F32),
            pltpu.VMEM((8, ROWS, 128), F32),
        ],
        compiler_params=params(),
    )(*pieces, *consts, *saved)


def middle_kernel(
    resA_ref, resB_ref, resN_ref, cot_ref, cta_ref, cha_ref, cdg_ref,
    mg1_ref, mw1_ref, mg2_ref, mw2_ref, g3_ref, p3_ref, ow3_ref, bias_ref, row_ref, col_ref,
    dA_ref, dB_ref, dN_ref, so_ref, sta_ref, sha_ref, sdg_ref,
    stage, stage2, xhat1, rstd1, xhat2, rstd2, cotw, k_s, v_s, qT_s, kT_s, vT_s, probs_s, oT_s, inv_s, doT_s, dqkv_s,
):
    sources = [(resA_ref, i) for i in range(5)] + [(resB_ref, i) for i in range(14)]
    sources += [(resN_ref, i) for i in range(9)]
    for i, (ref, at) in enumerate(sources):
        stage[:, i // 2, i % 2, 0:28, :] = ref[:, at].astype(F32)
    stage[:, :, :, 28:32, :] = jnp.zeros((4, 14, 2, 4, 128), F32)
    cotw[...] = jnp.zeros((4, 7, 8, 512), F32)
    cotw[0:2, 0:4, 0:7, :] = cot_ref[2:4, 3:7].astype(F32)
    cotw[2:4, 0:4, 0:7, :] = cta_ref[...].astype(F32)
    cotw[0:2, 4:7, 0:7, :] = cha_ref[...].astype(F32)
    cotw[2:4, 4:7, 0:7, :] = cdg_ref[...].astype(F32)

    def merge_one(f, _):
        pieces = [
            stage[f, :, q % 2, pl.ds(q // 2, 16, stride=2), :].reshape(ROWS, 128) for q in range(4)
        ]
        xhat, rstd = normalise(jnp.concatenate(pieces, 1))
        xhat1[f] = xhat
        rstd1[f] = jnp.broadcast_to(rstd, (ROWS, 128))
        merged = dot((xhat * mg1_ref[...]).astype(BF), mw1_ref[...]).astype(BF).astype(F32)
        for half in range(2):
            stage2[half, f] = merged[:, 128 * half : 128 * half + 128].reshape(7, 2, 16, 128)
        return 0

    lax.fori_loop(0, 4, merge_one, 0)
    pieces = [
        stage2[half, :, :, q % 2, pl.ds(q // 2, 8, stride=2), :].reshape(ROWS, 128)
        for q in range(4)
        for half in range(2)
    ]
    xhat, rstd = normalise(jnp.concatenate(pieces, 1))
    xhat2[...] = xhat
    rstd2[...] = jnp.broadcast_to(rstd, (ROWS, 128))
    merged_two = dot((xhat * mg2_ref[...]).astype(BF), mw2_ref[...]).astype(BF).astype(F32)
    xhat3, rstd3 = normalise(merged_two)
    n3 = (xhat3 * g3_ref[...]).astype(BF)
    for g in range(4):
        at = slice(128 * g, 128 * g + 128)
        q = dot(n3, p3_ref[:, 128 * g : 128 * g + 128])
        k = dot(n3, p3_ref[:, 512 + 128 * g : 640 + 128 * g])
        v = dot(n3, p3_ref[:, 1024 + 128 * g : 1152 + 128 * g])
        k_s[g] = k.astype(BF)
        v_s[g] = v.astype(BF)
        qT_s[g] = (lengthen(q).T * (SCALE * LOG2E)).astype(BF)
        kT_s[g] = lengthen(k).T.astype(BF)
        vT_s[g] = lengthen(v).T.astype(BF)
    mask = region_mask(col_ref[...], row_ref[...])

    def heads(g, _):
        def keep(h, probs):
            probs_s[g * 4 + h] = probs

        oT, inverses = attend_four(
            k_s[g], qT_s[g], vT_s[g], mask, lambda h: bias_ref[g * 4 + h], keep
        )
        oT_s[g] = oT
        inv_s[g] = jnp.concatenate(inverses + inverses, 0)
        return 0

    lax.fori_loop(0, 4, heads, 0)
    att = jnp.concatenate([oT_s[g].T[:ROWS].astype(BF) for g in range(4)], 1)
    mixed = dot(att, ow3_ref[...]).astype(BF).astype(F32)
    section = (merged_two + mixed).reshape(4, 7, 8, 512)
    so_ref[...] = section[0:2, 0:4, 0:7].astype(BF)
    sta_ref[...] = section[2:4, 0:4, 0:7].astype(BF)
    sha_ref[...] = section[0:2, 4:7, 0:7].astype(BF)
    sdg_ref[...] = section[2:4, 4:7, 0:7].astype(BF)

    cot = cotw[...].reshape(ROWS, 512)
    cot_long = lengthen(cot.astype(BF))
    for g in range(4):
        doT_s[g] = dot_nt(ow3_ref[128 * g : 128 * g + 128, :], cot_long)

    def heads_back(g, _):
        dq, dk, dv = attend_four_back(
            v_s[g], qT_s[g], kT_s[g], oT_s[g], doT_s[g],
            lambda h: inv_s[g, h : h + 1], lambda h: probs_s[g * 4 + h],
        )
        dqkv_s[g] = dq.astype(BF)
        dqkv_s[4 + g] = dk.astype(BF)
        dqkv_s[8 + g] = dv.astype(BF)
        return 0

    lax.fori_loop(0, 4, heads_back, 0)
    dpacked = jnp.concatenate([dqkv_s[i] for i in range(12)], 1)
    dn3 = dot_nt(dpacked, p3_ref[...])
    dm2 = cot + normalise_back(dn3 * g3_ref[...], xhat3, rstd3)
    dn2 = dot_nt(dm2.astype(BF), mw2_ref[...])
    dg2 = normalise_back(dn2 * mg2_ref[...], xhat2[...], rstd2[:, 0:1])
    for q in range(4):
        for half in range(2):
            at = 256 * q + 128 * half
            stage2[half, :, :, q % 2, pl.ds(q // 2, 8, stride=2), :] = dg2[:, at : at + 128].reshape(
                4, 7, 8, 128
            )

    def merge_one_back(f, _):
        dm1 = jnp.concatenate([stage2[half, f].reshape(ROWS, 128) for half in range(2)], 1).astype(BF)
        dn1 = dot_nt(dm1, mw1_ref[...])
        dg1 = normalise_back(dn1 * mg1_ref[...], xhat1[f], rstd1[f, :, 0:1])
        for q in range(4):
            stage[f, :, q % 2, pl.ds(q // 2, 16, stride=2), :] = dg1[
                :, 128 * q : 128 * q + 128
            ].reshape(14, 16, 128)
        return 0

    lax.fori_loop(0, 4, merge_one_back, 0)
    targets = [(dA_ref, i) for i in range(5)] + [(dB_ref, i) for i in range(14)]
    targets += [(dN_ref, i) for i in range(9)]
    for i, (ref, at) in enumerate(targets):
        ref[:, at] = stage[:, i // 2, i % 2, 0:28, :].astype(BF)


def middle(*operands):
    shapes = [
        (4, 5, 28, 128), (4, 14, 28, 128), (4, 9, 28, 128),
        (2, 4, 7, 512), (2, 4, 7, 512), (2, 3, 7, 512), (2, 3, 7, 512),
    ]
    return pl.pallas_call(
        middle_kernel,
        out_shape=[jax.ShapeDtypeStruct(s, BF) for s in shapes],
        scratch_shapes=[
            pltpu.VMEM((4, 14, 2, 32, 128), F32),
            pltpu.VMEM((2, 4, 7, 2, 16, 128), F32),
            pltpu.VMEM((4, ROWS, 512), F32),
            pltpu.VMEM((4, ROWS, 128), F32),
            pltpu.VMEM((ROWS, 1024), F32),
            pltpu.VMEM((ROWS, 128), F32),
            pltpu.VMEM((4, 7, 8, 512), F32),
            pltpu.VMEM((4, ROWS, 128), BF),
            pltpu.VMEM((4, ROWS, 128), BF),
            pltpu.VMEM((4, 128, LANES), BF),
            pltpu.VMEM((4, 128, LANES), BF),
            pltpu.VMEM((4, 128, LANES), BF),
            pltpu.VMEM((16, ROWS, LANES), BF),
            pltpu.VMEM((4, 128, LANES), F32),
            pltpu.VMEM((4, 8, LANES), F32),
            pltpu.VMEM((4, 128, LANES), F32),
            pltpu.VMEM((12, ROWS, 128), BF),
        ],
        compiler_params=params(),
    )(*operands)


def padded_ids(ids, section):
    frames, height, width = ids.shape
    if section == 3:
        ids = jnp.roll(ids, SS, 2)
    ids = ids.reshape(4, height // 7, 7, width // 7, 7)
    ids = jnp.pad(ids, ((0, 0),) * 4 + ((0, 1),), constant_values=-1)
    ids = jnp.transpose(ids, (1, 3, 0, 2, 4)).reshape(-1, ROWS)
    row = jnp.pad(ids, ((0, 0), (0, LANES - ROWS)), constant_values=-1)
    return row[:, None, :], ids[:, :, None]


def send(values, axes, by):
    if len(axes) == 1:
        n = lax.axis_size(axes[0])
        pairs = [(i, (i + by) % n) for i in range(n)]
        return lax.ppermute(values, axes[0], pairs)
    n, m = lax.axis_size(axes[0]), lax.axis_size(axes[1])
    pairs = [
        (i * m + j, (i + by) % n * m + (j + by) % m) for i in range(n) for j in range(m)
    ]
    return lax.ppermute(values, axes, pairs)


def per_device(
    tokens,
    regions_one,
    regions_three,
    gain_one,
    projection_one,
    outward_one,
    table_one,
    merge_gain_one,
    merge_weight_one,
    merge_gain_two,
    merge_weight_two,
    gain_three,
    projection_three,
    outward_three,
    table_three,
    cotangent,
):
    both = ("ha", "ta")
    ta_early = send(tokens[:2, 3:17], ("ta",), -1)
    ha_late = send(tokens[2:, :3], ("ha",), -1)
    dg_late = send(tokens[:2, :3], both, -1)
    ta_late = send(tokens[:2, 17:], ("ta",), -1)
    cot_ta = send(cotangent[:2, 3:], ("ta",), -1)
    cot_ha = send(cotangent[2:, :3], ("ha",), -1)
    cot_dg = send(cotangent[:2, :3], both, -1)

    bias_one, bias_three = build_biases(table_one, table_three)
    row_one, col_one = padded_ids(regions_one, 1)
    row_three, col_three = padded_ids(regions_three, 3)
    gain = gain_one[None]
    projT = jnp.transpose(projection_one)

    args = (gain, projection_one, projT, outward_one, bias_one)
    (res_send, res_a), saved_a = front(
        False, (tokens, ta_early), *args, row_one[:8], col_one[:8]
    )
    res_next = send(res_send, ("ha",), -1)
    (res_b,), saved_b = front(
        True, (tokens, ta_late, ha_late, dg_late), *args, row_one[8:], col_one[8:]
    )
    d_a, d_b, d_send, sec_own, sec_ta, sec_ha, sec_dg = middle(
        res_a, res_b, res_next, cotangent, cot_ta, cot_ha, cot_dg,
        merge_gain_one[None], merge_weight_one, merge_gain_two[None], merge_weight_two,
        gain_three[None], projection_three, outward_three, bias_three, row_three[0], col_three[0],
    )
    d_prev = send(d_send, ("ha",), 1)
    sec_ta = send(sec_ta, ("ta",), 1)
    sec_ha = send(sec_ha, ("ha",), 1)
    sec_dg = send(sec_dg, both, 1)
    own_b, ta_b, ha_b, dg_b = back(True, (d_b,), gain, projection_one, outward_one, saved_b)
    ta_b = send(ta_b, ("ta",), 1)
    ha_b = send(ha_b, ("ha",), 1)
    dg_b = send(dg_b, both, 1)
    own_a, ta_a = back(False, (d_prev, d_a), gain, projection_one, outward_one, saved_a)
    ta_a = send(ta_a, ("ta",), 1)

    def join(corner, side, rest):
        return jnp.concatenate(
            [jnp.concatenate([corner] + side, 1), jnp.concatenate(rest, 1)], 0
        )

    section = join(sec_dg, [sec_ta], [sec_ha, sec_own])
    grad = join(dg_b, [ta_a, ta_b], [ha_b, own_a, own_b])
    return (section, grad)


def solution(mesh):
    tile = P(("col", "ta"), "ha", None, None)
    ids = P(("col", "ta"), "ha", None)
    in_specs = (tile, ids, ids) + (P(),) * 12 + (tile,)
    return jax.shard_map(
        per_device, mesh=mesh, in_specs=in_specs, out_specs=(tile, tile), check_vma=False
    )
```

```python
import functools

import jax
import jax.numpy as jnp
import numpy as np
from jax import lax
from jax.experimental import pallas as pl
from jax.experimental.pallas import tpu as pltpu
from jax.sharding import PartitionSpec as P

HEADS1 = 4
HEADS3 = 16
WT = 4
WS = 7
ST = 2
SS = 3
EPSILON = 1e-05
LOG2E = 1.4426950408889634
HEAD = 32
SCALE = HEAD**-0.5
ROWS = WT * WS * 8
LANES = 256
SPAN = 1280
GONE = -1e30
PER_STEP = 2
STEPS = 8 // PER_STEP
BF = jnp.bfloat16
F32 = jnp.float32


def dot(a, b):
    return jnp.dot(a, b, preferred_element_type=F32)


def dot_nt(a, b):
    return lax.dot_general(a, b, (((1,), (1,)), ((), ())), preferred_element_type=F32)


def params(limit=60):
    return pltpu.CompilerParams(vmem_limit_bytes=limit * 1024 * 1024)


def normalise(x):
    centred = x - jnp.mean(x, -1, keepdims=True)
    rstd = lax.rsqrt(jnp.mean(centred * centred, -1, keepdims=True) + EPSILON)
    return centred * rstd, rstd


def normalise_back(grad, xhat, rstd):
    return rstd * (
        grad
        - jnp.mean(grad, -1, keepdims=True)
        - xhat * jnp.mean(grad * xhat, -1, keepdims=True)
    )


def head_rows(x, h):
    return x[HEAD * h : HEAD * (h + 1)]


def head_of_lane(shape):
    return lax.broadcasted_iota(jnp.int32, shape, 1) // HEAD


def by_head(x):
    lane = head_of_lane((1, 128))
    return jnp.concatenate([x * (lane == h).astype(F32).astype(BF) for h in range(4)], 0)


def pick_heads(stacked):
    lane = head_of_lane((ROWS, 128))
    got = stacked[:ROWS]
    for h in range(1, 4):
        got = jnp.where(lane == h, stacked[ROWS * h : ROWS * (h + 1)], got)
    return got


def lengthen(x):
    return jnp.concatenate([x, jnp.zeros((LANES - ROWS, x.shape[1]), x.dtype)], 0)


def region_mask(row):
    wide = jnp.broadcast_to(row.astype(F32), (128, LANES))
    column = wide.T[:ROWS]
    column = jnp.concatenate([column, column], 1)
    return jnp.where(column == wide[0:1], 0.0, GONE).astype(F32)


def attend_four(windows):
    scores = [dot(by_head(k), qT) for k, qT, _, _, _, _ in windows]
    results = []
    for s, (_, _, vT, mask, bias_at, keep_probs) in zip(scores, windows):
        outs, inverses = [], []
        for h in range(4):
            biased = s[ROWS * h : ROWS * (h + 1)] + (bias_at(h) + mask)
            peak = jnp.max(biased, 0, keepdims=True)
            probs = jnp.exp2(biased - peak).astype(BF)
            keep_probs(h, probs)
            extended = jnp.concatenate([head_rows(vT, h)[:, :ROWS], jnp.ones((16, ROWS), BF)], 0)
            out = dot(extended, probs)
            inverse = 1.0 / out[HEAD : HEAD + 1]
            outs.append(out[:HEAD] * inverse)
            inverses.append(inverse)
        results.append((jnp.concatenate(outs, 0), jnp.concatenate(inverses + inverses, 0)))
    return results


def attend_four_back(windows):
    first = []
    for v, qT, kT, oT, doT, inverse, probs_at in windows:
        scaled, deltas = [], []
        for h in range(4):
            part = head_rows(doT, h) * inverse[h : h + 1]
            deltas.append(jnp.sum(part * head_rows(oT, h), 0, keepdims=True))
            scaled.append(part)
        scaled = jnp.concatenate(scaled, 0).astype(BF)
        first.append((scaled, deltas, dot(by_head(v), scaled)))
    results = []
    for (scaled, deltas, dprobs), (v, qT, kT, oT, doT, inverse, probs_at) in zip(first, windows):
        probs = [probs_at(h) for h in range(4)]
        dscores = [
            (probs[h].astype(F32) * (dprobs[ROWS * h : ROWS * (h + 1)] - deltas[h])).astype(BF)
            for h in range(4)
        ]
        dv = pick_heads(dot_nt(jnp.concatenate(probs, 0), scaled))
        dk = pick_heads(dot_nt(jnp.concatenate(dscores, 0), qT))
        dqT = jnp.concatenate(
            [dot(head_rows(kT, h)[:, :ROWS], dscores[h]) for h in range(4)], 0
        )
        results.append((dqT.T[:ROWS] * SCALE, dk * (1.0 / LOG2E), dv))
    return results


def bias_kernel(t1_ref, t3_ref, s1_ref, s3_ref, o1_ref, o3_ref, x_ref):
    for t_ref, s_ref, o_ref, heads, section in (
        (t1_ref, s1_ref, o1_ref, HEADS1, 1),
        (t3_ref, s3_ref, o3_ref, HEADS3, 3),
    ):
        for head in range(heads):
            row = jnp.broadcast_to(t_ref[head : head + 1, :], (8, SPAN))
            turned = pltpu.roll(row, 0, 1, stride=1, stride_axis=0)
            if section == 3:
                turned = jnp.concatenate([turned[4:7], turned[0:5]], 0)
            x_ref[8 * head : 8 * head + 8, :] = turned
        chosen = s_ref[...]
        for tj in range(WT):
            rows = []
            for hj in range(WS):
                slabs = []
                for ti in range(WT):
                    start = (ti - tj + 3) * 169 + (6 - hj) * 13 + 6
                    low = start // 128 * 128
                    pair = x_ref[0 : 8 * heads, low : low + 256]
                    turn = start - low
                    slabs.append(pltpu.roll(pair, 256 - turn, 1)[:, :128] if turn else pair[:, :128])
                rows.append(jnp.concatenate(slabs, 1))
            left = jnp.concatenate(rows, 0)
            first = left.astype(BF)
            rest = left - first.astype(F32)
            second = rest.astype(BF)
            third = (rest - second.astype(F32)).astype(BF)
            got = dot(first, chosen) + dot(second, chosen) + dot(third, chosen)
            for hj in range(WS):
                for head in range(heads):
                    at = (hj * heads + head) * 8
                    o_ref[head, (tj * WS + hj) * 8 : (tj * WS + hj) * 8 + 8, :] = got[at : at + 8]


def column_order(section):
    return [(c + 4) % 7 if section == 3 else c for c in range(7)]


def chooser(section):
    chosen = np.zeros((WT * 128, LANES), np.float32)
    for ti in range(WT):
        for hi in range(WS):
            for c, wi in enumerate(column_order(section)):
                chosen[ti * 128 + 13 * hi + wi, ti * 56 + hi * 8 + c] = 1.0
    return jnp.asarray(chosen, BF)


def widen_table(table):
    return jnp.pad(jnp.transpose(table) * LOG2E, ((0, 0), (0, SPAN - table.shape[0])))


def build_biases(table_one, table_three):
    return pl.pallas_call(
        bias_kernel,
        out_shape=(
            jax.ShapeDtypeStruct((HEADS1, ROWS, LANES), F32),
            jax.ShapeDtypeStruct((HEADS3, ROWS, LANES), F32),
        ),
        scratch_shapes=[pltpu.VMEM((HEADS3 * 8, SPAN), F32)],
        compiler_params=params(),
    )(widen_table(table_one), widen_table(table_three), chooser(1), chooser(3))


def fold(values):
    return jnp.concatenate([values[..., 128 * g : 128 * g + 128] for g in range(4)], -2)


def unfold(values):
    return jnp.concatenate([values[..., 7 * g : 7 * g + 7, :] for g in range(4)], -1)


def pack_kernel(tok_ref, cot_ref, early_ref, late_ref, ha_ref, dg_ref):
    early_ref[...] = tok_ref[0:2, 3:17]
    late_ref[:, 0:11] = tok_ref[0:2, 17:28]
    late_ref[:, 11:15] = fold(cot_ref[0:2, 3:7].astype(F32)).astype(BF)
    ha_ref[:, 0:3] = tok_ref[2:4, 0:3]
    ha_ref[:, 3:6] = fold(cot_ref[2:4, 0:3].astype(F32)).astype(BF)
    dg_ref[:, 0:3] = tok_ref[0:2, 0:3]
    dg_ref[:, 3:6] = fold(cot_ref[0:2, 0:3].astype(F32)).astype(BF)


def pack(tokens, cotangent):
    return pl.pallas_call(
        pack_kernel,
        out_shape=[
            jax.ShapeDtypeStruct((2, n, 28, 128), BF) for n in (14, 15, 6, 6)
        ],
        compiler_params=params(),
    )(tokens, cotangent)


def put_rows(stage, frames, rows, values):
    values = values.astype(F32)
    stage[frames, rows, 0:28, :] = values
    stage[frames, rows, 28:36, :] = values[:, :, 0:8, :]


def cut_windows(stage, win):
    for hw in range(2):
        for ww in range(4):
            win[hw * 4 + ww] = stage[:, 7 * hw : 7 * hw + 7, 3 + 7 * ww : 11 + 7 * ww, :].reshape(
                ROWS, 128
            )


def join_windows(win, stage):
    for hw in range(2):
        for ww in range(4):
            stage[:, 7 * hw : 7 * hw + 7, 3 + 7 * ww : 11 + 7 * ww, :] = win[hw * 4 + ww].reshape(
                WT, WS, 8, 128
            )
    stage[:, :, 0:3, :] = stage[:, :, 28:31, :]


def front_kernel(late, *refs):
    n_in = 4 if late else 2
    pieces, refs = refs[:n_in], refs[n_in:]
    gain_ref, proj_ref, projT_ref, outw_ref, bias_ref, row_ref = refs[:6]
    refs = refs[6:]
    n_out = 1 if late else 2
    outs, refs = refs[:n_out], refs[n_out:]
    xw_ref, kv_ref, t_ref, p_ref, o_ref, inv_ref, stage, win = refs
    step = pl.program_id(0)

    @pl.when(step == 0)
    def _():
        own = pieces[0]
        if late:
            put_rows(stage, slice(0, 2), slice(0, 11), own[2:4, 17:28])
            put_rows(stage, slice(2, 4), slice(0, 11), pieces[1][:, 0:11])
            put_rows(stage, slice(0, 2), slice(11, 14), pieces[2][:, 0:3])
            put_rows(stage, slice(2, 4), slice(11, 14), pieces[3][:, 0:3])
        else:
            put_rows(stage, slice(0, 2), slice(0, 14), own[2:4, 3:17])
            put_rows(stage, slice(2, 4), slice(0, 14), pieces[1][...])
        cut_windows(stage, win)

    xs, operands = [], []
    for u in range(PER_STEP):
        x = win[step * PER_STEP + u]
        xs.append(x)
        xw_ref[u] = x.astype(BF)
        xhat, _ = normalise(x)
        n = (xhat * gain_ref[...]).astype(BF)
        kv = dot(n, proj_ref[:, 128:]).astype(BF)
        kv_ref[u] = kv
        t = dot_nt(projT_ref[...], lengthen(n))
        qT = (t[:128] * (SCALE * LOG2E)).astype(BF)
        rest = t[128:].astype(BF)
        t_ref[u, :128] = qT
        t_ref[u, 128:] = rest[:128]

        def keep(h, probs, u=u):
            p_ref[u, h] = probs

        operands.append(
            (kv[:, :128], qT, rest[128:], region_mask(row_ref[u]), lambda h: bias_ref[h], keep)
        )
    for u, (oT, inverse) in enumerate(attend_four(operands)):
        o_ref[u] = oT.astype(BF)
        inv_ref[u] = inverse
        mixed = dot(oT.T[:ROWS].astype(BF), outw_ref[...]).astype(BF).astype(F32)
        win[step * PER_STEP + u] = xs[u] + mixed

    @pl.when(step == STEPS - 1)
    def _():
        join_windows(win, stage)
        if late:
            outs[0][...] = stage[:, :, 0:28, :].astype(BF)
        else:
            outs[0][...] = stage[:, 0:9, 0:28, :].astype(BF)
            outs[1][...] = stage[:, 9:14, 0:28, :].astype(BF)


def whole(shape):
    return pl.BlockSpec(shape, lambda i: (0,) * len(shape))


def each(shape):
    return pl.BlockSpec((PER_STEP,) + shape, lambda i: (i,) + (0,) * len(shape))


SAVED = (
    ((ROWS, 128), BF),
    ((ROWS, 256), BF),
    ((256, LANES), BF),
    ((4, ROWS, LANES), BF),
    ((128, LANES), BF),
    ((8, LANES), F32),
)


def front(late, pieces, gain, proj, projT, outw, bias, row):
    consts = (gain, proj, projT, outw, bias)
    shapes = [(4, 14, 28, 128)] if late else [(4, 9, 28, 128), (4, 5, 28, 128)]
    out = pl.pallas_call(
        functools.partial(front_kernel, late),
        grid=(STEPS,),
        in_specs=[whole(a.shape) for a in tuple(pieces) + consts] + [each((1, LANES))],
        out_specs=[whole(s) for s in shapes] + [each(s) for s, _ in SAVED],
        out_shape=[jax.ShapeDtypeStruct(s, BF) for s in shapes]
        + [jax.ShapeDtypeStruct((8,) + s, d) for s, d in SAVED],
        scratch_shapes=[
            pltpu.VMEM((4, 14, 40, 128), F32),
            pltpu.VMEM((8, ROWS, 128), F32),
        ],
        compiler_params=params(),
    )(*pieces, *consts, row)
    return out[: len(shapes)], out[len(shapes) :]


def back_kernel(late, *refs):
    n_in = 4 if late else 2
    pieces, refs = refs[:n_in], refs[n_in:]
    gain_ref, proj_ref, outw_ref = refs[:3]
    xw_ref, kv_ref, t_ref, p_ref, o_ref, inv_ref = refs[3:9]
    refs = refs[9:]
    n_out = 4 if late else 2
    outs, refs = refs[:n_out], refs[n_out:]
    stage, win = refs
    step = pl.program_id(0)

    @pl.when(step == 0)
    def _():
        if late:
            put_rows(stage, slice(0, 4), slice(0, 14), pieces[0][...])
            outs[1][:, 11:15] = pieces[1][...]
            outs[2][:, 3:6] = pieces[2][...]
            outs[3][:, 3:6] = pieces[3][...]
        else:
            put_rows(stage, slice(0, 4), slice(0, 9), pieces[0][...])
            put_rows(stage, slice(0, 4), slice(9, 14), pieces[1][...])
        cut_windows(stage, win)

    drs, operands = [], []
    for u in range(PER_STEP):
        dr = win[step * PER_STEP + u]
        drs.append(dr)
        operands.append(
            (
                kv_ref[u, :, 128:],
                t_ref[u, :128],
                t_ref[u, 128:],
                o_ref[u].astype(F32),
                dot_nt(outw_ref[...], lengthen(dr.astype(BF))),
                inv_ref[u],
                lambda h, u=u: p_ref[u, h],
            )
        )
    for u, (dq, dk, dv) in enumerate(attend_four_back(operands)):
        dpacked = jnp.concatenate([dq.astype(BF), dk.astype(BF), dv.astype(BF)], 1)
        dn = dot_nt(dpacked, proj_ref[...])
        xhat, rstd = normalise(xw_ref[u].astype(F32))
        win[step * PER_STEP + u] = drs[u] + normalise_back(dn * gain_ref[...], xhat, rstd)

    @pl.when(step == STEPS - 1)
    def _():
        join_windows(win, stage)
        if late:
            outs[0][...] = stage[0:2, 0:11, 0:28, :].astype(BF)
            outs[1][:, 0:11] = stage[2:4, 0:11, 0:28, :].astype(BF)
            outs[2][:, 0:3] = stage[0:2, 11:14, 0:28, :].astype(BF)
            outs[3][:, 0:3] = stage[2:4, 11:14, 0:28, :].astype(BF)
        else:
            outs[0][...] = stage[0:2, :, 0:28, :].astype(BF)
            outs[1][...] = stage[2:4, :, 0:28, :].astype(BF)


def back(late, pieces, gain, proj, outw, saved):
    consts = (gain, proj, outw)
    if late:
        shapes = [(2, n, 28, 128) for n in (11, 15, 6, 6)]
    else:
        shapes = [(2, 14, 28, 128), (2, 14, 28, 128)]
    return pl.pallas_call(
        functools.partial(back_kernel, late),
        grid=(STEPS,),
        in_specs=[whole(a.shape) for a in tuple(pieces) + consts] + [each(s) for s, _ in SAVED],
        out_specs=[whole(s) for s in shapes],
        out_shape=[jax.ShapeDtypeStruct(s, BF) for s in shapes],
        scratch_shapes=[
            pltpu.VMEM((4, 14, 40, 128), F32),
            pltpu.VMEM((8, ROWS, 128), F32),
        ],
        compiler_params=params(),
    )(*pieces, *consts, *saved)


def middle_kernel(
    resA_ref, resB_ref, resN_ref, cot_ref, cta_ref, cha_ref, cdg_ref,
    mg1_ref, mg2_ref, g3_ref, row_ref, mw1_hbm, mw2_hbm, p3_hbm, bias_hbm, ow3_hbm,
    dA_ref, dB_ref, dN_ref, so_ref, sta_ref, sha_ref, sdg_ref,
    stage, stage2, xhat1, rstd1, xhat2, rstd2, cotw, k_s, v_s, qT_s, kT_s, vT_s, probs_s, oT_s, inv_s, doT_s, dqkv_s,
    mw1_ref, mw2_ref, p3_ref, bias_ref, ow3_ref, sems,
):
    fetches = [
        pltpu.make_async_copy(there, here, sems.at[i])
        for i, (there, here) in enumerate(
            (
                (mw1_hbm, mw1_ref),
                (mw2_hbm, mw2_ref),
                (p3_hbm, p3_ref),
                (bias_hbm, bias_ref),
                (ow3_hbm, ow3_ref),
            )
        )
    ]
    for fetch in fetches:
        fetch.start()
    sources = [(resA_ref, i) for i in range(5)] + [(resB_ref, i) for i in range(14)]
    sources += [(resN_ref, i) for i in range(9)]
    for i, (ref, at) in enumerate(sources):
        stage[:, i // 2, i % 2, 0:28, :] = ref[:, at].astype(F32)
    stage[:, :, :, 28:32, :] = jnp.zeros((4, 14, 2, 4, 128), F32)
    cotw[...] = jnp.zeros((4, 7, 8, 512), F32)
    cotw[0:2, 0:4, 0:7, :] = cot_ref[2:4, 3:7].astype(F32)
    cotw[2:4, 0:4, 0:7, :] = unfold(cta_ref[:, 11:15].astype(F32))
    cotw[0:2, 4:7, 0:7, :] = unfold(cha_ref[:, 3:6].astype(F32))
    cotw[2:4, 4:7, 0:7, :] = unfold(cdg_ref[:, 3:6].astype(F32))

    def merge_one(f, _):
        pieces = [
            stage[f, :, q % 2, pl.ds(q // 2, 16, stride=2), :].reshape(ROWS, 128) for q in range(4)
        ]
        xhat, rstd = normalise(jnp.concatenate(pieces, 1))
        xhat1[f] = xhat
        rstd1[f] = jnp.broadcast_to(rstd, (ROWS, 128))
        merged = dot((xhat * mg1_ref[...]).astype(BF), mw1_ref[...]).astype(BF).astype(F32)
        for half in range(2):
            stage2[half, f] = merged[:, 128 * half : 128 * half + 128].reshape(7, 2, 16, 128)
        return 0

    fetches[0].wait()
    lax.fori_loop(0, 4, merge_one, 0)
    fetches[1].wait()
    pieces = [
        stage2[half, :, :, q % 2, pl.ds(q // 2, 8, stride=2), :].reshape(ROWS, 128)
        for q in range(4)
        for half in range(2)
    ]
    xhat, rstd = normalise(jnp.concatenate(pieces, 1))
    xhat2[...] = xhat
    rstd2[...] = jnp.broadcast_to(rstd, (ROWS, 128))
    merged_two = dot((xhat * mg2_ref[...]).astype(BF), mw2_ref[...]).astype(BF).astype(F32)
    xhat3, rstd3 = normalise(merged_two)
    n3 = (xhat3 * g3_ref[...]).astype(BF)
    fetches[2].wait()
    for g in range(4):
        at = slice(128 * g, 128 * g + 128)
        q = dot(n3, p3_ref[:, 128 * g : 128 * g + 128])
        k = dot(n3, p3_ref[:, 512 + 128 * g : 640 + 128 * g])
        v = dot(n3, p3_ref[:, 1024 + 128 * g : 1152 + 128 * g])
        k_s[g] = k.astype(BF)
        v_s[g] = v.astype(BF)
        qT_s[g] = (lengthen(q).T * (SCALE * LOG2E)).astype(BF)
        kT_s[g] = lengthen(k).T.astype(BF)
        vT_s[g] = lengthen(v).T.astype(BF)
    mask = region_mask(row_ref[...])
    fetches[3].wait()

    def heads(g, _):
        def keep(h, probs):
            probs_s[g * 4 + h] = probs

        operands = (k_s[g], qT_s[g], vT_s[g], mask, lambda h: bias_ref[g * 4 + h], keep)
        ((oT_s[g], inv_s[g]),) = attend_four([operands])
        return 0

    lax.fori_loop(0, 4, heads, 0)
    fetches[4].wait()
    att = jnp.concatenate([oT_s[g].T[:ROWS].astype(BF) for g in range(4)], 1)
    mixed = dot(att, ow3_ref[...]).astype(BF).astype(F32)
    section = (merged_two + mixed).reshape(4, 7, 8, 512)
    section = fold(section[:, :, 0:7])
    so_ref[...] = section[0:2, 0:4].astype(BF)
    sta_ref[...] = section[2:4, 0:4].astype(BF)
    sha_ref[...] = section[0:2, 4:7].astype(BF)
    sdg_ref[...] = section[2:4, 4:7].astype(BF)

    cot = cotw[...].reshape(ROWS, 512)
    cot_long = lengthen(cot.astype(BF))
    for g in range(4):
        doT_s[g] = dot_nt(ow3_ref[128 * g : 128 * g + 128, :], cot_long)

    def heads_back(g, _):
        operands = (
            v_s[g], qT_s[g], kT_s[g], oT_s[g], doT_s[g], inv_s[g], lambda h: probs_s[g * 4 + h]
        )
        ((dq, dk, dv),) = attend_four_back([operands])
        dqkv_s[g] = dq.astype(BF)
        dqkv_s[4 + g] = dk.astype(BF)
        dqkv_s[8 + g] = dv.astype(BF)
        return 0

    lax.fori_loop(0, 4, heads_back, 0)
    dpacked = jnp.concatenate([dqkv_s[i] for i in range(12)], 1)
    dn3 = dot_nt(dpacked, p3_ref[...])
    dm2 = cot + normalise_back(dn3 * g3_ref[...], xhat3, rstd3)
    dn2 = dot_nt(dm2.astype(BF), mw2_ref[...])
    dg2 = normalise_back(dn2 * mg2_ref[...], xhat2[...], rstd2[:, 0:1])
    for q in range(4):
        for half in range(2):
            at = 256 * q + 128 * half
            stage2[half, :, :, q % 2, pl.ds(q // 2, 8, stride=2), :] = dg2[:, at : at + 128].reshape(
                4, 7, 8, 128
            )

    def merge_one_back(f, _):
        dm1 = jnp.concatenate([stage2[half, f].reshape(ROWS, 128) for half in range(2)], 1).astype(BF)
        dn1 = dot_nt(dm1, mw1_ref[...])
        dg1 = normalise_back(dn1 * mg1_ref[...], xhat1[f], rstd1[f, :, 0:1])
        for q in range(4):
            stage[f, :, q % 2, pl.ds(q // 2, 16, stride=2), :] = dg1[
                :, 128 * q : 128 * q + 128
            ].reshape(14, 16, 128)
        return 0

    lax.fori_loop(0, 4, merge_one_back, 0)
    targets = [(dA_ref, i) for i in range(5)] + [(dB_ref, i) for i in range(14)]
    targets += [(dN_ref, i) for i in range(9)]
    for i, (ref, at) in enumerate(targets):
        ref[:, at] = stage[:, i // 2, i % 2, 0:28, :].astype(BF)


def middle(*operands):
    shapes = [
        (4, 5, 28, 128), (4, 14, 28, 128), (4, 9, 28, 128),
        (2, 4, 28, 128), (2, 4, 28, 128), (2, 3, 28, 128), (2, 3, 28, 128),
    ]
    return pl.pallas_call(
        middle_kernel,
        in_specs=[pl.BlockSpec(memory_space=pltpu.VMEM)] * 11
        + [pl.BlockSpec(memory_space=pl.ANY)] * 5,
        out_shape=[jax.ShapeDtypeStruct(s, BF) for s in shapes],
        scratch_shapes=[
            pltpu.VMEM((4, 14, 2, 32, 128), F32),
            pltpu.VMEM((2, 4, 7, 2, 16, 128), F32),
            pltpu.VMEM((4, ROWS, 512), F32),
            pltpu.VMEM((4, ROWS, 128), F32),
            pltpu.VMEM((ROWS, 1024), F32),
            pltpu.VMEM((ROWS, 128), F32),
            pltpu.VMEM((4, 7, 8, 512), F32),
            pltpu.VMEM((4, ROWS, 128), BF),
            pltpu.VMEM((4, ROWS, 128), BF),
            pltpu.VMEM((4, 128, LANES), BF),
            pltpu.VMEM((4, 128, LANES), BF),
            pltpu.VMEM((4, 128, LANES), BF),
            pltpu.VMEM((16, ROWS, LANES), BF),
            pltpu.VMEM((4, 128, LANES), F32),
            pltpu.VMEM((4, 8, LANES), F32),
            pltpu.VMEM((4, 128, LANES), F32),
            pltpu.VMEM((12, ROWS, 128), BF),
            pltpu.VMEM((512, 256), BF),
            pltpu.VMEM((1024, 512), BF),
            pltpu.VMEM((512, 1536), BF),
            pltpu.VMEM((HEADS3, ROWS, LANES), F32),
            pltpu.VMEM((512, 512), BF),
            pltpu.SemaphoreType.DMA((5,)),
        ],
        compiler_params=params(),
    )(*operands)


def padded_ids(ids, section):
    frames, height, width = ids.shape
    if section == 3:
        ids = jnp.roll(ids, SS, 2)
    ids = ids.reshape(4, height // 7, 7, width // 7, 7)
    ids = jnp.pad(ids, ((0, 0),) * 4 + ((0, 1),), constant_values=-1)
    ids = jnp.transpose(ids, (1, 3, 0, 2, 4)).reshape(-1, ROWS)
    row = jnp.pad(ids, ((0, 0), (0, LANES - ROWS)), constant_values=-1)
    return row[:, None, :]


def send(values, axes, by):
    if len(axes) == 1:
        n = lax.axis_size(axes[0])
        pairs = [(i, (i + by) % n) for i in range(n)]
        return lax.ppermute(values, axes[0], pairs)
    n, m = lax.axis_size(axes[0]), lax.axis_size(axes[1])
    pairs = [
        (i * m + j, (i + by) % n * m + (j + by) % m) for i in range(n) for j in range(m)
    ]
    return lax.ppermute(values, axes, pairs)


def per_device(
    tokens,
    regions_one,
    regions_three,
    gain_one,
    projection_one,
    outward_one,
    table_one,
    merge_gain_one,
    merge_weight_one,
    merge_gain_two,
    merge_weight_two,
    gain_three,
    projection_three,
    outward_three,
    table_three,
    cotangent,
):
    both = ("ha", "ta")
    ta_early, ta_late, ha_late, dg_late = pack(tokens, cotangent)
    ta_early = send(ta_early, ("ta",), -1)
    ha_late = send(ha_late, ("ha",), -1)
    dg_late = send(dg_late, both, -1)
    ta_late = send(ta_late, ("ta",), -1)

    bias_one, bias_three = build_biases(table_one, table_three)
    row_one = padded_ids(regions_one, 1)
    row_three = padded_ids(regions_three, 3)
    gain = gain_one[None]
    projT = jnp.transpose(projection_one)

    args = (gain, projection_one, projT, outward_one, bias_one)
    (res_send, res_a), saved_a = front(False, (tokens, ta_early), *args, row_one[:8])
    res_next = send(res_send, ("ha",), -1)
    (res_b,), saved_b = front(True, (tokens, ta_late, ha_late, dg_late), *args, row_one[8:])
    d_a, d_b, d_send, sec_own, sec_ta, sec_ha, sec_dg = middle(
        res_a, res_b, res_next, cotangent, ta_late, ha_late, dg_late,
        merge_gain_one[None], merge_gain_two[None], gain_three[None], row_three[0],
        merge_weight_one, merge_weight_two, projection_three, bias_three, outward_three,
    )
    d_prev = send(d_send, ("ha",), 1)
    own_b, ta_b, ha_b, dg_b = back(
        True, (d_b, sec_ta, sec_ha, sec_dg), gain, projection_one, outward_one, saved_b
    )
    d_prev, own_b = lax.optimization_barrier((d_prev, own_b))
    ta_b = send(ta_b, ("ta",), 1)
    ha_b = send(ha_b, ("ha",), 1)
    dg_b = send(dg_b, both, 1)
    own_a, ta_a = back(False, (d_prev, d_a), gain, projection_one, outward_one, saved_a)
    ta_a = send(ta_a, ("ta",), 1)

    def join(corner, side, rest):
        return jnp.concatenate(
            [jnp.concatenate([corner] + side, 1), jnp.concatenate(rest, 1)], 0
        )

    section = join(dg_b[:, 3:], [ta_b[:, 11:]], [ha_b[:, 3:], sec_own])
    section = jnp.transpose(section.reshape(4, 7, 4, 7, 128), (0, 1, 3, 2, 4)).reshape(4, 7, 7, 512)
    grad = join(dg_b[:, :3], [ta_a, ta_b[:, :11]], [ha_b[:, :3], own_a, own_b])
    return (section, grad)


def solution(mesh):
    tile = P(("col", "ta"), "ha", None, None)
    ids = P(("col", "ta"), "ha", None)
    in_specs = (tile, ids, ids) + (P(),) * 12 + (tile,)
    return jax.shard_map(
        per_device, mesh=mesh, in_specs=in_specs, out_specs=(tile, tile), check_vma=False
    )
```

```python
import functools

import jax
import jax.numpy as jnp
import numpy as np
from jax import lax
from jax.experimental import pallas as pl
from jax.experimental.pallas import tpu as pltpu
from jax.sharding import PartitionSpec as P

HEADS1 = 4
HEADS3 = 16
WT = 4
WS = 7
ST = 2
SS = 3
EPSILON = 1e-05
NREL = 1183
LOG2E = 1.4426950408889634
HEAD = 32
SCALE = HEAD**-0.5
ROWS = WT * WS * 8
LANES = 256
SPAN = 1280
GONE = -1e30
PER_STEP = 2
STEPS = 8 // PER_STEP
BF = jnp.bfloat16
F32 = jnp.float32


def dot(a, b):
    return jnp.dot(a, b, preferred_element_type=F32)


def dot_nt(a, b):
    return lax.dot_general(a, b, (((1,), (1,)), ((), ())), preferred_element_type=F32)


def params(limit=24):
    return pltpu.CompilerParams(vmem_limit_bytes=limit * 1024 * 1024)


def cost(us):
    return pl.CostEstimate(flops=int(us * 1.1e9), bytes_accessed=int(us * 1e6), transcendentals=0)


def normalise(x):
    centred = x - jnp.mean(x, -1, keepdims=True)
    rstd = lax.rsqrt(jnp.mean(centred * centred, -1, keepdims=True) + EPSILON)
    return centred * rstd, rstd


def normalise_back(grad, xhat, rstd):
    return rstd * (
        grad
        - jnp.mean(grad, -1, keepdims=True)
        - xhat * jnp.mean(grad * xhat, -1, keepdims=True)
    )


def head_rows(x, h):
    return x[HEAD * h : HEAD * (h + 1)]


def head_of_lane(shape):
    return lax.broadcasted_iota(jnp.int32, shape, 1) // HEAD


def by_head(x):
    lane = head_of_lane((1, 128))
    return jnp.concatenate([x * (lane == h).astype(F32).astype(BF) for h in range(4)], 0)


def pick_heads(stacked):
    lane = head_of_lane((ROWS, 128))
    got = stacked[:ROWS]
    for h in range(1, 4):
        got = jnp.where(lane == h, stacked[ROWS * h : ROWS * (h + 1)], got)
    return got


def lengthen(x):
    return jnp.concatenate([x, jnp.zeros((LANES - ROWS, x.shape[1]), x.dtype)], 0)


def region_mask(row):
    wide = jnp.broadcast_to(row, (128, LANES))
    column = wide.T[:ROWS]
    column = jnp.concatenate([column, column], 1)
    return jnp.where(column == wide[0:1], 0.0, GONE).astype(F32)


def attend_four(windows):
    scores = [dot(by_head(k), qT) for k, qT, _, _, _, _ in windows]
    results = []
    for s, (_, _, vT, mask, bias_at, keep_probs) in zip(scores, windows):
        outs, inverses = [], []
        for h in range(4):
            biased = s[ROWS * h : ROWS * (h + 1)] + (bias_at(h) + mask)
            peak = jnp.max(biased, 0, keepdims=True)
            probs = jnp.exp2(biased - peak).astype(BF)
            keep_probs(h, probs)
            extended = jnp.concatenate([head_rows(vT, h)[:, :ROWS], jnp.ones((16, ROWS), BF)], 0)
            out = dot(extended, probs)
            inverse = 1.0 / out[HEAD : HEAD + 1]
            outs.append(out[:HEAD] * inverse)
            inverses.append(inverse)
        results.append((jnp.concatenate(outs, 0), jnp.concatenate(inverses + inverses, 0)))
    return results


def attend_four_back(windows):
    first = []
    for v, qT, kT, oT, doT, inverse, probs_at in windows:
        scaled, deltas = [], []
        for h in range(4):
            part = head_rows(doT, h) * inverse[h : h + 1]
            deltas.append(jnp.sum(part * head_rows(oT, h), 0, keepdims=True))
            scaled.append(part)
        scaled = jnp.concatenate(scaled, 0).astype(BF)
        first.append((scaled, deltas, dot(by_head(v), scaled)))
    results = []
    for (scaled, deltas, dprobs), (v, qT, kT, oT, doT, inverse, probs_at) in zip(first, windows):
        probs = [probs_at(h) for h in range(4)]
        dscores = [
            (probs[h].astype(F32) * (dprobs[ROWS * h : ROWS * (h + 1)] - deltas[h])).astype(BF)
            for h in range(4)
        ]
        dv = pick_heads(dot_nt(jnp.concatenate(probs, 0), scaled))
        dk = pick_heads(dot_nt(jnp.concatenate(dscores, 0), qT))
        dqT = jnp.concatenate(
            [dot(head_rows(kT, h)[:, :ROWS], dscores[h]) for h in range(4)], 0
        )
        results.append((dqT.T[:ROWS] * SCALE, dk * (1.0 / LOG2E), dv))
    return results


def lanes_of(shape):
    return lax.broadcasted_iota(jnp.int32, shape, 1)


def region_rows(ids, section):
    columns = ids.shape[1]
    count = columns // WS
    place = lax.broadcasted_iota(jnp.int32, (columns, LANES * count), 0)
    lane = lanes_of((columns, LANES * count))
    column = lane % 8
    real = (column < WS) & (lane % LANES < ROWS)
    if section == 3:
        column = jnp.where(column < 3, column + 4, column - 3)
    chosen = real & (place == lane // LANES * WS + column)
    spread = dot(ids.astype(F32).astype(BF), chosen.astype(F32).astype(BF))
    row = lax.broadcasted_iota(jnp.int32, spread.shape, 0)
    lane = lanes_of(spread.shape)
    real = (lane[:1] % 8 < WS) & (lane[:1] % LANES < ROWS)
    rows = []
    for hw in range(ids.shape[0] // (WT * WS)):
        mine = lane % LANES // 8 == row % 4 * WS + row // 4 - WS * hw
        inside = (row >= WT * WS * hw) & (row < WT * WS * (hw + 1))
        found = jnp.sum(jnp.where(mine & inside, spread, 0.0), 0, keepdims=True)
        found = jnp.where(real, found, -1.0)
        rows += [found[:, LANES * ww : LANES * (ww + 1)] for ww in range(count)]
    return rows


def prepare_kernel(
    t1_ref, t3_ref, s_ref, r1_ref, r3_ref, o1_ref, o3_ref, row1_ref, row3_ref, tab, spread
):
    tab[...] = jnp.zeros((24, SPAN), F32)
    tab[0:4, 0:NREL] = t1_ref[...] * LOG2E
    tab[8:24, 0:NREL] = t3_ref[...] * LOG2E
    slabs = []
    for dt in range(7):
        start = 169 * dt
        low = start // 128 * 128
        run = tab[:, low : low + 384]
        if start > low:
            run = pltpu.roll(run, 384 - (start - low), 1)
        slabs.append(run[:, :256])
    left = jnp.concatenate(slabs, 0)
    first = left.astype(BF)
    rest = left - first.astype(F32)
    second = rest.astype(BF)
    third = (rest - second.astype(F32)).astype(BF)
    chosen = s_ref[...]
    got = dot(first, chosen) + dot(second, chosen) + dot(third, chosen)
    lane16 = lanes_of((16, 128))
    for dt in range(7):
        for wj in range(8):
            part = got[24 * dt : 24 * dt + 24, 128 * wj : 128 * wj + 128]
            spread[dt, pl.ds(wj, 8, stride=8), :] = part[0:8]
            later = part[8:24]
            turned = jnp.where(lane16 % 8 < 3, pltpu.roll(later, 124, 1), pltpu.roll(later, 3, 1))
            spread[dt, pl.ds(64 + (7 if wj == 7 else (wj + 3) % 7), 16, stride=8), :] = turned
    for o_ref, heads, at in ((o1_ref, HEADS1, 0), (o3_ref, HEADS3, 64)):
        lane = lanes_of((heads * 8, 128))
        for tj in range(WT):
            for hj in range(WS):
                p0, p1, p2, p3 = (
                    pltpu.roll(
                        spread[ti - tj + 3, at : at + heads * 8, :], (ti * 56 - (6 - hj) * 8) % 128, 1
                    )
                    for ti in range(WT)
                )
                left = jnp.where(lane < 56, p0, jnp.where(lane < 112, p1, p2))
                right = jnp.where(lane < 40, p2, p3)
                row = (tj * WS + hj) * 8
                o_ref[:, row : row + 8, 0:128] = left.reshape(heads, 8, 128)
                o_ref[:, row : row + 8, 128:256] = right.reshape(heads, 8, 128)
    for i, found in enumerate(region_rows(r1_ref[...], 1)):
        row1_ref[i] = found
    row3_ref[...] = region_rows(r3_ref[...], 3)[0]


def chooser():
    chosen = np.zeros((256, 1024), np.float32)
    for wj in range(WS):
        for dh in range(13):
            for wi in range(WS):
                chosen[dh * 13 + wi - wj + 6, wj * 128 + dh * 8 + wi] = 1.0
    return jnp.asarray(chosen, BF)


def by_height(ids):
    return jnp.transpose(ids, (1, 0, 2)).reshape(-1, ids.shape[2])


def prepare(table_one, table_three, regions_one, regions_three):
    return pl.pallas_call(
        prepare_kernel,
        out_shape=(
            jax.ShapeDtypeStruct((HEADS1, ROWS, LANES), F32),
            jax.ShapeDtypeStruct((HEADS3, ROWS, LANES), F32),
            jax.ShapeDtypeStruct((16, 1, LANES), F32),
            jax.ShapeDtypeStruct((1, LANES), F32),
        ),
        scratch_shapes=[pltpu.VMEM((24, SPAN), F32), pltpu.VMEM((7, 24 * 8, 128), F32)],
        compiler_params=params(),
        cost_estimate=cost(3),
    )(
        jnp.transpose(table_one),
        jnp.transpose(table_three),
        chooser(),
        by_height(regions_one),
        by_height(regions_three),
    )


def fold(values):
    return jnp.concatenate([values[..., 128 * g : 128 * g + 128] for g in range(4)], -2)


def unfold(values):
    return jnp.concatenate([values[..., 7 * g : 7 * g + 7, :] for g in range(4)], -1)


def pack_kernel(tok_ref, cot_ref, early_ref, late_ref, ha_ref, dg_ref):
    early_ref[...] = tok_ref[0:2, 3:17]
    late_ref[:, 0:11] = tok_ref[0:2, 17:28]
    late_ref[:, 11:15] = fold(cot_ref[0:2, 3:7].astype(F32)).astype(BF)
    ha_ref[:, 0:3] = tok_ref[2:4, 0:3]
    ha_ref[:, 3:6] = fold(cot_ref[2:4, 0:3].astype(F32)).astype(BF)
    dg_ref[:, 0:3] = tok_ref[0:2, 0:3]
    dg_ref[:, 3:6] = fold(cot_ref[0:2, 0:3].astype(F32)).astype(BF)


def pack(tokens, cotangent):
    return pl.pallas_call(
        pack_kernel,
        out_shape=[
            jax.ShapeDtypeStruct((2, n, 28, 128), BF) for n in (14, 15, 6, 6)
        ],
        compiler_params=params(),
        cost_estimate=cost(2),
    )(tokens, cotangent)


def put_rows(stage, frames, rows, values):
    values = values.astype(F32)
    stage[frames, rows, 0:28, :] = values
    stage[frames, rows, 28:36, :] = values[:, :, 0:8, :]


def cut_windows(stage, win):
    for hw in range(2):
        for ww in range(4):
            win[hw * 4 + ww] = stage[:, 7 * hw : 7 * hw + 7, 3 + 7 * ww : 11 + 7 * ww, :].reshape(
                ROWS, 128
            )


def join_windows(win, stage):
    for hw in range(2):
        for ww in range(4):
            stage[:, 7 * hw : 7 * hw + 7, 3 + 7 * ww : 11 + 7 * ww, :] = win[hw * 4 + ww].reshape(
                WT, WS, 8, 128
            )
    stage[:, :, 0:3, :] = stage[:, :, 28:31, :]


def front_kernel(late, *refs):
    n_in = 4 if late else 2
    pieces, refs = refs[:n_in], refs[n_in:]
    gain_ref, proj_ref, outw_ref, bias_ref, row_ref = refs[:5]
    refs = refs[5:]
    n_out = 1 if late else 2
    outs, refs = refs[:n_out], refs[n_out:]
    xw_ref, kv_ref, t_ref, p_ref, o_ref, inv_ref, stage, win, projT = refs
    step = pl.program_id(0)

    @pl.when(step == 0)
    def _():
        own = pieces[0]
        if late:
            put_rows(stage, slice(0, 2), slice(0, 11), own[2:4, 17:28])
            put_rows(stage, slice(2, 4), slice(0, 11), pieces[1][:, 0:11])
            put_rows(stage, slice(0, 2), slice(11, 14), pieces[2][:, 0:3])
            put_rows(stage, slice(2, 4), slice(11, 14), pieces[3][:, 0:3])
        else:
            put_rows(stage, slice(0, 2), slice(0, 14), own[2:4, 3:17])
            put_rows(stage, slice(2, 4), slice(0, 14), pieces[1][...])
        for g in range(3):
            at = slice(128 * g, 128 * g + 128)
            projT[at, :] = proj_ref[:, at].astype(F32).T.astype(BF)
        cut_windows(stage, win)

    xs, operands = [], []
    for u in range(PER_STEP):
        x = win[step * PER_STEP + u]
        xs.append(x)
        xw_ref[u] = x.astype(BF)
        xhat, _ = normalise(x)
        n = (xhat * gain_ref[...]).astype(BF)
        kv = dot(n, proj_ref[:, 128:]).astype(BF)
        kv_ref[u] = kv
        t = dot_nt(projT[...], lengthen(n))
        qT = (t[:128] * (SCALE * LOG2E)).astype(BF)
        rest = t[128:].astype(BF)
        t_ref[u, :128] = qT
        t_ref[u, 128:] = rest[:128]

        def keep(h, probs, u=u):
            p_ref[u, h] = probs

        operands.append(
            (kv[:, :128], qT, rest[128:], region_mask(row_ref[u]), lambda h: bias_ref[h], keep)
        )
    for u, (oT, inverse) in enumerate(attend_four(operands)):
        o_ref[u] = oT.astype(BF)
        inv_ref[u] = inverse
        mixed = dot(oT.T[:ROWS].astype(BF), outw_ref[...]).astype(BF).astype(F32)
        win[step * PER_STEP + u] = xs[u] + mixed

    @pl.when(step == STEPS - 1)
    def _():
        join_windows(win, stage)
        if late:
            outs[0][...] = stage[:, :, 0:28, :].astype(BF)
        else:
            outs[0][...] = stage[:, 0:9, 0:28, :].astype(BF)
            outs[1][...] = stage[:, 9:14, 0:28, :].astype(BF)


def whole(shape):
    return pl.BlockSpec(shape, lambda i: (0,) * len(shape))


def each(shape):
    return pl.BlockSpec((PER_STEP,) + shape, lambda i: (i,) + (0,) * len(shape))


SAVED = (
    ((ROWS, 128), BF),
    ((ROWS, 256), BF),
    ((256, LANES), BF),
    ((4, ROWS, LANES), BF),
    ((128, LANES), BF),
    ((8, LANES), F32),
)


def front(late, pieces, gain, proj, outw, bias, row):
    consts = (gain, proj, outw, bias)
    shapes = [(4, 14, 28, 128)] if late else [(4, 9, 28, 128), (4, 5, 28, 128)]
    out = pl.pallas_call(
        functools.partial(front_kernel, late),
        grid=(STEPS,),
        in_specs=[whole(a.shape) for a in tuple(pieces) + consts] + [each((1, LANES))],
        out_specs=[whole(s) for s in shapes] + [each(s) for s, _ in SAVED],
        out_shape=[jax.ShapeDtypeStruct(s, BF) for s in shapes]
        + [jax.ShapeDtypeStruct((8,) + s, d) for s, d in SAVED],
        scratch_shapes=[
            pltpu.VMEM((4, 14, 40, 128), F32),
            pltpu.VMEM((8, ROWS, 128), F32),
            pltpu.VMEM((384, 128), BF),
        ],
        compiler_params=params(),
        cost_estimate=cost(9),
    )(*pieces, *consts, row)
    return out[: len(shapes)], out[len(shapes) :]


def back_kernel(late, *refs):
    n_in = 4 if late else 2
    pieces, refs = refs[:n_in], refs[n_in:]
    gain_ref, proj_ref, outw_ref = refs[:3]
    xw_ref, kv_ref, t_ref, p_ref, o_ref, inv_ref = refs[3:9]
    refs = refs[9:]
    n_out = 4 if late else 2
    outs, refs = refs[:n_out], refs[n_out:]
    stage, win = refs
    step = pl.program_id(0)

    @pl.when(step == 0)
    def _():
        if late:
            put_rows(stage, slice(0, 4), slice(0, 14), pieces[0][...])
            outs[1][:, 11:15] = pieces[1][...]
            outs[2][:, 3:6] = pieces[2][...]
            outs[3][:, 3:6] = pieces[3][...]
        else:
            put_rows(stage, slice(0, 4), slice(0, 9), pieces[0][...])
            put_rows(stage, slice(0, 4), slice(9, 14), pieces[1][...])
        cut_windows(stage, win)

    drs, operands = [], []
    for u in range(PER_STEP):
        dr = win[step * PER_STEP + u]
        drs.append(dr)
        operands.append(
            (
                kv_ref[u, :, 128:],
                t_ref[u, :128],
                t_ref[u, 128:],
                o_ref[u].astype(F32),
                dot_nt(outw_ref[...], lengthen(dr.astype(BF))),
                inv_ref[u],
                lambda h, u=u: p_ref[u, h],
            )
        )
    for u, (dq, dk, dv) in enumerate(attend_four_back(operands)):
        dpacked = jnp.concatenate([dq.astype(BF), dk.astype(BF), dv.astype(BF)], 1)
        dn = dot_nt(dpacked, proj_ref[...])
        xhat, rstd = normalise(xw_ref[u].astype(F32))
        win[step * PER_STEP + u] = drs[u] + normalise_back(dn * gain_ref[...], xhat, rstd)

    @pl.when(step == STEPS - 1)
    def _():
        join_windows(win, stage)
        if late:
            outs[0][...] = stage[0:2, 0:11, 0:28, :].astype(BF)
            outs[1][:, 0:11] = stage[2:4, 0:11, 0:28, :].astype(BF)
            outs[2][:, 0:3] = stage[0:2, 11:14, 0:28, :].astype(BF)
            outs[3][:, 0:3] = stage[2:4, 11:14, 0:28, :].astype(BF)
        else:
            outs[0][...] = stage[0:2, :, 0:28, :].astype(BF)
            outs[1][...] = stage[2:4, :, 0:28, :].astype(BF)


def back(late, pieces, gain, proj, outw, saved):
    consts = (gain, proj, outw)
    if late:
        shapes = [(2, n, 28, 128) for n in (11, 15, 6, 6)]
    else:
        shapes = [(2, 14, 28, 128), (2, 14, 28, 128)]
    return pl.pallas_call(
        functools.partial(back_kernel, late),
        grid=(STEPS,),
        in_specs=[whole(a.shape) for a in tuple(pieces) + consts] + [each(s) for s, _ in SAVED],
        out_specs=[whole(s) for s in shapes],
        out_shape=[jax.ShapeDtypeStruct(s, BF) for s in shapes],
        scratch_shapes=[
            pltpu.VMEM((4, 14, 40, 128), F32),
            pltpu.VMEM((8, ROWS, 128), F32),
        ],
        compiler_params=params(),
        cost_estimate=cost(10),
    )(*pieces, *consts, *saved)


def middle_kernel(
    resA_ref, resB_ref, resN_ref, cot_ref, cta_ref, cha_ref, cdg_ref,
    mg1_ref, mg2_ref, g3_ref, row_ref, mw1_hbm, mw2_hbm, p3_hbm, bias_hbm, ow3_hbm,
    dA_ref, dB_ref, dN_ref, so_ref, sta_ref, sha_ref, sdg_ref,
    stage, stage2, xhat1, rstd1, xhat2, rstd2, cotw, k_s, v_s, qT_s, kT_s, vT_s, probs_s, oT_s, inv_s, doT_s, dqkv_s,
    mw1_ref, mw2_ref, p3_ref, bias_ref, ow3_ref, sems,
):
    fetches = [
        pltpu.make_async_copy(there, here, sems.at[i])
        for i, (there, here) in enumerate(
            (
                (mw1_hbm, mw1_ref),
                (mw2_hbm, mw2_ref),
                (p3_hbm, p3_ref),
                (bias_hbm, bias_ref),
                (ow3_hbm, ow3_ref),
            )
        )
    ]
    for fetch in fetches:
        fetch.start()
    sources = [(resA_ref, i) for i in range(5)] + [(resB_ref, i) for i in range(14)]
    sources += [(resN_ref, i) for i in range(9)]
    for i, (ref, at) in enumerate(sources):
        stage[:, i // 2, i % 2, 0:28, :] = ref[:, at].astype(F32)
    stage[:, :, :, 28:32, :] = jnp.zeros((4, 14, 2, 4, 128), F32)
    cotw[...] = jnp.zeros((4, 7, 8, 512), F32)
    cotw[0:2, 0:4, 0:7, :] = cot_ref[2:4, 3:7].astype(F32)
    cotw[2:4, 0:4, 0:7, :] = unfold(cta_ref[:, 11:15].astype(F32))
    cotw[0:2, 4:7, 0:7, :] = unfold(cha_ref[:, 3:6].astype(F32))
    cotw[2:4, 4:7, 0:7, :] = unfold(cdg_ref[:, 3:6].astype(F32))

    def merge_one(f, _):
        pieces = [
            stage[f, :, q % 2, pl.ds(q // 2, 16, stride=2), :].reshape(ROWS, 128) for q in range(4)
        ]
        xhat, rstd = normalise(jnp.concatenate(pieces, 1))
        xhat1[f] = xhat
        rstd1[f] = jnp.broadcast_to(rstd, (ROWS, 128))
        merged = dot((xhat * mg1_ref[...]).astype(BF), mw1_ref[...]).astype(BF).astype(F32)
        for half in range(2):
            stage2[half, f] = merged[:, 128 * half : 128 * half + 128].reshape(7, 2, 16, 128)
        return 0

    fetches[0].wait()
    lax.fori_loop(0, 4, merge_one, 0)
    fetches[1].wait()
    pieces = [
        stage2[half, :, :, q % 2, pl.ds(q // 2, 8, stride=2), :].reshape(ROWS, 128)
        for q in range(4)
        for half in range(2)
    ]
    xhat, rstd = normalise(jnp.concatenate(pieces, 1))
    xhat2[...] = xhat
    rstd2[...] = jnp.broadcast_to(rstd, (ROWS, 128))
    merged_two = dot((xhat * mg2_ref[...]).astype(BF), mw2_ref[...]).astype(BF).astype(F32)
    xhat3, rstd3 = normalise(merged_two)
    n3 = (xhat3 * g3_ref[...]).astype(BF)
    fetches[2].wait()
    for g in range(4):
        at = slice(128 * g, 128 * g + 128)
        q = dot(n3, p3_ref[:, 128 * g : 128 * g + 128])
        k = dot(n3, p3_ref[:, 512 + 128 * g : 640 + 128 * g])
        v = dot(n3, p3_ref[:, 1024 + 128 * g : 1152 + 128 * g])
        k_s[g] = k.astype(BF)
        v_s[g] = v.astype(BF)
        qT_s[g] = (lengthen(q).T * (SCALE * LOG2E)).astype(BF)
        kT_s[g] = lengthen(k).T.astype(BF)
        vT_s[g] = lengthen(v).T.astype(BF)
    mask = region_mask(row_ref[...])
    fetches[3].wait()

    def heads(g, _):
        def keep(h, probs):
            probs_s[g * 4 + h] = probs

        operands = (k_s[g], qT_s[g], vT_s[g], mask, lambda h: bias_ref[g * 4 + h], keep)
        ((oT_s[g], inv_s[g]),) = attend_four([operands])
        return 0

    lax.fori_loop(0, 4, heads, 0)
    fetches[4].wait()
    att = jnp.concatenate([oT_s[g].T[:ROWS].astype(BF) for g in range(4)], 1)
    mixed = dot(att, ow3_ref[...]).astype(BF).astype(F32)
    section = (merged_two + mixed).reshape(4, 7, 8, 512)
    section = fold(section[:, :, 0:7])
    so_ref[...] = section[0:2, 0:4].astype(BF)
    sta_ref[...] = section[2:4, 0:4].astype(BF)
    sha_ref[...] = section[0:2, 4:7].astype(BF)
    sdg_ref[...] = section[2:4, 4:7].astype(BF)

    cot = cotw[...].reshape(ROWS, 512)
    cot_long = lengthen(cot.astype(BF))
    for g in range(4):
        doT_s[g] = dot_nt(ow3_ref[128 * g : 128 * g + 128, :], cot_long)

    def heads_back(g, _):
        operands = (
            v_s[g], qT_s[g], kT_s[g], oT_s[g], doT_s[g], inv_s[g], lambda h: probs_s[g * 4 + h]
        )
        ((dq, dk, dv),) = attend_four_back([operands])
        dqkv_s[g] = dq.astype(BF)
        dqkv_s[4 + g] = dk.astype(BF)
        dqkv_s[8 + g] = dv.astype(BF)
        return 0

    lax.fori_loop(0, 4, heads_back, 0)
    dpacked = jnp.concatenate([dqkv_s[i] for i in range(12)], 1)
    dn3 = dot_nt(dpacked, p3_ref[...])
    dm2 = cot + normalise_back(dn3 * g3_ref[...], xhat3, rstd3)
    dn2 = dot_nt(dm2.astype(BF), mw2_ref[...])
    dg2 = normalise_back(dn2 * mg2_ref[...], xhat2[...], rstd2[:, 0:1])
    for q in range(4):
        for half in range(2):
            at = 256 * q + 128 * half
            stage2[half, :, :, q % 2, pl.ds(q // 2, 8, stride=2), :] = dg2[:, at : at + 128].reshape(
                4, 7, 8, 128
            )

    def merge_one_back(f, _):
        dm1 = jnp.concatenate([stage2[half, f].reshape(ROWS, 128) for half in range(2)], 1).astype(BF)
        dn1 = dot_nt(dm1, mw1_ref[...])
        dg1 = normalise_back(dn1 * mg1_ref[...], xhat1[f], rstd1[f, :, 0:1])
        for q in range(4):
            stage[f, :, q % 2, pl.ds(q // 2, 16, stride=2), :] = dg1[
                :, 128 * q : 128 * q + 128
            ].reshape(14, 16, 128)
        return 0

    lax.fori_loop(0, 4, merge_one_back, 0)
    targets = [(dA_ref, i) for i in range(5)] + [(dB_ref, i) for i in range(14)]
    targets += [(dN_ref, i) for i in range(9)]
    for i, (ref, at) in enumerate(targets):
        ref[:, at] = stage[:, i // 2, i % 2, 0:28, :].astype(BF)


def middle(*operands):
    shapes = [
        (4, 5, 28, 128), (4, 14, 28, 128), (4, 9, 28, 128),
        (2, 4, 28, 128), (2, 4, 28, 128), (2, 3, 28, 128), (2, 3, 28, 128),
    ]
    return pl.pallas_call(
        middle_kernel,
        in_specs=[pl.BlockSpec(memory_space=pltpu.VMEM)] * 11
        + [pl.BlockSpec(memory_space=pl.ANY)] * 5,
        out_shape=[jax.ShapeDtypeStruct(s, BF) for s in shapes],
        scratch_shapes=[
            pltpu.VMEM((4, 14, 2, 32, 128), F32),
            pltpu.VMEM((2, 4, 7, 2, 16, 128), F32),
            pltpu.VMEM((4, ROWS, 512), F32),
            pltpu.VMEM((4, ROWS, 128), F32),
            pltpu.VMEM((ROWS, 1024), F32),
            pltpu.VMEM((ROWS, 128), F32),
            pltpu.VMEM((4, 7, 8, 512), F32),
            pltpu.VMEM((4, ROWS, 128), BF),
            pltpu.VMEM((4, ROWS, 128), BF),
            pltpu.VMEM((4, 128, LANES), BF),
            pltpu.VMEM((4, 128, LANES), BF),
            pltpu.VMEM((4, 128, LANES), BF),
            pltpu.VMEM((16, ROWS, LANES), BF),
            pltpu.VMEM((4, 128, LANES), F32),
            pltpu.VMEM((4, 8, LANES), F32),
            pltpu.VMEM((4, 128, LANES), F32),
            pltpu.VMEM((12, ROWS, 128), BF),
            pltpu.VMEM((512, 256), BF),
            pltpu.VMEM((1024, 512), BF),
            pltpu.VMEM((512, 1536), BF),
            pltpu.VMEM((HEADS3, ROWS, LANES), F32),
            pltpu.VMEM((512, 512), BF),
            pltpu.SemaphoreType.DMA((5,)),
        ],
        compiler_params=params(36),
        cost_estimate=cost(14),
    )(*operands)


def send(values, axes, by):
    if len(axes) == 1:
        n = lax.axis_size(axes[0])
        pairs = [(i, (i + by) % n) for i in range(n)]
        return lax.ppermute(values, axes[0], pairs)
    n, m = lax.axis_size(axes[0]), lax.axis_size(axes[1])
    pairs = [
        (i * m + j, (i + by) % n * m + (j + by) % m) for i in range(n) for j in range(m)
    ]
    return lax.ppermute(values, axes, pairs)


def per_device(
    tokens,
    regions_one,
    regions_three,
    gain_one,
    projection_one,
    outward_one,
    table_one,
    merge_gain_one,
    merge_weight_one,
    merge_gain_two,
    merge_weight_two,
    gain_three,
    projection_three,
    outward_three,
    table_three,
    cotangent,
):
    both = ("ha", "ta")
    ta_early, ta_late, ha_late, dg_late = pack(tokens, cotangent)
    ta_early = send(ta_early, ("ta",), -1)
    ha_late = send(ha_late, ("ha",), -1)
    dg_late = send(dg_late, both, -1)
    ta_late = send(ta_late, ("ta",), -1)

    bias_one, bias_three, row_one, row_three = prepare(
        table_one, table_three, regions_one, regions_three
    )
    args = (gain_one[None], projection_one, outward_one, bias_one)
    (res_send, res_a), saved_a = front(False, (tokens, ta_early), *args, row_one[:8])
    res_next = send(res_send, ("ha",), -1)
    (res_b,), saved_b = front(True, (tokens, ta_late, ha_late, dg_late), *args, row_one[8:])
    d_a, d_b, d_send, sec_own, sec_ta, sec_ha, sec_dg = middle(
        res_a, res_b, res_next, cotangent, ta_late, ha_late, dg_late,
        merge_gain_one[None], merge_gain_two[None], gain_three[None], row_three,
        merge_weight_one, merge_weight_two, projection_three, bias_three, outward_three,
    )
    d_prev = send(d_send, ("ha",), 1)
    own_b, ta_b, ha_b, dg_b = back(
        True, (d_b, sec_ta, sec_ha, sec_dg), gain_one[None], projection_one, outward_one, saved_b
    )
    d_prev, own_b = lax.optimization_barrier((d_prev, own_b))
    ta_b = send(ta_b, ("ta",), 1)
    ha_b = send(ha_b, ("ha",), 1)
    dg_b = send(dg_b, both, 1)
    own_a, ta_a = back(False, (d_prev, d_a), gain_one[None], projection_one, outward_one, saved_a)
    ta_b, ha_b, dg_b, own_a = lax.optimization_barrier((ta_b, ha_b, dg_b, own_a))
    ta_a = send(ta_a, ("ta",), 1)

    def join(corner, side, rest):
        return jnp.concatenate(
            [jnp.concatenate([corner] + side, 1), jnp.concatenate(rest, 1)], 0
        )

    section = join(dg_b[:, 3:], [ta_b[:, 11:]], [ha_b[:, 3:], sec_own])
    section = jnp.transpose(section.reshape(4, 7, 4, 7, 128), (0, 1, 3, 2, 4)).reshape(4, 7, 7, 512)
    grad = join(dg_b[:, :3], [ta_a, ta_b[:, :11]], [ha_b[:, :3], own_a, own_b])
    return (section, grad)


def solution(mesh):
    tile = P(("col", "ta"), "ha", None, None)
    ids = P(("col", "ta"), "ha", None)
    in_specs = (tile, ids, ids) + (P(),) * 12 + (tile,)
    return jax.shard_map(
        per_device, mesh=mesh, in_specs=in_specs, out_specs=(tile, tile), check_vma=False
    )
```

```python
import functools

import jax
import jax.numpy as jnp
import numpy as np
from jax import lax
from jax.experimental import pallas as pl
from jax.experimental.layout import Layout, with_layout_constraint
from jax.experimental.pallas import tpu as pltpu
from jax.sharding import PartitionSpec as P

HEADS1 = 4
HEADS3 = 16
WT = 4
WS = 7
ST = 2
SS = 3
EPSILON = 1e-05
NREL = 1183
LOG2E = 1.4426950408889634
HEAD = 32
SCALE = HEAD**-0.5
ROWS = WT * WS * 8
LANES = 256
SPAN = 1280
GONE = -1e30
PER_STEP = 4
STEPS = 8 // PER_STEP
BF = jnp.bfloat16
F32 = jnp.float32


def dot(a, b):
    return jnp.dot(a, b, preferred_element_type=F32)


def dot_nt(a, b):
    return lax.dot_general(a, b, (((1,), (1,)), ((), ())), preferred_element_type=F32)


def params(limit=28):
    return pltpu.CompilerParams(vmem_limit_bytes=limit * 1024 * 1024)


def cost(us):
    return pl.CostEstimate(flops=int(us * 1.1e9), bytes_accessed=int(us * 1e6), transcendentals=0)


def normalise(x):
    centred = x - jnp.mean(x, -1, keepdims=True)
    rstd = lax.rsqrt(jnp.mean(centred * centred, -1, keepdims=True) + EPSILON)
    return centred * rstd, rstd


def normalise_back(grad, xhat, rstd):
    return rstd * (
        grad
        - jnp.mean(grad, -1, keepdims=True)
        - xhat * jnp.mean(grad * xhat, -1, keepdims=True)
    )


def head_rows(x, h):
    return x[HEAD * h : HEAD * (h + 1)]


def head_of_lane(shape):
    return lax.broadcasted_iota(jnp.int32, shape, 1) // HEAD


def by_head(x):
    lane = head_of_lane((1, 128))
    return jnp.concatenate([x * (lane == h).astype(F32).astype(BF) for h in range(4)], 0)


def pick_heads(stacked):
    lane = head_of_lane((ROWS, 128))
    got = stacked[:ROWS]
    for h in range(1, 4):
        got = jnp.where(lane == h, stacked[ROWS * h : ROWS * (h + 1)], got)
    return got


def lengthen(x):
    return jnp.concatenate([x, jnp.zeros((LANES - ROWS, x.shape[1]), x.dtype)], 0)


def region_mask(row):
    wide = jnp.broadcast_to(row, (128, LANES))
    column = wide.T[:ROWS]
    column = jnp.concatenate([column, column], 1)
    return jnp.where(column == wide[0:1], 0.0, GONE).astype(F32)


def attend_four(windows):
    scores = [dot(by_head(k), qT) for k, qT, _, _, _, _ in windows]
    results = []
    for s, (_, _, vT, mask, bias_at, keep_probs) in zip(scores, windows):
        outs, inverses = [], []
        for h in range(4):
            biased = s[ROWS * h : ROWS * (h + 1)] + (bias_at(h) + mask)
            peak = jnp.max(biased, 0, keepdims=True)
            probs = jnp.exp2(biased - peak).astype(BF)
            keep_probs(h, probs)
            extended = jnp.concatenate([head_rows(vT, h)[:, :ROWS], jnp.ones((16, ROWS), BF)], 0)
            out = dot(extended, probs)
            inverse = 1.0 / out[HEAD : HEAD + 1]
            outs.append(out[:HEAD] * inverse)
            inverses.append(inverse)
        results.append((jnp.concatenate(outs, 0), jnp.concatenate(inverses + inverses, 0)))
    return results


def attend_four_back(windows):
    first = []
    for v, qT, kT, oT, doT, inverse, probs_at in windows:
        scaled, deltas = [], []
        for h in range(4):
            part = head_rows(doT, h) * inverse[h : h + 1]
            deltas.append(jnp.sum(part * head_rows(oT, h), 0, keepdims=True))
            scaled.append(part)
        scaled = jnp.concatenate(scaled, 0).astype(BF)
        first.append((scaled, deltas, dot(by_head(v), scaled)))
    results = []
    for (scaled, deltas, dprobs), (v, qT, kT, oT, doT, inverse, probs_at) in zip(first, windows):
        probs = [probs_at(h) for h in range(4)]
        dscores = [
            (probs[h].astype(F32) * (dprobs[ROWS * h : ROWS * (h + 1)] - deltas[h])).astype(BF)
            for h in range(4)
        ]
        dv = pick_heads(dot_nt(jnp.concatenate(probs, 0), scaled))
        dk = pick_heads(dot_nt(jnp.concatenate(dscores, 0), qT))
        dqT = jnp.concatenate(
            [dot(head_rows(kT, h)[:, :ROWS], dscores[h]) for h in range(4)], 0
        )
        results.append((dqT.T[:ROWS] * SCALE, dk * (1.0 / LOG2E), dv))
    return results


def lanes_of(shape):
    return lax.broadcasted_iota(jnp.int32, shape, 1)


def region_rows(ids, section):
    columns = ids.shape[1]
    count = columns // WS
    place = lax.broadcasted_iota(jnp.int32, (columns, LANES * count), 0)
    lane = lanes_of((columns, LANES * count))
    column = lane % 8
    real = (column < WS) & (lane % LANES < ROWS)
    if section == 3:
        column = jnp.where(column < 3, column + 4, column - 3)
    chosen = real & (place == lane // LANES * WS + column)
    spread = dot(ids.astype(F32).astype(BF), chosen.astype(F32).astype(BF))
    row = lax.broadcasted_iota(jnp.int32, spread.shape, 0)
    lane = lanes_of(spread.shape)
    real = (lane[:1] % 8 < WS) & (lane[:1] % LANES < ROWS)
    rows = []
    for hw in range(ids.shape[0] // (WT * WS)):
        mine = lane % LANES // 8 == row % 4 * WS + row // 4 - WS * hw
        inside = (row >= WT * WS * hw) & (row < WT * WS * (hw + 1))
        found = jnp.sum(jnp.where(mine & inside, spread, 0.0), 0, keepdims=True)
        found = jnp.where(real, found, -1.0)
        rows += [found[:, LANES * ww : LANES * (ww + 1)] for ww in range(count)]
    return rows


def prepare_kernel(
    t1_ref, t3_ref, s_ref, r1_ref, r3_ref, o1_ref, o3_ref, row1_ref, row3_ref, tab, spread
):
    tab[...] = jnp.zeros((24, SPAN), F32)
    tab[0:4, 0:NREL] = t1_ref[...] * LOG2E
    tab[8:24, 0:NREL] = t3_ref[...] * LOG2E
    slabs = []
    for dt in range(7):
        start = 169 * dt
        low = start // 128 * 128
        run = tab[:, low : low + 384]
        if start > low:
            run = pltpu.roll(run, 384 - (start - low), 1)
        slabs.append(run[:, :256])
    left = jnp.concatenate(slabs, 0)
    first = left.astype(BF)
    rest = left - first.astype(F32)
    second = rest.astype(BF)
    third = (rest - second.astype(F32)).astype(BF)
    chosen = s_ref[...]
    got = dot(first, chosen) + dot(second, chosen) + dot(third, chosen)
    lane16 = lanes_of((16, 128))
    for dt in range(7):
        for wj in range(8):
            part = got[24 * dt : 24 * dt + 24, 128 * wj : 128 * wj + 128]
            spread[dt, pl.ds(wj, 8, stride=8), :] = part[0:8]
            later = part[8:24]
            turned = jnp.where(lane16 % 8 < 3, pltpu.roll(later, 124, 1), pltpu.roll(later, 3, 1))
            spread[dt, pl.ds(64 + (7 if wj == 7 else (wj + 3) % 7), 16, stride=8), :] = turned
    for o_ref, heads, at in ((o1_ref, HEADS1, 0), (o3_ref, HEADS3, 64)):
        lane = lanes_of((heads * 8, 128))
        for tj in range(WT):
            for hj in range(WS):
                p0, p1, p2, p3 = (
                    pltpu.roll(
                        spread[ti - tj + 3, at : at + heads * 8, :], (ti * 56 - (6 - hj) * 8) % 128, 1
                    )
                    for ti in range(WT)
                )
                left = jnp.where(lane < 56, p0, jnp.where(lane < 112, p1, p2))
                right = jnp.where(lane < 40, p2, p3)
                row = (tj * WS + hj) * 8
                o_ref[:, row : row + 8, 0:128] = left.reshape(heads, 8, 128)
                o_ref[:, row : row + 8, 128:256] = right.reshape(heads, 8, 128)
    for i, found in enumerate(region_rows(r1_ref[...], 1)):
        row1_ref[i] = found
    row3_ref[...] = region_rows(r3_ref[...], 3)[0]


def chooser():
    chosen = np.zeros((256, 1024), np.float32)
    for wj in range(WS):
        for dh in range(13):
            for wi in range(WS):
                chosen[dh * 13 + wi - wj + 6, wj * 128 + dh * 8 + wi] = 1.0
    return jnp.asarray(chosen, BF)


def by_height(ids):
    return jnp.transpose(ids, (1, 0, 2)).reshape(-1, ids.shape[2])


def prepare(table_one, table_three, regions_one, regions_three):
    return pl.pallas_call(
        prepare_kernel,
        out_shape=(
            jax.ShapeDtypeStruct((HEADS1, ROWS, LANES), F32),
            jax.ShapeDtypeStruct((HEADS3, ROWS, LANES), F32),
            jax.ShapeDtypeStruct((16, 1, LANES), F32),
            jax.ShapeDtypeStruct((1, LANES), F32),
        ),
        scratch_shapes=[pltpu.VMEM((24, SPAN), F32), pltpu.VMEM((7, 24 * 8, 128), F32)],
        compiler_params=params(),
        cost_estimate=cost(3),
    )(
        jnp.transpose(table_one),
        jnp.transpose(table_three),
        chooser(),
        by_height(regions_one),
        by_height(regions_three),
    )


def fold(values):
    return jnp.concatenate([values[..., 128 * g : 128 * g + 128] for g in range(4)], -2)


def unfold(values):
    return jnp.concatenate([values[..., 7 * g : 7 * g + 7, :] for g in range(4)], -1)


def early_kernel(tok_ref, early_ref):
    early_ref[...] = tok_ref[0:2, 3:17]


def rows_kernel(tok_ref, cot_ref, ha_ref):
    ha_ref[:, 0:3] = tok_ref[:, 0:3]
    ha_ref[:, 3:6] = fold(cot_ref[:, 0:3].astype(F32)).astype(BF)


def late_kernel(tok_ref, cot_ref, ha_ref, late_ref):
    late_ref[:, 0:11] = tok_ref[0:2, 17:28]
    late_ref[:, 11:14] = ha_ref[0:2, 0:3]
    late_ref[:, 14:18] = fold(cot_ref[0:2, 3:7].astype(F32)).astype(BF)
    late_ref[:, 18:21] = ha_ref[0:2, 3:6]


def rows_back_kernel(own_ref, ta_ref, ha_ref):
    ha_ref[0:2, 0:3] = ta_ref[:, 11:14]
    ha_ref[0:2, 3:6] = ta_ref[:, 18:21]
    ha_ref[2:4] = own_ref[...]


def arrange(kernel, shape, *operands):
    return pl.pallas_call(
        kernel,
        out_shape=jax.ShapeDtypeStruct(shape, BF),
        compiler_params=params(8),
        cost_estimate=cost(0.3),
    )(*operands)


def put_rows(stage, frames, rows, values):
    values = values.astype(F32)
    stage[frames, rows, 0:28, :] = values
    stage[frames, rows, 28:36, :] = values[:, :, 0:8, :]


def cut_windows(stage, win):
    for hw in range(2):
        for ww in range(4):
            win[hw * 4 + ww] = stage[:, 7 * hw : 7 * hw + 7, 3 + 7 * ww : 11 + 7 * ww, :].reshape(
                ROWS, 128
            )


def join_windows(win, stage):
    for hw in range(2):
        for ww in range(4):
            stage[:, 7 * hw : 7 * hw + 7, 3 + 7 * ww : 11 + 7 * ww, :] = win[hw * 4 + ww].reshape(
                WT, WS, 8, 128
            )
    stage[:, :, 0:3, :] = stage[:, :, 28:31, :]


def front_kernel(late, *refs):
    n_in = 3 if late else 2
    pieces, refs = refs[:n_in], refs[n_in:]
    gain_ref, proj_ref, outw_ref, bias_ref, row_ref = refs[:5]
    refs = refs[5:]
    n_out = 1 if late else 2
    outs, refs = refs[:n_out], refs[n_out:]
    xw_ref, kv_ref, t_ref, p_ref, o_ref, inv_ref, stage, win, projT = refs
    step = pl.program_id(0)

    @pl.when(step == 0)
    def _():
        own = pieces[0]
        if late:
            put_rows(stage, slice(0, 2), slice(0, 11), own[2:4, 17:28])
            put_rows(stage, slice(2, 4), slice(0, 14), pieces[1][:, 0:14])
            put_rows(stage, slice(0, 2), slice(11, 14), pieces[2][2:4, 0:3])
        else:
            put_rows(stage, slice(0, 2), slice(0, 14), own[2:4, 3:17])
            put_rows(stage, slice(2, 4), slice(0, 14), pieces[1][...])
        for g in range(3):
            at = slice(128 * g, 128 * g + 128)
            projT[at, :] = proj_ref[:, at].astype(F32).T.astype(BF)
        cut_windows(stage, win)

    xs, operands = [], []
    for u in range(PER_STEP):
        x = win[step * PER_STEP + u]
        xs.append(x)
        xw_ref[u] = x.astype(BF)
        xhat, _ = normalise(x)
        n = (xhat * gain_ref[...]).astype(BF)
        kv = dot(n, proj_ref[:, 128:]).astype(BF)
        kv_ref[u] = kv
        t = dot_nt(projT[...], lengthen(n))
        qT = (t[:128] * (SCALE * LOG2E)).astype(BF)
        rest = t[128:].astype(BF)
        t_ref[u, :128] = qT
        t_ref[u, 128:] = rest[:128]

        def keep(h, probs, u=u):
            p_ref[u, h] = probs

        operands.append(
            (kv[:, :128], qT, rest[128:], region_mask(row_ref[u]), lambda h: bias_ref[h], keep)
        )
    for u, (oT, inverse) in enumerate(attend_four(operands)):
        o_ref[u] = oT.astype(BF)
        inv_ref[u] = inverse
        mixed = dot(oT.T[:ROWS].astype(BF), outw_ref[...]).astype(BF).astype(F32)
        win[step * PER_STEP + u] = xs[u] + mixed

    @pl.when(step == STEPS - 1)
    def _():
        join_windows(win, stage)
        if late:
            outs[0][...] = stage[:, :, 0:28, :].astype(BF)
        else:
            outs[0][...] = stage[:, 0:9, 0:28, :].astype(BF)
            outs[1][...] = stage[:, 9:14, 0:28, :].astype(BF)


def whole(shape):
    return pl.BlockSpec(shape, lambda i: (0,) * len(shape))


def each(shape):
    return pl.BlockSpec((PER_STEP,) + shape, lambda i: (i,) + (0,) * len(shape))


SAVED = (
    ((ROWS, 128), BF),
    ((ROWS, 256), BF),
    ((256, LANES), BF),
    ((4, ROWS, LANES), BF),
    ((128, LANES), BF),
    ((8, LANES), F32),
)


def front(late, pieces, gain, proj, outw, bias, row):
    consts = (gain, proj, outw, bias)
    shapes = [(4, 14, 28, 128)] if late else [(4, 9, 28, 128), (4, 5, 28, 128)]
    out = pl.pallas_call(
        functools.partial(front_kernel, late),
        grid=(STEPS,),
        in_specs=[whole(a.shape) for a in tuple(pieces) + consts] + [each((1, LANES))],
        out_specs=[whole(s) for s in shapes] + [each(s) for s, _ in SAVED],
        out_shape=[jax.ShapeDtypeStruct(s, BF) for s in shapes]
        + [jax.ShapeDtypeStruct((8,) + s, d) for s, d in SAVED],
        scratch_shapes=[
            pltpu.VMEM((4, 14, 40, 128), F32),
            pltpu.VMEM((8, ROWS, 128), F32),
            pltpu.VMEM((384, 128), BF),
        ],
        compiler_params=params(),
        cost_estimate=cost(9),
    )(*pieces, *consts, row)
    return out[: len(shapes)], out[len(shapes) :]


def back_kernel(late, *refs):
    n_in = 3 if late else 2
    pieces, refs = refs[:n_in], refs[n_in:]
    gain_ref, proj_ref, outw_ref = refs[:3]
    xw_ref, kv_ref, t_ref, p_ref, o_ref, inv_ref = refs[3:9]
    refs = refs[9:]
    n_out = 3 if late else 2
    outs, refs = refs[:n_out], refs[n_out:]
    stage, win = refs
    step = pl.program_id(0)

    @pl.when(step == 0)
    def _():
        if late:
            put_rows(stage, slice(0, 4), slice(0, 14), pieces[0][...])
            outs[1][:, 14:21] = pieces[1][...]
            outs[2][:, 3:6] = pieces[2][...]
        else:
            put_rows(stage, slice(0, 4), slice(0, 9), pieces[0][...])
            put_rows(stage, slice(0, 4), slice(9, 14), pieces[1][...])
        cut_windows(stage, win)

    drs, operands = [], []
    for u in range(PER_STEP):
        dr = win[step * PER_STEP + u]
        drs.append(dr)
        operands.append(
            (
                kv_ref[u, :, 128:],
                t_ref[u, :128],
                t_ref[u, 128:],
                o_ref[u].astype(F32),
                dot_nt(outw_ref[...], lengthen(dr.astype(BF))),
                inv_ref[u],
                lambda h, u=u: p_ref[u, h],
            )
        )
    for u, (dq, dk, dv) in enumerate(attend_four_back(operands)):
        dpacked = jnp.concatenate([dq.astype(BF), dk.astype(BF), dv.astype(BF)], 1)
        dn = dot_nt(dpacked, proj_ref[...])
        xhat, rstd = normalise(xw_ref[u].astype(F32))
        win[step * PER_STEP + u] = drs[u] + normalise_back(dn * gain_ref[...], xhat, rstd)

    @pl.when(step == STEPS - 1)
    def _():
        join_windows(win, stage)
        if late:
            outs[0][...] = stage[0:2, 0:11, 0:28, :].astype(BF)
            outs[1][:, 0:14] = stage[2:4, :, 0:28, :].astype(BF)
            outs[2][:, 0:3] = stage[0:2, 11:14, 0:28, :].astype(BF)
        else:
            outs[0][...] = stage[0:2, :, 0:28, :].astype(BF)
            outs[1][...] = stage[2:4, :, 0:28, :].astype(BF)


def back(late, pieces, gain, proj, outw, saved):
    consts = (gain, proj, outw)
    if late:
        shapes = [(2, n, 28, 128) for n in (11, 21, 6)]
    else:
        shapes = [(2, 14, 28, 128), (2, 14, 28, 128)]
    return pl.pallas_call(
        functools.partial(back_kernel, late),
        grid=(STEPS,),
        in_specs=[whole(a.shape) for a in tuple(pieces) + consts] + [each(s) for s, _ in SAVED],
        out_specs=[whole(s) for s in shapes],
        out_shape=[jax.ShapeDtypeStruct(s, BF) for s in shapes],
        scratch_shapes=[
            pltpu.VMEM((4, 14, 40, 128), F32),
            pltpu.VMEM((8, ROWS, 128), F32),
        ],
        compiler_params=params(),
        cost_estimate=cost(10),
    )(*pieces, *consts, *saved)


def middle_kernel(
    resA_ref, resB_ref, resN_ref, cot_ref, cta_ref, cha_ref,
    mg1_ref, mg2_ref, g3_ref, row_ref, mw1_hbm, mw2_hbm, p3_hbm, bias_hbm, ow3_hbm,
    dA_ref, dB_ref, dN_ref, so_ref, sta_ref, sha_ref,
    stage, stage2, xhat1, rstd1, xhat2, rstd2, cotw, k_s, v_s, qT_s, kT_s, vT_s, probs_s, oT_s, inv_s, doT_s, dqkv_s,
    mw1_ref, mw2_ref, p3_ref, bias_ref, ow3_ref, sems,
):
    fetches = [
        pltpu.make_async_copy(there, here, sems.at[i])
        for i, (there, here) in enumerate(
            (
                (mw1_hbm, mw1_ref),
                (mw2_hbm, mw2_ref),
                (p3_hbm, p3_ref),
                (bias_hbm, bias_ref),
                (ow3_hbm, ow3_ref),
            )
        )
    ]
    for fetch in fetches:
        fetch.start()
    sources = [(resA_ref, i) for i in range(5)] + [(resB_ref, i) for i in range(14)]
    sources += [(resN_ref, i) for i in range(9)]
    for i, (ref, at) in enumerate(sources):
        stage[:, i // 2, i % 2, 0:28, :] = ref[:, at].astype(F32)
    stage[:, :, :, 28:32, :] = jnp.zeros((4, 14, 2, 4, 128), F32)
    cotw[...] = jnp.zeros((4, 7, 8, 512), F32)
    cotw[0:2, 0:4, 0:7, :] = cot_ref[2:4, 3:7].astype(F32)
    cotw[2:4, :, 0:7, :] = unfold(cta_ref[:, 14:21].astype(F32))
    cotw[0:2, 4:7, 0:7, :] = unfold(cha_ref[2:4, 3:6].astype(F32))

    def merge_one(f, _):
        pieces = [
            stage[f, :, q % 2, pl.ds(q // 2, 16, stride=2), :].reshape(ROWS, 128) for q in range(4)
        ]
        xhat, rstd = normalise(jnp.concatenate(pieces, 1))
        xhat1[f] = xhat
        rstd1[f] = jnp.broadcast_to(rstd, (ROWS, 128))
        merged = dot((xhat * mg1_ref[...]).astype(BF), mw1_ref[...]).astype(BF).astype(F32)
        for half in range(2):
            stage2[half, f] = merged[:, 128 * half : 128 * half + 128].reshape(7, 2, 16, 128)
        return 0

    fetches[0].wait()
    lax.fori_loop(0, 4, merge_one, 0)
    fetches[1].wait()
    pieces = [
        stage2[half, :, :, q % 2, pl.ds(q // 2, 8, stride=2), :].reshape(ROWS, 128)
        for q in range(4)
        for half in range(2)
    ]
    xhat, rstd = normalise(jnp.concatenate(pieces, 1))
    xhat2[...] = xhat
    rstd2[...] = jnp.broadcast_to(rstd, (ROWS, 128))
    merged_two = dot((xhat * mg2_ref[...]).astype(BF), mw2_ref[...]).astype(BF).astype(F32)
    xhat3, rstd3 = normalise(merged_two)
    n3 = (xhat3 * g3_ref[...]).astype(BF)
    fetches[2].wait()
    packed = [dot(n3, p3_ref[:, 512 * i : 512 * i + 512]) for i in range(3)]
    for g in range(4):
        q, k, v = (part[:, 128 * g : 128 * g + 128] for part in packed)
        k_s[g] = k.astype(BF)
        v_s[g] = v.astype(BF)
        qT_s[g] = (lengthen(q).T * (SCALE * LOG2E)).astype(BF)
        kT_s[g] = lengthen(k).T.astype(BF)
        vT_s[g] = lengthen(v).T.astype(BF)
    mask = region_mask(row_ref[...])
    fetches[3].wait()

    def heads(i, _):
        operands = []
        for g in (2 * i, 2 * i + 1):

            def keep(h, probs, g=g):
                probs_s[g * 4 + h] = probs

            operands.append(
                (k_s[g], qT_s[g], vT_s[g], mask, lambda h, g=g: bias_ref[g * 4 + h], keep)
            )
        for u, (oT, inverse) in enumerate(attend_four(operands)):
            oT_s[2 * i + u] = oT
            inv_s[2 * i + u] = inverse
        return 0

    lax.fori_loop(0, 2, heads, 0)
    fetches[4].wait()
    att = jnp.concatenate([oT_s[g].T[:ROWS].astype(BF) for g in range(4)], 1)
    mixed = dot(att, ow3_ref[...]).astype(BF).astype(F32)
    section = (merged_two + mixed).reshape(4, 7, 8, 512)
    section = fold(section[:, :, 0:7])
    so_ref[...] = section[0:2, 0:4].astype(BF)
    sta_ref[...] = section[2:4].astype(BF)
    sha_ref[...] = section[0:2, 4:7].astype(BF)

    cot = cotw[...].reshape(ROWS, 512)
    cot_long = lengthen(cot.astype(BF))
    doT = dot_nt(ow3_ref[...], cot_long)
    for g in range(4):
        doT_s[g] = doT[128 * g : 128 * g + 128]

    def heads_back(i, _):
        operands = [
            (
                v_s[g], qT_s[g], kT_s[g], oT_s[g], doT_s[g], inv_s[g],
                lambda h, g=g: probs_s[g * 4 + h],
            )
            for g in (2 * i, 2 * i + 1)
        ]
        for u, (dq, dk, dv) in enumerate(attend_four_back(operands)):
            dqkv_s[2 * i + u] = dq.astype(BF)
            dqkv_s[4 + 2 * i + u] = dk.astype(BF)
            dqkv_s[8 + 2 * i + u] = dv.astype(BF)
        return 0

    lax.fori_loop(0, 2, heads_back, 0)
    dpacked = jnp.concatenate([dqkv_s[i] for i in range(12)], 1)
    dn3 = dot_nt(dpacked, p3_ref[...])
    dm2 = cot + normalise_back(dn3 * g3_ref[...], xhat3, rstd3)
    dn2 = dot_nt(dm2.astype(BF), mw2_ref[...])
    dg2 = normalise_back(dn2 * mg2_ref[...], xhat2[...], rstd2[:, 0:1])
    for q in range(4):
        for half in range(2):
            at = 256 * q + 128 * half
            stage2[half, :, :, q % 2, pl.ds(q // 2, 8, stride=2), :] = dg2[:, at : at + 128].reshape(
                4, 7, 8, 128
            )

    def merge_one_back(f, _):
        dm1 = jnp.concatenate([stage2[half, f].reshape(ROWS, 128) for half in range(2)], 1).astype(BF)
        dn1 = dot_nt(dm1, mw1_ref[...])
        dg1 = normalise_back(dn1 * mg1_ref[...], xhat1[f], rstd1[f, :, 0:1])
        for q in range(4):
            stage[f, :, q % 2, pl.ds(q // 2, 16, stride=2), :] = dg1[
                :, 128 * q : 128 * q + 128
            ].reshape(14, 16, 128)
        return 0

    lax.fori_loop(0, 4, merge_one_back, 0)
    targets = [(dA_ref, i) for i in range(5)] + [(dB_ref, i) for i in range(14)]
    targets += [(dN_ref, i) for i in range(9)]
    for i, (ref, at) in enumerate(targets):
        ref[:, at] = stage[:, i // 2, i % 2, 0:28, :].astype(BF)


def middle(*operands):
    shapes = [
        (4, 5, 28, 128), (4, 14, 28, 128), (4, 9, 28, 128),
        (2, 4, 28, 128), (2, 7, 28, 128), (2, 3, 28, 128),
    ]
    return pl.pallas_call(
        middle_kernel,
        in_specs=[pl.BlockSpec(memory_space=pltpu.VMEM)] * 10
        + [pl.BlockSpec(memory_space=pl.ANY)] * 5,
        out_shape=[jax.ShapeDtypeStruct(s, BF) for s in shapes],
        scratch_shapes=[
            pltpu.VMEM((4, 14, 2, 32, 128), F32),
            pltpu.VMEM((2, 4, 7, 2, 16, 128), F32),
            pltpu.VMEM((4, ROWS, 512), F32),
            pltpu.VMEM((4, ROWS, 128), F32),
            pltpu.VMEM((ROWS, 1024), F32),
            pltpu.VMEM((ROWS, 128), F32),
            pltpu.VMEM((4, 7, 8, 512), F32),
            pltpu.VMEM((4, ROWS, 128), BF),
            pltpu.VMEM((4, ROWS, 128), BF),
            pltpu.VMEM((4, 128, LANES), BF),
            pltpu.VMEM((4, 128, LANES), BF),
            pltpu.VMEM((4, 128, LANES), BF),
            pltpu.VMEM((16, ROWS, LANES), BF),
            pltpu.VMEM((4, 128, LANES), F32),
            pltpu.VMEM((4, 8, LANES), F32),
            pltpu.VMEM((4, 128, LANES), F32),
            pltpu.VMEM((12, ROWS, 128), BF),
            pltpu.VMEM((512, 256), BF),
            pltpu.VMEM((1024, 512), BF),
            pltpu.VMEM((512, 1536), BF),
            pltpu.VMEM((HEADS3, ROWS, LANES), F32),
            pltpu.VMEM((512, 512), BF),
            pltpu.SemaphoreType.DMA((5,)),
        ],
        compiler_params=params(36),
        cost_estimate=cost(14),
    )(*operands)


def send(values, axis, by):
    n = lax.axis_size(axis)
    return lax.ppermute(values, axis, [(i, (i + by) % n) for i in range(n)])


def per_device(
    tokens,
    regions_one,
    regions_three,
    gain_one,
    projection_one,
    outward_one,
    table_one,
    merge_gain_one,
    merge_weight_one,
    merge_gain_two,
    merge_weight_two,
    gain_three,
    projection_three,
    outward_three,
    table_three,
    cotangent,
):
    ta_early = send(arrange(early_kernel, (2, 14, 28, 128), tokens), "ta", -1)
    ha_late = send(arrange(rows_kernel, (4, 6, 28, 128), tokens, cotangent), "ha", -1)
    bias_one, bias_three, row_one, row_three = prepare(
        table_one, table_three, regions_one, regions_three
    )
    ta_late = send(
        arrange(late_kernel, (2, 21, 28, 128), tokens, cotangent, ha_late), "ta", -1
    )
    args = (gain_one[None], projection_one, outward_one, bias_one)
    (res_send, res_a), saved_a = front(False, (tokens, ta_early), *args, row_one[:8])
    res_next = send(res_send, "ha", -1)
    (res_b,), saved_b = front(True, (tokens, ta_late, ha_late), *args, row_one[8:])
    d_a, d_b, d_send, sec_own, sec_ta, sec_ha = middle(
        res_a, res_b, res_next, cotangent, ta_late, ha_late,
        merge_gain_one[None], merge_gain_two[None], gain_three[None], row_three,
        merge_weight_one, merge_weight_two, projection_three, bias_three, outward_three,
    )
    d_prev = send(d_send, "ha", 1)
    own_b, ta_b, ha_b = back(
        True, (d_b, sec_ta, sec_ha), gain_one[None], projection_one, outward_one, saved_b
    )
    d_prev, own_b = lax.optimization_barrier((d_prev, own_b))
    ta_b = send(ta_b, "ta", 1)
    own_a, ta_a = back(False, (d_prev, d_a), gain_one[None], projection_one, outward_one, saved_a)
    ta_b, own_a = lax.optimization_barrier((ta_b, own_a))
    ta_a = send(ta_a, "ta", 1)
    ha = send(arrange(rows_back_kernel, (4, 6, 28, 128), ha_b, ta_b), "ha", 1)

    section = jnp.concatenate(
        [ha[:, 3:], jnp.concatenate([ta_b[:, 14:18], sec_own], 0)], 1
    )
    section = jnp.transpose(section.reshape(4, 7, 4, 7, 128), (0, 1, 3, 2, 4)).reshape(4, 7, 7, 512)
    grad = jnp.concatenate(
        [
            ha[:, :3],
            jnp.concatenate([jnp.zeros_like(ta_a), own_a], 0),
            jnp.concatenate([ta_b[:, :11], own_b], 0),
        ],
        1,
    )
    in_order = Layout(major_to_minor=(0, 1, 2, 3))
    grad = with_layout_constraint(jnp.transpose(grad, (1, 2, 0, 3)), in_order)
    grad = lax.dynamic_update_slice(grad, jnp.transpose(ta_a, (1, 2, 0, 3)), (3, 0, 0, 0))
    grad = with_layout_constraint(grad, in_order)
    return (section, jnp.transpose(grad, (2, 0, 1, 3)))


def solution(mesh):
    tile = P(("col", "ta"), "ha", None, None)
    ids = P(("col", "ta"), "ha", None)
    in_specs = (tile, ids, ids) + (P(),) * 12 + (tile,)
    return jax.shard_map(
        per_device, mesh=mesh, in_specs=in_specs, out_specs=(tile, tile), check_vma=False
    )
```

```python
import functools

import jax
import jax.numpy as jnp
import numpy as np
from jax import lax
from jax.experimental import pallas as pl
from jax.experimental.layout import Layout, with_layout_constraint
from jax.experimental.pallas import tpu as pltpu
from jax.sharding import PartitionSpec as P

HEADS1 = 4
HEADS3 = 16
WT = 4
WS = 7
ST = 2
SS = 3
EPSILON = 1e-05
NREL = 1183
LOG2E = 1.4426950408889634
HEAD = 32
SCALE = HEAD**-0.5
ROWS = WT * WS * 8
LANES = 256
SPAN = 1280
GONE = -1e30
PER_STEP = 4
STEPS = 8 // PER_STEP
BF = jnp.bfloat16
F32 = jnp.float32


def dot(a, b):
    return jnp.dot(a, b, preferred_element_type=F32)


def dot_nt(a, b):
    return lax.dot_general(a, b, (((1,), (1,)), ((), ())), preferred_element_type=F32)


def params(limit=28):
    return pltpu.CompilerParams(vmem_limit_bytes=limit * 1024 * 1024)


def cost(us):
    return pl.CostEstimate(flops=int(us * 1.1e9), bytes_accessed=int(us * 1e6), transcendentals=0)


def normalise(x):
    centred = x - jnp.mean(x, -1, keepdims=True)
    rstd = lax.rsqrt(jnp.mean(centred * centred, -1, keepdims=True) + EPSILON)
    return centred * rstd, rstd


def normalise_back(grad, xhat, rstd):
    return rstd * (
        grad
        - jnp.mean(grad, -1, keepdims=True)
        - xhat * jnp.mean(grad * xhat, -1, keepdims=True)
    )


def head_rows(x, h):
    return x[HEAD * h : HEAD * (h + 1)]


def head_of_lane(shape):
    return lax.broadcasted_iota(jnp.int32, shape, 1) // HEAD


def by_head(x):
    lane = head_of_lane((1, 128))
    return jnp.concatenate([x * (lane == h).astype(F32).astype(BF) for h in range(4)], 0)


def pick_heads(stacked):
    lane = head_of_lane((ROWS, 128))
    got = stacked[:ROWS]
    for h in range(1, 4):
        got = jnp.where(lane == h, stacked[ROWS * h : ROWS * (h + 1)], got)
    return got


def lengthen(x):
    return jnp.concatenate([x, jnp.zeros((LANES - ROWS, x.shape[1]), x.dtype)], 0)


def region_mask(row):
    wide = jnp.broadcast_to(row, (128, LANES))
    column = wide.T[:ROWS]
    column = jnp.concatenate([column, column], 1)
    return jnp.where(column == wide[0:1], 0.0, GONE).astype(F32)


def attend_four(windows):
    scores = [dot(by_head(k), qT) for k, qT, _, _, _, _ in windows]
    results = []
    for s, (_, _, vT, mask, bias_at, keep_probs) in zip(scores, windows):
        outs, inverses = [], []
        for h in range(4):
            biased = s[ROWS * h : ROWS * (h + 1)] + (bias_at(h) + mask)
            peak = jnp.max(biased, 0, keepdims=True)
            probs = jnp.exp2(biased - peak).astype(BF)
            keep_probs(h, probs)
            extended = jnp.concatenate([head_rows(vT, h)[:, :ROWS], jnp.ones((16, ROWS), BF)], 0)
            out = dot(extended, probs)
            inverse = 1.0 / out[HEAD : HEAD + 1]
            outs.append(out[:HEAD] * inverse)
            inverses.append(inverse)
        results.append((jnp.concatenate(outs, 0), jnp.concatenate(inverses + inverses, 0)))
    return results


def attend_four_back(windows):
    first = []
    for v, qT, kT, oT, doT, inverse, probs_at in windows:
        scaled, deltas = [], []
        for h in range(4):
            part = head_rows(doT, h) * inverse[h : h + 1]
            deltas.append(jnp.sum(part * head_rows(oT, h), 0, keepdims=True))
            scaled.append(part)
        scaled = jnp.concatenate(scaled, 0).astype(BF)
        first.append((scaled, deltas, dot(by_head(v), scaled)))
    results = []
    for (scaled, deltas, dprobs), (v, qT, kT, oT, doT, inverse, probs_at) in zip(first, windows):
        probs = [probs_at(h) for h in range(4)]
        dscores = [
            (probs[h].astype(F32) * (dprobs[ROWS * h : ROWS * (h + 1)] - deltas[h])).astype(BF)
            for h in range(4)
        ]
        dv = pick_heads(dot_nt(jnp.concatenate(probs, 0), scaled))
        dk = pick_heads(dot_nt(jnp.concatenate(dscores, 0), qT))
        dqT = jnp.concatenate(
            [dot(head_rows(kT, h)[:, :ROWS], dscores[h]) for h in range(4)], 0
        )
        results.append((dqT.T[:ROWS] * SCALE, dk * (1.0 / LOG2E), dv))
    return results


def lanes_of(shape):
    return lax.broadcasted_iota(jnp.int32, shape, 1)


def region_rows(ids, section):
    columns = ids.shape[1]
    count = columns // WS
    place = lax.broadcasted_iota(jnp.int32, (columns, LANES * count), 0)
    lane = lanes_of((columns, LANES * count))
    column = lane % 8
    real = (column < WS) & (lane % LANES < ROWS)
    if section == 3:
        column = jnp.where(column < 3, column + 4, column - 3)
    chosen = real & (place == lane // LANES * WS + column)
    spread = dot(ids.astype(F32).astype(BF), chosen.astype(F32).astype(BF))
    row = lax.broadcasted_iota(jnp.int32, spread.shape, 0)
    lane = lanes_of(spread.shape)
    real = (lane[:1] % 8 < WS) & (lane[:1] % LANES < ROWS)
    rows = []
    for hw in range(ids.shape[0] // (WT * WS)):
        mine = lane % LANES // 8 == row % 4 * WS + row // 4 - WS * hw
        inside = (row >= WT * WS * hw) & (row < WT * WS * (hw + 1))
        found = jnp.sum(jnp.where(mine & inside, spread, 0.0), 0, keepdims=True)
        found = jnp.where(real, found, -1.0)
        rows += [found[:, LANES * ww : LANES * (ww + 1)] for ww in range(count)]
    return rows


def prepare_kernel(
    t1_ref, t3_ref, s_ref, r1_ref, r3_ref, o1_ref, o3_ref, row1_ref, row3_ref, tab, spread
):
    tab[...] = jnp.zeros((24, SPAN), F32)
    tab[0:4, 0:NREL] = t1_ref[...] * LOG2E
    tab[8:24, 0:NREL] = t3_ref[...] * LOG2E
    slabs = []
    for dt in range(7):
        start = 169 * dt
        low = start // 128 * 128
        run = tab[:, low : low + 384]
        if start > low:
            run = pltpu.roll(run, 384 - (start - low), 1)
        slabs.append(run[:, :256])
    left = jnp.concatenate(slabs, 0)
    first = left.astype(BF)
    rest = left - first.astype(F32)
    second = rest.astype(BF)
    third = (rest - second.astype(F32)).astype(BF)
    chosen = s_ref[...]
    got = dot(first, chosen) + dot(second, chosen) + dot(third, chosen)
    lane16 = lanes_of((16, 128))
    for dt in range(7):
        for wj in range(8):
            part = got[24 * dt : 24 * dt + 24, 128 * wj : 128 * wj + 128]
            spread[dt, pl.ds(wj, 8, stride=8), :] = part[0:8]
            later = part[8:24]
            turned = jnp.where(lane16 % 8 < 3, pltpu.roll(later, 124, 1), pltpu.roll(later, 3, 1))
            spread[dt, pl.ds(64 + (7 if wj == 7 else (wj + 3) % 7), 16, stride=8), :] = turned
    for o_ref, heads, at in ((o1_ref, HEADS1, 0), (o3_ref, HEADS3, 64)):
        lane = lanes_of((heads * 8, 128))
        for tj in range(WT):
            for hj in range(WS):
                p0, p1, p2, p3 = (
                    pltpu.roll(
                        spread[ti - tj + 3, at : at + heads * 8, :], (ti * 56 - (6 - hj) * 8) % 128, 1
                    )
                    for ti in range(WT)
                )
                left = jnp.where(lane < 56, p0, jnp.where(lane < 112, p1, p2))
                right = jnp.where(lane < 40, p2, p3)
                row = (tj * WS + hj) * 8
                o_ref[:, row : row + 8, 0:128] = left.reshape(heads, 8, 128)
                o_ref[:, row : row + 8, 128:256] = right.reshape(heads, 8, 128)
    for i, found in enumerate(region_rows(r1_ref[...], 1)):
        row1_ref[i] = found
    row3_ref[...] = region_rows(r3_ref[...], 3)[0]


def chooser():
    chosen = np.zeros((256, 1024), np.float32)
    for wj in range(WS):
        for dh in range(13):
            for wi in range(WS):
                chosen[dh * 13 + wi - wj + 6, wj * 128 + dh * 8 + wi] = 1.0
    return jnp.asarray(chosen, BF)


def by_height(ids):
    return jnp.transpose(ids, (1, 0, 2)).reshape(-1, ids.shape[2])


def prepare(table_one, table_three, regions_one, regions_three):
    return pl.pallas_call(
        prepare_kernel,
        out_shape=(
            jax.ShapeDtypeStruct((HEADS1, ROWS, LANES), F32),
            jax.ShapeDtypeStruct((HEADS3, ROWS, LANES), F32),
            jax.ShapeDtypeStruct((16, 1, LANES), F32),
            jax.ShapeDtypeStruct((1, LANES), F32),
        ),
        scratch_shapes=[pltpu.VMEM((24, SPAN), F32), pltpu.VMEM((7, 24 * 8, 128), F32)],
        compiler_params=params(),
        cost_estimate=cost(3),
    )(
        jnp.transpose(table_one),
        jnp.transpose(table_three),
        chooser(),
        by_height(regions_one),
        by_height(regions_three),
    )


def fold(values):
    return jnp.concatenate([values[..., 128 * g : 128 * g + 128] for g in range(4)], -2)


def unfold(values):
    return jnp.concatenate([values[..., 7 * g : 7 * g + 7, :] for g in range(4)], -1)


def late_kernel(tok_ref, cot_ref, ha_ref, ch_ref, late_ref):
    late_ref[:, 0:11] = tok_ref[0:2, 17:28]
    late_ref[:, 11:14] = ha_ref[0:2]
    late_ref[:, 14:18] = fold(cot_ref[0:2, 3:7].astype(F32)).astype(BF)
    late_ref[:, 18:21] = ch_ref[0:2]


def arrange(kernel, shape, *operands):
    return pl.pallas_call(
        kernel,
        out_shape=jax.ShapeDtypeStruct(shape, BF),
        compiler_params=params(8),
        cost_estimate=cost(0.3),
    )(*operands)


def put_rows(stage, frames, rows, values):
    values = values.astype(F32)
    stage[frames, rows, 0:28, :] = values
    stage[frames, rows, 28:36, :] = values[:, :, 0:8, :]


def cut_windows(stage, win):
    for hw in range(2):
        for ww in range(4):
            win[hw * 4 + ww] = stage[:, 7 * hw : 7 * hw + 7, 3 + 7 * ww : 11 + 7 * ww, :].reshape(
                ROWS, 128
            )


def join_windows(win, stage):
    for hw in range(2):
        for ww in range(4):
            stage[:, 7 * hw : 7 * hw + 7, 3 + 7 * ww : 11 + 7 * ww, :] = win[hw * 4 + ww].reshape(
                WT, WS, 8, 128
            )
    stage[:, :, 0:3, :] = stage[:, :, 28:31, :]


def front_kernel(late, *refs):
    n_in = 3 if late else 2
    pieces, refs = refs[:n_in], refs[n_in:]
    gain_ref, proj_ref, outw_ref, bias_ref, row_ref = refs[:5]
    refs = refs[5:]
    n_out = 1 if late else 2
    outs, refs = refs[:n_out], refs[n_out:]
    xw_ref, kv_ref, t_ref, p_ref, o_ref, inv_ref, stage, win, projT = refs
    step = pl.program_id(0)

    @pl.when(step == 0)
    def _():
        own = pieces[0]
        if late:
            put_rows(stage, slice(0, 2), slice(0, 11), own[2:4, 17:28])
            put_rows(stage, slice(2, 4), slice(0, 14), pieces[1][:, 0:14])
            put_rows(stage, slice(0, 2), slice(11, 14), pieces[2][2:4])
        else:
            put_rows(stage, slice(0, 2), slice(0, 14), own[2:4, 3:17])
            put_rows(stage, slice(2, 4), slice(0, 14), pieces[1][...])
        for g in range(3):
            at = slice(128 * g, 128 * g + 128)
            projT[at, :] = proj_ref[:, at].astype(F32).T.astype(BF)
        cut_windows(stage, win)

    xs, operands = [], []
    for u in range(PER_STEP):
        x = win[step * PER_STEP + u]
        xs.append(x)
        xw_ref[u] = x.astype(BF)
        xhat, _ = normalise(x)
        n = (xhat * gain_ref[...]).astype(BF)
        kv = dot(n, proj_ref[:, 128:]).astype(BF)
        kv_ref[u] = kv
        t = dot_nt(projT[...], lengthen(n))
        qT = (t[:128] * (SCALE * LOG2E)).astype(BF)
        rest = t[128:].astype(BF)
        t_ref[u, :128] = qT
        t_ref[u, 128:] = rest[:128]

        def keep(h, probs, u=u):
            p_ref[u, h] = probs

        operands.append(
            (kv[:, :128], qT, rest[128:], region_mask(row_ref[u]), lambda h: bias_ref[h], keep)
        )
    for u, (oT, inverse) in enumerate(attend_four(operands)):
        o_ref[u] = oT.astype(BF)
        inv_ref[u] = inverse
        mixed = dot(oT.T[:ROWS].astype(BF), outw_ref[...]).astype(BF).astype(F32)
        win[step * PER_STEP + u] = xs[u] + mixed

    @pl.when(step == STEPS - 1)
    def _():
        join_windows(win, stage)
        if late:
            outs[0][...] = stage[:, :, 0:28, :].astype(BF)
        else:
            outs[0][...] = stage[:, 0:9, 0:28, :].astype(BF)
            outs[1][...] = stage[:, 9:14, 0:28, :].astype(BF)


def whole(shape):
    return pl.BlockSpec(shape, lambda i: (0,) * len(shape))


def each(shape):
    return pl.BlockSpec((PER_STEP,) + shape, lambda i: (i,) + (0,) * len(shape))


SAVED = (
    ((ROWS, 128), BF),
    ((ROWS, 256), BF),
    ((256, LANES), BF),
    ((4, ROWS, LANES), BF),
    ((128, LANES), BF),
    ((8, LANES), F32),
)


def front(late, pieces, gain, proj, outw, bias, row):
    consts = (gain, proj, outw, bias)
    shapes = [(4, 14, 28, 128)] if late else [(4, 9, 28, 128), (4, 5, 28, 128)]
    out = pl.pallas_call(
        functools.partial(front_kernel, late),
        grid=(STEPS,),
        in_specs=[whole(a.shape) for a in tuple(pieces) + consts] + [each((1, LANES))],
        out_specs=[whole(s) for s in shapes] + [each(s) for s, _ in SAVED],
        out_shape=[jax.ShapeDtypeStruct(s, BF) for s in shapes]
        + [jax.ShapeDtypeStruct((8,) + s, d) for s, d in SAVED],
        scratch_shapes=[
            pltpu.VMEM((4, 14, 40, 128), F32),
            pltpu.VMEM((8, ROWS, 128), F32),
            pltpu.VMEM((384, 128), BF),
        ],
        compiler_params=params(),
        cost_estimate=cost(9),
    )(*pieces, *consts, row)
    return out[: len(shapes)], out[len(shapes) :]


def back_kernel(late, *refs):
    n_in = 3 if late else 2
    pieces, refs = refs[:n_in], refs[n_in:]
    gain_ref, proj_ref, outw_ref = refs[:3]
    xw_ref, kv_ref, t_ref, p_ref, o_ref, inv_ref = refs[3:9]
    refs = refs[9:]
    n_out = 4 if late else 2
    outs, refs = refs[:n_out], refs[n_out:]
    stage, win = refs
    step = pl.program_id(0)

    @pl.when(step == 0)
    def _():
        if late:
            put_rows(stage, slice(0, 4), slice(0, 14), pieces[0][...])
            outs[1][:, 11:15] = pieces[1][:, 0:4]
            outs[2][:, 3:6] = pieces[2][...]
            outs[3][:, 3:6] = pieces[1][:, 4:7]
        else:
            put_rows(stage, slice(0, 4), slice(0, 9), pieces[0][...])
            put_rows(stage, slice(0, 4), slice(9, 14), pieces[1][...])
        cut_windows(stage, win)

    drs, operands = [], []
    for u in range(PER_STEP):
        dr = win[step * PER_STEP + u]
        drs.append(dr)
        operands.append(
            (
                kv_ref[u, :, 128:],
                t_ref[u, :128],
                t_ref[u, 128:],
                o_ref[u].astype(F32),
                dot_nt(outw_ref[...], lengthen(dr.astype(BF))),
                inv_ref[u],
                lambda h, u=u: p_ref[u, h],
            )
        )
    for u, (dq, dk, dv) in enumerate(attend_four_back(operands)):
        dpacked = jnp.concatenate([dq.astype(BF), dk.astype(BF), dv.astype(BF)], 1)
        dn = dot_nt(dpacked, proj_ref[...])
        xhat, rstd = normalise(xw_ref[u].astype(F32))
        win[step * PER_STEP + u] = drs[u] + normalise_back(dn * gain_ref[...], xhat, rstd)

    @pl.when(step == STEPS - 1)
    def _():
        join_windows(win, stage)
        if late:
            outs[0][...] = stage[0:2, 0:11, 0:28, :].astype(BF)
            outs[1][:, 0:11] = stage[2:4, 0:11, 0:28, :].astype(BF)
            outs[2][:, 0:3] = stage[0:2, 11:14, 0:28, :].astype(BF)
            outs[3][:, 0:3] = stage[2:4, 11:14, 0:28, :].astype(BF)
        else:
            outs[0][...] = stage[0:2, :, 0:28, :].astype(BF)
            outs[1][...] = stage[2:4, :, 0:28, :].astype(BF)


def back(late, pieces, gain, proj, outw, saved):
    consts = (gain, proj, outw)
    if late:
        shapes = [(2, n, 28, 128) for n in (11, 15, 6, 6)]
    else:
        shapes = [(2, 14, 28, 128), (2, 14, 28, 128)]
    return pl.pallas_call(
        functools.partial(back_kernel, late),
        grid=(STEPS,),
        in_specs=[whole(a.shape) for a in tuple(pieces) + consts] + [each(s) for s, _ in SAVED],
        out_specs=[whole(s) for s in shapes],
        out_shape=[jax.ShapeDtypeStruct(s, BF) for s in shapes],
        scratch_shapes=[
            pltpu.VMEM((4, 14, 40, 128), F32),
            pltpu.VMEM((8, ROWS, 128), F32),
        ],
        compiler_params=params(),
        cost_estimate=cost(10),
    )(*pieces, *consts, *saved)


def middle_kernel(
    resA_ref, resB_ref, resN_ref, cot_ref, cta_ref, cha_ref,
    mg1_ref, mg2_ref, g3_ref, row_ref, mw1_hbm, mw2_hbm, p3_hbm, bias_hbm, ow3_hbm,
    dA_ref, dB_ref, dN_ref, so_ref, sta_ref, sha_ref,
    stage, stage2, xhat1, rstd1, xhat2, rstd2, cotw, k_s, v_s, qT_s, kT_s, vT_s, probs_s, oT_s, inv_s, doT_s, dqkv_s,
    mw1_ref, mw2_ref, p3_ref, bias_ref, ow3_ref, sems,
):
    fetches = [
        pltpu.make_async_copy(there, here, sems.at[i])
        for i, (there, here) in enumerate(
            (
                (mw1_hbm, mw1_ref),
                (mw2_hbm, mw2_ref),
                (p3_hbm, p3_ref),
                (bias_hbm, bias_ref),
                (ow3_hbm, ow3_ref),
            )
        )
    ]
    for fetch in fetches:
        fetch.start()
    sources = [(resA_ref, i) for i in range(5)] + [(resB_ref, i) for i in range(14)]
    sources += [(resN_ref, i) for i in range(9)]
    for i, (ref, at) in enumerate(sources):
        stage[:, i // 2, i % 2, 0:28, :] = ref[:, at].astype(F32)
    stage[:, :, :, 28:32, :] = jnp.zeros((4, 14, 2, 4, 128), F32)
    cotw[...] = jnp.zeros((4, 7, 8, 512), F32)
    cotw[0:2, 0:4, 0:7, :] = cot_ref[2:4, 3:7].astype(F32)
    cotw[2:4, :, 0:7, :] = unfold(cta_ref[:, 14:21].astype(F32))
    cotw[0:2, 4:7, 0:7, :] = unfold(cha_ref[2:4].astype(F32))

    def merge_one(f, _):
        pieces = [
            stage[f, :, q % 2, pl.ds(q // 2, 16, stride=2), :].reshape(ROWS, 128) for q in range(4)
        ]
        xhat, rstd = normalise(jnp.concatenate(pieces, 1))
        xhat1[f] = xhat
        rstd1[f] = jnp.broadcast_to(rstd, (ROWS, 128))
        merged = dot((xhat * mg1_ref[...]).astype(BF), mw1_ref[...]).astype(BF).astype(F32)
        for half in range(2):
            stage2[half, f] = merged[:, 128 * half : 128 * half + 128].reshape(7, 2, 16, 128)
        return 0

    fetches[0].wait()
    lax.fori_loop(0, 4, merge_one, 0)
    fetches[1].wait()
    pieces = [
        stage2[half, :, :, q % 2, pl.ds(q // 2, 8, stride=2), :].reshape(ROWS, 128)
        for q in range(4)
        for half in range(2)
    ]
    xhat, rstd = normalise(jnp.concatenate(pieces, 1))
    xhat2[...] = xhat
    rstd2[...] = jnp.broadcast_to(rstd, (ROWS, 128))
    merged_two = dot((xhat * mg2_ref[...]).astype(BF), mw2_ref[...]).astype(BF).astype(F32)
    xhat3, rstd3 = normalise(merged_two)
    n3 = (xhat3 * g3_ref[...]).astype(BF)
    fetches[2].wait()
    packed = [dot(n3, p3_ref[:, 512 * i : 512 * i + 512]) for i in range(3)]
    for g in range(4):
        q, k, v = (part[:, 128 * g : 128 * g + 128] for part in packed)
        k_s[g] = k.astype(BF)
        v_s[g] = v.astype(BF)
        qT_s[g] = (lengthen(q).T * (SCALE * LOG2E)).astype(BF)
        kT_s[g] = lengthen(k).T.astype(BF)
        vT_s[g] = lengthen(v).T.astype(BF)
    mask = region_mask(row_ref[...])
    fetches[3].wait()

    def heads(i, _):
        operands = []
        for g in (2 * i, 2 * i + 1):

            def keep(h, probs, g=g):
                probs_s[g * 4 + h] = probs

            operands.append(
                (k_s[g], qT_s[g], vT_s[g], mask, lambda h, g=g: bias_ref[g * 4 + h], keep)
            )
        for u, (oT, inverse) in enumerate(attend_four(operands)):
            oT_s[2 * i + u] = oT
            inv_s[2 * i + u] = inverse
        return 0

    lax.fori_loop(0, 2, heads, 0)
    fetches[4].wait()
    att = jnp.concatenate([oT_s[g].T[:ROWS].astype(BF) for g in range(4)], 1)
    mixed = dot(att, ow3_ref[...]).astype(BF).astype(F32)
    section = (merged_two + mixed).reshape(4, 7, 8, 512)
    section = fold(section[:, :, 0:7])
    so_ref[...] = section[0:2, 0:4].astype(BF)
    sta_ref[...] = section[2:4].astype(BF)
    sha_ref[...] = section[0:2, 4:7].astype(BF)

    cot = cotw[...].reshape(ROWS, 512)
    cot_long = lengthen(cot.astype(BF))
    doT = dot_nt(ow3_ref[...], cot_long)
    for g in range(4):
        doT_s[g] = doT[128 * g : 128 * g + 128]

    def heads_back(i, _):
        operands = [
            (
                v_s[g], qT_s[g], kT_s[g], oT_s[g], doT_s[g], inv_s[g],
                lambda h, g=g: probs_s[g * 4 + h],
            )
            for g in (2 * i, 2 * i + 1)
        ]
        for u, (dq, dk, dv) in enumerate(attend_four_back(operands)):
            dqkv_s[2 * i + u] = dq.astype(BF)
            dqkv_s[4 + 2 * i + u] = dk.astype(BF)
            dqkv_s[8 + 2 * i + u] = dv.astype(BF)
        return 0

    lax.fori_loop(0, 2, heads_back, 0)
    dpacked = jnp.concatenate([dqkv_s[i] for i in range(12)], 1)
    dn3 = dot_nt(dpacked, p3_ref[...])
    dm2 = cot + normalise_back(dn3 * g3_ref[...], xhat3, rstd3)
    dn2 = dot_nt(dm2.astype(BF), mw2_ref[...])
    dg2 = normalise_back(dn2 * mg2_ref[...], xhat2[...], rstd2[:, 0:1])
    for q in range(4):
        for half in range(2):
            at = 256 * q + 128 * half
            stage2[half, :, :, q % 2, pl.ds(q // 2, 8, stride=2), :] = dg2[:, at : at + 128].reshape(
                4, 7, 8, 128
            )

    def merge_one_back(f, _):
        dm1 = jnp.concatenate([stage2[half, f].reshape(ROWS, 128) for half in range(2)], 1).astype(BF)
        dn1 = dot_nt(dm1, mw1_ref[...])
        dg1 = normalise_back(dn1 * mg1_ref[...], xhat1[f], rstd1[f, :, 0:1])
        for q in range(4):
            stage[f, :, q % 2, pl.ds(q // 2, 16, stride=2), :] = dg1[
                :, 128 * q : 128 * q + 128
            ].reshape(14, 16, 128)
        return 0

    lax.fori_loop(0, 4, merge_one_back, 0)
    targets = [(dA_ref, i) for i in range(5)] + [(dB_ref, i) for i in range(14)]
    targets += [(dN_ref, i) for i in range(9)]
    for i, (ref, at) in enumerate(targets):
        ref[:, at] = stage[:, i // 2, i % 2, 0:28, :].astype(BF)


def middle(*operands):
    shapes = [
        (4, 5, 28, 128), (4, 14, 28, 128), (4, 9, 28, 128),
        (2, 4, 28, 128), (2, 7, 28, 128), (2, 3, 28, 128),
    ]
    return pl.pallas_call(
        middle_kernel,
        in_specs=[pl.BlockSpec(memory_space=pltpu.VMEM)] * 10
        + [pl.BlockSpec(memory_space=pl.ANY)] * 5,
        out_shape=[jax.ShapeDtypeStruct(s, BF) for s in shapes],
        scratch_shapes=[
            pltpu.VMEM((4, 14, 2, 32, 128), F32),
            pltpu.VMEM((2, 4, 7, 2, 16, 128), F32),
            pltpu.VMEM((4, ROWS, 512), F32),
            pltpu.VMEM((4, ROWS, 128), F32),
            pltpu.VMEM((ROWS, 1024), F32),
            pltpu.VMEM((ROWS, 128), F32),
            pltpu.VMEM((4, 7, 8, 512), F32),
            pltpu.VMEM((4, ROWS, 128), BF),
            pltpu.VMEM((4, ROWS, 128), BF),
            pltpu.VMEM((4, 128, LANES), BF),
            pltpu.VMEM((4, 128, LANES), BF),
            pltpu.VMEM((4, 128, LANES), BF),
            pltpu.VMEM((16, ROWS, LANES), BF),
            pltpu.VMEM((4, 128, LANES), F32),
            pltpu.VMEM((4, 8, LANES), F32),
            pltpu.VMEM((4, 128, LANES), F32),
            pltpu.VMEM((12, ROWS, 128), BF),
            pltpu.VMEM((512, 256), BF),
            pltpu.VMEM((1024, 512), BF),
            pltpu.VMEM((512, 1536), BF),
            pltpu.VMEM((HEADS3, ROWS, LANES), F32),
            pltpu.VMEM((512, 512), BF),
            pltpu.SemaphoreType.DMA((5,)),
        ],
        compiler_params=params(36),
        cost_estimate=cost(14),
    )(*operands)


IN_ORDER = Layout(major_to_minor=(0, 1, 2, 3))


def inward(values):
    return with_layout_constraint(jnp.transpose(values, (1, 2, 0, 3)), IN_ORDER)


def outward(values):
    return jnp.transpose(with_layout_constraint(values, IN_ORDER), (2, 0, 1, 3))


def send(values, axes, by):
    axes = axes.split()
    sizes = [lax.axis_size(a) for a in axes]
    if len(axes) == 1:
        pairs = [(i, (i + by) % sizes[0]) for i in range(sizes[0])]
    else:
        n, m = sizes
        pairs = [
            (i * m + j, (i + by) % n * m + (j + by) % m) for i in range(n) for j in range(m)
        ]
    return outward(lax.ppermute(inward(values), tuple(axes), pairs))


def per_device(
    tokens,
    regions_one,
    regions_three,
    gain_one,
    projection_one,
    outward_one,
    table_one,
    merge_gain_one,
    merge_weight_one,
    merge_gain_two,
    merge_weight_two,
    gain_three,
    projection_three,
    outward_three,
    table_three,
    cotangent,
):
    ta_early = send(tokens[:2, 3:17], "ta", -1)
    folded = cotangent[:, :3].reshape(4, 3, 7, 4, 128)
    folded = jnp.transpose(folded, (0, 1, 3, 2, 4)).reshape(4, 3, 28, 128)
    ha_late = send(jnp.concatenate([tokens[:, :3], folded], 1), "ha", -1)
    ha_late, cot_ha = ha_late[:, :3], ha_late[:, 3:]
    bias_one, bias_three, row_one, row_three = prepare(
        table_one, table_three, regions_one, regions_three
    )
    ta_late = send(
        arrange(late_kernel, (2, 21, 28, 128), tokens, cotangent, ha_late, cot_ha), "ta", -1
    )
    args = (gain_one[None], projection_one, outward_one, bias_one)
    (res_send, res_a), saved_a = front(False, (tokens, ta_early), *args, row_one[:8])
    res_next = send(res_send, "ha", -1)
    (res_b,), saved_b = front(True, (tokens, ta_late, ha_late), *args, row_one[8:])
    d_a, d_b, d_send, sec_own, sec_ta, sec_ha = middle(
        res_a, res_b, res_next, cotangent, ta_late, cot_ha,
        merge_gain_one[None], merge_gain_two[None], gain_three[None], row_three,
        merge_weight_one, merge_weight_two, projection_three, bias_three, outward_three,
    )
    d_prev = send(d_send, "ha", 1)
    own_b, ta_b, ha_b, dg_b = back(
        True, (d_b, sec_ta, sec_ha), gain_one[None], projection_one, outward_one, saved_b
    )
    d_prev, own_b = lax.optimization_barrier((d_prev, own_b))
    ta_b = send(ta_b, "ta", 1)
    ha_b = send(ha_b, "ha", 1)
    dg_b = send(dg_b, "ha ta", 1)
    own_a, ta_a = back(False, (d_prev, d_a), gain_one[None], projection_one, outward_one, saved_a)
    ta_b, ha_b, dg_b, own_a = lax.optimization_barrier((ta_b, ha_b, dg_b, own_a))
    ta_a = send(ta_a, "ta", 1)

    def join(corner, side, rest):
        return jnp.concatenate(
            [jnp.concatenate([corner] + side, 1), jnp.concatenate(rest, 1)], 0
        )

    section = join(dg_b[:, 3:], [ta_b[:, 11:]], [ha_b[:, 3:], sec_own])
    section = jnp.transpose(section.reshape(4, 7, 4, 7, 128), (0, 1, 3, 2, 4)).reshape(4, 7, 7, 512)
    grad = join(
        dg_b[:, :3], [jnp.zeros_like(ta_a), ta_b[:, :11]], [ha_b[:, :3], own_a, own_b]
    )
    grad = lax.dynamic_update_slice(inward(grad), inward(ta_a), (3, 0, 0, 0))
    return (section, outward(grad))


def solution(mesh):
    tile = P(("col", "ta"), "ha", None, None)
    ids = P(("col", "ta"), "ha", None)
    in_specs = (tile, ids, ids) + (P(),) * 12 + (tile,)
    return jax.shard_map(
        per_device, mesh=mesh, in_specs=in_specs, out_specs=(tile, tile), check_vma=False
    )
```

```python
import functools

import jax
import jax.numpy as jnp
import numpy as np
from jax import lax
from jax.experimental import pallas as pl
from jax.experimental.layout import Layout, with_layout_constraint
from jax.experimental.pallas import tpu as pltpu
from jax.sharding import PartitionSpec as P

HEADS1 = 4
HEADS3 = 16
WT = 4
WS = 7
ST = 2
SS = 3
EPSILON = 1e-05
NREL = 1183
LOG2E = 1.4426950408889634
HEAD = 32
SCALE = HEAD**-0.5
ROWS = WT * WS * 8
LANES = 256
SPAN = 1280
GONE = -1e30
PER_STEP = 4
STEPS = 8 // PER_STEP
BF = jnp.bfloat16
F32 = jnp.float32


def dot(a, b):
    return jnp.dot(a, b, preferred_element_type=F32)


def dot_nt(a, b):
    return lax.dot_general(a, b, (((1,), (1,)), ((), ())), preferred_element_type=F32)


def params(limit=28):
    return pltpu.CompilerParams(vmem_limit_bytes=limit * 1024 * 1024)


def cost(us):
    return pl.CostEstimate(flops=int(us * 1.1e9), bytes_accessed=int(us * 1e6), transcendentals=0)


def normalise(x):
    centred = x - jnp.mean(x, -1, keepdims=True)
    rstd = lax.rsqrt(jnp.mean(centred * centred, -1, keepdims=True) + EPSILON)
    return centred * rstd, rstd


def normalise_back(grad, xhat, rstd):
    return rstd * (
        grad
        - jnp.mean(grad, -1, keepdims=True)
        - xhat * jnp.mean(grad * xhat, -1, keepdims=True)
    )


def head_rows(x, h):
    return x[HEAD * h : HEAD * (h + 1)]


def head_of_lane(shape):
    return lax.broadcasted_iota(jnp.int32, shape, 1) // HEAD


def by_head(x):
    lane = head_of_lane((1, 128))
    return jnp.concatenate([x * (lane == h).astype(F32).astype(BF) for h in range(4)], 0)


def pick_heads(stacked):
    lane = head_of_lane((ROWS, 128))
    got = stacked[:ROWS]
    for h in range(1, 4):
        got = jnp.where(lane == h, stacked[ROWS * h : ROWS * (h + 1)], got)
    return got


def lengthen(x):
    return jnp.concatenate([x, jnp.zeros((LANES - ROWS, x.shape[1]), x.dtype)], 0)


def region_mask(row):
    wide = jnp.broadcast_to(row, (128, LANES))
    column = wide.T[:ROWS]
    column = jnp.concatenate([column, column], 1)
    return jnp.where(column == wide[0:1], 0.0, GONE).astype(F32)


def attend_four(windows):
    scores = [dot(by_head(k), qT) for k, qT, _, _, _, _ in windows]
    results = []
    for s, (_, _, vT, mask, bias_at, keep_probs) in zip(scores, windows):
        outs, inverses = [], []
        for h in range(4):
            biased = s[ROWS * h : ROWS * (h + 1)] + (bias_at(h) + mask)
            peak = jnp.max(biased, 0, keepdims=True)
            probs = jnp.exp2(biased - peak).astype(BF)
            keep_probs(h, probs)
            extended = jnp.concatenate([head_rows(vT, h)[:, :ROWS], jnp.ones((16, ROWS), BF)], 0)
            out = dot(extended, probs)
            inverse = 1.0 / out[HEAD : HEAD + 1]
            outs.append(out[:HEAD] * inverse)
            inverses.append(inverse)
        results.append((jnp.concatenate(outs, 0), jnp.concatenate(inverses + inverses, 0)))
    return results


def attend_four_back(windows):
    first = []
    for v, qT, kT, oT, doT, inverse, probs_at in windows:
        scaled, deltas = [], []
        for h in range(4):
            part = head_rows(doT, h) * inverse[h : h + 1]
            deltas.append(jnp.sum(part * head_rows(oT, h), 0, keepdims=True))
            scaled.append(part)
        scaled = jnp.concatenate(scaled, 0).astype(BF)
        first.append((scaled, deltas, dot(by_head(v), scaled)))
    results = []
    for (scaled, deltas, dprobs), (v, qT, kT, oT, doT, inverse, probs_at) in zip(first, windows):
        probs = [probs_at(h) for h in range(4)]
        dscores = [
            (probs[h].astype(F32) * (dprobs[ROWS * h : ROWS * (h + 1)] - deltas[h])).astype(BF)
            for h in range(4)
        ]
        dv = pick_heads(dot_nt(jnp.concatenate(probs, 0), scaled))
        dk = pick_heads(dot_nt(jnp.concatenate(dscores, 0), qT))
        dqT = jnp.concatenate(
            [dot(head_rows(kT, h)[:, :ROWS], dscores[h]) for h in range(4)], 0
        )
        results.append((dqT.T[:ROWS] * SCALE, dk * (1.0 / LOG2E), dv))
    return results


def lanes_of(shape):
    return lax.broadcasted_iota(jnp.int32, shape, 1)


def region_rows(ids, section):
    columns = ids.shape[1]
    count = columns // WS
    place = lax.broadcasted_iota(jnp.int32, (columns, LANES * count), 0)
    lane = lanes_of((columns, LANES * count))
    column = lane % 8
    real = (column < WS) & (lane % LANES < ROWS)
    if section == 3:
        column = jnp.where(column < 3, column + 4, column - 3)
    chosen = real & (place == lane // LANES * WS + column)
    spread = dot(ids.astype(F32).astype(BF), chosen.astype(F32).astype(BF))
    row = lax.broadcasted_iota(jnp.int32, spread.shape, 0)
    lane = lanes_of(spread.shape)
    real = (lane[:1] % 8 < WS) & (lane[:1] % LANES < ROWS)
    rows = []
    for hw in range(ids.shape[0] // (WT * WS)):
        mine = lane % LANES // 8 == row % 4 * WS + row // 4 - WS * hw
        inside = (row >= WT * WS * hw) & (row < WT * WS * (hw + 1))
        found = jnp.sum(jnp.where(mine & inside, spread, 0.0), 0, keepdims=True)
        found = jnp.where(real, found, -1.0)
        rows += [found[:, LANES * ww : LANES * (ww + 1)] for ww in range(count)]
    return rows


def prepare_kernel(
    t1_ref, t3_ref, s_ref, r1_ref, r3_ref, o1_ref, o3_ref, row1_ref, row3_ref, tab, spread
):
    tab[...] = jnp.zeros((24, SPAN), F32)
    tab[0:4, 0:NREL] = t1_ref[...] * LOG2E
    tab[8:24, 0:NREL] = t3_ref[...] * LOG2E
    slabs = []
    for dt in range(7):
        start = 169 * dt
        low = start // 128 * 128
        run = tab[:, low : low + 384]
        if start > low:
            run = pltpu.roll(run, 384 - (start - low), 1)
        slabs.append(run[:, :256])
    left = jnp.concatenate(slabs, 0)
    first = left.astype(BF)
    rest = left - first.astype(F32)
    second = rest.astype(BF)
    third = (rest - second.astype(F32)).astype(BF)
    chosen = s_ref[...]
    got = dot(first, chosen) + dot(second, chosen) + dot(third, chosen)
    lane16 = lanes_of((16, 128))
    for dt in range(7):
        for wj in range(8):
            part = got[24 * dt : 24 * dt + 24, 128 * wj : 128 * wj + 128]
            spread[dt, pl.ds(wj, 8, stride=8), :] = part[0:8]
            later = part[8:24]
            turned = jnp.where(lane16 % 8 < 3, pltpu.roll(later, 124, 1), pltpu.roll(later, 3, 1))
            spread[dt, pl.ds(64 + (7 if wj == 7 else (wj + 3) % 7), 16, stride=8), :] = turned
    for o_ref, heads, at in ((o1_ref, HEADS1, 0), (o3_ref, HEADS3, 64)):
        lane = lanes_of((heads * 8, 128))
        for tj in range(WT):
            for hj in range(WS):
                p0, p1, p2, p3 = (
                    pltpu.roll(
                        spread[ti - tj + 3, at : at + heads * 8, :], (ti * 56 - (6 - hj) * 8) % 128, 1
                    )
                    for ti in range(WT)
                )
                left = jnp.where(lane < 56, p0, jnp.where(lane < 112, p1, p2))
                right = jnp.where(lane < 40, p2, p3)
                row = (tj * WS + hj) * 8
                o_ref[:, row : row + 8, 0:128] = left.reshape(heads, 8, 128)
                o_ref[:, row : row + 8, 128:256] = right.reshape(heads, 8, 128)
    for i, found in enumerate(region_rows(r1_ref[...], 1)):
        row1_ref[i] = found
    row3_ref[...] = region_rows(r3_ref[...], 3)[0]


def chooser():
    chosen = np.zeros((256, 1024), np.float32)
    for wj in range(WS):
        for dh in range(13):
            for wi in range(WS):
                chosen[dh * 13 + wi - wj + 6, wj * 128 + dh * 8 + wi] = 1.0
    return jnp.asarray(chosen, BF)


def by_height(ids):
    return jnp.transpose(ids, (1, 0, 2)).reshape(-1, ids.shape[2])


def prepare(table_one, table_three, regions_one, regions_three):
    return pl.pallas_call(
        prepare_kernel,
        out_shape=(
            jax.ShapeDtypeStruct((HEADS1, ROWS, LANES), F32),
            jax.ShapeDtypeStruct((HEADS3, ROWS, LANES), F32),
            jax.ShapeDtypeStruct((16, 1, LANES), F32),
            jax.ShapeDtypeStruct((1, LANES), F32),
        ),
        scratch_shapes=[pltpu.VMEM((24, SPAN), F32), pltpu.VMEM((7, 24 * 8, 128), F32)],
        compiler_params=params(),
        cost_estimate=cost(3),
    )(
        jnp.transpose(table_one),
        jnp.transpose(table_three),
        chooser(),
        by_height(regions_one),
        by_height(regions_three),
    )


def fold(values):
    return jnp.concatenate([values[..., 128 * g : 128 * g + 128] for g in range(4)], -2)


def unfold(values):
    return jnp.concatenate([values[..., 7 * g : 7 * g + 7, :] for g in range(4)], -1)


def early_kernel(tok_ref, early_ref):
    early_ref[...] = tok_ref[0:2, 3:17]


def rows_kernel(tok_ref, cot_ref, ha_ref):
    ha_ref[:, 0:3] = tok_ref[:, 0:3]
    ha_ref[:, 3:6] = fold(cot_ref[:, 0:3].astype(F32)).astype(BF)


def late_kernel(tok_ref, cot_ref, ha_ref, late_ref):
    late_ref[:, 0:11] = tok_ref[0:2, 17:28]
    late_ref[:, 11:14] = ha_ref[0:2, 0:3]
    late_ref[:, 14:18] = fold(cot_ref[0:2, 3:7].astype(F32)).astype(BF)
    late_ref[:, 18:21] = ha_ref[0:2, 3:6]


def arrange(kernel, shape, *operands):
    return pl.pallas_call(
        kernel,
        out_shape=jax.ShapeDtypeStruct(shape, BF),
        compiler_params=params(8),
        cost_estimate=cost(0.3),
    )(*operands)


def put_rows(stage, frames, rows, values):
    values = values.astype(F32)
    stage[frames, rows, 0:28, :] = values
    stage[frames, rows, 28:36, :] = values[:, :, 0:8, :]


def cut_windows(stage, win):
    for hw in range(2):
        for ww in range(4):
            win[hw * 4 + ww] = stage[:, 7 * hw : 7 * hw + 7, 3 + 7 * ww : 11 + 7 * ww, :].reshape(
                ROWS, 128
            )


def join_windows(win, stage):
    for hw in range(2):
        for ww in range(4):
            stage[:, 7 * hw : 7 * hw + 7, 3 + 7 * ww : 11 + 7 * ww, :] = win[hw * 4 + ww].reshape(
                WT, WS, 8, 128
            )
    stage[:, :, 0:3, :] = stage[:, :, 28:31, :]


def front_kernel(late, *refs):
    n_in = 3 if late else 2
    pieces, refs = refs[:n_in], refs[n_in:]
    gain_ref, proj_ref, outw_ref, bias_ref, row_ref = refs[:5]
    refs = refs[5:]
    n_out = 1 if late else 2
    outs, refs = refs[:n_out], refs[n_out:]
    xw_ref, kv_ref, t_ref, p_ref, o_ref, inv_ref, stage, win, projT = refs
    step = pl.program_id(0)

    @pl.when(step == 0)
    def _():
        own = pieces[0]
        if late:
            put_rows(stage, slice(0, 2), slice(0, 11), own[2:4, 17:28])
            put_rows(stage, slice(2, 4), slice(0, 14), pieces[1][:, 0:14])
            put_rows(stage, slice(0, 2), slice(11, 14), pieces[2][2:4, 0:3])
        else:
            put_rows(stage, slice(0, 2), slice(0, 14), own[2:4, 3:17])
            put_rows(stage, slice(2, 4), slice(0, 14), pieces[1][...])
        for g in range(3):
            at = slice(128 * g, 128 * g + 128)
            projT[at, :] = proj_ref[:, at].astype(F32).T.astype(BF)
        cut_windows(stage, win)

    xs, operands = [], []
    for u in range(PER_STEP):
        x = win[step * PER_STEP + u]
        xs.append(x)
        xw_ref[u] = x.astype(BF)
        xhat, _ = normalise(x)
        n = (xhat * gain_ref[...]).astype(BF)
        kv = dot(n, proj_ref[:, 128:]).astype(BF)
        kv_ref[u] = kv
        t = dot_nt(projT[...], lengthen(n))
        qT = (t[:128] * (SCALE * LOG2E)).astype(BF)
        rest = t[128:].astype(BF)
        t_ref[u, :128] = qT
        t_ref[u, 128:] = rest[:128]

        def keep(h, probs, u=u):
            p_ref[u, h] = probs

        operands.append(
            (kv[:, :128], qT, rest[128:], region_mask(row_ref[u]), lambda h: bias_ref[h], keep)
        )
    for u, (oT, inverse) in enumerate(attend_four(operands)):
        o_ref[u] = oT.astype(BF)
        inv_ref[u] = inverse
        mixed = dot(oT.T[:ROWS].astype(BF), outw_ref[...]).astype(BF).astype(F32)
        win[step * PER_STEP + u] = xs[u] + mixed

    @pl.when(step == STEPS - 1)
    def _():
        join_windows(win, stage)
        if late:
            outs[0][...] = stage[:, :, 0:28, :].astype(BF)
        else:
            outs[0][...] = stage[:, 0:9, 0:28, :].astype(BF)
            outs[1][...] = stage[:, 9:14, 0:28, :].astype(BF)


def whole(shape):
    return pl.BlockSpec(shape, lambda i: (0,) * len(shape))


def each(shape):
    return pl.BlockSpec((PER_STEP,) + shape, lambda i: (i,) + (0,) * len(shape))


SAVED = (
    ((ROWS, 128), BF),
    ((ROWS, 256), BF),
    ((256, LANES), BF),
    ((4, ROWS, LANES), BF),
    ((128, LANES), BF),
    ((8, LANES), F32),
)


def front(late, pieces, gain, proj, outw, bias, row):
    consts = (gain, proj, outw, bias)
    shapes = [(4, 14, 28, 128)] if late else [(4, 9, 28, 128), (4, 5, 28, 128)]
    out = pl.pallas_call(
        functools.partial(front_kernel, late),
        grid=(STEPS,),
        in_specs=[whole(a.shape) for a in tuple(pieces) + consts] + [each((1, LANES))],
        out_specs=[whole(s) for s in shapes] + [each(s) for s, _ in SAVED],
        out_shape=[jax.ShapeDtypeStruct(s, BF) for s in shapes]
        + [jax.ShapeDtypeStruct((8,) + s, d) for s, d in SAVED],
        scratch_shapes=[
            pltpu.VMEM((4, 14, 40, 128), F32),
            pltpu.VMEM((8, ROWS, 128), F32),
            pltpu.VMEM((384, 128), BF),
        ],
        compiler_params=params(),
        cost_estimate=cost(4.6),
    )(*pieces, *consts, row)
    return out[: len(shapes)], out[len(shapes) :]


def back_kernel(late, *refs):
    n_in = 3 if late else 2
    pieces, refs = refs[:n_in], refs[n_in:]
    gain_ref, proj_ref, outw_ref = refs[:3]
    xw_ref, kv_ref, t_ref, p_ref, o_ref, inv_ref = refs[3:9]
    refs = refs[9:]
    n_out = 4 if late else 2
    outs, refs = refs[:n_out], refs[n_out:]
    stage, win = refs
    step = pl.program_id(0)

    @pl.when(step == 0)
    def _():
        if late:
            put_rows(stage, slice(0, 4), slice(0, 14), pieces[0][...])
            outs[1][:, 11:15] = pieces[1][:, 0:4]
            outs[2][:, 3:6] = pieces[2][...]
            outs[3][:, 3:6] = pieces[1][:, 4:7]
        else:
            put_rows(stage, slice(0, 4), slice(0, 9), pieces[0][...])
            put_rows(stage, slice(0, 4), slice(9, 14), pieces[1][...])
        cut_windows(stage, win)

    drs, operands = [], []
    for u in range(PER_STEP):
        dr = win[step * PER_STEP + u]
        drs.append(dr)
        operands.append(
            (
                kv_ref[u, :, 128:],
                t_ref[u, :128],
                t_ref[u, 128:],
                o_ref[u].astype(F32),
                dot_nt(outw_ref[...], lengthen(dr.astype(BF))),
                inv_ref[u],
                lambda h, u=u: p_ref[u, h],
            )
        )
    for u, (dq, dk, dv) in enumerate(attend_four_back(operands)):
        dpacked = jnp.concatenate([dq.astype(BF), dk.astype(BF), dv.astype(BF)], 1)
        dn = dot_nt(dpacked, proj_ref[...])
        xhat, rstd = normalise(xw_ref[u].astype(F32))
        win[step * PER_STEP + u] = drs[u] + normalise_back(dn * gain_ref[...], xhat, rstd)

    @pl.when(step == STEPS - 1)
    def _():
        join_windows(win, stage)
        if late:
            outs[0][...] = stage[0:2, 0:11, 0:28, :].astype(BF)
            outs[1][:, 0:11] = stage[2:4, 0:11, 0:28, :].astype(BF)
            outs[2][:, 0:3] = stage[0:2, 11:14, 0:28, :].astype(BF)
            outs[3][:, 0:3] = stage[2:4, 11:14, 0:28, :].astype(BF)
        else:
            outs[0][...] = stage[0:2, :, 0:28, :].astype(BF)
            outs[1][...] = stage[2:4, :, 0:28, :].astype(BF)


def back(late, pieces, gain, proj, outw, saved):
    consts = (gain, proj, outw)
    if late:
        shapes = [(2, n, 28, 128) for n in (11, 15, 6, 6)]
    else:
        shapes = [(2, 14, 28, 128), (2, 14, 28, 128)]
    return pl.pallas_call(
        functools.partial(back_kernel, late),
        grid=(STEPS,),
        in_specs=[whole(a.shape) for a in tuple(pieces) + consts] + [each(s) for s, _ in SAVED],
        out_specs=[whole(s) for s in shapes],
        out_shape=[jax.ShapeDtypeStruct(s, BF) for s in shapes],
        scratch_shapes=[
            pltpu.VMEM((4, 14, 40, 128), F32),
            pltpu.VMEM((8, ROWS, 128), F32),
        ],
        compiler_params=params(),
        cost_estimate=cost(5.5),
    )(*pieces, *consts, *saved)


def merge_pairs(stage, gain_ref, weight):
    pairs = stage.shape[1]
    pieces = [
        stage[:, :, q % 2, pl.ds(q // 2, 16, stride=2), :].reshape(WT * pairs * 16, 128)
        for q in range(4)
    ]
    xhat, rstd = normalise(jnp.concatenate(pieces, 1))
    merged = dot((xhat * gain_ref[...]).astype(BF), weight).astype(BF).astype(F32)
    return merged, xhat, rstd


def merge_pairs_back(grad, xhat, rstd, gain_ref, weight, stage):
    pairs = stage.shape[1]
    dn = dot_nt(grad.astype(BF), weight)
    dg = normalise_back(dn * gain_ref[...], xhat, rstd)
    for q in range(4):
        stage[:, :, q % 2, pl.ds(q // 2, 16, stride=2), :] = dg[
            :, 128 * q : 128 * q + 128
        ].reshape(WT, pairs, 16, 128)


def put_pair_row(stage, at, values):
    stage[:, at // 2, at % 2, 0:28, :] = values.astype(F32)


def clear_pads(stage):
    stage[:, :, :, 28:32, :] = jnp.zeros((WT, stage.shape[1], 2, 4, 128), F32)


def pair_row(stage, at):
    return stage[:, at // 2, at % 2, 0:28, :].astype(BF)


def fold_merged(merged, pairs):
    halves = [
        merged[:, 128 * i : 128 * i + 128].reshape(WT, pairs, 16, 128)[:, :, 0:14] for i in range(2)
    ]
    return jnp.concatenate(halves, 2)


def unfold_merged(folded):
    pad = jnp.zeros(folded.shape[:2] + (2, 128), F32)
    halves = [
        jnp.concatenate([folded[:, :, 14 * i : 14 * i + 14], pad], 2).reshape(-1, 128)
        for i in range(2)
    ]
    return jnp.concatenate(halves, 1)


def send_kernel(res_ref, gain_ref, weight_ref, send_ref, xhat_ref, rstd_ref, stage):
    clear_pads(stage)
    for i in range(8):
        put_pair_row(stage, i, res_ref[:, 1 + i])
    merged, xhat, rstd = merge_pairs(stage, gain_ref, weight_ref[...])
    xhat_ref[...] = xhat
    rstd_ref[...] = jnp.broadcast_to(rstd, rstd_ref.shape)
    send_ref[:, 0:1] = res_ref[:, 0:1]
    send_ref[:, 1:5] = fold_merged(merged, 4).astype(BF)


def local_kernel(resA_ref, resB_ref, gain_ref, weight_ref, merged_ref, xhat_ref, rstd_ref, stage):
    clear_pads(stage)
    for i in range(5):
        put_pair_row(stage, i, resA_ref[:, i])
    for i in range(13):
        put_pair_row(stage, 5 + i, resB_ref[:, i])
    merged, xhat, rstd = merge_pairs(stage, gain_ref, weight_ref[...])
    xhat_ref[...] = xhat
    rstd_ref[...] = jnp.broadcast_to(rstd, rstd_ref.shape)
    merged_ref[...] = merged


def local_back_kernel(
    grad_ref, d30_ref, xhat_ref, rstd_ref, gain_ref, weight_ref, dA_ref, dB_ref, stage
):
    merge_pairs_back(
        grad_ref[...], xhat_ref[...], rstd_ref[:, 0:1], gain_ref, weight_ref[...], stage
    )
    for i in range(5):
        dA_ref[:, i] = pair_row(stage, i)
    for i in range(13):
        dB_ref[:, i] = pair_row(stage, 5 + i)
    dB_ref[:, 13] = d30_ref[...]


def receive_kernel(got_ref, xhat_ref, rstd_ref, gain_ref, weight_ref, d_ref, stage):
    grad = unfold_merged(got_ref[:, 1:5].astype(F32))
    merge_pairs_back(grad, xhat_ref[...], rstd_ref[:, 0:1], gain_ref, weight_ref[...], stage)
    d_ref[:, 0:1] = got_ref[:, 0:1]
    for i in range(8):
        d_ref[:, 1 + i] = pair_row(stage, i)


def merge_call(kernel, us, shapes, pairs, *operands):
    return pl.pallas_call(
        kernel,
        out_shape=[jax.ShapeDtypeStruct(shape, kind) for shape, kind in shapes],
        scratch_shapes=[pltpu.VMEM((WT, pairs, 2, 32, 128), F32)],
        compiler_params=params(),
        cost_estimate=cost(us),
    )(*operands)


def middle_kernel(
    merged_ref, resB_ref, next_ref, cot_ref, cta_ref, cha_ref,
    mg1_ref, mg2_ref, g3_ref, row_ref, mw1_hbm, mw2_hbm, p3_hbm, bias_hbm, ow3_hbm,
    dm_ref, d30_ref, dN_ref, so_ref, sta_ref, sha_ref,
    stage, stage2, xhat2, rstd2, cotw, k_s, v_s, qT_s, kT_s, vT_s, probs_s, oT_s, inv_s, doT_s, dqkv_s,
    mw1_ref, mw2_ref, p3_ref, bias_ref, ow3_ref, sems,
):
    fetches = [
        pltpu.make_async_copy(there, here, sems.at[i])
        for i, (there, here) in enumerate(
            (
                (mw1_hbm, mw1_ref),
                (mw2_hbm, mw2_ref),
                (p3_hbm, p3_ref),
                (bias_hbm, bias_ref),
                (ow3_hbm, ow3_ref),
            )
        )
    ]
    for fetch in fetches:
        fetch.start()
    cotw[...] = jnp.zeros((4, 7, 8, 512), F32)
    cotw[0:2, 0:4, 0:7, :] = cot_ref[2:4, 3:7].astype(F32)
    cotw[2:4, :, 0:7, :] = unfold(cta_ref[:, 14:21].astype(F32))
    cotw[0:2, 4:7, 0:7, :] = unfold(cha_ref[2:4, 3:6].astype(F32))

    def put_merged(first, count, values):
        for half in range(2):
            block = values[:, 128 * half : 128 * half + 128].reshape(WT, count, 16, 128)
            for i in range(count):
                stage2[half, :, (first + i) // 2, (first + i) % 2] = block[:, i]

    def take_merged(first, count):
        halves = [
            jnp.concatenate(
                [
                    stage2[half, :, (first + i) // 2, (first + i) % 2].reshape(WT, 1, 16, 128)
                    for i in range(count)
                ],
                1,
            ).reshape(WT * count * 16, 128)
            for half in range(2)
        ]
        return jnp.concatenate(halves, 1)

    put_merged(0, 9, merged_ref[...])
    put_merged(10, 4, unfold_merged(next_ref[:, 1:5].astype(F32)))
    clear_pads(stage)
    put_pair_row(stage, 0, resB_ref[:, 13])
    put_pair_row(stage, 1, next_ref[:, 0])
    fetches[0].wait()
    merged, xhat_seam, rstd_seam = merge_pairs(stage, mg1_ref, mw1_ref[...])
    put_merged(9, 1, merged)
    fetches[1].wait()
    pieces = [
        stage2[half, :, :, q % 2, pl.ds(q // 2, 8, stride=2), :].reshape(ROWS, 128)
        for q in range(4)
        for half in range(2)
    ]
    xhat, rstd = normalise(jnp.concatenate(pieces, 1))
    xhat2[...] = xhat
    rstd2[...] = jnp.broadcast_to(rstd, (ROWS, 128))
    merged_two = dot((xhat * mg2_ref[...]).astype(BF), mw2_ref[...]).astype(BF).astype(F32)
    xhat3, rstd3 = normalise(merged_two)
    n3 = (xhat3 * g3_ref[...]).astype(BF)
    fetches[2].wait()
    packed = [dot(n3, p3_ref[:, 512 * i : 512 * i + 512]) for i in range(3)]
    for g in range(4):
        q, k, v = (part[:, 128 * g : 128 * g + 128] for part in packed)
        k_s[g] = k.astype(BF)
        v_s[g] = v.astype(BF)
        qT_s[g] = (lengthen(q).T * (SCALE * LOG2E)).astype(BF)
        kT_s[g] = lengthen(k).T.astype(BF)
        vT_s[g] = lengthen(v).T.astype(BF)
    mask = region_mask(row_ref[...])
    fetches[3].wait()

    def heads(i, _):
        operands = []
        for g in (2 * i, 2 * i + 1):

            def keep(h, probs, g=g):
                probs_s[g * 4 + h] = probs

            operands.append(
                (k_s[g], qT_s[g], vT_s[g], mask, lambda h, g=g: bias_ref[g * 4 + h], keep)
            )
        for u, (oT, inverse) in enumerate(attend_four(operands)):
            oT_s[2 * i + u] = oT
            inv_s[2 * i + u] = inverse
        return 0

    lax.fori_loop(0, 2, heads, 0)
    fetches[4].wait()
    att = jnp.concatenate([oT_s[g].T[:ROWS].astype(BF) for g in range(4)], 1)
    mixed = dot(att, ow3_ref[...]).astype(BF).astype(F32)
    section = (merged_two + mixed).reshape(4, 7, 8, 512)
    section = fold(section[:, :, 0:7])
    so_ref[...] = section[0:2, 0:4].astype(BF)
    sta_ref[...] = section[2:4].astype(BF)
    sha_ref[...] = section[0:2, 4:7].astype(BF)

    cot = cotw[...].reshape(ROWS, 512)
    cot_long = lengthen(cot.astype(BF))
    doT = dot_nt(ow3_ref[...], cot_long)
    for g in range(4):
        doT_s[g] = doT[128 * g : 128 * g + 128]

    def heads_back(i, _):
        operands = [
            (
                v_s[g], qT_s[g], kT_s[g], oT_s[g], doT_s[g], inv_s[g],
                lambda h, g=g: probs_s[g * 4 + h],
            )
            for g in (2 * i, 2 * i + 1)
        ]
        for u, (dq, dk, dv) in enumerate(attend_four_back(operands)):
            dqkv_s[2 * i + u] = dq.astype(BF)
            dqkv_s[4 + 2 * i + u] = dk.astype(BF)
            dqkv_s[8 + 2 * i + u] = dv.astype(BF)
        return 0

    lax.fori_loop(0, 2, heads_back, 0)
    dpacked = jnp.concatenate([dqkv_s[i] for i in range(12)], 1)
    dn3 = dot_nt(dpacked, p3_ref[...])
    dm2 = cot + normalise_back(dn3 * g3_ref[...], xhat3, rstd3)
    dn2 = dot_nt(dm2.astype(BF), mw2_ref[...])
    dg2 = normalise_back(dn2 * mg2_ref[...], xhat2[...], rstd2[:, 0:1])
    for q in range(4):
        for half in range(2):
            at = 256 * q + 128 * half
            stage2[half, :, :, q % 2, pl.ds(q // 2, 8, stride=2), :] = dg2[:, at : at + 128].reshape(
                4, 7, 8, 128
            )

    dm_ref[...] = take_merged(0, 9)
    merge_pairs_back(take_merged(9, 1), xhat_seam, rstd_seam, mg1_ref, mw1_ref[...], stage)
    d30_ref[...] = pair_row(stage, 0)
    dN_ref[:, 0] = pair_row(stage, 1)
    dN_ref[:, 1:5] = fold_merged(take_merged(10, 4), 4).astype(BF)


def middle(*operands):
    shapes = [
        (4, 28, 128), (4, 5, 28, 128), (2, 4, 28, 128), (2, 7, 28, 128), (2, 3, 28, 128),
    ]
    return pl.pallas_call(
        middle_kernel,
        in_specs=[pl.BlockSpec(memory_space=pltpu.VMEM)] * 10
        + [pl.BlockSpec(memory_space=pl.ANY)] * 5,
        out_shape=[jax.ShapeDtypeStruct((576, 256), F32)]
        + [jax.ShapeDtypeStruct(s, BF) for s in shapes],
        scratch_shapes=[
            pltpu.VMEM((4, 1, 2, 32, 128), F32),
            pltpu.VMEM((2, 4, 7, 2, 16, 128), F32),
            pltpu.VMEM((ROWS, 1024), F32),
            pltpu.VMEM((ROWS, 128), F32),
            pltpu.VMEM((4, 7, 8, 512), F32),
            pltpu.VMEM((4, ROWS, 128), BF),
            pltpu.VMEM((4, ROWS, 128), BF),
            pltpu.VMEM((4, 128, LANES), BF),
            pltpu.VMEM((4, 128, LANES), BF),
            pltpu.VMEM((4, 128, LANES), BF),
            pltpu.VMEM((16, ROWS, LANES), BF),
            pltpu.VMEM((4, 128, LANES), F32),
            pltpu.VMEM((4, 8, LANES), F32),
            pltpu.VMEM((4, 128, LANES), F32),
            pltpu.VMEM((12, ROWS, 128), BF),
            pltpu.VMEM((512, 256), BF),
            pltpu.VMEM((1024, 512), BF),
            pltpu.VMEM((512, 1536), BF),
            pltpu.VMEM((HEADS3, ROWS, LANES), F32),
            pltpu.VMEM((512, 512), BF),
            pltpu.SemaphoreType.DMA((5,)),
        ],
        compiler_params=params(36),
        cost_estimate=cost(9),
    )(*operands)


def join_kernel(dg_ref, ha_ref, ta_ref, own_ref, so_ref, grad_ref, section_ref, wide, narrow):
    for t in range(WT):
        turn = pl.ds(t, 28, stride=4)
        corner = dg_ref if t < 2 else ha_ref
        wide[0:3, turn, :] = corner[t % 2, 0:3].astype(F32)
        wide[3:14, turn, :] = (ta_ref if t < 2 else own_ref)[t % 2, 0:11].astype(F32)
        high = corner[t % 2, 3:6].astype(F32)
        low = (ta_ref[t, 11:15] if t < 2 else so_ref[t - 2]).astype(F32)
        for g in range(4):
            narrow[g, 0:3, pl.ds(t, 7, stride=4), :] = high[:, 7 * g : 7 * g + 7]
            narrow[g, 3:7, pl.ds(t, 7, stride=4), :] = low[:, 7 * g : 7 * g + 7]
    for i in range(14):
        grad_ref[i if i < 3 else i + 14] = wide[i].reshape(28, 4, 128).astype(BF)
    for i in range(7):
        row = jnp.concatenate([narrow[g, i] for g in range(4)], 1)
        section_ref[i] = row.reshape(7, 4, 512).astype(BF)


def join(dg, ha, ta, own, section_own):
    return pl.pallas_call(
        join_kernel,
        out_shape=[
            jax.ShapeDtypeStruct((28, 28, 4, 128), BF),
            jax.ShapeDtypeStruct((7, 7, 4, 512), BF),
        ],
        scratch_shapes=[pltpu.VMEM((14, 112, 128), F32), pltpu.VMEM((4, 7, 28, 128), F32)],
        compiler_params=params(),
        cost_estimate=cost(2),
    )(dg, ha, ta, own, section_own)


def last_kernel(grad_hbm, ta_ref, own_ref, out_hbm, wide, rows, sem):
    del grad_hbm
    for t in range(WT):
        wide[:, pl.ds(t, 28, stride=4), :] = (ta_ref if t < 2 else own_ref)[t % 2].astype(F32)
    for i in range(14):
        rows[i] = wide[i].reshape(28, 4, 128).astype(BF)
    copy = pltpu.make_async_copy(rows, out_hbm.at[3:17], sem)
    copy.start()
    copy.wait()


def join_last(grad, ta, own):
    return pl.pallas_call(
        last_kernel,
        in_specs=[pl.BlockSpec(memory_space=pl.ANY)] + [pl.BlockSpec(memory_space=pltpu.VMEM)] * 2,
        out_specs=pl.BlockSpec(memory_space=pl.ANY),
        out_shape=jax.ShapeDtypeStruct((28, 28, 4, 128), BF),
        scratch_shapes=[
            pltpu.VMEM((14, 112, 128), F32),
            pltpu.VMEM((14, 28, 4, 128), BF),
            pltpu.SemaphoreType.DMA,
        ],
        input_output_aliases={0: 0},
        compiler_params=params(),
        cost_estimate=cost(1),
    )(grad, ta, own)


IN_ORDER = Layout(major_to_minor=(0, 1, 2, 3))


def inward(values):
    return with_layout_constraint(jnp.transpose(values, (1, 2, 0, 3)), IN_ORDER)


def outward(values):
    return jnp.transpose(with_layout_constraint(values, IN_ORDER), (2, 0, 1, 3))


def send(values, axes, by):
    axes = axes.split()
    sizes = [lax.axis_size(a) for a in axes]
    if len(axes) == 1:
        pairs = [(i, (i + by) % sizes[0]) for i in range(sizes[0])]
    else:
        n, m = sizes
        pairs = [
            (i * m + j, (i + by) % n * m + (j + by) % m) for i in range(n) for j in range(m)
        ]
    return lax.ppermute(values, tuple(axes), pairs)


def per_device(
    tokens,
    regions_one,
    regions_three,
    gain_one,
    projection_one,
    outward_one,
    table_one,
    merge_gain_one,
    merge_weight_one,
    merge_gain_two,
    merge_weight_two,
    gain_three,
    projection_three,
    outward_three,
    table_three,
    cotangent,
):
    ta_early = send(inward(arrange(early_kernel, (2, 14, 28, 128), tokens)), "ta", -1)
    ha_late = send(arrange(rows_kernel, (4, 6, 28, 128), tokens, cotangent), "ha", -1)
    bias_one, bias_three, row_one, row_three = prepare(
        table_one, table_three, regions_one, regions_three
    )
    ta_late = send(
        inward(arrange(late_kernel, (2, 21, 28, 128), tokens, cotangent, ha_late)), "ta", -1
    )
    gain, merge_gain, seam = gain_one[None], merge_gain_one[None], merge_weight_one
    args = (gain, projection_one, outward_one, bias_one)
    (res_send, res_a), saved_a = front(False, (tokens, outward(ta_early)), *args, row_one[:8])
    row_send, *early_norm = merge_call(
        send_kernel, 0.5, [((4, 5, 28, 128), BF), ((256, 512), F32), ((256, 128), F32)], 4,
        res_send, merge_gain, seam,
    )
    row_next = send(row_send, "ha", -1)
    ta_late, res_a = lax.optimization_barrier((ta_late, res_a))
    ta_late = outward(ta_late)
    (res_b,), saved_b = front(True, (tokens, ta_late, ha_late), *args, row_one[8:])
    merged, *local_norm = merge_call(
        local_kernel, 1, [((576, 256), F32), ((576, 512), F32), ((576, 128), F32)], 9,
        res_a, res_b, merge_gain, seam,
    )
    row_next, merged = lax.optimization_barrier((row_next, merged))
    d_merged, d_30, d_send, sec_own, sec_ta, sec_ha = middle(
        merged, res_b, row_next, cotangent, ta_late, ha_late,
        merge_gain, merge_gain_two[None], gain_three[None], row_three,
        merge_weight_one, merge_weight_two, projection_three, bias_three, outward_three,
    )
    d_prev = send(d_send, "ha", 1)
    d_a, d_b = merge_call(
        local_back_kernel, 1, [((4, 5, 28, 128), BF), ((4, 14, 28, 128), BF)], 9,
        d_merged, d_30, *local_norm, merge_gain, seam,
    )
    own_b, ta_b, ha_b, dg_b = back(
        True, (d_b, sec_ta, sec_ha), gain, projection_one, outward_one, saved_b
    )
    d_prev, own_b = lax.optimization_barrier((d_prev, own_b))
    ta_b = send(inward(ta_b), "ta", 1)
    ha_b = send(ha_b, "ha", 1)
    dg_b = send(dg_b, "ha ta", 1)
    (d_first,) = merge_call(
        receive_kernel, 0.5, [((4, 9, 28, 128), BF)], 4, d_prev, *early_norm, merge_gain, seam
    )
    own_a, ta_a = back(False, (d_first, d_a), gain, projection_one, outward_one, saved_a)
    ta_b, ha_b, dg_b, own_a = lax.optimization_barrier((ta_b, ha_b, dg_b, own_a))
    ta_a = send(inward(ta_a), "ta", 1)
    grad, section = join(dg_b, ha_b, outward(ta_b), own_b, sec_own)
    ta_a, grad = lax.optimization_barrier((ta_a, grad))
    grad = join_last(grad, outward(ta_a), own_a)
    return (jnp.transpose(section, (2, 0, 1, 3)), jnp.transpose(grad, (2, 0, 1, 3)))


def solution(mesh):
    tile = P(("col", "ta"), "ha", None, None)
    ids = P(("col", "ta"), "ha", None)
    in_specs = (tile, ids, ids) + (P(),) * 12 + (tile,)
    return jax.shard_map(
        per_device, mesh=mesh, in_specs=in_specs, out_specs=(tile, tile), check_vma=False
    )
```

```python
import functools

import jax
import jax.numpy as jnp
import numpy as np
from jax import lax
from jax.experimental import pallas as pl
from jax.experimental.layout import Layout, with_layout_constraint
from jax.experimental.pallas import tpu as pltpu
from jax.sharding import PartitionSpec as P

HEADS1 = 4
HEADS3 = 16
WT = 4
WS = 7
ST = 2
SS = 3
EPSILON = 1e-05
NREL = 1183
LOG2E = 1.4426950408889634
HEAD = 32
SCALE = HEAD**-0.5
ROWS = WT * WS * 8
LANES = 256
SPAN = 1280
GONE = -1e30
PER_STEP = 4
STEPS = 8 // PER_STEP
BF = jnp.bfloat16
F32 = jnp.float32


def dot(a, b):
    return jnp.dot(a, b, preferred_element_type=F32)


def dot_nt(a, b):
    return lax.dot_general(a, b, (((1,), (1,)), ((), ())), preferred_element_type=F32)


def params(limit=20):
    return pltpu.CompilerParams(vmem_limit_bytes=limit * 1024 * 1024)


def cost(us):
    return pl.CostEstimate(flops=int(us * 1.1e9), bytes_accessed=int(us * 1e6), transcendentals=0)


def normalise(x):
    centred = x - jnp.mean(x, -1, keepdims=True)
    rstd = lax.rsqrt(jnp.mean(centred * centred, -1, keepdims=True) + EPSILON)
    return centred * rstd, rstd


def normalise_back(grad, xhat, rstd):
    return rstd * (
        grad
        - jnp.mean(grad, -1, keepdims=True)
        - xhat * jnp.mean(grad * xhat, -1, keepdims=True)
    )


def head_rows(x, h):
    return x[HEAD * h : HEAD * (h + 1)]


def head_of_lane(shape):
    return lax.broadcasted_iota(jnp.int32, shape, 1) // HEAD


def by_head(x):
    lane = head_of_lane((1, 128))
    return jnp.concatenate([x * (lane == h).astype(F32).astype(BF) for h in range(4)], 0)


def pick_heads(stacked):
    lane = head_of_lane((ROWS, 128))
    got = stacked[:ROWS]
    for h in range(1, 4):
        got = jnp.where(lane == h, stacked[ROWS * h : ROWS * (h + 1)], got)
    return got


def lengthen(x):
    return jnp.concatenate([x, jnp.zeros((LANES - ROWS, x.shape[1]), x.dtype)], 0)


def identity(size):
    row = lax.broadcasted_iota(jnp.int32, (size, size), 0)
    return (row == lax.broadcasted_iota(jnp.int32, (size, size), 1)).astype(F32).astype(BF)


def turn(eye, x):
    return dot_nt(eye, x).astype(BF)


def region_mask(column, row):
    return jnp.where(jnp.concatenate([column, column], 1) == row, 0.0, GONE).astype(F32)


def attend_four(windows):
    scores = [dot(by_head(k), qT) for k, qT, _, _, _, _ in windows]
    results = []
    for s, (_, _, vT, mask, bias_at, keep_probs) in zip(scores, windows):
        outs, inverses = [], []
        for h in range(4):
            biased = s[ROWS * h : ROWS * (h + 1)] + (bias_at(h) + mask)
            peak = jnp.max(biased, 0, keepdims=True)
            probs = jnp.exp2(biased - peak).astype(BF)
            keep_probs(h, probs)
            extended = jnp.concatenate([head_rows(vT, h)[:, :ROWS], jnp.ones((16, ROWS), BF)], 0)
            out = dot(extended, probs)
            inverse = 1.0 / out[HEAD : HEAD + 1]
            outs.append(out[:HEAD] * inverse)
            inverses.append(inverse)
        results.append((jnp.concatenate(outs, 0), jnp.concatenate(inverses + inverses, 0)))
    return results


def attend_four_back(windows, eye):
    first = []
    for v, qT, kT, oT, doT, inverse, probs_at in windows:
        scaled, deltas = [], []
        for h in range(4):
            part = head_rows(doT, h) * inverse[h : h + 1]
            deltas.append(jnp.sum(part * head_rows(oT, h), 0, keepdims=True))
            scaled.append(part)
        scaled = jnp.concatenate(scaled, 0).astype(BF)
        first.append((scaled, deltas, dot(by_head(v), scaled)))
    results = []
    for (scaled, deltas, dprobs), (v, qT, kT, oT, doT, inverse, probs_at) in zip(first, windows):
        probs = [probs_at(h) for h in range(4)]
        dscores = [
            (probs[h].astype(F32) * (dprobs[ROWS * h : ROWS * (h + 1)] - deltas[h])).astype(BF)
            for h in range(4)
        ]
        dv = pick_heads(dot_nt(jnp.concatenate(probs, 0), scaled))
        dk = pick_heads(dot_nt(jnp.concatenate(dscores, 0), qT))
        dqT = jnp.concatenate(
            [dot(head_rows(kT, h)[:, :ROWS], dscores[h]) for h in range(4)], 0
        )
        dq = turn(eye, (dqT * SCALE).astype(BF))[:ROWS]
        results.append((dq, (dk * (1.0 / LOG2E)).astype(BF), dv.astype(BF)))
    return results


def lanes_of(shape):
    return lax.broadcasted_iota(jnp.int32, shape, 1)


def region_rows(ids, section):
    columns = ids.shape[1]
    count = columns // WS
    place = lax.broadcasted_iota(jnp.int32, (columns, LANES * count), 0)
    lane = lanes_of((columns, LANES * count))
    column = lane % 8
    real = (column < WS) & (lane % LANES < ROWS)
    if section == 3:
        column = jnp.where(column < 3, column + 4, column - 3)
    chosen = real & (place == lane // LANES * WS + column)
    spread = dot(ids.astype(F32).astype(BF), chosen.astype(F32).astype(BF))
    row = lax.broadcasted_iota(jnp.int32, spread.shape, 0)
    lane = lanes_of(spread.shape)
    real = (lane[:1] % 8 < WS) & (lane[:1] % LANES < ROWS)
    rows = []
    for hw in range(ids.shape[0] // (WT * WS)):
        mine = lane % LANES // 8 == row % 4 * WS + row // 4 - WS * hw
        inside = (row >= WT * WS * hw) & (row < WT * WS * (hw + 1))
        found = jnp.sum(jnp.where(mine & inside, spread, 0.0), 0, keepdims=True)
        found = jnp.where(real, found, -1.0)
        rows += [found[:, LANES * ww : LANES * (ww + 1)] for ww in range(count)]
    return rows


def region_columns(ids, section):
    columns = ids.shape[1]
    count = columns // WS
    source = ids.astype(F32).astype(BF)
    token = lax.broadcasted_iota(jnp.int32, (ROWS, ids.shape[0]), 0)
    place = lanes_of((ROWS, ids.shape[0]))
    column = lax.broadcasted_iota(jnp.int32, (ROWS, columns), 0) % 8
    lane = lanes_of((ROWS, columns))
    if section == 3:
        column = jnp.where(column < 3, column + 4, jnp.where(column == 7, 8, column - 3))
    ones = jnp.ones((columns, 128), BF)
    pad = lax.broadcasted_iota(jnp.int32, (ROWS, 128), 0) % 8 == 7
    found = []
    for hw in range(ids.shape[0] // (WT * WS)):
        chosen = place == (token // 8 % WS + WS * hw) * WT + token // 56
        picked = dot(chosen.astype(F32).astype(BF), source)
        for ww in range(count):
            mine = jnp.where(lane == WS * ww + column, picked, 0.0).astype(BF)
            found.append(jnp.where(pad, -1.0, dot(mine, ones)))
    return found


def prepare_kernel(
    t1_ref, t3_ref, s_ref, r1_ref, r3_ref, o1_ref, o3_ref, row1_ref, row3_ref, col1_ref, col3_ref,
    tab, spread
):
    tab[...] = jnp.zeros((24, SPAN), F32)
    tab[0:4, 0:NREL] = t1_ref[...] * LOG2E
    tab[8:24, 0:NREL] = t3_ref[...] * LOG2E
    slabs = []
    for dt in range(7):
        start = 169 * dt
        low = start // 128 * 128
        run = tab[:, low : low + 384]
        if start > low:
            run = pltpu.roll(run, 384 - (start - low), 1)
        slabs.append(run[:, :256])
    left = jnp.concatenate(slabs, 0)
    first = left.astype(BF)
    rest = left - first.astype(F32)
    second = rest.astype(BF)
    third = (rest - second.astype(F32)).astype(BF)
    chosen = s_ref[...]
    got = dot(first, chosen) + dot(second, chosen) + dot(third, chosen)
    lane16 = lanes_of((16, 128))
    for dt in range(7):
        for wj in range(8):
            part = got[24 * dt : 24 * dt + 24, 128 * wj : 128 * wj + 128]
            spread[dt, pl.ds(wj, 8, stride=8), :] = part[0:8]
            later = part[8:24]
            turned = jnp.where(lane16 % 8 < 3, pltpu.roll(later, 124, 1), pltpu.roll(later, 3, 1))
            spread[dt, pl.ds(64 + (7 if wj == 7 else (wj + 3) % 7), 16, stride=8), :] = turned
    for o_ref, heads, at in ((o1_ref, HEADS1, 0), (o3_ref, HEADS3, 64)):
        lane = lanes_of((heads * 8, 128))
        for tj in range(WT):
            for hj in range(WS):
                p0, p1, p2, p3 = (
                    pltpu.roll(
                        spread[ti - tj + 3, at : at + heads * 8, :], (ti * 56 - (6 - hj) * 8) % 128, 1
                    )
                    for ti in range(WT)
                )
                left = jnp.where(lane < 56, p0, jnp.where(lane < 112, p1, p2))
                right = jnp.where(lane < 40, p2, p3)
                row = (tj * WS + hj) * 8
                o_ref[:, row : row + 8, 0:128] = left.reshape(heads, 8, 128)
                o_ref[:, row : row + 8, 128:256] = right.reshape(heads, 8, 128)
    for i, found in enumerate(region_rows(r1_ref[...], 1)):
        row1_ref[i] = found
    row3_ref[...] = region_rows(r3_ref[...], 3)[0]
    for i, found in enumerate(region_columns(r1_ref[...], 1)):
        col1_ref[i] = found
    col3_ref[...] = region_columns(r3_ref[...], 3)[0]


def chooser():
    chosen = np.zeros((256, 1024), np.float32)
    for wj in range(WS):
        for dh in range(13):
            for wi in range(WS):
                chosen[dh * 13 + wi - wj + 6, wj * 128 + dh * 8 + wi] = 1.0
    return jnp.asarray(chosen, BF)


def by_height(ids):
    return jnp.transpose(ids, (1, 0, 2)).reshape(-1, ids.shape[2])


def prepare(table_one, table_three, regions_one, regions_three):
    return pl.pallas_call(
        prepare_kernel,
        out_shape=(
            jax.ShapeDtypeStruct((HEADS1, ROWS, LANES), F32),
            jax.ShapeDtypeStruct((HEADS3, ROWS, LANES), F32),
            jax.ShapeDtypeStruct((16, 1, LANES), F32),
            jax.ShapeDtypeStruct((1, LANES), F32),
            jax.ShapeDtypeStruct((16, ROWS, 128), F32),
            jax.ShapeDtypeStruct((ROWS, 128), F32),
        ),
        scratch_shapes=[pltpu.VMEM((24, SPAN), F32), pltpu.VMEM((7, 24 * 8, 128), F32)],
        compiler_params=params(),
        cost_estimate=cost(3),
    )(
        jnp.transpose(table_one),
        jnp.transpose(table_three),
        chooser(),
        by_height(regions_one),
        by_height(regions_three),
    )


def fold(values):
    return jnp.concatenate([values[..., 128 * g : 128 * g + 128] for g in range(4)], -2)


def unfold(values):
    return jnp.concatenate([values[..., 7 * g : 7 * g + 7, :] for g in range(4)], -1)


def early_kernel(tok_ref, early_ref):
    early_ref[...] = tok_ref[0:2, 3:17]


def rows_kernel(tok_ref, cot_ref, ha_ref):
    ha_ref[:, 0:3] = tok_ref[:, 0:3]
    ha_ref[:, 3:6] = fold(cot_ref[:, 0:3].astype(F32)).astype(BF)


def late_kernel(tok_ref, cot_ref, ha_ref, late_ref):
    late_ref[:, 0:11] = tok_ref[0:2, 17:28]
    late_ref[:, 11:14] = ha_ref[0:2, 0:3]
    late_ref[:, 14:18] = fold(cot_ref[0:2, 3:7].astype(F32)).astype(BF)
    late_ref[:, 18:21] = ha_ref[0:2, 3:6]


def arrange(kernel, shape, *operands):
    return pl.pallas_call(
        kernel,
        out_shape=jax.ShapeDtypeStruct(shape, BF),
        compiler_params=params(8),
        cost_estimate=cost(0.3),
    )(*operands)


def put_rows(stage, frames, rows, values):
    values = values.astype(F32)
    stage[frames, rows, 0:28, :] = values
    stage[frames, rows, 28:36, :] = values[:, :, 0:8, :]


def cut_windows(stage, win):
    for hw in range(2):
        for ww in range(4):
            win[hw * 4 + ww] = stage[:, 7 * hw : 7 * hw + 7, 3 + 7 * ww : 11 + 7 * ww, :].reshape(
                ROWS, 128
            )


def join_windows(win, stage):
    for hw in range(2):
        for ww in range(4):
            stage[:, 7 * hw : 7 * hw + 7, 3 + 7 * ww : 11 + 7 * ww, :] = win[hw * 4 + ww].reshape(
                WT, WS, 8, 128
            )
    stage[:, :, 0:3, :] = stage[:, :, 28:31, :]


def front_kernel(late, *refs):
    n_in = 3 if late else 2
    pieces, refs = refs[:n_in], refs[n_in:]
    gain_ref, proj_ref, outw_ref, bias_ref, row_ref, col_ref = refs[:6]
    refs = refs[6:]
    n_out = 1 if late else 2
    outs, refs = refs[:n_out], refs[n_out:]
    xhat_ref, rstd_ref, kv_ref, t_ref, p_ref, o_ref, inv_ref, stage, win, projT, eye = refs
    step = pl.program_id(0)

    @pl.when(step == 0)
    def _():
        own = pieces[0]
        if late:
            put_rows(stage, slice(0, 2), slice(0, 11), own[2:4, 17:28])
            put_rows(stage, slice(2, 4), slice(0, 14), pieces[1][:, 0:14])
            put_rows(stage, slice(0, 2), slice(11, 14), pieces[2][2:4, 0:3])
        else:
            put_rows(stage, slice(0, 2), slice(0, 14), own[2:4, 3:17])
            put_rows(stage, slice(2, 4), slice(0, 14), pieces[1][...])
        for g in range(3):
            at = slice(128 * g, 128 * g + 128)
            projT[at, :] = turn(identity(128), proj_ref[:, at])
        eye[...] = identity(LANES)
        cut_windows(stage, win)

    xs, operands = [], []
    for u in range(PER_STEP):
        x = win[step * PER_STEP + u]
        xs.append(x)
        xhat, rstd = normalise(x)
        xhat_ref[u] = xhat
        rstd_ref[u] = jnp.broadcast_to(rstd, (ROWS, 128))
        n = (xhat * gain_ref[...]).astype(BF)
        kv = dot(n, proj_ref[:, 128:]).astype(BF)
        kv_ref[u] = kv
        t = dot_nt(projT[...], lengthen(n))
        qT = (t[:128] * (SCALE * LOG2E)).astype(BF)
        rest = t[128:].astype(BF)
        t_ref[u, :128] = qT
        t_ref[u, 128:] = rest[:128]

        def keep(h, probs, u=u):
            p_ref[u, h] = probs

        operands.append(
            (kv[:, :128], qT, rest[128:], region_mask(col_ref[u], row_ref[u]), lambda h: bias_ref[h], keep)
        )
    for u, (oT, inverse) in enumerate(attend_four(operands)):
        oT = oT.astype(BF)
        o_ref[u] = oT
        inv_ref[u] = inverse
        mixed = dot(turn(eye[...], oT)[:ROWS], outw_ref[...]).astype(BF).astype(F32)
        win[step * PER_STEP + u] = xs[u] + mixed

    @pl.when(step == STEPS - 1)
    def _():
        join_windows(win, stage)
        if late:
            outs[0][...] = stage[:, :, 0:28, :].astype(BF)
        else:
            outs[0][...] = stage[:, 0:9, 0:28, :].astype(BF)
            outs[1][...] = stage[:, 9:14, 0:28, :].astype(BF)


def whole(shape):
    return pl.BlockSpec(shape, lambda i: (0,) * len(shape))


def each(shape, first=0):
    return pl.BlockSpec((PER_STEP,) + shape, lambda i: (i + first,) + (0,) * len(shape))


SAVED = (
    ((ROWS, 128), F32),
    ((ROWS, 128), F32),
    ((ROWS, 256), BF),
    ((256, LANES), BF),
    ((4, ROWS, LANES), BF),
    ((128, LANES), BF),
    ((8, LANES), F32),
)


def front(late, pieces, gain, proj, outw, bias, row, column):
    consts = (gain, proj, outw, bias)
    shapes = [(4, 14, 28, 128)] if late else [(4, 9, 28, 128), (4, 5, 28, 128)]
    out = pl.pallas_call(
        functools.partial(front_kernel, late),
        grid=(STEPS,),
        in_specs=[whole(a.shape) for a in tuple(pieces) + consts] + [each((1, LANES), STEPS * late), each((ROWS, 128), STEPS * late)],
        out_specs=[whole(s) for s in shapes] + [each(s) for s, _ in SAVED],
        out_shape=[jax.ShapeDtypeStruct(s, BF) for s in shapes]
        + [jax.ShapeDtypeStruct((8,) + s, d) for s, d in SAVED],
        scratch_shapes=[
            pltpu.VMEM((4, 14, 40, 128), F32),
            pltpu.VMEM((8, ROWS, 128), F32),
            pltpu.VMEM((384, 128), BF),
            pltpu.VMEM((LANES, LANES), BF),
        ],
        compiler_params=params(),
        cost_estimate=cost(4.6),
    )(*pieces, *consts, row, column)
    return out[: len(shapes)], out[len(shapes) :]


def back_kernel(late, *refs):
    n_in = 3 if late else 2
    pieces, refs = refs[:n_in], refs[n_in:]
    gain_ref, proj_ref, outw_ref = refs[:3]
    xhat_ref, rstd_ref, kv_ref, t_ref, p_ref, o_ref, inv_ref = refs[3:10]
    refs = refs[10:]
    n_out = 4 if late else 2
    outs, refs = refs[:n_out], refs[n_out:]
    stage, win, eye = refs
    step = pl.program_id(0)

    @pl.when(step == 0)
    def _():
        if late:
            put_rows(stage, slice(0, 4), slice(0, 14), pieces[0][...])
            outs[1][:, 11:15] = pieces[1][:, 0:4]
            outs[2][:, 3:6] = pieces[2][...]
            outs[3][:, 3:6] = pieces[1][:, 4:7]
        else:
            put_rows(stage, slice(0, 4), slice(0, 9), pieces[0][...])
            put_rows(stage, slice(0, 4), slice(9, 14), pieces[1][...])
        eye[...] = identity(LANES)
        cut_windows(stage, win)

    drs, operands = [], []
    for u in range(PER_STEP):
        dr = win[step * PER_STEP + u]
        drs.append(dr)
        operands.append(
            (
                kv_ref[u, :, 128:],
                t_ref[u, :128],
                t_ref[u, 128:],
                o_ref[u].astype(F32),
                dot_nt(outw_ref[...], lengthen(dr.astype(BF))),
                inv_ref[u],
                lambda h, u=u: p_ref[u, h],
            )
        )
    for u, (dq, dk, dv) in enumerate(attend_four_back(operands, eye[...])):
        dpacked = jnp.concatenate([dq, dk, dv], 1)
        dn = dot_nt(dpacked, proj_ref[...])
        dx = normalise_back(dn * gain_ref[...], xhat_ref[u], rstd_ref[u])
        win[step * PER_STEP + u] = drs[u] + dx

    @pl.when(step == STEPS - 1)
    def _():
        join_windows(win, stage)
        if late:
            outs[0][...] = stage[0:2, 0:11, 0:28, :].astype(BF)
            outs[1][:, 0:11] = stage[2:4, 0:11, 0:28, :].astype(BF)
            outs[2][:, 0:3] = stage[0:2, 11:14, 0:28, :].astype(BF)
            outs[3][:, 0:3] = stage[2:4, 11:14, 0:28, :].astype(BF)
        else:
            outs[0][...] = stage[0:2, :, 0:28, :].astype(BF)
            outs[1][...] = stage[2:4, :, 0:28, :].astype(BF)


def back(late, pieces, gain, proj, outw, saved):
    consts = (gain, proj, outw)
    if late:
        shapes = [(2, n, 28, 128) for n in (11, 15, 6, 6)]
    else:
        shapes = [(2, 14, 28, 128), (2, 14, 28, 128)]
    return pl.pallas_call(
        functools.partial(back_kernel, late),
        grid=(STEPS,),
        in_specs=[whole(a.shape) for a in tuple(pieces) + consts] + [each(s) for s, _ in SAVED],
        out_specs=[whole(s) for s in shapes],
        out_shape=[jax.ShapeDtypeStruct(s, BF) for s in shapes],
        scratch_shapes=[
            pltpu.VMEM((4, 14, 40, 128), F32),
            pltpu.VMEM((8, ROWS, 128), F32),
            pltpu.VMEM((LANES, LANES), BF),
        ],
        compiler_params=params(),
        cost_estimate=cost(5.5),
    )(*pieces, *consts, *saved)


def merge_pairs(stage, gain_ref, weight):
    pairs = stage.shape[1]
    pieces = [
        stage[:, :, q % 2, pl.ds(q // 2, 16, stride=2), :].reshape(WT * pairs * 16, 128)
        for q in range(4)
    ]
    xhat, rstd = normalise(jnp.concatenate(pieces, 1))
    merged = dot((xhat * gain_ref[...]).astype(BF), weight).astype(BF).astype(F32)
    return merged, xhat, rstd


def merge_pairs_back(grad, xhat, rstd, gain_ref, weight, stage):
    pairs = stage.shape[1]
    dn = dot_nt(grad.astype(BF), weight)
    dg = normalise_back(dn * gain_ref[...], xhat, rstd)
    for q in range(4):
        stage[:, :, q % 2, pl.ds(q // 2, 16, stride=2), :] = dg[
            :, 128 * q : 128 * q + 128
        ].reshape(WT, pairs, 16, 128)


def put_pair_row(stage, at, values):
    stage[:, at // 2, at % 2, 0:28, :] = values.astype(F32)


def clear_pads(stage):
    stage[:, :, :, 28:32, :] = jnp.zeros((WT, stage.shape[1], 2, 4, 128), F32)


def pair_row(stage, at):
    return stage[:, at // 2, at % 2, 0:28, :].astype(BF)


def fold_merged(merged, pairs):
    halves = [
        merged[:, 128 * i : 128 * i + 128].reshape(WT, pairs, 16, 128)[:, :, 0:14] for i in range(2)
    ]
    return jnp.concatenate(halves, 2)


def unfold_merged(folded):
    pad = jnp.zeros(folded.shape[:2] + (2, 128), F32)
    halves = [
        jnp.concatenate([folded[:, :, 14 * i : 14 * i + 14], pad], 2).reshape(-1, 128)
        for i in range(2)
    ]
    return jnp.concatenate(halves, 1)


def send_kernel(res_ref, gain_ref, weight_ref, send_ref, xhat_ref, rstd_ref, stage):
    clear_pads(stage)
    for i in range(8):
        put_pair_row(stage, i, res_ref[:, 1 + i])
    merged, xhat, rstd = merge_pairs(stage, gain_ref, weight_ref[...])
    xhat_ref[...] = xhat
    rstd_ref[...] = jnp.broadcast_to(rstd, rstd_ref.shape)
    send_ref[:, 0:1] = res_ref[:, 0:1]
    send_ref[:, 1:5] = fold_merged(merged, 4).astype(BF)


def local_kernel(resA_ref, resB_ref, gain_ref, weight_ref, merged_ref, xhat_ref, rstd_ref, stage):
    clear_pads(stage)
    for i in range(5):
        put_pair_row(stage, i, resA_ref[:, i])
    for i in range(13):
        put_pair_row(stage, 5 + i, resB_ref[:, i])
    merged, xhat, rstd = merge_pairs(stage, gain_ref, weight_ref[...])
    xhat_ref[...] = xhat
    rstd_ref[...] = jnp.broadcast_to(rstd, rstd_ref.shape)
    merged_ref[...] = merged


def local_back_kernel(
    grad_ref, d30_ref, xhat_ref, rstd_ref, gain_ref, weight_ref, dA_ref, dB_ref, stage
):
    merge_pairs_back(
        grad_ref[...], xhat_ref[...], rstd_ref[:, 0:1], gain_ref, weight_ref[...], stage
    )
    for i in range(5):
        dA_ref[:, i] = pair_row(stage, i)
    for i in range(13):
        dB_ref[:, i] = pair_row(stage, 5 + i)
    dB_ref[:, 13] = d30_ref[...]


def receive_kernel(got_ref, xhat_ref, rstd_ref, gain_ref, weight_ref, d_ref, stage):
    grad = unfold_merged(got_ref[:, 1:5].astype(F32))
    merge_pairs_back(grad, xhat_ref[...], rstd_ref[:, 0:1], gain_ref, weight_ref[...], stage)
    d_ref[:, 0:1] = got_ref[:, 0:1]
    for i in range(8):
        d_ref[:, 1 + i] = pair_row(stage, i)


def merge_call(kernel, us, shapes, pairs, *operands):
    return pl.pallas_call(
        kernel,
        out_shape=[jax.ShapeDtypeStruct(shape, kind) for shape, kind in shapes],
        scratch_shapes=[pltpu.VMEM((WT, pairs, 2, 32, 128), F32)],
        compiler_params=params(),
        cost_estimate=cost(us),
    )(*operands)


def middle_kernel(
    merged_ref, resB_ref, next_ref, cot_ref, cta_ref, cha_ref,
    mg1_ref, mg2_ref, g3_ref, row_ref, col_ref, mw1_hbm, mw2_hbm, p3_hbm, bias_hbm, ow3_hbm,
    dm_ref, d30_ref, dN_ref, so_ref, sta_ref, sha_ref,
    stage, stage2, xhat2, rstd2, cotw, k_s, v_s, qT_s, kT_s, vT_s, probs_s, oT_s, inv_s, doT_s, dqkv_s,
    mw1_ref, mw2_ref, p3_ref, bias_ref, ow3_ref, sems,
):
    fetches = [
        pltpu.make_async_copy(there, here, sems.at[i])
        for i, (there, here) in enumerate(
            (
                (mw1_hbm, mw1_ref),
                (mw2_hbm, mw2_ref),
                (p3_hbm, p3_ref),
                (bias_hbm, bias_ref),
                (ow3_hbm, ow3_ref),
            )
        )
    ]
    for fetch in fetches:
        fetch.start()
    cotw[...] = jnp.zeros((4, 7, 8, 512), F32)
    cotw[0:2, 0:4, 0:7, :] = cot_ref[2:4, 3:7].astype(F32)
    cotw[2:4, :, 0:7, :] = unfold(cta_ref[:, 14:21].astype(F32))
    cotw[0:2, 4:7, 0:7, :] = unfold(cha_ref[2:4, 3:6].astype(F32))

    def put_merged(first, count, values):
        for half in range(2):
            block = values[:, 128 * half : 128 * half + 128].reshape(WT, count, 16, 128)
            for i in range(count):
                stage2[half, :, (first + i) // 2, (first + i) % 2] = block[:, i]

    def take_merged(first, count):
        halves = [
            jnp.concatenate(
                [
                    stage2[half, :, (first + i) // 2, (first + i) % 2].reshape(WT, 1, 16, 128)
                    for i in range(count)
                ],
                1,
            ).reshape(WT * count * 16, 128)
            for half in range(2)
        ]
        return jnp.concatenate(halves, 1)

    put_merged(0, 9, merged_ref[...])
    put_merged(10, 4, unfold_merged(next_ref[:, 1:5].astype(F32)))
    clear_pads(stage)
    put_pair_row(stage, 0, resB_ref[:, 13])
    put_pair_row(stage, 1, next_ref[:, 0])
    fetches[0].wait()
    merged, xhat_seam, rstd_seam = merge_pairs(stage, mg1_ref, mw1_ref[...])
    put_merged(9, 1, merged)
    fetches[1].wait()
    pieces = [
        stage2[half, :, :, q % 2, pl.ds(q // 2, 8, stride=2), :].reshape(ROWS, 128)
        for q in range(4)
        for half in range(2)
    ]
    xhat, rstd = normalise(jnp.concatenate(pieces, 1))
    xhat2[...] = xhat
    rstd2[...] = jnp.broadcast_to(rstd, (ROWS, 128))
    merged_two = dot((xhat * mg2_ref[...]).astype(BF), mw2_ref[...]).astype(BF).astype(F32)
    xhat3, rstd3 = normalise(merged_two)
    n3 = (xhat3 * g3_ref[...]).astype(BF)
    fetches[2].wait()
    small, eye = identity(128), identity(LANES)
    packed = [dot(n3, p3_ref[:, 512 * i : 512 * i + 512]) for i in range(3)]
    for g in range(4):
        q, k, v = (part[:, 128 * g : 128 * g + 128] for part in packed)
        q = lengthen((q * (SCALE * LOG2E)).astype(BF))
        k, v = k.astype(BF), v.astype(BF)
        k_s[g] = k
        v_s[g] = v
        qT_s[g] = turn(small, q)
        kT_s[g] = turn(small, lengthen(k))
        vT_s[g] = turn(small, lengthen(v))
    mask = region_mask(col_ref[...], row_ref[...])
    fetches[3].wait()

    def heads(i, _):
        operands = []
        for g in (2 * i, 2 * i + 1):

            def keep(h, probs, g=g):
                probs_s[g * 4 + h] = probs

            operands.append(
                (k_s[g], qT_s[g], vT_s[g], mask, lambda h, g=g: bias_ref[g * 4 + h], keep)
            )
        for u, (oT, inverse) in enumerate(attend_four(operands)):
            oT_s[2 * i + u] = oT
            inv_s[2 * i + u] = inverse
        return 0

    lax.fori_loop(0, 2, heads, 0)
    fetches[4].wait()
    att = jnp.concatenate([turn(eye, oT_s[g].astype(BF))[:ROWS] for g in range(4)], 1)
    mixed = dot(att, ow3_ref[...]).astype(BF).astype(F32)
    section = (merged_two + mixed).reshape(4, 7, 8, 512)
    section = fold(section[:, :, 0:7])
    so_ref[...] = section[0:2, 0:4].astype(BF)
    sta_ref[...] = section[2:4].astype(BF)
    sha_ref[...] = section[0:2, 4:7].astype(BF)

    cot = cotw[...].reshape(ROWS, 512)
    cot_long = lengthen(cot.astype(BF))
    doT = dot_nt(ow3_ref[...], cot_long)
    for g in range(4):
        doT_s[g] = doT[128 * g : 128 * g + 128]

    def heads_back(i, _):
        operands = [
            (
                v_s[g], qT_s[g], kT_s[g], oT_s[g], doT_s[g], inv_s[g],
                lambda h, g=g: probs_s[g * 4 + h],
            )
            for g in (2 * i, 2 * i + 1)
        ]
        for u, (dq, dk, dv) in enumerate(attend_four_back(operands, eye)):
            dqkv_s[2 * i + u] = dq
            dqkv_s[4 + 2 * i + u] = dk
            dqkv_s[8 + 2 * i + u] = dv
        return 0

    lax.fori_loop(0, 2, heads_back, 0)
    dpacked = jnp.concatenate([dqkv_s[i] for i in range(12)], 1)
    dn3 = dot_nt(dpacked, p3_ref[...])
    dm2 = cot + normalise_back(dn3 * g3_ref[...], xhat3, rstd3)
    dn2 = dot_nt(dm2.astype(BF), mw2_ref[...])
    dg2 = normalise_back(dn2 * mg2_ref[...], xhat2[...], rstd2[:, 0:1])
    for q in range(4):
        for half in range(2):
            at = 256 * q + 128 * half
            stage2[half, :, :, q % 2, pl.ds(q // 2, 8, stride=2), :] = dg2[:, at : at + 128].reshape(
                4, 7, 8, 128
            )

    dm_ref[...] = take_merged(0, 9)
    merge_pairs_back(take_merged(9, 1), xhat_seam, rstd_seam, mg1_ref, mw1_ref[...], stage)
    d30_ref[...] = pair_row(stage, 0)
    dN_ref[:, 0] = pair_row(stage, 1)
    dN_ref[:, 1:5] = fold_merged(take_merged(10, 4), 4).astype(BF)


def middle(*operands):
    shapes = [
        (4, 28, 128), (4, 5, 28, 128), (2, 4, 28, 128), (2, 7, 28, 128), (2, 3, 28, 128),
    ]
    return pl.pallas_call(
        middle_kernel,
        in_specs=[pl.BlockSpec(memory_space=pltpu.VMEM)] * 11
        + [pl.BlockSpec(memory_space=pltpu.HBM)] * 3
        + [pl.BlockSpec(memory_space=pl.ANY)]
        + [pl.BlockSpec(memory_space=pltpu.HBM)],
        out_shape=[jax.ShapeDtypeStruct((576, 256), F32)]
        + [jax.ShapeDtypeStruct(s, BF) for s in shapes],
        scratch_shapes=[
            pltpu.VMEM((4, 1, 2, 32, 128), F32),
            pltpu.VMEM((2, 4, 7, 2, 16, 128), F32),
            pltpu.VMEM((ROWS, 1024), F32),
            pltpu.VMEM((ROWS, 128), F32),
            pltpu.VMEM((4, 7, 8, 512), F32),
            pltpu.VMEM((4, ROWS, 128), BF),
            pltpu.VMEM((4, ROWS, 128), BF),
            pltpu.VMEM((4, 128, LANES), BF),
            pltpu.VMEM((4, 128, LANES), BF),
            pltpu.VMEM((4, 128, LANES), BF),
            pltpu.VMEM((16, ROWS, LANES), BF),
            pltpu.VMEM((4, 128, LANES), F32),
            pltpu.VMEM((4, 8, LANES), F32),
            pltpu.VMEM((4, 128, LANES), F32),
            pltpu.VMEM((12, ROWS, 128), BF),
            pltpu.VMEM((512, 256), BF),
            pltpu.VMEM((1024, 512), BF),
            pltpu.VMEM((512, 1536), BF),
            pltpu.VMEM((HEADS3, ROWS, LANES), F32),
            pltpu.VMEM((512, 512), BF),
            pltpu.SemaphoreType.DMA((5,)),
        ],
        compiler_params=params(28),
        cost_estimate=cost(9),
    )(*operands)


def join_kernel(ta_ref, own_ref, so_ref, grad_ref, section_ref, wide, narrow):
    for t in range(WT):
        wide[:, pl.ds(t, 28, stride=4), :] = (ta_ref if t < 2 else own_ref)[t % 2, 0:11].astype(F32)
        low = (ta_ref[t, 11:15] if t < 2 else so_ref[t - 2]).astype(F32)
        for g in range(4):
            narrow[g, :, pl.ds(t, 7, stride=4), :] = low[:, 7 * g : 7 * g + 7]
    for i in range(11):
        grad_ref[17 + i] = wide[i].reshape(28, 4, 128).astype(BF)
    for i in range(4):
        row = jnp.concatenate([narrow[g, i] for g in range(4)], 1)
        section_ref[3 + i] = row.reshape(7, 4, 512).astype(BF)


JOINED = [
    jax.ShapeDtypeStruct((28, 28, 4, 128), BF),
    jax.ShapeDtypeStruct((7, 7, 4, 512), BF),
]


def join(ta, own, section_own):
    return pl.pallas_call(
        join_kernel,
        out_shape=JOINED,
        scratch_shapes=[pltpu.VMEM((11, 112, 128), F32), pltpu.VMEM((4, 4, 28, 128), F32)],
        compiler_params=params(),
        cost_estimate=cost(2),
    )(ta, own, section_own)


def last_kernel(
    grad_hbm, section_hbm, ta_ref, own_ref, dg_ref, ha_ref, grad_out, section_out,
    wide, narrow, rows, section_rows, sems,
):
    del grad_hbm, section_hbm
    for t in range(WT):
        corner = dg_ref if t < 2 else ha_ref
        wide[0:3, pl.ds(t, 28, stride=4), :] = corner[t % 2, 0:3].astype(F32)
        wide[3:17, pl.ds(t, 28, stride=4), :] = (ta_ref if t < 2 else own_ref)[t % 2].astype(F32)
        high = corner[t % 2, 3:6].astype(F32)
        for g in range(4):
            narrow[g, :, pl.ds(t, 7, stride=4), :] = high[:, 7 * g : 7 * g + 7]
    for i in range(17):
        rows[i] = wide[i].reshape(28, 4, 128).astype(BF)
    copy = pltpu.make_async_copy(rows, grad_out.at[0:17], sems.at[0])
    copy.start()
    for i in range(3):
        row = jnp.concatenate([narrow[g, i] for g in range(4)], 1)
        section_rows[i] = row.reshape(7, 4, 512).astype(BF)
    other = pltpu.make_async_copy(section_rows, section_out.at[0:3], sems.at[1])
    other.start()
    copy.wait()
    other.wait()


def join_last(grad, section, ta, own, dg, ha):
    return pl.pallas_call(
        last_kernel,
        in_specs=[pl.BlockSpec(memory_space=pl.ANY)] * 2
        + [pl.BlockSpec(memory_space=pltpu.VMEM)] * 4,
        out_specs=[pl.BlockSpec(memory_space=pl.ANY)] * 2,
        out_shape=JOINED,
        scratch_shapes=[
            pltpu.VMEM((17, 112, 128), F32),
            pltpu.VMEM((4, 3, 28, 128), F32),
            pltpu.VMEM((17, 28, 4, 128), BF),
            pltpu.VMEM((3, 7, 4, 512), BF),
            pltpu.SemaphoreType.DMA((2,)),
        ],
        input_output_aliases={0: 0, 1: 1},
        compiler_params=params(),
        cost_estimate=cost(1),
    )(grad, section, ta, own, dg, ha)


IN_ORDER = Layout(major_to_minor=(0, 1, 2, 3))


def inward(values):
    return with_layout_constraint(jnp.transpose(values, (1, 2, 0, 3)), IN_ORDER)


def outward(values):
    return jnp.transpose(with_layout_constraint(values, IN_ORDER), (2, 0, 1, 3))


def send(values, axes, by):
    axes = axes.split()
    sizes = [lax.axis_size(a) for a in axes]
    if len(axes) == 1:
        pairs = [(i, (i + by) % sizes[0]) for i in range(sizes[0])]
    else:
        n, m = sizes
        pairs = [
            (i * m + j, (i + by) % n * m + (j + by) % m) for i in range(n) for j in range(m)
        ]
    return lax.ppermute(values, tuple(axes), pairs)


def per_device(
    tokens,
    regions_one,
    regions_three,
    gain_one,
    projection_one,
    outward_one,
    table_one,
    merge_gain_one,
    merge_weight_one,
    merge_gain_two,
    merge_weight_two,
    gain_three,
    projection_three,
    outward_three,
    table_three,
    cotangent,
):
    ta_early = send(inward(arrange(early_kernel, (2, 14, 28, 128), tokens)), "ta", -1)
    ha_late = send(arrange(rows_kernel, (4, 6, 28, 128), tokens, cotangent), "ha", -1)
    bias_one, bias_three, row_one, row_three, col_one, col_three = prepare(
        table_one, table_three, regions_one, regions_three
    )
    ta_late = send(
        inward(arrange(late_kernel, (2, 21, 28, 128), tokens, cotangent, ha_late)), "ta", -1
    )
    gain, merge_gain, seam = gain_one[None], merge_gain_one[None], merge_weight_one
    args = (gain, projection_one, outward_one, bias_one)
    (res_send, res_a), saved_a = front(False, (tokens, outward(ta_early)), *args, row_one, col_one)
    row_send, *early_norm = merge_call(
        send_kernel, 0.5, [((4, 5, 28, 128), BF), ((256, 512), F32), ((256, 128), F32)], 4,
        res_send, merge_gain, seam,
    )
    row_next = send(row_send, "ha", -1)
    ta_late, res_a = lax.optimization_barrier((ta_late, res_a))
    ta_late = outward(ta_late)
    (res_b,), saved_b = front(True, (tokens, ta_late, ha_late), *args, row_one, col_one)
    merged, *local_norm = merge_call(
        local_kernel, 1, [((576, 256), F32), ((576, 512), F32), ((576, 128), F32)], 9,
        res_a, res_b, merge_gain, seam,
    )
    row_next, merged = lax.optimization_barrier((row_next, merged))
    d_merged, d_30, d_send, sec_own, sec_ta, sec_ha = middle(
        merged, res_b, row_next, cotangent, ta_late, ha_late,
        merge_gain, merge_gain_two[None], gain_three[None], row_three, col_three,
        merge_weight_one, merge_weight_two, projection_three, bias_three, outward_three,
    )
    d_prev = send(d_send, "ha", 1)
    d_a, d_b = merge_call(
        local_back_kernel, 1, [((4, 5, 28, 128), BF), ((4, 14, 28, 128), BF)], 9,
        d_merged, d_30, *local_norm, merge_gain, seam,
    )
    own_b, ta_b, ha_b, dg_b = back(
        True, (d_b, sec_ta, sec_ha), gain, projection_one, outward_one, saved_b
    )
    d_prev, own_b = lax.optimization_barrier((d_prev, own_b))
    ta_b = send(inward(ta_b), "ta", 1)
    (d_first,) = merge_call(
        receive_kernel, 0.5, [((4, 9, 28, 128), BF)], 4, d_prev, *early_norm, merge_gain, seam
    )
    own_a, ta_a = back(False, (d_first, d_a), gain, projection_one, outward_one, saved_a)
    ta_b, ha_b, dg_b, own_a = lax.optimization_barrier((ta_b, ha_b, dg_b, own_a))
    ta_a = send(inward(ta_a), "ta", 1)
    ha_b = send(ha_b, "ha", 1)
    dg_b = send(dg_b, "ha ta", 1)
    grad, section = join(outward(ta_b), own_b, sec_own)
    ta_a, ha_b, dg_b, grad = lax.optimization_barrier((ta_a, ha_b, dg_b, grad))
    grad, section = join_last(grad, section, outward(ta_a), own_a, dg_b, ha_b)
    return (jnp.transpose(section, (2, 0, 1, 3)), jnp.transpose(grad, (2, 0, 1, 3)))


def solution(mesh):
    tile = P(("col", "ta"), "ha", None, None)
    ids = P(("col", "ta"), "ha", None)
    in_specs = (tile, ids, ids) + (P(),) * 12 + (tile,)
    return jax.shard_map(
        per_device, mesh=mesh, in_specs=in_specs, out_specs=(tile, tile), check_vma=False
    )
```

```python
import functools

import jax
import jax.numpy as jnp
import numpy as np
from jax import lax
from jax.experimental import pallas as pl
from jax.experimental.layout import Layout, with_layout_constraint
from jax.experimental.pallas import tpu as pltpu
from jax.sharding import PartitionSpec as P

HEADS1 = 4
HEADS3 = 16
WT = 4
WS = 7
ST = 2
SS = 3
EPSILON = 1e-05
NREL = 1183
LOG2E = 1.4426950408889634
HEAD = 32
SCALE = HEAD**-0.5
ROWS = WT * WS * 8
LANES = 256
SPAN = 1280
GONE = -1e30
PER_STEP = 4
STEPS = 8 // PER_STEP
BF = jnp.bfloat16
F32 = jnp.float32


def dot(a, b):
    return jnp.dot(a, b, preferred_element_type=F32)


def dot_nt(a, b):
    return lax.dot_general(a, b, (((1,), (1,)), ((), ())), preferred_element_type=F32)


def params(limit=20):
    return pltpu.CompilerParams(vmem_limit_bytes=limit * 1024 * 1024)


def cost(us):
    return pl.CostEstimate(flops=int(us * 1.1e9), bytes_accessed=int(us * 1e6), transcendentals=0)


def normalise(x):
    centred = x - jnp.mean(x, -1, keepdims=True)
    rstd = lax.rsqrt(jnp.mean(centred * centred, -1, keepdims=True) + EPSILON)
    return centred * rstd, rstd


def normalise_back(grad, xhat, rstd):
    return rstd * (
        grad
        - jnp.mean(grad, -1, keepdims=True)
        - xhat * jnp.mean(grad * xhat, -1, keepdims=True)
    )


def head_rows(x, h):
    return x[HEAD * h : HEAD * (h + 1)]


def head_of_lane(shape):
    return lax.broadcasted_iota(jnp.int32, shape, 1) // HEAD


def by_head(x):
    lane = head_of_lane((1, 128))
    return jnp.concatenate([x * (lane == h).astype(F32).astype(BF) for h in range(4)], 0)


def pick_heads(stacked):
    lane = head_of_lane((ROWS, 128))
    got = stacked[:ROWS]
    for h in range(1, 4):
        got = jnp.where(lane == h, stacked[ROWS * h : ROWS * (h + 1)], got)
    return got


def lengthen(x):
    return jnp.concatenate([x, jnp.zeros((LANES - ROWS, x.shape[1]), x.dtype)], 0)


def region_mask(column, row):
    return jnp.where(jnp.concatenate([column, column], 1) == row, 0.0, GONE).astype(F32)


def attend_four(windows):
    scores = [dot(by_head(k), qT) for k, qT, _, _, _, _ in windows]
    results = []
    for s, (_, _, vT, mask, bias_at, keep_probs) in zip(scores, windows):
        outs, inverses = [], []
        for h in range(4):
            biased = s[ROWS * h : ROWS * (h + 1)] + (bias_at(h) + mask)
            peak = jnp.max(biased, 0, keepdims=True)
            probs = jnp.exp2(biased - peak).astype(BF)
            keep_probs(h, probs)
            extended = jnp.concatenate([head_rows(vT, h)[:, :ROWS], jnp.ones((16, ROWS), BF)], 0)
            out = dot(extended, probs)
            inverse = 1.0 / out[HEAD : HEAD + 1]
            outs.append(out[:HEAD] * inverse)
            inverses.append(inverse)
        results.append((jnp.concatenate(outs, 0), jnp.concatenate(inverses + inverses, 0)))
    return results


def attend_four_back(windows):
    first = []
    for v, qT, kT, oT, doT, inverse, probs_at in windows:
        scaled, deltas = [], []
        for h in range(4):
            part = head_rows(doT, h) * inverse[h : h + 1]
            deltas.append(jnp.sum(part * head_rows(oT, h), 0, keepdims=True))
            scaled.append(part)
        scaled = jnp.concatenate(scaled, 0).astype(BF)
        first.append((scaled, deltas, dot(by_head(v), scaled)))
    results = []
    for (scaled, deltas, dprobs), (v, qT, kT, oT, doT, inverse, probs_at) in zip(first, windows):
        probs = [probs_at(h) for h in range(4)]
        dscores = [
            (probs[h].astype(F32) * (dprobs[ROWS * h : ROWS * (h + 1)] - deltas[h])).astype(BF)
            for h in range(4)
        ]
        dv = pick_heads(dot_nt(jnp.concatenate(probs, 0), scaled))
        dk = pick_heads(dot_nt(jnp.concatenate(dscores, 0), qT))
        dqT = jnp.concatenate(
            [dot(head_rows(kT, h)[:, :ROWS], dscores[h]) for h in range(4)], 0
        )
        dq = (dqT * SCALE).astype(BF).T[:ROWS]
        results.append((dq, (dk * (1.0 / LOG2E)).astype(BF), dv.astype(BF)))
    return results


def lanes_of(shape):
    return lax.broadcasted_iota(jnp.int32, shape, 1)


def region_rows(ids, section):
    columns = ids.shape[1]
    count = columns // WS
    place = lax.broadcasted_iota(jnp.int32, (columns, LANES * count), 0)
    lane = lanes_of((columns, LANES * count))
    column = lane % 8
    real = (column < WS) & (lane % LANES < ROWS)
    if section == 3:
        column = jnp.where(column < 3, column + 4, column - 3)
    chosen = real & (place == lane // LANES * WS + column)
    spread = dot(ids.astype(F32).astype(BF), chosen.astype(F32).astype(BF))
    row = lax.broadcasted_iota(jnp.int32, spread.shape, 0)
    lane = lanes_of(spread.shape)
    real = (lane[:1] % 8 < WS) & (lane[:1] % LANES < ROWS)
    rows = []
    for hw in range(ids.shape[0] // (WT * WS)):
        mine = lane % LANES // 8 == row % 4 * WS + row // 4 - WS * hw
        inside = (row >= WT * WS * hw) & (row < WT * WS * (hw + 1))
        found = jnp.sum(jnp.where(mine & inside, spread, 0.0), 0, keepdims=True)
        found = jnp.where(real, found, -1.0)
        rows += [found[:, LANES * ww : LANES * (ww + 1)] for ww in range(count)]
    return rows


def region_columns(ids, section):
    columns = ids.shape[1]
    count = columns // WS
    source = ids.astype(F32).astype(BF)
    token = lax.broadcasted_iota(jnp.int32, (ROWS, ids.shape[0]), 0)
    place = lanes_of((ROWS, ids.shape[0]))
    column = lax.broadcasted_iota(jnp.int32, (ROWS, columns), 0) % 8
    lane = lanes_of((ROWS, columns))
    if section == 3:
        column = jnp.where(column < 3, column + 4, jnp.where(column == 7, 8, column - 3))
    ones = jnp.ones((columns, 128), BF)
    pad = lax.broadcasted_iota(jnp.int32, (ROWS, 128), 0) % 8 == 7
    found = []
    for hw in range(ids.shape[0] // (WT * WS)):
        chosen = place == (token // 8 % WS + WS * hw) * WT + token // 56
        picked = dot(chosen.astype(F32).astype(BF), source)
        for ww in range(count):
            mine = jnp.where(lane == WS * ww + column, picked, 0.0).astype(BF)
            found.append(jnp.where(pad, -1.0, dot(mine, ones)))
    return found


def prepare_kernel(
    t1_ref, t3_ref, s_ref, r1_ref, r3_ref, o1_ref, o3_ref, row1_ref, row3_ref, col1_ref, col3_ref,
    tab, spread
):
    tab[...] = jnp.zeros((24, SPAN), F32)
    tab[0:4, 0:NREL] = t1_ref[...] * LOG2E
    tab[8:24, 0:NREL] = t3_ref[...] * LOG2E
    slabs = []
    for dt in range(7):
        start = 169 * dt
        low = start // 128 * 128
        run = tab[:, low : low + 384]
        if start > low:
            run = pltpu.roll(run, 384 - (start - low), 1)
        slabs.append(run[:, :256])
    left = jnp.concatenate(slabs, 0)
    first = left.astype(BF)
    rest = left - first.astype(F32)
    second = rest.astype(BF)
    third = (rest - second.astype(F32)).astype(BF)
    chosen = s_ref[...]
    got = dot(first, chosen) + dot(second, chosen) + dot(third, chosen)
    lane16 = lanes_of((16, 128))
    for dt in range(7):
        for wj in range(8):
            part = got[24 * dt : 24 * dt + 24, 128 * wj : 128 * wj + 128]
            spread[dt, pl.ds(wj, 8, stride=8), :] = part[0:8]
            later = part[8:24]
            turned = jnp.where(lane16 % 8 < 3, pltpu.roll(later, 124, 1), pltpu.roll(later, 3, 1))
            spread[dt, pl.ds(64 + (7 if wj == 7 else (wj + 3) % 7), 16, stride=8), :] = turned
    for o_ref, heads, at in ((o1_ref, HEADS1, 0), (o3_ref, HEADS3, 64)):
        lane = lanes_of((heads * 8, 128))
        for tj in range(WT):
            for hj in range(WS):
                p0, p1, p2, p3 = (
                    pltpu.roll(
                        spread[ti - tj + 3, at : at + heads * 8, :], (ti * 56 - (6 - hj) * 8) % 128, 1
                    )
                    for ti in range(WT)
                )
                left = jnp.where(lane < 56, p0, jnp.where(lane < 112, p1, p2))
                right = jnp.where(lane < 40, p2, p3)
                row = (tj * WS + hj) * 8
                o_ref[:, row : row + 8, 0:128] = left.reshape(heads, 8, 128)
                o_ref[:, row : row + 8, 128:256] = right.reshape(heads, 8, 128)
    for i, found in enumerate(region_rows(r1_ref[...], 1)):
        row1_ref[i] = found
    row3_ref[...] = region_rows(r3_ref[...], 3)[0]
    for i, found in enumerate(region_columns(r1_ref[...], 1)):
        col1_ref[i] = found
    col3_ref[...] = region_columns(r3_ref[...], 3)[0]


def chooser():
    chosen = np.zeros((256, 1024), np.float32)
    for wj in range(WS):
        for dh in range(13):
            for wi in range(WS):
                chosen[dh * 13 + wi - wj + 6, wj * 128 + dh * 8 + wi] = 1.0
    return jnp.asarray(chosen, BF)


def by_height(ids):
    return jnp.transpose(ids, (1, 0, 2)).reshape(-1, ids.shape[2])


def prepare(table_one, table_three, regions_one, regions_three):
    return pl.pallas_call(
        prepare_kernel,
        out_shape=(
            jax.ShapeDtypeStruct((HEADS1, ROWS, LANES), F32),
            jax.ShapeDtypeStruct((HEADS3, ROWS, LANES), F32),
            jax.ShapeDtypeStruct((16, 1, LANES), F32),
            jax.ShapeDtypeStruct((1, LANES), F32),
            jax.ShapeDtypeStruct((16, ROWS, 128), F32),
            jax.ShapeDtypeStruct((ROWS, 128), F32),
        ),
        scratch_shapes=[pltpu.VMEM((24, SPAN), F32), pltpu.VMEM((7, 24 * 8, 128), F32)],
        compiler_params=params(),
        cost_estimate=cost(3),
    )(
        jnp.transpose(table_one),
        jnp.transpose(table_three),
        chooser(),
        by_height(regions_one),
        by_height(regions_three),
    )


def fold(values):
    return jnp.concatenate([values[..., 128 * g : 128 * g + 128] for g in range(4)], -2)


def unfold(values):
    return jnp.concatenate([values[..., 7 * g : 7 * g + 7, :] for g in range(4)], -1)


def early_kernel(tok_ref, early_ref):
    early_ref[...] = tok_ref[0:2, 3:17]


def late_kernel(tok_ref, cot_ref, late_ref, ha_ref, dg_ref):
    late_ref[:, 0:11] = tok_ref[0:2, 17:28]
    late_ref[:, 11:15] = fold(cot_ref[0:2, 3:7].astype(F32)).astype(BF)
    ha_ref[:, 0:3] = tok_ref[2:4, 0:3]
    ha_ref[:, 3:6] = fold(cot_ref[2:4, 0:3].astype(F32)).astype(BF)
    dg_ref[:, 0:3] = tok_ref[0:2, 0:3]
    dg_ref[:, 3:6] = fold(cot_ref[0:2, 0:3].astype(F32)).astype(BF)


def arrange(kernel, rows, *operands):
    return pl.pallas_call(
        kernel,
        out_shape=[jax.ShapeDtypeStruct((2, n, 28, 128), BF) for n in rows],
        compiler_params=params(8),
        cost_estimate=cost(0.3),
    )(*operands)


def put_rows(stage, frames, rows, values):
    values = values.astype(F32)
    stage[frames, rows, 0:28, :] = values
    stage[frames, rows, 28:36, :] = values[:, :, 0:8, :]


def cut_windows(stage, win):
    for hw in range(2):
        for ww in range(4):
            win[hw * 4 + ww] = stage[:, 7 * hw : 7 * hw + 7, 3 + 7 * ww : 11 + 7 * ww, :].reshape(
                ROWS, 128
            )


def join_windows(win, stage):
    for hw in range(2):
        for ww in range(4):
            stage[:, 7 * hw : 7 * hw + 7, 3 + 7 * ww : 11 + 7 * ww, :] = win[hw * 4 + ww].reshape(
                WT, WS, 8, 128
            )
    stage[:, :, 0:3, :] = stage[:, :, 28:31, :]


def front_kernel(late, *refs):
    n_in = 4 if late else 2
    pieces, refs = refs[:n_in], refs[n_in:]
    gain_ref, proj_ref, outw_ref, bias_ref, row_ref, col_ref = refs[:6]
    refs = refs[6:]
    n_out = 1 if late else 2
    outs, refs = refs[:n_out], refs[n_out:]
    xw_ref, kv_ref, t_ref, p_ref, o_ref, inv_ref, stage, win = refs
    step = pl.program_id(0)

    @pl.when(step == 0)
    def _():
        own = pieces[0]
        if late:
            put_rows(stage, slice(0, 2), slice(0, 11), own[2:4, 17:28])
            put_rows(stage, slice(2, 4), slice(0, 11), pieces[1][:, 0:11])
            put_rows(stage, slice(0, 2), slice(11, 14), pieces[2][:, 0:3])
            put_rows(stage, slice(2, 4), slice(11, 14), pieces[3][:, 0:3])
        else:
            put_rows(stage, slice(0, 2), slice(0, 14), own[2:4, 3:17])
            put_rows(stage, slice(2, 4), slice(0, 14), pieces[1][...])
        cut_windows(stage, win)

    xs, operands = [], []
    for u in range(PER_STEP):
        x = win[step * PER_STEP + u]
        xs.append(x)
        xw_ref[u] = x.astype(BF)
        xhat, _ = normalise(x)
        packed = dot((xhat * gain_ref[...]).astype(BF), proj_ref[...])
        q = (packed[:, :128] * (SCALE * LOG2E)).astype(BF)
        kv = packed[:, 128:].astype(BF)
        kv_ref[u] = kv
        qT, kT, vT = (lengthen(part).T for part in (q, kv[:, :128], kv[:, 128:]))
        t_ref[u, :128] = qT
        t_ref[u, 128:] = kT

        def keep(h, probs, u=u):
            p_ref[u, h] = probs

        operands.append(
            (kv[:, :128], qT, vT, region_mask(col_ref[u], row_ref[u]), lambda h: bias_ref[h], keep)
        )
    for u, (oT, inverse) in enumerate(attend_four(operands)):
        oT = oT.astype(BF)
        o_ref[u] = oT
        inv_ref[u] = inverse
        mixed = dot(oT.T[:ROWS], outw_ref[...]).astype(BF).astype(F32)
        win[step * PER_STEP + u] = xs[u] + mixed

    @pl.when(step == STEPS - 1)
    def _():
        join_windows(win, stage)
        if late:
            outs[0][...] = stage[:, :, 0:28, :].astype(BF)
        else:
            outs[0][...] = stage[:, 0:9, 0:28, :].astype(BF)
            outs[1][...] = stage[:, 9:14, 0:28, :].astype(BF)


def whole(shape):
    return pl.BlockSpec(shape, lambda i: (0,) * len(shape))


def each(shape, first=0):
    return pl.BlockSpec((PER_STEP,) + shape, lambda i: (i + first,) + (0,) * len(shape))


SAVED = (
    ((ROWS, 128), BF),
    ((ROWS, 256), BF),
    ((256, LANES), BF),
    ((4, ROWS, LANES), BF),
    ((128, LANES), BF),
    ((8, LANES), F32),
)


def front(late, pieces, gain, proj, outw, bias, row, column):
    consts = (gain, proj, outw, bias)
    shapes = [(4, 14, 28, 128)] if late else [(4, 9, 28, 128), (4, 5, 28, 128)]
    out = pl.pallas_call(
        functools.partial(front_kernel, late),
        grid=(STEPS,),
        in_specs=[whole(a.shape) for a in tuple(pieces) + consts] + [each((1, LANES), STEPS * late), each((ROWS, 128), STEPS * late)],
        out_specs=[whole(s) for s in shapes] + [each(s) for s, _ in SAVED],
        out_shape=[jax.ShapeDtypeStruct(s, BF) for s in shapes]
        + [jax.ShapeDtypeStruct((8,) + s, d) for s, d in SAVED],
        scratch_shapes=[
            pltpu.VMEM((4, 14, 40, 128), F32),
            pltpu.VMEM((8, ROWS, 128), F32),
        ],
        compiler_params=params(),
        cost_estimate=cost(4.6),
    )(*pieces, *consts, row, column)
    return out[: len(shapes)], out[len(shapes) :]


def back_kernel(late, *refs):
    n_in = 3 if late else 2
    pieces, refs = refs[:n_in], refs[n_in:]
    gain_ref, proj_ref, outw_ref = refs[:3]
    xw_ref, kv_ref, t_ref, p_ref, o_ref, inv_ref = refs[3:9]
    refs = refs[9:]
    n_out = 3 if late else 2
    outs, refs = refs[:n_out], refs[n_out:]
    stage, win = refs
    step = pl.program_id(0)

    @pl.when(step == 0)
    def _():
        if late:
            put_rows(stage, slice(0, 4), slice(0, 14), pieces[0][...])
            outs[1][:, 11:15] = pieces[1][:, 0:4]
            outs[2][0:2, 3:6] = pieces[2][...]
            outs[2][2:4, 3:6] = pieces[1][:, 4:7]
        else:
            put_rows(stage, slice(0, 4), slice(0, 9), pieces[0][...])
            put_rows(stage, slice(0, 4), slice(9, 14), pieces[1][...])
        cut_windows(stage, win)

    drs, operands = [], []
    for u in range(PER_STEP):
        dr = win[step * PER_STEP + u]
        drs.append(dr)
        operands.append(
            (
                kv_ref[u, :, 128:],
                t_ref[u, :128],
                t_ref[u, 128:],
                o_ref[u].astype(F32),
                dot_nt(outw_ref[...], lengthen(dr.astype(BF))),
                inv_ref[u],
                lambda h, u=u: p_ref[u, h],
            )
        )
    for u, (dq, dk, dv) in enumerate(attend_four_back(operands)):
        dpacked = jnp.concatenate([dq, dk, dv], 1)
        dn = dot_nt(dpacked, proj_ref[...])
        xhat, rstd = normalise(xw_ref[u].astype(F32))
        dx = normalise_back(dn * gain_ref[...], xhat, rstd)
        win[step * PER_STEP + u] = drs[u] + dx

    @pl.when(step == STEPS - 1)
    def _():
        join_windows(win, stage)
        if late:
            outs[0][...] = stage[0:2, 0:11, 0:28, :].astype(BF)
            outs[1][:, 0:11] = stage[2:4, 0:11, 0:28, :].astype(BF)
            outs[2][:, 0:3] = stage[:, 11:14, 0:28, :].astype(BF)
        else:
            outs[0][...] = stage[0:2, :, 0:28, :].astype(BF)
            outs[1][...] = stage[2:4, :, 0:28, :].astype(BF)


def back(late, pieces, gain, proj, outw, saved):
    consts = (gain, proj, outw)
    if late:
        shapes = [(2, 11, 28, 128), (2, 15, 28, 128), (4, 6, 28, 128)]
    else:
        shapes = [(2, 14, 28, 128), (2, 14, 28, 128)]
    return pl.pallas_call(
        functools.partial(back_kernel, late),
        grid=(STEPS,),
        in_specs=[whole(a.shape) for a in tuple(pieces) + consts] + [each(s) for s, _ in SAVED],
        out_specs=[whole(s) for s in shapes],
        out_shape=[jax.ShapeDtypeStruct(s, BF) for s in shapes],
        scratch_shapes=[
            pltpu.VMEM((4, 14, 40, 128), F32),
            pltpu.VMEM((8, ROWS, 128), F32),
        ],
        compiler_params=params(),
        cost_estimate=cost(5.5),
    )(*pieces, *consts, *saved)


def merge_pairs(stage, gain_ref, weight):
    pairs = stage.shape[1]
    pieces = [
        stage[:, :, q % 2, pl.ds(q // 2, 16, stride=2), :].reshape(WT * pairs * 16, 128)
        for q in range(4)
    ]
    xhat, rstd = normalise(jnp.concatenate(pieces, 1))
    merged = dot((xhat * gain_ref[...]).astype(BF), weight).astype(BF).astype(F32)
    return merged, xhat, rstd


def merge_pairs_back(grad, xhat, rstd, gain_ref, weight, stage):
    pairs = stage.shape[1]
    dn = dot_nt(grad.astype(BF), weight)
    dg = normalise_back(dn * gain_ref[...], xhat, rstd)
    for q in range(4):
        stage[:, :, q % 2, pl.ds(q // 2, 16, stride=2), :] = dg[
            :, 128 * q : 128 * q + 128
        ].reshape(WT, pairs, 16, 128)


def put_pair_row(stage, at, values):
    stage[:, at // 2, at % 2, 0:28, :] = values.astype(F32)


def clear_pads(stage):
    stage[:, :, :, 28:32, :] = jnp.zeros((WT, stage.shape[1], 2, 4, 128), F32)


def pair_row(stage, at):
    return stage[:, at // 2, at % 2, 0:28, :].astype(BF)


def fold_merged(merged, pairs):
    halves = [
        merged[:, 128 * i : 128 * i + 128].reshape(WT, pairs, 16, 128)[:, :, 0:14] for i in range(2)
    ]
    return jnp.concatenate(halves, 2)


def unfold_merged(folded):
    pad = jnp.zeros(folded.shape[:2] + (2, 128), F32)
    halves = [
        jnp.concatenate([folded[:, :, 14 * i : 14 * i + 14], pad], 2).reshape(-1, 128)
        for i in range(2)
    ]
    return jnp.concatenate(halves, 1)


def send_kernel(res_ref, gain_ref, weight_ref, send_ref, xhat_ref, rstd_ref, stage):
    clear_pads(stage)
    for i in range(8):
        put_pair_row(stage, i, res_ref[:, 1 + i])
    merged, xhat, rstd = merge_pairs(stage, gain_ref, weight_ref[...])
    xhat_ref[...] = xhat
    rstd_ref[...] = jnp.broadcast_to(rstd, rstd_ref.shape)
    send_ref[:, 0:1] = res_ref[:, 0:1]
    send_ref[:, 1:5] = fold_merged(merged, 4).astype(BF)


def local_kernel(resA_ref, resB_ref, gain_ref, weight_ref, merged_ref, xhat_ref, rstd_ref, stage):
    clear_pads(stage)
    for i in range(5):
        put_pair_row(stage, i, resA_ref[:, i])
    for i in range(13):
        put_pair_row(stage, 5 + i, resB_ref[:, i])
    merged, xhat, rstd = merge_pairs(stage, gain_ref, weight_ref[...])
    xhat_ref[...] = xhat
    rstd_ref[...] = jnp.broadcast_to(rstd, rstd_ref.shape)
    merged_ref[...] = merged


def local_back_kernel(
    grad_ref, d30_ref, xhat_ref, rstd_ref, gain_ref, weight_ref, dA_ref, dB_ref, stage
):
    merge_pairs_back(
        grad_ref[...], xhat_ref[...], rstd_ref[:, 0:1], gain_ref, weight_ref[...], stage
    )
    for i in range(5):
        dA_ref[:, i] = pair_row(stage, i)
    for i in range(13):
        dB_ref[:, i] = pair_row(stage, 5 + i)
    dB_ref[:, 13] = d30_ref[...]


def receive_kernel(got_ref, xhat_ref, rstd_ref, gain_ref, weight_ref, d_ref, stage):
    grad = unfold_merged(got_ref[:, 1:5].astype(F32))
    merge_pairs_back(grad, xhat_ref[...], rstd_ref[:, 0:1], gain_ref, weight_ref[...], stage)
    d_ref[:, 0:1] = got_ref[:, 0:1]
    for i in range(8):
        d_ref[:, 1 + i] = pair_row(stage, i)


def merge_call(kernel, us, shapes, pairs, *operands):
    return pl.pallas_call(
        kernel,
        out_shape=[jax.ShapeDtypeStruct(shape, kind) for shape, kind in shapes],
        scratch_shapes=[pltpu.VMEM((WT, pairs, 2, 32, 128), F32)],
        compiler_params=params(),
        cost_estimate=cost(us),
    )(*operands)


def middle_kernel(
    merged_ref, resB_ref, next_ref, cot_ref, cta_ref, cha_ref, cdg_ref,
    mg1_ref, mg2_ref, g3_ref, row_ref, col_ref, mw1_hbm, mw2_hbm, p3_hbm, bias_hbm, ow3_hbm,
    dm_ref, d30_ref, dN_ref, so_ref, sta_ref, sha_ref,
    stage, stage2, xhat2, rstd2, cotw, k_s, v_s, qT_s, kT_s, vT_s, probs_s, oT_s, inv_s, doT_s, dqkv_s,
    mw1_ref, mw2_ref, p3_ref, bias_ref, ow3_ref, sems,
):
    fetches = [
        pltpu.make_async_copy(there, here, sems.at[i])
        for i, (there, here) in enumerate(
            (
                (mw1_hbm, mw1_ref),
                (mw2_hbm, mw2_ref),
                (p3_hbm, p3_ref),
                (bias_hbm, bias_ref),
                (ow3_hbm, ow3_ref),
            )
        )
    ]
    for fetch in fetches:
        fetch.start()
    cotw[...] = jnp.zeros((4, 7, 8, 512), F32)
    cotw[0:2, 0:4, 0:7, :] = cot_ref[2:4, 3:7].astype(F32)
    cotw[2:4, 0:4, 0:7, :] = unfold(cta_ref[:, 11:15].astype(F32))
    cotw[0:2, 4:7, 0:7, :] = unfold(cha_ref[:, 3:6].astype(F32))
    cotw[2:4, 4:7, 0:7, :] = unfold(cdg_ref[:, 3:6].astype(F32))

    def put_merged(first, count, values):
        for half in range(2):
            block = values[:, 128 * half : 128 * half + 128].reshape(WT, count, 16, 128)
            for i in range(count):
                stage2[half, :, (first + i) // 2, (first + i) % 2] = block[:, i]

    def take_merged(first, count):
        halves = [
            jnp.concatenate(
                [
                    stage2[half, :, (first + i) // 2, (first + i) % 2].reshape(WT, 1, 16, 128)
                    for i in range(count)
                ],
                1,
            ).reshape(WT * count * 16, 128)
            for half in range(2)
        ]
        return jnp.concatenate(halves, 1)

    put_merged(0, 9, merged_ref[...])
    put_merged(10, 4, unfold_merged(next_ref[:, 1:5].astype(F32)))
    clear_pads(stage)
    put_pair_row(stage, 0, resB_ref[:, 13])
    put_pair_row(stage, 1, next_ref[:, 0])
    fetches[0].wait()
    merged, xhat_seam, rstd_seam = merge_pairs(stage, mg1_ref, mw1_ref[...])
    put_merged(9, 1, merged)
    fetches[1].wait()
    pieces = [
        stage2[half, :, :, q % 2, pl.ds(q // 2, 8, stride=2), :].reshape(ROWS, 128)
        for q in range(4)
        for half in range(2)
    ]
    xhat, rstd = normalise(jnp.concatenate(pieces, 1))
    xhat2[...] = xhat
    rstd2[...] = jnp.broadcast_to(rstd, (ROWS, 128))
    merged_two = dot((xhat * mg2_ref[...]).astype(BF), mw2_ref[...]).astype(BF).astype(F32)
    xhat3, rstd3 = normalise(merged_two)
    n3 = (xhat3 * g3_ref[...]).astype(BF)
    fetches[2].wait()
    packed = [dot(n3, p3_ref[:, 512 * i : 512 * i + 512]) for i in range(3)]
    for g in range(4):
        q, k, v = (part[:, 128 * g : 128 * g + 128] for part in packed)
        q = lengthen((q * (SCALE * LOG2E)).astype(BF))
        k, v = k.astype(BF), v.astype(BF)
        k_s[g] = k
        v_s[g] = v
        qT_s[g] = q.T
        kT_s[g] = lengthen(k).T
        vT_s[g] = lengthen(v).T
    mask = region_mask(col_ref[...], row_ref[...])
    fetches[3].wait()

    def heads(i, _):
        operands = []
        for g in (2 * i, 2 * i + 1):

            def keep(h, probs, g=g):
                probs_s[g * 4 + h] = probs

            operands.append(
                (k_s[g], qT_s[g], vT_s[g], mask, lambda h, g=g: bias_ref[g * 4 + h], keep)
            )
        for u, (oT, inverse) in enumerate(attend_four(operands)):
            oT_s[2 * i + u] = oT
            inv_s[2 * i + u] = inverse
        return 0

    lax.fori_loop(0, 2, heads, 0)
    fetches[4].wait()
    att = jnp.concatenate([oT_s[g].astype(BF).T[:ROWS] for g in range(4)], 1)
    mixed = dot(att, ow3_ref[...]).astype(BF).astype(F32)
    section = (merged_two + mixed).reshape(4, 7, 8, 512)
    section = fold(section[:, :, 0:7])
    so_ref[...] = section[0:2, 0:4].astype(BF)
    sta_ref[...] = section[2:4].astype(BF)
    sha_ref[...] = section[0:2, 4:7].astype(BF)

    cot = cotw[...].reshape(ROWS, 512)
    cot_long = lengthen(cot.astype(BF))
    doT = dot_nt(ow3_ref[...], cot_long)
    for g in range(4):
        doT_s[g] = doT[128 * g : 128 * g + 128]

    def heads_back(i, _):
        operands = [
            (
                v_s[g], qT_s[g], kT_s[g], oT_s[g], doT_s[g], inv_s[g],
                lambda h, g=g: probs_s[g * 4 + h],
            )
            for g in (2 * i, 2 * i + 1)
        ]
        for u, (dq, dk, dv) in enumerate(attend_four_back(operands)):
            dqkv_s[2 * i + u] = dq
            dqkv_s[4 + 2 * i + u] = dk
            dqkv_s[8 + 2 * i + u] = dv
        return 0

    lax.fori_loop(0, 2, heads_back, 0)
    dpacked = jnp.concatenate([dqkv_s[i] for i in range(12)], 1)
    dn3 = dot_nt(dpacked, p3_ref[...])
    dm2 = cot + normalise_back(dn3 * g3_ref[...], xhat3, rstd3)
    dn2 = dot_nt(dm2.astype(BF), mw2_ref[...])
    dg2 = normalise_back(dn2 * mg2_ref[...], xhat2[...], rstd2[:, 0:1])
    for q in range(4):
        for half in range(2):
            at = 256 * q + 128 * half
            stage2[half, :, :, q % 2, pl.ds(q // 2, 8, stride=2), :] = dg2[:, at : at + 128].reshape(
                4, 7, 8, 128
            )

    dm_ref[...] = take_merged(0, 9)
    merge_pairs_back(take_merged(9, 1), xhat_seam, rstd_seam, mg1_ref, mw1_ref[...], stage)
    d30_ref[...] = pair_row(stage, 0)
    dN_ref[:, 0] = pair_row(stage, 1)
    dN_ref[:, 1:5] = fold_merged(take_merged(10, 4), 4).astype(BF)


def middle(*operands):
    shapes = [
        (4, 28, 128), (4, 5, 28, 128), (2, 4, 28, 128), (2, 7, 28, 128), (2, 3, 28, 128),
    ]
    return pl.pallas_call(
        middle_kernel,
        in_specs=[pl.BlockSpec(memory_space=pltpu.VMEM)] * 12
        + [pl.BlockSpec(memory_space=pl.ANY)] * 5,
        out_shape=[jax.ShapeDtypeStruct((576, 256), F32)]
        + [jax.ShapeDtypeStruct(s, BF) for s in shapes],
        scratch_shapes=[
            pltpu.VMEM((4, 1, 2, 32, 128), F32),
            pltpu.VMEM((2, 4, 7, 2, 16, 128), F32),
            pltpu.VMEM((ROWS, 1024), F32),
            pltpu.VMEM((ROWS, 128), F32),
            pltpu.VMEM((4, 7, 8, 512), F32),
            pltpu.VMEM((4, ROWS, 128), BF),
            pltpu.VMEM((4, ROWS, 128), BF),
            pltpu.VMEM((4, 128, LANES), BF),
            pltpu.VMEM((4, 128, LANES), BF),
            pltpu.VMEM((4, 128, LANES), BF),
            pltpu.VMEM((16, ROWS, LANES), BF),
            pltpu.VMEM((4, 128, LANES), F32),
            pltpu.VMEM((4, 8, LANES), F32),
            pltpu.VMEM((4, 128, LANES), F32),
            pltpu.VMEM((12, ROWS, 128), BF),
            pltpu.VMEM((512, 256), BF),
            pltpu.VMEM((1024, 512), BF),
            pltpu.VMEM((512, 1536), BF),
            pltpu.VMEM((HEADS3, ROWS, LANES), F32),
            pltpu.VMEM((512, 512), BF),
            pltpu.SemaphoreType.DMA((5,)),
        ],
        compiler_params=params(28),
        cost_estimate=cost(9),
    )(*operands)


def join_kernel(ta_ref, own_ref, so_ref, grad_ref, section_ref, wide, narrow):
    for t in range(WT):
        wide[:, pl.ds(t, 28, stride=4), :] = (ta_ref if t < 2 else own_ref)[t % 2, 0:11].astype(F32)
        low = (ta_ref[t, 11:15] if t < 2 else so_ref[t - 2]).astype(F32)
        for g in range(4):
            narrow[g, :, pl.ds(t, 7, stride=4), :] = low[:, 7 * g : 7 * g + 7]
    for i in range(11):
        grad_ref[17 + i] = wide[i].reshape(28, 4, 128).astype(BF)
    for i in range(4):
        row = jnp.concatenate([narrow[g, i] for g in range(4)], 1)
        section_ref[3 + i] = row.reshape(7, 4, 512).astype(BF)


JOINED = [
    jax.ShapeDtypeStruct((28, 28, 4, 128), BF),
    jax.ShapeDtypeStruct((7, 7, 4, 512), BF),
]


def join(ta, own, section_own):
    return pl.pallas_call(
        join_kernel,
        out_shape=JOINED,
        scratch_shapes=[pltpu.VMEM((11, 112, 128), F32), pltpu.VMEM((4, 4, 28, 128), F32)],
        compiler_params=params(),
        cost_estimate=cost(2),
    )(ta, own, section_own)


def last_kernel(
    grad_hbm, section_hbm, ta_ref, own_ref, dg_ref, ha_ref, grad_out, section_out,
    wide, narrow, rows, section_rows, sems,
):
    del grad_hbm, section_hbm
    for t in range(WT):
        corner = dg_ref if t < 2 else ha_ref
        wide[0:3, pl.ds(t, 28, stride=4), :] = corner[t % 2, 0:3].astype(F32)
        wide[3:17, pl.ds(t, 28, stride=4), :] = (ta_ref if t < 2 else own_ref)[t % 2].astype(F32)
        high = corner[t % 2, 3:6].astype(F32)
        for g in range(4):
            narrow[g, :, pl.ds(t, 7, stride=4), :] = high[:, 7 * g : 7 * g + 7]
    for i in range(17):
        rows[i] = wide[i].reshape(28, 4, 128).astype(BF)
    copy = pltpu.make_async_copy(rows, grad_out.at[0:17], sems.at[0])
    copy.start()
    for i in range(3):
        row = jnp.concatenate([narrow[g, i] for g in range(4)], 1)
        section_rows[i] = row.reshape(7, 4, 512).astype(BF)
    other = pltpu.make_async_copy(section_rows, section_out.at[0:3], sems.at[1])
    other.start()
    copy.wait()
    other.wait()


def join_last(grad, section, ta, own, dg, ha):
    return pl.pallas_call(
        last_kernel,
        in_specs=[pl.BlockSpec(memory_space=pl.ANY)] * 2
        + [pl.BlockSpec(memory_space=pltpu.VMEM)] * 4,
        out_specs=[pl.BlockSpec(memory_space=pl.ANY)] * 2,
        out_shape=JOINED,
        scratch_shapes=[
            pltpu.VMEM((17, 112, 128), F32),
            pltpu.VMEM((4, 3, 28, 128), F32),
            pltpu.VMEM((17, 28, 4, 128), BF),
            pltpu.VMEM((3, 7, 4, 512), BF),
            pltpu.SemaphoreType.DMA((2,)),
        ],
        input_output_aliases={0: 0, 1: 1},
        compiler_params=params(),
        cost_estimate=cost(1),
    )(grad, section, ta, own, dg, ha)


IN_ORDER = Layout(major_to_minor=(0, 1, 2, 3))


def inward(values):
    return with_layout_constraint(jnp.transpose(values, (1, 2, 0, 3)), IN_ORDER)


def outward(values):
    return jnp.transpose(with_layout_constraint(values, IN_ORDER), (2, 0, 1, 3))


def send(values, axes, by):
    axes = axes.split()
    sizes = [lax.axis_size(a) for a in axes]
    if len(axes) == 1:
        pairs = [(i, (i + by) % sizes[0]) for i in range(sizes[0])]
    else:
        n, m = sizes
        pairs = [
            (i * m + j, (i + by) % n * m + (j + by) % m) for i in range(n) for j in range(m)
        ]
    return lax.ppermute(values, tuple(axes), pairs)


def per_device(
    tokens,
    regions_one,
    regions_three,
    gain_one,
    projection_one,
    outward_one,
    table_one,
    merge_gain_one,
    merge_weight_one,
    merge_gain_two,
    merge_weight_two,
    gain_three,
    projection_three,
    outward_three,
    table_three,
    cotangent,
):
    (early,) = arrange(early_kernel, (14,), tokens)
    ta_early = send(inward(early), "ta", -1)
    late, ha_late, dg_late = arrange(late_kernel, (15, 6, 6), tokens, cotangent)
    ha_late = send(ha_late, "ha", -1)
    dg_late = send(dg_late, "ha ta", -1)
    ta_late = send(inward(late), "ta", -1)
    bias_one, bias_three, row_one, row_three, col_one, col_three = prepare(
        table_one, table_three, regions_one, regions_three
    )
    gain, merge_gain, seam = gain_one[None], merge_gain_one[None], merge_weight_one
    args = (gain, projection_one, outward_one, bias_one)
    (res_send, res_a), saved_a = front(False, (tokens, outward(ta_early)), *args, row_one, col_one)
    row_send, *early_norm = merge_call(
        send_kernel, 0.5, [((4, 5, 28, 128), BF), ((256, 512), F32), ((256, 128), F32)], 4,
        res_send, merge_gain, seam,
    )
    row_next = send(row_send, "ha", -1)
    ta_late, res_a = lax.optimization_barrier((ta_late, res_a))
    ta_late = outward(ta_late)
    (res_b,), saved_b = front(True, (tokens, ta_late, ha_late, dg_late), *args, row_one, col_one)
    merged, *local_norm = merge_call(
        local_kernel, 0.1, [((576, 256), F32), ((576, 512), F32), ((576, 128), F32)], 9,
        res_a, res_b, merge_gain, seam,
    )
    row_next, merged = lax.optimization_barrier((row_next, merged))
    d_merged, d_30, d_send, sec_own, sec_ta, sec_ha = middle(
        merged, res_b, row_next, cotangent, ta_late, ha_late, dg_late,
        merge_gain, merge_gain_two[None], gain_three[None], row_three, col_three,
        merge_weight_one, merge_weight_two, projection_three, bias_three, outward_three,
    )
    d_prev = send(d_send, "ha", 1)
    d_a, d_b = merge_call(
        local_back_kernel, 1, [((4, 5, 28, 128), BF), ((4, 14, 28, 128), BF)], 9,
        d_merged, d_30, *local_norm, merge_gain, seam,
    )
    own_b, ta_b, ha_b = back(
        True, (d_b, sec_ta, sec_ha), gain, projection_one, outward_one, saved_b
    )
    d_prev, own_b = lax.optimization_barrier((d_prev, own_b))
    ta_b = send(inward(ta_b), "ta", 1)
    ha_b = send(ha_b, "ha", 1)
    (d_first,) = merge_call(
        receive_kernel, 0.5, [((4, 9, 28, 128), BF)], 4, d_prev, *early_norm, merge_gain, seam
    )
    own_a, ta_a = back(False, (d_first, d_a), gain, projection_one, outward_one, saved_a)
    ta_b, ha_b, own_a = lax.optimization_barrier((ta_b, ha_b, own_a))
    ta_a = send(inward(ta_a), "ta", 1)
    dg_b = send(ha_b[2:], "ta", 1)
    grad, section = join(outward(ta_b), own_b, sec_own)
    ta_a, dg_b, grad = lax.optimization_barrier((ta_a, dg_b, grad))
    grad, section = join_last(grad, section, outward(ta_a), own_a, dg_b, ha_b)
    return (jnp.transpose(section, (2, 0, 1, 3)), jnp.transpose(grad, (2, 0, 1, 3)))


def solution(mesh):
    tile = P(("col", "ta"), "ha", None, None)
    ids = P(("col", "ta"), "ha", None)
    in_specs = (tile, ids, ids) + (P(),) * 12 + (tile,)
    return jax.shard_map(
        per_device, mesh=mesh, in_specs=in_specs, out_specs=(tile, tile), check_vma=False
    )
```

```python
import functools

import jax
import jax.numpy as jnp
import numpy as np
from jax import lax
from jax.experimental import pallas as pl
from jax.experimental.layout import Layout, with_layout_constraint
from jax.experimental.pallas import tpu as pltpu
from jax.sharding import PartitionSpec as P

HEADS1 = 4
HEADS3 = 16
WT = 4
WS = 7
ST = 2
SS = 3
EPSILON = 1e-05
NREL = 1183
LOG2E = 1.4426950408889634
HEAD = 32
SCALE = HEAD**-0.5
ROWS = WT * WS * 8
LANES = 256
SPAN = 1280
GONE = -1e30
PER_STEP = 4
STEPS = 8 // PER_STEP
BF = jnp.bfloat16
F32 = jnp.float32


def dot(a, b):
    return jnp.dot(a, b, preferred_element_type=F32)


def dot_nt(a, b):
    return lax.dot_general(a, b, (((1,), (1,)), ((), ())), preferred_element_type=F32)


def params(limit=20):
    return pltpu.CompilerParams(vmem_limit_bytes=limit * 1024 * 1024)


def cost(us):
    return pl.CostEstimate(flops=int(us * 1.1e9), bytes_accessed=int(us * 1e6), transcendentals=0)


def normalise(x):
    centred = x - jnp.mean(x, -1, keepdims=True)
    rstd = lax.rsqrt(jnp.mean(centred * centred, -1, keepdims=True) + EPSILON)
    return centred * rstd, rstd


def normalise_back(grad, xhat, rstd):
    return rstd * (
        grad
        - jnp.mean(grad, -1, keepdims=True)
        - xhat * jnp.mean(grad * xhat, -1, keepdims=True)
    )


def head_rows(x, h):
    return x[HEAD * h : HEAD * (h + 1)]


def head_of_lane(shape):
    return lax.broadcasted_iota(jnp.int32, shape, 1) // HEAD


def by_head(x):
    lane = head_of_lane((1, 128))
    return jnp.concatenate([x * (lane == h).astype(F32).astype(BF) for h in range(4)], 0)


def pick_heads(stacked):
    lane = head_of_lane((ROWS, 128))
    got = stacked[:ROWS]
    for h in range(1, 4):
        got = jnp.where(lane == h, stacked[ROWS * h : ROWS * (h + 1)], got)
    return got


def lengthen(x):
    return jnp.concatenate([x, jnp.zeros((LANES - ROWS, x.shape[1]), x.dtype)], 0)


def region_mask(column, row):
    return jnp.where(jnp.concatenate([column, column], 1) == row, 0.0, GONE).astype(F32)


def attend_four(windows):
    scores = [dot(by_head(k), qT) for k, qT, _, _, _, _ in windows]
    results = []
    for s, (_, _, vT, mask, bias_at, keep_probs) in zip(scores, windows):
        outs, inverses = [], []
        for h in range(4):
            biased = s[ROWS * h : ROWS * (h + 1)] + (bias_at(h) + mask)
            peak = jnp.max(biased, 0, keepdims=True)
            probs = jnp.exp2(biased - peak).astype(BF)
            keep_probs(h, probs)
            extended = jnp.concatenate([head_rows(vT, h)[:, :ROWS], jnp.ones((16, ROWS), BF)], 0)
            out = dot(extended, probs)
            inverse = 1.0 / out[HEAD : HEAD + 1]
            outs.append(out[:HEAD] * inverse)
            inverses.append(inverse)
        results.append((jnp.concatenate(outs, 0), jnp.concatenate(inverses + inverses, 0)))
    return results


def attend_four_back(windows):
    first = []
    for v, qT, kT, oT, doT, inverse, probs_at in windows:
        scaled, deltas = [], []
        for h in range(4):
            part = head_rows(doT, h) * inverse[h : h + 1]
            deltas.append(jnp.sum(part * head_rows(oT, h), 0, keepdims=True))
            scaled.append(part)
        scaled = jnp.concatenate(scaled, 0).astype(BF)
        first.append((scaled, deltas, dot(by_head(v), scaled)))
    results = []
    for (scaled, deltas, dprobs), (v, qT, kT, oT, doT, inverse, probs_at) in zip(first, windows):
        probs = [probs_at(h) for h in range(4)]
        dscores = [
            (probs[h].astype(F32) * (dprobs[ROWS * h : ROWS * (h + 1)] - deltas[h])).astype(BF)
            for h in range(4)
        ]
        dv = pick_heads(dot_nt(jnp.concatenate(probs, 0), scaled))
        dk = pick_heads(dot_nt(jnp.concatenate(dscores, 0), qT))
        dqT = jnp.concatenate(
            [dot(head_rows(kT, h)[:, :ROWS], dscores[h]) for h in range(4)], 0
        )
        dq = (dqT * SCALE).astype(BF).T[:ROWS]
        results.append((dq, (dk * (1.0 / LOG2E)).astype(BF), dv.astype(BF)))
    return results


def lanes_of(shape):
    return lax.broadcasted_iota(jnp.int32, shape, 1)


def region_rows(ids, section):
    columns = ids.shape[1]
    count = columns // WS
    place = lax.broadcasted_iota(jnp.int32, (columns, LANES * count), 0)
    lane = lanes_of((columns, LANES * count))
    column = lane % 8
    real = (column < WS) & (lane % LANES < ROWS)
    if section == 3:
        column = jnp.where(column < 3, column + 4, column - 3)
    chosen = real & (place == lane // LANES * WS + column)
    spread = dot(ids.astype(F32).astype(BF), chosen.astype(F32).astype(BF))
    row = lax.broadcasted_iota(jnp.int32, spread.shape, 0)
    lane = lanes_of(spread.shape)
    real = (lane[:1] % 8 < WS) & (lane[:1] % LANES < ROWS)
    rows = []
    for hw in range(ids.shape[0] // (WT * WS)):
        mine = lane % LANES // 8 == row % 4 * WS + row // 4 - WS * hw
        inside = (row >= WT * WS * hw) & (row < WT * WS * (hw + 1))
        found = jnp.sum(jnp.where(mine & inside, spread, 0.0), 0, keepdims=True)
        found = jnp.where(real, found, -1.0)
        rows += [found[:, LANES * ww : LANES * (ww + 1)] for ww in range(count)]
    return rows


def region_columns(ids, section):
    columns = ids.shape[1]
    count = columns // WS
    source = ids.astype(F32).astype(BF)
    token = lax.broadcasted_iota(jnp.int32, (ROWS, ids.shape[0]), 0)
    place = lanes_of((ROWS, ids.shape[0]))
    column = lax.broadcasted_iota(jnp.int32, (ROWS, columns), 0) % 8
    lane = lanes_of((ROWS, columns))
    if section == 3:
        column = jnp.where(column < 3, column + 4, jnp.where(column == 7, 8, column - 3))
    ones = jnp.ones((columns, 128), BF)
    pad = lax.broadcasted_iota(jnp.int32, (ROWS, 128), 0) % 8 == 7
    found = []
    for hw in range(ids.shape[0] // (WT * WS)):
        chosen = place == (token // 8 % WS + WS * hw) * WT + token // 56
        picked = dot(chosen.astype(F32).astype(BF), source)
        for ww in range(count):
            mine = jnp.where(lane == WS * ww + column, picked, 0.0).astype(BF)
            found.append(jnp.where(pad, -1.0, dot(mine, ones)))
    return found


def prepare_kernel(
    t1_ref, t3_ref, s_ref, r1_ref, r3_ref, o1_ref, o3_ref, row1_ref, row3_ref, col1_ref, col3_ref,
    tab, spread
):
    tab[...] = jnp.zeros((24, SPAN), F32)
    tab[0:4, 0:NREL] = t1_ref[...] * LOG2E
    tab[8:24, 0:NREL] = t3_ref[...] * LOG2E
    slabs = []
    for dt in range(7):
        start = 169 * dt
        low = start // 128 * 128
        run = tab[:, low : low + 384]
        if start > low:
            run = pltpu.roll(run, 384 - (start - low), 1)
        slabs.append(run[:, :256])
    left = jnp.concatenate(slabs, 0)
    first = left.astype(BF)
    rest = left - first.astype(F32)
    second = rest.astype(BF)
    third = (rest - second.astype(F32)).astype(BF)
    chosen = s_ref[...]
    got = dot(first, chosen) + dot(second, chosen) + dot(third, chosen)
    lane16 = lanes_of((16, 128))
    for dt in range(7):
        for wj in range(8):
            part = got[24 * dt : 24 * dt + 24, 128 * wj : 128 * wj + 128]
            spread[dt, pl.ds(wj, 8, stride=8), :] = part[0:8]
            later = part[8:24]
            turned = jnp.where(lane16 % 8 < 3, pltpu.roll(later, 124, 1), pltpu.roll(later, 3, 1))
            spread[dt, pl.ds(64 + (7 if wj == 7 else (wj + 3) % 7), 16, stride=8), :] = turned
    for o_ref, heads, at in ((o1_ref, HEADS1, 0), (o3_ref, HEADS3, 64)):
        lane = lanes_of((heads * 8, 128))
        for tj in range(WT):
            for hj in range(WS):
                p0, p1, p2, p3 = (
                    pltpu.roll(
                        spread[ti - tj + 3, at : at + heads * 8, :], (ti * 56 - (6 - hj) * 8) % 128, 1
                    )
                    for ti in range(WT)
                )
                left = jnp.where(lane < 56, p0, jnp.where(lane < 112, p1, p2))
                right = jnp.where(lane < 40, p2, p3)
                row = (tj * WS + hj) * 8
                o_ref[:, row : row + 8, 0:128] = left.reshape(heads, 8, 128)
                o_ref[:, row : row + 8, 128:256] = right.reshape(heads, 8, 128)
    for i, found in enumerate(region_rows(r1_ref[...], 1)):
        row1_ref[i] = found
    row3_ref[...] = region_rows(r3_ref[...], 3)[0]
    for i, found in enumerate(region_columns(r1_ref[...], 1)):
        col1_ref[i] = found
    col3_ref[...] = region_columns(r3_ref[...], 3)[0]


def chooser():
    chosen = np.zeros((256, 1024), np.float32)
    for wj in range(WS):
        for dh in range(13):
            for wi in range(WS):
                chosen[dh * 13 + wi - wj + 6, wj * 128 + dh * 8 + wi] = 1.0
    return jnp.asarray(chosen, BF)


def by_height(ids):
    return jnp.transpose(ids, (1, 0, 2)).reshape(-1, ids.shape[2])


def prepare(table_one, table_three, regions_one, regions_three):
    return pl.pallas_call(
        prepare_kernel,
        out_shape=(
            jax.ShapeDtypeStruct((HEADS1, ROWS, LANES), F32),
            jax.ShapeDtypeStruct((HEADS3, ROWS, LANES), F32),
            jax.ShapeDtypeStruct((16, 1, LANES), F32),
            jax.ShapeDtypeStruct((1, LANES), F32),
            jax.ShapeDtypeStruct((16, ROWS, 128), F32),
            jax.ShapeDtypeStruct((ROWS, 128), F32),
        ),
        scratch_shapes=[pltpu.VMEM((24, SPAN), F32), pltpu.VMEM((7, 24 * 8, 128), F32)],
        compiler_params=params(),
        cost_estimate=cost(3),
    )(
        jnp.transpose(table_one),
        jnp.transpose(table_three),
        chooser(),
        by_height(regions_one),
        by_height(regions_three),
    )


def fold(values):
    return jnp.concatenate([values[..., 128 * g : 128 * g + 128] for g in range(4)], -2)


def unfold(values):
    return jnp.concatenate([values[..., 7 * g : 7 * g + 7, :] for g in range(4)], -1)


def early_kernel(tok_ref, early_ref):
    early_ref[...] = tok_ref[0:2, 3:17]


def late_kernel(tok_ref, cot_ref, late_ref, ha_ref, dg_ref):
    late_ref[:, 0:11] = tok_ref[0:2, 17:28]
    late_ref[:, 11:15] = fold(cot_ref[0:2, 3:7].astype(F32)).astype(BF)
    ha_ref[:, 0:3] = tok_ref[2:4, 0:3]
    ha_ref[:, 3:6] = fold(cot_ref[2:4, 0:3].astype(F32)).astype(BF)
    dg_ref[:, 0:3] = tok_ref[0:2, 0:3]
    dg_ref[:, 3:6] = fold(cot_ref[0:2, 0:3].astype(F32)).astype(BF)


def arrange(kernel, rows, *operands):
    return pl.pallas_call(
        kernel,
        out_shape=[jax.ShapeDtypeStruct((2, n, 28, 128), BF) for n in rows],
        compiler_params=params(8),
        cost_estimate=cost(0.3),
    )(*operands)


def put_rows(stage, frames, rows, values):
    values = values.astype(F32)
    stage[frames, rows, 0:28, :] = values
    stage[frames, rows, 28:36, :] = values[:, :, 0:8, :]


def cut_windows(stage, win):
    for hw in range(stage.shape[1] // 7):
        for ww in range(4):
            win[hw * 4 + ww] = stage[:, 7 * hw : 7 * hw + 7, 3 + 7 * ww : 11 + 7 * ww, :].reshape(
                ROWS, 128
            )


def join_windows(win, stage):
    for hw in range(stage.shape[1] // 7):
        for ww in range(4):
            stage[:, 7 * hw : 7 * hw + 7, 3 + 7 * ww : 11 + 7 * ww, :] = win[hw * 4 + ww].reshape(
                WT, WS, 8, 128
            )
    stage[:, :, 0:3, :] = stage[:, :, 28:31, :]


def front_kernel(late, *refs):
    n_in = 4 if late else 2
    pieces, refs = refs[:n_in], refs[n_in:]
    gain_ref, proj_ref, outw_ref, bias_ref, row_ref, col_ref = refs[:6]
    refs = refs[6:]
    n_out = 1 if late else 2
    outs, refs = refs[:n_out], refs[n_out:]
    xw_ref, kv_ref, t_ref, p_ref, o_ref, inv_ref, stage, win = refs
    step = pl.program_id(0)

    @pl.when(step == 0)
    def _():
        own = pieces[0]
        if late:
            put_rows(stage, slice(0, 2), slice(0, 11), own[2:4, 17:28])
            put_rows(stage, slice(2, 4), slice(0, 11), pieces[1][:, 0:11])
            put_rows(stage, slice(0, 2), slice(11, 14), pieces[2][:, 0:3])
            put_rows(stage, slice(2, 4), slice(11, 14), pieces[3][:, 0:3])
        else:
            put_rows(stage, slice(0, 2), slice(0, 14), own[2:4, 3:17])
            put_rows(stage, slice(2, 4), slice(0, 14), pieces[1][...])
        cut_windows(stage, win)

    xs, operands = [], []
    for u in range(PER_STEP):
        x = win[step * PER_STEP + u]
        xs.append(x)
        xw_ref[u] = x.astype(BF)
        xhat, _ = normalise(x)
        packed = dot((xhat * gain_ref[...]).astype(BF), proj_ref[...])
        q = (packed[:, :128] * (SCALE * LOG2E)).astype(BF)
        kv = packed[:, 128:].astype(BF)
        kv_ref[u] = kv
        qT, kT, vT = (lengthen(part).T for part in (q, kv[:, :128], kv[:, 128:]))
        t_ref[u, :128] = qT
        t_ref[u, 128:] = kT

        def keep(h, probs, u=u):
            p_ref[u, h] = probs

        operands.append(
            (kv[:, :128], qT, vT, region_mask(col_ref[u], row_ref[u]), lambda h: bias_ref[h], keep)
        )
    for u, (oT, inverse) in enumerate(attend_four(operands)):
        oT = oT.astype(BF)
        o_ref[u] = oT
        inv_ref[u] = inverse
        mixed = dot(oT.T[:ROWS], outw_ref[...]).astype(BF).astype(F32)
        win[step * PER_STEP + u] = xs[u] + mixed

    @pl.when(step == STEPS - 1)
    def _():
        join_windows(win, stage)
        if late:
            outs[0][...] = stage[:, :, 0:28, :].astype(BF)
        else:
            outs[0][...] = stage[:, 0:9, 0:28, :].astype(BF)
            outs[1][...] = stage[:, 9:14, 0:28, :].astype(BF)


def whole(shape):
    return pl.BlockSpec(shape, lambda i: (0,) * len(shape))


def each(shape, first=0):
    return pl.BlockSpec((PER_STEP,) + shape, lambda i: (i + first,) + (0,) * len(shape))


SAVED = (
    ((ROWS, 128), BF),
    ((ROWS, 256), BF),
    ((256, LANES), BF),
    ((4, ROWS, LANES), BF),
    ((128, LANES), BF),
    ((8, LANES), F32),
)


def front(late, pieces, gain, proj, outw, bias, row, column):
    consts = (gain, proj, outw, bias)
    shapes = [(4, 14, 28, 128)] if late else [(4, 9, 28, 128), (4, 5, 28, 128)]
    out = pl.pallas_call(
        functools.partial(front_kernel, late),
        grid=(STEPS,),
        in_specs=[whole(a.shape) for a in tuple(pieces) + consts] + [each((1, LANES), STEPS * late), each((ROWS, 128), STEPS * late)],
        out_specs=[whole(s) for s in shapes] + [each(s) for s, _ in SAVED],
        out_shape=[jax.ShapeDtypeStruct(s, BF) for s in shapes]
        + [jax.ShapeDtypeStruct((8,) + s, d) for s, d in SAVED],
        scratch_shapes=[
            pltpu.VMEM((4, 14, 40, 128), F32),
            pltpu.VMEM((8, ROWS, 128), F32),
        ],
        compiler_params=params(),
        cost_estimate=cost(4.6),
    )(*pieces, *consts, row, column)
    return out[: len(shapes)], out[len(shapes) :]


def back_kernel(part, *refs):
    n_in = (1, 2, 3)[part]
    pieces, refs = refs[:n_in], refs[n_in:]
    gain_ref, proj_ref, outw_ref = refs[:3]
    xw_ref, kv_ref, t_ref, p_ref, o_ref, inv_ref = refs[3:9]
    refs = refs[9:]
    n_out = 3 if part == 2 else 2
    outs, refs = refs[:n_out], refs[n_out:]
    stage, win = refs
    step = pl.program_id(0)

    @pl.when(step == 0)
    def _():
        if part == 2:
            put_rows(stage, slice(0, 4), slice(0, 14), pieces[0][...])
            outs[1][:, 11:15] = pieces[1][:, 0:4]
            outs[2][0:2, 3:6] = pieces[2][...]
            outs[2][2:4, 3:6] = pieces[1][:, 4:7]
        elif part == 1:
            put_rows(stage, slice(0, 4), slice(0, 2), pieces[0][...])
            put_rows(stage, slice(0, 4), slice(2, 7), pieces[1][...])
        else:
            put_rows(stage, slice(0, 4), slice(0, 7), pieces[0][...])
        cut_windows(stage, win)

    drs, operands = [], []
    for u in range(PER_STEP):
        dr = win[step * PER_STEP + u]
        drs.append(dr)
        operands.append(
            (
                kv_ref[u, :, 128:],
                t_ref[u, :128],
                t_ref[u, 128:],
                o_ref[u].astype(F32),
                dot_nt(outw_ref[...], lengthen(dr.astype(BF))),
                inv_ref[u],
                lambda h, u=u: p_ref[u, h],
            )
        )
    for u, (dq, dk, dv) in enumerate(attend_four_back(operands)):
        dpacked = jnp.concatenate([dq, dk, dv], 1)
        dn = dot_nt(dpacked, proj_ref[...])
        xhat, rstd = normalise(xw_ref[u].astype(F32))
        dx = normalise_back(dn * gain_ref[...], xhat, rstd)
        win[step * PER_STEP + u] = drs[u] + dx

    @pl.when(step == pl.num_programs(0) - 1)
    def _():
        join_windows(win, stage)
        if part == 2:
            outs[0][...] = stage[0:2, 0:11, 0:28, :].astype(BF)
            outs[1][:, 0:11] = stage[2:4, 0:11, 0:28, :].astype(BF)
            outs[2][:, 0:3] = stage[:, 11:14, 0:28, :].astype(BF)
        else:
            outs[0][...] = stage[0:2, :, 0:28, :].astype(BF)
            outs[1][...] = stage[2:4, :, 0:28, :].astype(BF)


def back(part, pieces, gain, proj, outw, saved):
    consts = (gain, proj, outw)
    if part == 2:
        shapes = [(2, 11, 28, 128), (2, 15, 28, 128), (4, 6, 28, 128)]
    else:
        shapes = [(2, 7, 28, 128), (2, 7, 28, 128)]
    half = 2 if part == 2 else 1
    return pl.pallas_call(
        functools.partial(back_kernel, part),
        grid=(half * 4 // PER_STEP,),
        in_specs=[whole(a.shape) for a in tuple(pieces) + consts]
        + [each(s, 4 // PER_STEP * (part == 1)) for s, _ in SAVED],
        out_specs=[whole(s) for s in shapes],
        out_shape=[jax.ShapeDtypeStruct(s, BF) for s in shapes],
        scratch_shapes=[
            pltpu.VMEM((4, 7 * half, 40, 128), F32),
            pltpu.VMEM((4 * half, ROWS, 128), F32),
        ],
        compiler_params=params(),
        cost_estimate=cost(2.75 * half),
    )(*pieces, *consts, *saved)


def merge_pairs(stage, gain_ref, weight):
    pairs = stage.shape[1]
    pieces = [
        stage[:, :, q % 2, pl.ds(q // 2, 16, stride=2), :].reshape(WT * pairs * 16, 128)
        for q in range(4)
    ]
    xhat, rstd = normalise(jnp.concatenate(pieces, 1))
    merged = dot((xhat * gain_ref[...]).astype(BF), weight).astype(BF).astype(F32)
    return merged, xhat, rstd


def merge_pairs_back(grad, xhat, rstd, gain_ref, weight, stage):
    pairs = stage.shape[1]
    dn = dot_nt(grad.astype(BF), weight)
    dg = normalise_back(dn * gain_ref[...], xhat, rstd)
    for q in range(4):
        stage[:, :, q % 2, pl.ds(q // 2, 16, stride=2), :] = dg[
            :, 128 * q : 128 * q + 128
        ].reshape(WT, pairs, 16, 128)


def put_pair_row(stage, at, values):
    stage[:, at // 2, at % 2, 0:28, :] = values.astype(F32)


def clear_pads(stage):
    stage[:, :, :, 28:32, :] = jnp.zeros((WT, stage.shape[1], 2, 4, 128), F32)


def pair_row(stage, at):
    return stage[:, at // 2, at % 2, 0:28, :].astype(BF)


def fold_merged(merged, pairs):
    halves = [
        merged[:, 128 * i : 128 * i + 128].reshape(WT, pairs, 16, 128)[:, :, 0:14] for i in range(2)
    ]
    return jnp.concatenate(halves, 2)


def unfold_merged(folded):
    pad = jnp.zeros(folded.shape[:2] + (2, 128), F32)
    halves = [
        jnp.concatenate([folded[:, :, 14 * i : 14 * i + 14], pad], 2).reshape(-1, 128)
        for i in range(2)
    ]
    return jnp.concatenate(halves, 1)


def send_kernel(res_ref, gain_ref, weight_ref, send_ref, xhat_ref, rstd_ref, stage):
    clear_pads(stage)
    for i in range(8):
        put_pair_row(stage, i, res_ref[:, 1 + i])
    merged, xhat, rstd = merge_pairs(stage, gain_ref, weight_ref[...])
    xhat_ref[...] = xhat
    rstd_ref[...] = jnp.broadcast_to(rstd, rstd_ref.shape)
    send_ref[:, 0:1] = res_ref[:, 0:1]
    send_ref[:, 1:5] = fold_merged(merged, 4).astype(BF)


def local_kernel(resA_ref, resB_ref, gain_ref, weight_ref, merged_ref, xhat_ref, rstd_ref, stage):
    clear_pads(stage)
    for i in range(5):
        put_pair_row(stage, i, resA_ref[:, i])
    for i in range(13):
        put_pair_row(stage, 5 + i, resB_ref[:, i])
    merged, xhat, rstd = merge_pairs(stage, gain_ref, weight_ref[...])
    xhat_ref[...] = xhat
    rstd_ref[...] = jnp.broadcast_to(rstd, rstd_ref.shape)
    merged_ref[...] = merged


def local_back_kernel(
    grad_ref, d30_ref, xhat_ref, rstd_ref, gain_ref, weight_ref, dA_ref, dB_ref, stage
):
    merge_pairs_back(
        grad_ref[...], xhat_ref[...], rstd_ref[:, 0:1], gain_ref, weight_ref[...], stage
    )
    for i in range(5):
        dA_ref[:, i] = pair_row(stage, i)
    for i in range(13):
        dB_ref[:, i] = pair_row(stage, 5 + i)
    dB_ref[:, 13] = d30_ref[...]


def receive_kernel(got_ref, xhat_ref, rstd_ref, gain_ref, weight_ref, d3_ref, d10_ref, stage):
    grad = unfold_merged(got_ref[:, 1:5].astype(F32))
    merge_pairs_back(grad, xhat_ref[...], rstd_ref[:, 0:1], gain_ref, weight_ref[...], stage)
    d3_ref[:, 0:1] = got_ref[:, 0:1]
    for i in range(6):
        d3_ref[:, 1 + i] = pair_row(stage, i)
    for i in range(2):
        d10_ref[:, i] = pair_row(stage, 6 + i)


def merge_call(kernel, us, shapes, pairs, *operands):
    return pl.pallas_call(
        kernel,
        out_shape=[jax.ShapeDtypeStruct(shape, kind) for shape, kind in shapes],
        scratch_shapes=[pltpu.VMEM((WT, pairs, 2, 32, 128), F32)],
        compiler_params=params(),
        cost_estimate=cost(us),
    )(*operands)


def middle_kernel(
    merged_ref, resB_ref, next_ref, cot_ref, cta_ref, cha_ref, cdg_ref,
    mg1_ref, mg2_ref, g3_ref, row_ref, col_ref, mw1_hbm, mw2_hbm, p3_hbm, bias_hbm, ow3_hbm,
    dm_ref, d30_ref, dN_ref, so_ref, sta_ref, sha_ref,
    stage, stage2, xhat2, rstd2, cotw, k_s, v_s, qT_s, kT_s, vT_s, probs_s, oT_s, inv_s, doT_s, dqkv_s,
    mw1_ref, mw2_ref, p3_ref, bias_ref, ow3_ref, sems,
):
    fetches = [
        pltpu.make_async_copy(there, here, sems.at[i])
        for i, (there, here) in enumerate(
            (
                (mw1_hbm, mw1_ref),
                (mw2_hbm, mw2_ref),
                (p3_hbm, p3_ref),
                (bias_hbm, bias_ref),
                (ow3_hbm, ow3_ref),
            )
        )
    ]
    for fetch in fetches:
        fetch.start()
    cotw[...] = jnp.zeros((4, 7, 8, 512), F32)
    cotw[0:2, 0:4, 0:7, :] = cot_ref[2:4, 3:7].astype(F32)
    cotw[2:4, 0:4, 0:7, :] = unfold(cta_ref[:, 11:15].astype(F32))
    cotw[0:2, 4:7, 0:7, :] = unfold(cha_ref[:, 3:6].astype(F32))
    cotw[2:4, 4:7, 0:7, :] = unfold(cdg_ref[:, 3:6].astype(F32))

    def put_merged(first, count, values):
        for half in range(2):
            block = values[:, 128 * half : 128 * half + 128].reshape(WT, count, 16, 128)
            for i in range(count):
                stage2[half, :, (first + i) // 2, (first + i) % 2] = block[:, i]

    def take_merged(first, count):
        halves = [
            jnp.concatenate(
                [
                    stage2[half, :, (first + i) // 2, (first + i) % 2].reshape(WT, 1, 16, 128)
                    for i in range(count)
                ],
                1,
            ).reshape(WT * count * 16, 128)
            for half in range(2)
        ]
        return jnp.concatenate(halves, 1)

    put_merged(0, 9, merged_ref[...])
    put_merged(10, 4, unfold_merged(next_ref[:, 1:5].astype(F32)))
    clear_pads(stage)
    put_pair_row(stage, 0, resB_ref[:, 13])
    put_pair_row(stage, 1, next_ref[:, 0])
    fetches[0].wait()
    merged, xhat_seam, rstd_seam = merge_pairs(stage, mg1_ref, mw1_ref[...])
    put_merged(9, 1, merged)
    fetches[1].wait()
    pieces = [
        stage2[half, :, :, q % 2, pl.ds(q // 2, 8, stride=2), :].reshape(ROWS, 128)
        for q in range(4)
        for half in range(2)
    ]
    xhat, rstd = normalise(jnp.concatenate(pieces, 1))
    xhat2[...] = xhat
    rstd2[...] = jnp.broadcast_to(rstd, (ROWS, 128))
    merged_two = dot((xhat * mg2_ref[...]).astype(BF), mw2_ref[...]).astype(BF).astype(F32)
    xhat3, rstd3 = normalise(merged_two)
    n3 = (xhat3 * g3_ref[...]).astype(BF)
    fetches[2].wait()
    packed = [dot(n3, p3_ref[:, 512 * i : 512 * i + 512]) for i in range(3)]
    for g in range(4):
        q, k, v = (part[:, 128 * g : 128 * g + 128] for part in packed)
        q = lengthen((q * (SCALE * LOG2E)).astype(BF))
        k, v = k.astype(BF), v.astype(BF)
        k_s[g] = k
        v_s[g] = v
        qT_s[g] = q.T
        kT_s[g] = lengthen(k).T
        vT_s[g] = lengthen(v).T
    mask = region_mask(col_ref[...], row_ref[...])
    fetches[3].wait()

    def heads(i, _):
        operands = []
        for g in (2 * i, 2 * i + 1):

            def keep(h, probs, g=g):
                probs_s[g * 4 + h] = probs

            operands.append(
                (k_s[g], qT_s[g], vT_s[g], mask, lambda h, g=g: bias_ref[g * 4 + h], keep)
            )
        for u, (oT, inverse) in enumerate(attend_four(operands)):
            oT_s[2 * i + u] = oT
            inv_s[2 * i + u] = inverse
        return 0

    lax.fori_loop(0, 2, heads, 0)
    fetches[4].wait()
    att = jnp.concatenate([oT_s[g].astype(BF).T[:ROWS] for g in range(4)], 1)
    mixed = dot(att, ow3_ref[...]).astype(BF).astype(F32)
    section = (merged_two + mixed).reshape(4, 7, 8, 512)
    section = fold(section[:, :, 0:7])
    so_ref[...] = section[0:2, 0:4].astype(BF)
    sta_ref[...] = section[2:4].astype(BF)
    sha_ref[...] = section[0:2, 4:7].astype(BF)

    cot = cotw[...].reshape(ROWS, 512)
    cot_long = lengthen(cot.astype(BF))
    doT = dot_nt(ow3_ref[...], cot_long)
    for g in range(4):
        doT_s[g] = doT[128 * g : 128 * g + 128]

    def heads_back(i, _):
        operands = [
            (
                v_s[g], qT_s[g], kT_s[g], oT_s[g], doT_s[g], inv_s[g],
                lambda h, g=g: probs_s[g * 4 + h],
            )
            for g in (2 * i, 2 * i + 1)
        ]
        for u, (dq, dk, dv) in enumerate(attend_four_back(operands)):
            dqkv_s[2 * i + u] = dq
            dqkv_s[4 + 2 * i + u] = dk
            dqkv_s[8 + 2 * i + u] = dv
        return 0

    lax.fori_loop(0, 2, heads_back, 0)
    dpacked = jnp.concatenate([dqkv_s[i] for i in range(12)], 1)
    dn3 = dot_nt(dpacked, p3_ref[...])
    dm2 = cot + normalise_back(dn3 * g3_ref[...], xhat3, rstd3)
    dn2 = dot_nt(dm2.astype(BF), mw2_ref[...])
    dg2 = normalise_back(dn2 * mg2_ref[...], xhat2[...], rstd2[:, 0:1])
    for q in range(4):
        for half in range(2):
            at = 256 * q + 128 * half
            stage2[half, :, :, q % 2, pl.ds(q // 2, 8, stride=2), :] = dg2[:, at : at + 128].reshape(
                4, 7, 8, 128
            )

    dm_ref[...] = take_merged(0, 9)
    merge_pairs_back(take_merged(9, 1), xhat_seam, rstd_seam, mg1_ref, mw1_ref[...], stage)
    d30_ref[...] = pair_row(stage, 0)
    dN_ref[:, 0] = pair_row(stage, 1)
    dN_ref[:, 1:5] = fold_merged(take_merged(10, 4), 4).astype(BF)


def middle(*operands):
    shapes = [
        (4, 28, 128), (4, 5, 28, 128), (2, 4, 28, 128), (2, 7, 28, 128), (2, 3, 28, 128),
    ]
    return pl.pallas_call(
        middle_kernel,
        in_specs=[pl.BlockSpec(memory_space=pltpu.VMEM)] * 12
        + [pl.BlockSpec(memory_space=pl.ANY)] * 5,
        out_shape=[jax.ShapeDtypeStruct((576, 256), F32)]
        + [jax.ShapeDtypeStruct(s, BF) for s in shapes],
        scratch_shapes=[
            pltpu.VMEM((4, 1, 2, 32, 128), F32),
            pltpu.VMEM((2, 4, 7, 2, 16, 128), F32),
            pltpu.VMEM((ROWS, 1024), F32),
            pltpu.VMEM((ROWS, 128), F32),
            pltpu.VMEM((4, 7, 8, 512), F32),
            pltpu.VMEM((4, ROWS, 128), BF),
            pltpu.VMEM((4, ROWS, 128), BF),
            pltpu.VMEM((4, 128, LANES), BF),
            pltpu.VMEM((4, 128, LANES), BF),
            pltpu.VMEM((4, 128, LANES), BF),
            pltpu.VMEM((16, ROWS, LANES), BF),
            pltpu.VMEM((4, 128, LANES), F32),
            pltpu.VMEM((4, 8, LANES), F32),
            pltpu.VMEM((4, 128, LANES), F32),
            pltpu.VMEM((12, ROWS, 128), BF),
            pltpu.VMEM((512, 256), BF),
            pltpu.VMEM((1024, 512), BF),
            pltpu.VMEM((512, 1536), BF),
            pltpu.VMEM((HEADS3, ROWS, LANES), F32),
            pltpu.VMEM((512, 512), BF),
            pltpu.SemaphoreType.DMA((5,)),
        ],
        compiler_params=params(28),
        cost_estimate=cost(9),
    )(*operands)


def join_kernel(
    mid_ref, ta_ref, own_mid_ref, own_ref, so_ref, grad_ref, section_ref, wide, narrow
):
    for t in range(WT):
        turn = pl.ds(t, 28, stride=4)
        wide[0:7, turn, :] = (mid_ref if t < 2 else own_mid_ref)[t % 2].astype(F32)
        wide[7:18, turn, :] = (ta_ref if t < 2 else own_ref)[t % 2, 0:11].astype(F32)
        low = (ta_ref[t, 11:15] if t < 2 else so_ref[t - 2]).astype(F32)
        for g in range(4):
            narrow[g, :, pl.ds(t, 7, stride=4), :] = low[:, 7 * g : 7 * g + 7]
    for i in range(18):
        grad_ref[10 + i] = wide[i].reshape(28, 4, 128).astype(BF)
    for i in range(4):
        row = jnp.concatenate([narrow[g, i] for g in range(4)], 1)
        section_ref[3 + i] = row.reshape(7, 4, 512).astype(BF)


JOINED = [
    jax.ShapeDtypeStruct((28, 28, 4, 128), BF),
    jax.ShapeDtypeStruct((7, 7, 4, 512), BF),
]


def join(mid, ta, own_mid, own, section_own):
    return pl.pallas_call(
        join_kernel,
        out_shape=JOINED,
        scratch_shapes=[pltpu.VMEM((18, 112, 128), F32), pltpu.VMEM((4, 4, 28, 128), F32)],
        compiler_params=params(),
        cost_estimate=cost(2),
    )(mid, ta, own_mid, own, section_own)


def last_kernel(
    grad_hbm, section_hbm, ta_ref, own_ref, dg_ref, ha_ref, grad_out, section_out,
    wide, narrow, rows, section_rows, sems,
):
    del grad_hbm, section_hbm
    for t in range(WT):
        corner = dg_ref if t < 2 else ha_ref
        wide[0:3, pl.ds(t, 28, stride=4), :] = corner[t % 2, 0:3].astype(F32)
        wide[3:10, pl.ds(t, 28, stride=4), :] = (ta_ref if t < 2 else own_ref)[t % 2].astype(F32)
        high = corner[t % 2, 3:6].astype(F32)
        for g in range(4):
            narrow[g, :, pl.ds(t, 7, stride=4), :] = high[:, 7 * g : 7 * g + 7]
    for i in range(10):
        rows[i] = wide[i].reshape(28, 4, 128).astype(BF)
    copy = pltpu.make_async_copy(rows, grad_out.at[0:10], sems.at[0])
    copy.start()
    for i in range(3):
        row = jnp.concatenate([narrow[g, i] for g in range(4)], 1)
        section_rows[i] = row.reshape(7, 4, 512).astype(BF)
    other = pltpu.make_async_copy(section_rows, section_out.at[0:3], sems.at[1])
    other.start()
    copy.wait()
    other.wait()


def join_last(grad, section, ta, own, dg, ha):
    return pl.pallas_call(
        last_kernel,
        in_specs=[pl.BlockSpec(memory_space=pl.ANY)] * 2
        + [pl.BlockSpec(memory_space=pltpu.VMEM)] * 4,
        out_specs=[pl.BlockSpec(memory_space=pl.ANY)] * 2,
        out_shape=JOINED,
        scratch_shapes=[
            pltpu.VMEM((10, 112, 128), F32),
            pltpu.VMEM((4, 3, 28, 128), F32),
            pltpu.VMEM((10, 28, 4, 128), BF),
            pltpu.VMEM((3, 7, 4, 512), BF),
            pltpu.SemaphoreType.DMA((2,)),
        ],
        input_output_aliases={0: 0, 1: 1},
        compiler_params=params(),
        cost_estimate=cost(1),
    )(grad, section, ta, own, dg, ha)


IN_ORDER = Layout(major_to_minor=(0, 1, 2, 3))


def inward(values):
    return with_layout_constraint(jnp.transpose(values, (1, 2, 0, 3)), IN_ORDER)


def outward(values):
    return jnp.transpose(with_layout_constraint(values, IN_ORDER), (2, 0, 1, 3))


def send(values, axes, by):
    axes = axes.split()
    sizes = [lax.axis_size(a) for a in axes]
    if len(axes) == 1:
        pairs = [(i, (i + by) % sizes[0]) for i in range(sizes[0])]
    else:
        n, m = sizes
        pairs = [
            (i * m + j, (i + by) % n * m + (j + by) % m) for i in range(n) for j in range(m)
        ]
    return lax.ppermute(values, tuple(axes), pairs)


def per_device(
    tokens,
    regions_one,
    regions_three,
    gain_one,
    projection_one,
    outward_one,
    table_one,
    merge_gain_one,
    merge_weight_one,
    merge_gain_two,
    merge_weight_two,
    gain_three,
    projection_three,
    outward_three,
    table_three,
    cotangent,
):
    (early,) = arrange(early_kernel, (14,), tokens)
    ta_early = send(inward(early), "ta", -1)
    late, ha_late, dg_late = arrange(late_kernel, (15, 6, 6), tokens, cotangent)
    ha_late = send(ha_late, "ha", -1)
    dg_late = send(dg_late, "ha ta", -1)
    ta_late = send(inward(late), "ta", -1)
    bias_one, bias_three, row_one, row_three, col_one, col_three = prepare(
        table_one, table_three, regions_one, regions_three
    )
    ha_late, ta_early = lax.optimization_barrier((ha_late, ta_early))
    gain, merge_gain, seam = gain_one[None], merge_gain_one[None], merge_weight_one
    args = (gain, projection_one, outward_one, bias_one)
    (res_send, res_a), saved_a = front(False, (tokens, outward(ta_early)), *args, row_one, col_one)
    row_send, *early_norm = merge_call(
        send_kernel, 0.5, [((4, 5, 28, 128), BF), ((256, 512), F32), ((256, 128), F32)], 4,
        res_send, merge_gain, seam,
    )
    row_next = send(row_send, "ha", -1)
    ta_late, res_a = lax.optimization_barrier((ta_late, res_a))
    ta_late = outward(ta_late)
    (res_b,), saved_b = front(True, (tokens, ta_late, ha_late, dg_late), *args, row_one, col_one)
    merged, *local_norm = merge_call(
        local_kernel, 0.1, [((576, 256), F32), ((576, 512), F32), ((576, 128), F32)], 9,
        res_a, res_b, merge_gain, seam,
    )
    row_next, merged = lax.optimization_barrier((row_next, merged))
    d_merged, d_30, d_send, sec_own, sec_ta, sec_ha = middle(
        merged, res_b, row_next, cotangent, ta_late, ha_late, dg_late,
        merge_gain, merge_gain_two[None], gain_three[None], row_three, col_three,
        merge_weight_one, merge_weight_two, projection_three, bias_three, outward_three,
    )
    d_prev = send(d_send, "ha", 1)
    d_a, d_b = merge_call(
        local_back_kernel, 1, [((4, 5, 28, 128), BF), ((4, 14, 28, 128), BF)], 9,
        d_merged, d_30, *local_norm, merge_gain, seam,
    )
    own_b, ta_b, ha_b = back(
        2, (d_b, sec_ta, sec_ha), gain, projection_one, outward_one, saved_b
    )
    d_prev, own_b = lax.optimization_barrier((d_prev, own_b))
    ta_b = send(inward(ta_b), "ta", 1)
    ha_b = send(ha_b, "ha", 1)
    d_3, d_10 = merge_call(
        receive_kernel, 0.5, [((4, 7, 28, 128), BF), ((4, 2, 28, 128), BF)], 4,
        d_prev, *early_norm, merge_gain, seam,
    )
    own_mid, ta_mid = back(1, (d_10, d_a), gain, projection_one, outward_one, saved_a)
    ta_mid = send(inward(ta_mid), "ta", 1)
    d_3, own_mid = lax.optimization_barrier((d_3, own_mid))
    own_a, ta_a = back(0, (d_3,), gain, projection_one, outward_one, saved_a)
    ta_b, ta_mid, ha_b, own_a = lax.optimization_barrier((ta_b, ta_mid, ha_b, own_a))
    ta_a = send(inward(ta_a), "ta", 1)
    dg_b = send(ha_b[2:], "ta", 1)
    grad, section = join(outward(ta_mid), outward(ta_b), own_mid, own_b, sec_own)
    ta_a, dg_b, grad = lax.optimization_barrier((ta_a, dg_b, grad))
    grad, section = join_last(grad, section, outward(ta_a), own_a, dg_b, ha_b)
    return (jnp.transpose(section, (2, 0, 1, 3)), jnp.transpose(grad, (2, 0, 1, 3)))


def solution(mesh):
    tile = P(("col", "ta"), "ha", None, None)
    ids = P(("col", "ta"), "ha", None)
    in_specs = (tile, ids, ids) + (P(),) * 12 + (tile,)
    return jax.shard_map(
        per_device, mesh=mesh, in_specs=in_specs, out_specs=(tile, tile), check_vma=False
    )
```

```python
import functools

import jax
import jax.numpy as jnp
import numpy as np
from jax import lax
from jax.experimental import pallas as pl
from jax.experimental.layout import Layout, with_layout_constraint
from jax.experimental.pallas import tpu as pltpu
from jax.sharding import PartitionSpec as P

HEADS1 = 4
HEADS3 = 16
WT = 4
WS = 7
ST = 2
SS = 3
EPSILON = 1e-05
NREL = 1183
LOG2E = 1.4426950408889634
HEAD = 32
SCALE = HEAD**-0.5
ROWS = WT * WS * 8
LANES = 256
SPAN = 1280
GONE = -1e30
PER_STEP = 4
STEPS = 8 // PER_STEP
BF = jnp.bfloat16
F32 = jnp.float32


def dot(a, b):
    return jnp.dot(a, b, preferred_element_type=F32)


def dot_nt(a, b):
    return lax.dot_general(a, b, (((1,), (1,)), ((), ())), preferred_element_type=F32)


def params(limit=20):
    return pltpu.CompilerParams(vmem_limit_bytes=limit * 1024 * 1024)


def cost(us):
    return pl.CostEstimate(flops=int(us * 1.1e9), bytes_accessed=int(us * 1e6), transcendentals=0)


def normalise(x):
    centred = x - jnp.mean(x, -1, keepdims=True)
    rstd = lax.rsqrt(jnp.mean(centred * centred, -1, keepdims=True) + EPSILON)
    return centred * rstd, rstd


def normalise_back(grad, xhat, rstd):
    return rstd * (
        grad
        - jnp.mean(grad, -1, keepdims=True)
        - xhat * jnp.mean(grad * xhat, -1, keepdims=True)
    )


def head_rows(x, h):
    return x[HEAD * h : HEAD * (h + 1)]


def head_of_lane(shape):
    return lax.broadcasted_iota(jnp.int32, shape, 1) // HEAD


def by_head(x):
    lane = head_of_lane((1, 128))
    return jnp.concatenate([x * (lane == h).astype(F32).astype(BF) for h in range(4)], 0)


def pick_heads(stacked):
    lane = head_of_lane((ROWS, 128))
    got = stacked[:ROWS]
    for h in range(1, 4):
        got = jnp.where(lane == h, stacked[ROWS * h : ROWS * (h + 1)], got)
    return got


def lengthen(x):
    return jnp.concatenate([x, jnp.zeros((LANES - ROWS, x.shape[1]), x.dtype)], 0)


def region_mask(column, row):
    return jnp.where(jnp.concatenate([column, column], 1) == row, 0.0, GONE).astype(F32)


def attend_four(windows):
    scores = [dot(by_head(k), qT) for k, qT, _, _, _, _ in windows]
    results = []
    for s, (_, _, vT, mask, bias_at, keep_probs) in zip(scores, windows):
        outs, inverses = [], []
        for h in range(4):
            biased = s[ROWS * h : ROWS * (h + 1)] + (bias_at(h) + mask)
            peak = jnp.max(biased, 0, keepdims=True)
            probs = jnp.exp2(biased - peak).astype(BF)
            keep_probs(h, probs)
            extended = jnp.concatenate([head_rows(vT, h)[:, :ROWS], jnp.ones((16, ROWS), BF)], 0)
            out = dot(extended, probs)
            inverse = 1.0 / out[HEAD : HEAD + 1]
            outs.append(out[:HEAD] * inverse)
            inverses.append(inverse)
        results.append((jnp.concatenate(outs, 0), jnp.concatenate(inverses + inverses, 0)))
    return results


def attend_four_back(windows):
    first = []
    for v, qT, kT, oT, doT, inverse, probs_at in windows:
        scaled, deltas = [], []
        for h in range(4):
            part = head_rows(doT, h) * inverse[h : h + 1]
            deltas.append(jnp.sum(part * head_rows(oT, h), 0, keepdims=True))
            scaled.append(part)
        scaled = jnp.concatenate(scaled, 0).astype(BF)
        first.append((scaled, deltas, dot(by_head(v), scaled)))
    results = []
    for (scaled, deltas, dprobs), (v, qT, kT, oT, doT, inverse, probs_at) in zip(first, windows):
        probs = [probs_at(h) for h in range(4)]
        dscores = [
            (probs[h].astype(F32) * (dprobs[ROWS * h : ROWS * (h + 1)] - deltas[h])).astype(BF)
            for h in range(4)
        ]
        dv = pick_heads(dot_nt(jnp.concatenate(probs, 0), scaled))
        dk = pick_heads(dot_nt(jnp.concatenate(dscores, 0), qT))
        dqT = jnp.concatenate(
            [dot(head_rows(kT, h)[:, :ROWS], dscores[h]) for h in range(4)], 0
        )
        dq = (dqT * SCALE).astype(BF).T[:ROWS]
        results.append((dq, (dk * (1.0 / LOG2E)).astype(BF), dv.astype(BF)))
    return results


def lanes_of(shape):
    return lax.broadcasted_iota(jnp.int32, shape, 1)


def region_rows(ids, section):
    columns = ids.shape[1]
    count = columns // WS
    place = lax.broadcasted_iota(jnp.int32, (columns, LANES * count), 0)
    lane = lanes_of((columns, LANES * count))
    column = lane % 8
    real = (column < WS) & (lane % LANES < ROWS)
    if section == 3:
        column = jnp.where(column < 3, column + 4, column - 3)
    chosen = real & (place == lane // LANES * WS + column)
    spread = dot(ids.astype(F32).astype(BF), chosen.astype(F32).astype(BF))
    row = lax.broadcasted_iota(jnp.int32, spread.shape, 0)
    lane = lanes_of(spread.shape)
    real = (lane[:1] % 8 < WS) & (lane[:1] % LANES < ROWS)
    rows = []
    for hw in range(ids.shape[0] // (WT * WS)):
        mine = lane % LANES // 8 == row % 4 * WS + row // 4 - WS * hw
        inside = (row >= WT * WS * hw) & (row < WT * WS * (hw + 1))
        found = jnp.sum(jnp.where(mine & inside, spread, 0.0), 0, keepdims=True)
        found = jnp.where(real, found, -1.0)
        rows += [found[:, LANES * ww : LANES * (ww + 1)] for ww in range(count)]
    return rows


def region_columns(ids, section):
    columns = ids.shape[1]
    count = columns // WS
    source = ids.astype(F32).astype(BF)
    token = lax.broadcasted_iota(jnp.int32, (ROWS, ids.shape[0]), 0)
    place = lanes_of((ROWS, ids.shape[0]))
    column = lax.broadcasted_iota(jnp.int32, (ROWS, columns), 0) % 8
    lane = lanes_of((ROWS, columns))
    if section == 3:
        column = jnp.where(column < 3, column + 4, jnp.where(column == 7, 8, column - 3))
    ones = jnp.ones((columns, 128), BF)
    pad = lax.broadcasted_iota(jnp.int32, (ROWS, 128), 0) % 8 == 7
    found = []
    for hw in range(ids.shape[0] // (WT * WS)):
        chosen = place == (token // 8 % WS + WS * hw) * WT + token // 56
        picked = dot(chosen.astype(F32).astype(BF), source)
        for ww in range(count):
            mine = jnp.where(lane == WS * ww + column, picked, 0.0).astype(BF)
            found.append(jnp.where(pad, -1.0, dot(mine, ones)))
    return found


def prepare_kernel(
    t1_ref, t3_ref, s_ref, r1_ref, r3_ref, o1_ref, o3_ref, row1_ref, row3_ref, col1_ref, col3_ref,
    tab, spread
):
    tab[...] = jnp.zeros((24, SPAN), F32)
    tab[0:4, 0:NREL] = t1_ref[...] * LOG2E
    tab[8:24, 0:NREL] = t3_ref[...] * LOG2E
    slabs = []
    for dt in range(7):
        start = 169 * dt
        low = start // 128 * 128
        run = tab[:, low : low + 384]
        if start > low:
            run = pltpu.roll(run, 384 - (start - low), 1)
        slabs.append(run[:, :256])
    left = jnp.concatenate(slabs, 0)
    first = left.astype(BF)
    rest = left - first.astype(F32)
    second = rest.astype(BF)
    third = (rest - second.astype(F32)).astype(BF)
    chosen = s_ref[...]
    got = dot(first, chosen) + dot(second, chosen) + dot(third, chosen)
    lane16 = lanes_of((16, 128))
    for dt in range(7):
        for wj in range(8):
            part = got[24 * dt : 24 * dt + 24, 128 * wj : 128 * wj + 128]
            spread[dt, pl.ds(wj, 8, stride=8), :] = part[0:8]
            later = part[8:24]
            turned = jnp.where(lane16 % 8 < 3, pltpu.roll(later, 124, 1), pltpu.roll(later, 3, 1))
            spread[dt, pl.ds(64 + (7 if wj == 7 else (wj + 3) % 7), 16, stride=8), :] = turned
    for o_ref, heads, at in ((o1_ref, HEADS1, 0), (o3_ref, HEADS3, 64)):
        lane = lanes_of((heads * 8, 128))
        for tj in range(WT):
            for hj in range(WS):
                p0, p1, p2, p3 = (
                    pltpu.roll(
                        spread[ti - tj + 3, at : at + heads * 8, :], (ti * 56 - (6 - hj) * 8) % 128, 1
                    )
                    for ti in range(WT)
                )
                left = jnp.where(lane < 56, p0, jnp.where(lane < 112, p1, p2))
                right = jnp.where(lane < 40, p2, p3)
                row = (tj * WS + hj) * 8
                o_ref[:, row : row + 8, 0:128] = left.reshape(heads, 8, 128)
                o_ref[:, row : row + 8, 128:256] = right.reshape(heads, 8, 128)
    for i, found in enumerate(region_rows(r1_ref[...], 1)):
        row1_ref[i] = found
    row3_ref[...] = region_rows(r3_ref[...], 3)[0]
    for i, found in enumerate(region_columns(r1_ref[...], 1)):
        col1_ref[i] = found
    col3_ref[...] = region_columns(r3_ref[...], 3)[0]


def chooser():
    chosen = np.zeros((256, 1024), np.float32)
    for wj in range(WS):
        for dh in range(13):
            for wi in range(WS):
                chosen[dh * 13 + wi - wj + 6, wj * 128 + dh * 8 + wi] = 1.0
    return jnp.asarray(chosen, BF)


def by_height(ids):
    return jnp.transpose(ids, (1, 0, 2)).reshape(-1, ids.shape[2])


def prepare(table_one, table_three, regions_one, regions_three):
    return pl.pallas_call(
        prepare_kernel,
        out_shape=(
            jax.ShapeDtypeStruct((HEADS1, ROWS, LANES), F32),
            jax.ShapeDtypeStruct((HEADS3, ROWS, LANES), F32),
            jax.ShapeDtypeStruct((16, 1, LANES), F32),
            jax.ShapeDtypeStruct((1, LANES), F32),
            jax.ShapeDtypeStruct((16, ROWS, 128), F32),
            jax.ShapeDtypeStruct((ROWS, 128), F32),
        ),
        scratch_shapes=[pltpu.VMEM((24, SPAN), F32), pltpu.VMEM((7, 24 * 8, 128), F32)],
        compiler_params=params(),
        cost_estimate=cost(3),
    )(
        jnp.transpose(table_one),
        jnp.transpose(table_three),
        chooser(),
        by_height(regions_one),
        by_height(regions_three),
    )


def fold(values):
    return jnp.concatenate([values[..., 128 * g : 128 * g + 128] for g in range(4)], -2)


def unfold(values):
    return jnp.concatenate([values[..., 7 * g : 7 * g + 7, :] for g in range(4)], -1)


def early_kernel(tok_ref, early_ref):
    early_ref[...] = tok_ref[0:2, 3:17]


def late_kernel(tok_ref, cot_ref, late_ref, ha_ref):
    late_ref[:, 0:11] = tok_ref[0:2, 17:28]
    late_ref[:, 11:15] = fold(cot_ref[0:2, 3:7].astype(F32)).astype(BF)
    ha_ref[:, 0:3] = tok_ref[:, 0:3]
    ha_ref[:, 3:6] = fold(cot_ref[:, 0:3].astype(F32)).astype(BF)


def arrange(kernel, sizes, *operands):
    return pl.pallas_call(
        kernel,
        out_shape=[jax.ShapeDtypeStruct(size + (28, 128), BF) for size in sizes],
        compiler_params=params(8),
        cost_estimate=cost(0.3),
    )(*operands)


def put_rows(stage, frames, rows, values):
    values = values.astype(F32)
    stage[frames, rows, 0:28, :] = values
    stage[frames, rows, 28:36, :] = values[:, :, 0:8, :]


def cut_windows(stage, win):
    for hw in range(stage.shape[1] // 7):
        for ww in range(4):
            win[hw * 4 + ww] = stage[:, 7 * hw : 7 * hw + 7, 3 + 7 * ww : 11 + 7 * ww, :].reshape(
                ROWS, 128
            )


def join_windows(win, stage):
    for hw in range(stage.shape[1] // 7):
        for ww in range(4):
            stage[:, 7 * hw : 7 * hw + 7, 3 + 7 * ww : 11 + 7 * ww, :] = win[hw * 4 + ww].reshape(
                WT, WS, 8, 128
            )
    stage[:, :, 0:3, :] = stage[:, :, 28:31, :]


def front_kernel(late, *refs):
    n_in = 4 if late else 2
    pieces, refs = refs[:n_in], refs[n_in:]
    gain_ref, proj_ref, outw_ref, bias_ref, row_ref, col_ref = refs[:6]
    refs = refs[6:]
    n_out = 1 if late else 2
    outs, refs = refs[:n_out], refs[n_out:]
    xw_ref, kv_ref, t_ref, p_ref, o_ref, inv_ref, stage, win = refs
    step = pl.program_id(0)

    @pl.when(step == 0)
    def _():
        own = pieces[0]
        if late:
            put_rows(stage, slice(0, 2), slice(0, 11), own[2:4, 17:28])
            put_rows(stage, slice(2, 4), slice(0, 11), pieces[1][:, 0:11])
            put_rows(stage, slice(0, 2), slice(11, 14), pieces[2][2:4, 0:3])
            put_rows(stage, slice(2, 4), slice(11, 14), pieces[3][:, 0:3])
        else:
            put_rows(stage, slice(0, 2), slice(0, 14), own[2:4, 3:17])
            put_rows(stage, slice(2, 4), slice(0, 14), pieces[1][...])
        cut_windows(stage, win)

    xs, operands = [], []
    for u in range(PER_STEP):
        x = win[step * PER_STEP + u]
        xs.append(x)
        xw_ref[u] = x.astype(BF)
        xhat, _ = normalise(x)
        packed = dot((xhat * gain_ref[...]).astype(BF), proj_ref[...])
        q = (packed[:, :128] * (SCALE * LOG2E)).astype(BF)
        kv = packed[:, 128:].astype(BF)
        kv_ref[u] = kv
        qT, kT, vT = (lengthen(part).T for part in (q, kv[:, :128], kv[:, 128:]))
        t_ref[u, :128] = qT
        t_ref[u, 128:] = kT

        def keep(h, probs, u=u):
            p_ref[u, h] = probs

        operands.append(
            (kv[:, :128], qT, vT, region_mask(col_ref[u], row_ref[u]), lambda h: bias_ref[h], keep)
        )
    for u, (oT, inverse) in enumerate(attend_four(operands)):
        oT = oT.astype(BF)
        o_ref[u] = oT
        inv_ref[u] = inverse
        mixed = dot(oT.T[:ROWS], outw_ref[...]).astype(BF).astype(F32)
        win[step * PER_STEP + u] = xs[u] + mixed

    @pl.when(step == STEPS - 1)
    def _():
        join_windows(win, stage)
        if late:
            outs[0][...] = stage[:, :, 0:28, :].astype(BF)
        else:
            outs[0][...] = stage[:, 0:9, 0:28, :].astype(BF)
            outs[1][...] = stage[:, 9:14, 0:28, :].astype(BF)


def whole(shape):
    return pl.BlockSpec(shape, lambda i: (0,) * len(shape))


def each(shape, first=0):
    return pl.BlockSpec((PER_STEP,) + shape, lambda i: (i + first,) + (0,) * len(shape))


SAVED = (
    ((ROWS, 128), BF),
    ((ROWS, 256), BF),
    ((256, LANES), BF),
    ((4, ROWS, LANES), BF),
    ((128, LANES), BF),
    ((8, LANES), F32),
)


def front(late, pieces, gain, proj, outw, bias, row, column):
    consts = (gain, proj, outw, bias)
    shapes = [(4, 14, 28, 128)] if late else [(4, 9, 28, 128), (4, 5, 28, 128)]
    out = pl.pallas_call(
        functools.partial(front_kernel, late),
        grid=(STEPS,),
        in_specs=[whole(a.shape) for a in tuple(pieces) + consts] + [each((1, LANES), STEPS * late), each((ROWS, 128), STEPS * late)],
        out_specs=[whole(s) for s in shapes] + [each(s) for s, _ in SAVED],
        out_shape=[jax.ShapeDtypeStruct(s, BF) for s in shapes]
        + [jax.ShapeDtypeStruct((8,) + s, d) for s, d in SAVED],
        scratch_shapes=[
            pltpu.VMEM((4, 14, 40, 128), F32),
            pltpu.VMEM((8, ROWS, 128), F32),
        ],
        compiler_params=params(),
        cost_estimate=cost(4.6),
    )(*pieces, *consts, row, column)
    return out[: len(shapes)], out[len(shapes) :]


def back_kernel(part, *refs):
    n_in = (1, 2, 3)[part]
    pieces, refs = refs[:n_in], refs[n_in:]
    gain_ref, proj_ref, outw_ref = refs[:3]
    xw_ref, kv_ref, t_ref, p_ref, o_ref, inv_ref = refs[3:9]
    refs = refs[9:]
    n_out = 3 if part == 2 else 2
    outs, refs = refs[:n_out], refs[n_out:]
    stage, win = refs
    step = pl.program_id(0)

    @pl.when(step == 0)
    def _():
        if part == 2:
            put_rows(stage, slice(0, 4), slice(0, 14), pieces[0][...])
            outs[1][:, 11:15] = pieces[1][:, 0:4]
            outs[2][0:2, 3:6] = pieces[2][...]
            outs[2][2:4, 3:6] = pieces[1][:, 4:7]
        elif part == 1:
            put_rows(stage, slice(0, 4), slice(0, 2), pieces[0][...])
            put_rows(stage, slice(0, 4), slice(2, 7), pieces[1][...])
        else:
            put_rows(stage, slice(0, 4), slice(0, 7), pieces[0][...])
        cut_windows(stage, win)

    drs, operands = [], []
    for u in range(PER_STEP):
        dr = win[step * PER_STEP + u]
        drs.append(dr)
        operands.append(
            (
                kv_ref[u, :, 128:],
                t_ref[u, :128],
                t_ref[u, 128:],
                o_ref[u].astype(F32),
                dot_nt(outw_ref[...], lengthen(dr.astype(BF))),
                inv_ref[u],
                lambda h, u=u: p_ref[u, h],
            )
        )
    for u, (dq, dk, dv) in enumerate(attend_four_back(operands)):
        dpacked = jnp.concatenate([dq, dk, dv], 1)
        dn = dot_nt(dpacked, proj_ref[...])
        xhat, rstd = normalise(xw_ref[u].astype(F32))
        dx = normalise_back(dn * gain_ref[...], xhat, rstd)
        win[step * PER_STEP + u] = drs[u] + dx

    @pl.when(step == pl.num_programs(0) - 1)
    def _():
        join_windows(win, stage)
        if part == 2:
            outs[0][...] = stage[0:2, 0:11, 0:28, :].astype(BF)
            outs[1][:, 0:11] = stage[2:4, 0:11, 0:28, :].astype(BF)
            outs[2][:, 0:3] = stage[:, 11:14, 0:28, :].astype(BF)
        else:
            outs[0][...] = stage[0:2, :, 0:28, :].astype(BF)
            outs[1][...] = stage[2:4, :, 0:28, :].astype(BF)


def back(part, pieces, gain, proj, outw, saved):
    consts = (gain, proj, outw)
    if part == 2:
        shapes = [(2, 11, 28, 128), (2, 15, 28, 128), (4, 6, 28, 128)]
    else:
        shapes = [(2, 7, 28, 128), (2, 7, 28, 128)]
    half = 2 if part == 2 else 1
    return pl.pallas_call(
        functools.partial(back_kernel, part),
        grid=(half * 4 // PER_STEP,),
        in_specs=[whole(a.shape) for a in tuple(pieces) + consts]
        + [each(s, 4 // PER_STEP * (part == 1)) for s, _ in SAVED],
        out_specs=[whole(s) for s in shapes],
        out_shape=[jax.ShapeDtypeStruct(s, BF) for s in shapes],
        scratch_shapes=[
            pltpu.VMEM((4, 7 * half, 40, 128), F32),
            pltpu.VMEM((4 * half, ROWS, 128), F32),
        ],
        compiler_params=params(),
        cost_estimate=cost(2.75 * half),
    )(*pieces, *consts, *saved)


def merge_pairs(stage, gain_ref, weight):
    pairs = stage.shape[1]
    pieces = [
        stage[:, :, q % 2, pl.ds(q // 2, 16, stride=2), :].reshape(WT * pairs * 16, 128)
        for q in range(4)
    ]
    xhat, rstd = normalise(jnp.concatenate(pieces, 1))
    merged = dot((xhat * gain_ref[...]).astype(BF), weight).astype(BF).astype(F32)
    return merged, xhat, rstd


def merge_pairs_back(grad, xhat, rstd, gain_ref, weight, stage):
    pairs = stage.shape[1]
    dn = dot_nt(grad.astype(BF), weight)
    dg = normalise_back(dn * gain_ref[...], xhat, rstd)
    for q in range(4):
        stage[:, :, q % 2, pl.ds(q // 2, 16, stride=2), :] = dg[
            :, 128 * q : 128 * q + 128
        ].reshape(WT, pairs, 16, 128)


def put_pair_row(stage, at, values):
    stage[:, at // 2, at % 2, 0:28, :] = values.astype(F32)


def clear_pads(stage):
    stage[:, :, :, 28:32, :] = jnp.zeros((WT, stage.shape[1], 2, 4, 128), F32)


def pair_row(stage, at):
    return stage[:, at // 2, at % 2, 0:28, :].astype(BF)


def fold_merged(merged, pairs):
    halves = [
        merged[:, 128 * i : 128 * i + 128].reshape(WT, pairs, 16, 128)[:, :, 0:14] for i in range(2)
    ]
    return jnp.concatenate(halves, 2)


def unfold_merged(folded):
    pad = jnp.zeros(folded.shape[:2] + (2, 128), F32)
    halves = [
        jnp.concatenate([folded[:, :, 14 * i : 14 * i + 14], pad], 2).reshape(-1, 128)
        for i in range(2)
    ]
    return jnp.concatenate(halves, 1)


def send_kernel(res_ref, gain_ref, weight_ref, send_ref, xhat_ref, rstd_ref, stage):
    clear_pads(stage)
    for i in range(8):
        put_pair_row(stage, i, res_ref[:, 1 + i])
    merged, xhat, rstd = merge_pairs(stage, gain_ref, weight_ref[...])
    xhat_ref[...] = xhat
    rstd_ref[...] = jnp.broadcast_to(rstd, rstd_ref.shape)
    send_ref[:, 0:1] = res_ref[:, 0:1]
    send_ref[:, 1:5] = fold_merged(merged, 4).astype(BF)


def local_kernel(resA_ref, resB_ref, gain_ref, weight_ref, merged_ref, xhat_ref, rstd_ref, stage):
    clear_pads(stage)
    for i in range(5):
        put_pair_row(stage, i, resA_ref[:, i])
    for i in range(13):
        put_pair_row(stage, 5 + i, resB_ref[:, i])
    merged, xhat, rstd = merge_pairs(stage, gain_ref, weight_ref[...])
    xhat_ref[...] = xhat
    rstd_ref[...] = jnp.broadcast_to(rstd, rstd_ref.shape)
    merged_ref[...] = merged


def local_back_kernel(
    grad_ref, d30_ref, xhat_ref, rstd_ref, gain_ref, weight_ref, dA_ref, dB_ref, stage
):
    merge_pairs_back(
        grad_ref[...], xhat_ref[...], rstd_ref[:, 0:1], gain_ref, weight_ref[...], stage
    )
    for i in range(5):
        dA_ref[:, i] = pair_row(stage, i)
    for i in range(13):
        dB_ref[:, i] = pair_row(stage, 5 + i)
    dB_ref[:, 13] = d30_ref[...]


def receive_kernel(got_ref, xhat_ref, rstd_ref, gain_ref, weight_ref, d3_ref, d10_ref, stage):
    grad = unfold_merged(got_ref[:, 1:5].astype(F32))
    merge_pairs_back(grad, xhat_ref[...], rstd_ref[:, 0:1], gain_ref, weight_ref[...], stage)
    d3_ref[:, 0:1] = got_ref[:, 0:1]
    for i in range(6):
        d3_ref[:, 1 + i] = pair_row(stage, i)
    for i in range(2):
        d10_ref[:, i] = pair_row(stage, 6 + i)


def merge_call(kernel, us, shapes, pairs, *operands):
    return pl.pallas_call(
        kernel,
        out_shape=[jax.ShapeDtypeStruct(shape, kind) for shape, kind in shapes],
        scratch_shapes=[pltpu.VMEM((WT, pairs, 2, 32, 128), F32)],
        compiler_params=params(),
        cost_estimate=cost(us),
    )(*operands)


def middle_kernel(
    merged_ref, resB_ref, next_ref, cot_ref, cta_ref, cha_ref, cdg_ref,
    mg1_ref, mg2_ref, g3_ref, row_ref, col_ref, mw1_hbm, mw2_hbm, p3_hbm, bias_hbm, ow3_hbm,
    dm_ref, d30_ref, dN_ref, so_ref, sta_ref, sha_ref,
    stage, stage2, xhat2, rstd2, cotw, k_s, v_s, qT_s, kT_s, vT_s, probs_s, oT_s, inv_s, doT_s, dqkv_s,
    mw1_ref, mw2_ref, p3_ref, bias_ref, ow3_ref, sems,
):
    fetches = [
        pltpu.make_async_copy(there, here, sems.at[i])
        for i, (there, here) in enumerate(
            (
                (mw1_hbm, mw1_ref),
                (mw2_hbm, mw2_ref),
                (p3_hbm, p3_ref),
                (bias_hbm, bias_ref),
                (ow3_hbm, ow3_ref),
            )
        )
    ]
    for fetch in fetches:
        fetch.start()
    cotw[...] = jnp.zeros((4, 7, 8, 512), F32)
    cotw[0:2, 0:4, 0:7, :] = cot_ref[2:4, 3:7].astype(F32)
    cotw[2:4, 0:4, 0:7, :] = unfold(cta_ref[:, 11:15].astype(F32))
    cotw[0:2, 4:7, 0:7, :] = unfold(cha_ref[2:4, 3:6].astype(F32))
    cotw[2:4, 4:7, 0:7, :] = unfold(cdg_ref[:, 3:6].astype(F32))

    def put_merged(first, count, values):
        for half in range(2):
            block = values[:, 128 * half : 128 * half + 128].reshape(WT, count, 16, 128)
            for i in range(count):
                stage2[half, :, (first + i) // 2, (first + i) % 2] = block[:, i]

    def take_merged(first, count):
        halves = [
            jnp.concatenate(
                [
                    stage2[half, :, (first + i) // 2, (first + i) % 2].reshape(WT, 1, 16, 128)
                    for i in range(count)
                ],
                1,
            ).reshape(WT * count * 16, 128)
            for half in range(2)
        ]
        return jnp.concatenate(halves, 1)

    put_merged(0, 9, merged_ref[...])
    put_merged(10, 4, unfold_merged(next_ref[:, 1:5].astype(F32)))
    clear_pads(stage)
    put_pair_row(stage, 0, resB_ref[:, 13])
    put_pair_row(stage, 1, next_ref[:, 0])
    fetches[0].wait()
    merged, xhat_seam, rstd_seam = merge_pairs(stage, mg1_ref, mw1_ref[...])
    put_merged(9, 1, merged)
    fetches[1].wait()
    pieces = [
        stage2[half, :, :, q % 2, pl.ds(q // 2, 8, stride=2), :].reshape(ROWS, 128)
        for q in range(4)
        for half in range(2)
    ]
    xhat, rstd = normalise(jnp.concatenate(pieces, 1))
    xhat2[...] = xhat
    rstd2[...] = jnp.broadcast_to(rstd, (ROWS, 128))
    merged_two = dot((xhat * mg2_ref[...]).astype(BF), mw2_ref[...]).astype(BF).astype(F32)
    xhat3, rstd3 = normalise(merged_two)
    n3 = (xhat3 * g3_ref[...]).astype(BF)
    fetches[2].wait()
    packed = [dot(n3, p3_ref[:, 512 * i : 512 * i + 512]) for i in range(3)]
    for g in range(4):
        q, k, v = (part[:, 128 * g : 128 * g + 128] for part in packed)
        q = lengthen((q * (SCALE * LOG2E)).astype(BF))
        k, v = k.astype(BF), v.astype(BF)
        k_s[g] = k
        v_s[g] = v
        qT_s[g] = q.T
        kT_s[g] = lengthen(k).T
        vT_s[g] = lengthen(v).T
    mask = region_mask(col_ref[...], row_ref[...])
    fetches[3].wait()

    def heads(i, _):
        operands = []
        for g in (2 * i, 2 * i + 1):

            def keep(h, probs, g=g):
                probs_s[g * 4 + h] = probs

            operands.append(
                (k_s[g], qT_s[g], vT_s[g], mask, lambda h, g=g: bias_ref[g * 4 + h], keep)
            )
        for u, (oT, inverse) in enumerate(attend_four(operands)):
            oT_s[2 * i + u] = oT
            inv_s[2 * i + u] = inverse
        return 0

    lax.fori_loop(0, 2, heads, 0)
    fetches[4].wait()
    att = jnp.concatenate([oT_s[g].astype(BF).T[:ROWS] for g in range(4)], 1)
    mixed = dot(att, ow3_ref[...]).astype(BF).astype(F32)
    section = (merged_two + mixed).reshape(4, 7, 8, 512)
    section = fold(section[:, :, 0:7])
    so_ref[...] = section[0:2, 0:4].astype(BF)
    sta_ref[...] = section[2:4].astype(BF)
    sha_ref[...] = section[0:2, 4:7].astype(BF)

    cot = cotw[...].reshape(ROWS, 512)
    cot_long = lengthen(cot.astype(BF))
    doT = dot_nt(ow3_ref[...], cot_long)
    for g in range(4):
        doT_s[g] = doT[128 * g : 128 * g + 128]

    def heads_back(i, _):
        operands = [
            (
                v_s[g], qT_s[g], kT_s[g], oT_s[g], doT_s[g], inv_s[g],
                lambda h, g=g: probs_s[g * 4 + h],
            )
            for g in (2 * i, 2 * i + 1)
        ]
        for u, (dq, dk, dv) in enumerate(attend_four_back(operands)):
            dqkv_s[2 * i + u] = dq
            dqkv_s[4 + 2 * i + u] = dk
            dqkv_s[8 + 2 * i + u] = dv
        return 0

    lax.fori_loop(0, 2, heads_back, 0)
    dpacked = jnp.concatenate([dqkv_s[i] for i in range(12)], 1)
    dn3 = dot_nt(dpacked, p3_ref[...])
    dm2 = cot + normalise_back(dn3 * g3_ref[...], xhat3, rstd3)
    dn2 = dot_nt(dm2.astype(BF), mw2_ref[...])
    dg2 = normalise_back(dn2 * mg2_ref[...], xhat2[...], rstd2[:, 0:1])
    for q in range(4):
        for half in range(2):
            at = 256 * q + 128 * half
            stage2[half, :, :, q % 2, pl.ds(q // 2, 8, stride=2), :] = dg2[:, at : at + 128].reshape(
                4, 7, 8, 128
            )

    dm_ref[...] = take_merged(0, 9)
    merge_pairs_back(take_merged(9, 1), xhat_seam, rstd_seam, mg1_ref, mw1_ref[...], stage)
    d30_ref[...] = pair_row(stage, 0)
    dN_ref[:, 0] = pair_row(stage, 1)
    dN_ref[:, 1:5] = fold_merged(take_merged(10, 4), 4).astype(BF)


def middle(*operands):
    shapes = [
        (4, 28, 128), (4, 5, 28, 128), (2, 4, 28, 128), (2, 7, 28, 128), (2, 3, 28, 128),
    ]
    return pl.pallas_call(
        middle_kernel,
        in_specs=[pl.BlockSpec(memory_space=pltpu.VMEM)] * 12
        + [pl.BlockSpec(memory_space=pl.ANY)] * 5,
        out_shape=[jax.ShapeDtypeStruct((576, 256), F32)]
        + [jax.ShapeDtypeStruct(s, BF) for s in shapes],
        scratch_shapes=[
            pltpu.VMEM((4, 1, 2, 32, 128), F32),
            pltpu.VMEM((2, 4, 7, 2, 16, 128), F32),
            pltpu.VMEM((ROWS, 1024), F32),
            pltpu.VMEM((ROWS, 128), F32),
            pltpu.VMEM((4, 7, 8, 512), F32),
            pltpu.VMEM((4, ROWS, 128), BF),
            pltpu.VMEM((4, ROWS, 128), BF),
            pltpu.VMEM((4, 128, LANES), BF),
            pltpu.VMEM((4, 128, LANES), BF),
            pltpu.VMEM((4, 128, LANES), BF),
            pltpu.VMEM((16, ROWS, LANES), BF),
            pltpu.VMEM((4, 128, LANES), F32),
            pltpu.VMEM((4, 8, LANES), F32),
            pltpu.VMEM((4, 128, LANES), F32),
            pltpu.VMEM((12, ROWS, 128), BF),
            pltpu.VMEM((512, 256), BF),
            pltpu.VMEM((1024, 512), BF),
            pltpu.VMEM((512, 1536), BF),
            pltpu.VMEM((HEADS3, ROWS, LANES), F32),
            pltpu.VMEM((512, 512), BF),
            pltpu.SemaphoreType.DMA((5,)),
        ],
        compiler_params=params(28),
        cost_estimate=cost(9),
    )(*operands)


def join_kernel(
    mid_ref, ta_ref, own_mid_ref, own_ref, so_ref, grad_ref, section_ref, wide, narrow
):
    for t in range(WT):
        turn = pl.ds(t, 28, stride=4)
        wide[0:7, turn, :] = (mid_ref if t < 2 else own_mid_ref)[t % 2].astype(F32)
        wide[7:18, turn, :] = (ta_ref if t < 2 else own_ref)[t % 2, 0:11].astype(F32)
        low = (ta_ref[t, 11:15] if t < 2 else so_ref[t - 2]).astype(F32)
        for g in range(4):
            narrow[g, :, pl.ds(t, 7, stride=4), :] = low[:, 7 * g : 7 * g + 7]
    for i in range(18):
        grad_ref[10 + i] = wide[i].reshape(28, 4, 128).astype(BF)
    for i in range(4):
        row = jnp.concatenate([narrow[g, i] for g in range(4)], 1)
        section_ref[3 + i] = row.reshape(7, 4, 512).astype(BF)


JOINED = [
    jax.ShapeDtypeStruct((28, 28, 4, 128), BF),
    jax.ShapeDtypeStruct((7, 7, 4, 512), BF),
]


def join(mid, ta, own_mid, own, section_own):
    return pl.pallas_call(
        join_kernel,
        out_shape=JOINED,
        scratch_shapes=[pltpu.VMEM((18, 112, 128), F32), pltpu.VMEM((4, 4, 28, 128), F32)],
        compiler_params=params(),
        cost_estimate=cost(2),
    )(mid, ta, own_mid, own, section_own)


def last_kernel(
    grad_hbm, section_hbm, ta_ref, own_ref, ha_ref, grad_out, section_out,
    wide, narrow, rows, section_rows, sems,
):
    del grad_hbm, section_hbm
    for t in range(WT):
        turn = pl.ds(t, 28, stride=4)
        corner = ta_ref[t, 7:13] if t < 2 else ha_ref[t - 2]
        wide[0:3, turn, :] = corner[0:3].astype(F32)
        wide[3:10, turn, :] = (ta_ref[t, 0:7] if t < 2 else own_ref[t - 2]).astype(F32)
        high = corner[3:6].astype(F32)
        for g in range(4):
            narrow[g, :, pl.ds(t, 7, stride=4), :] = high[:, 7 * g : 7 * g + 7]
    for i in range(10):
        rows[i] = wide[i].reshape(28, 4, 128).astype(BF)
    copy = pltpu.make_async_copy(rows, grad_out.at[0:10], sems.at[0])
    copy.start()
    for i in range(3):
        row = jnp.concatenate([narrow[g, i] for g in range(4)], 1)
        section_rows[i] = row.reshape(7, 4, 512).astype(BF)
    other = pltpu.make_async_copy(section_rows, section_out.at[0:3], sems.at[1])
    other.start()
    copy.wait()
    other.wait()


def join_last(grad, section, ta, own, ha):
    return pl.pallas_call(
        last_kernel,
        in_specs=[pl.BlockSpec(memory_space=pl.ANY)] * 2
        + [pl.BlockSpec(memory_space=pltpu.VMEM)] * 3,
        out_specs=[pl.BlockSpec(memory_space=pl.ANY)] * 2,
        out_shape=JOINED,
        scratch_shapes=[
            pltpu.VMEM((10, 112, 128), F32),
            pltpu.VMEM((4, 3, 28, 128), F32),
            pltpu.VMEM((10, 28, 4, 128), BF),
            pltpu.VMEM((3, 7, 4, 512), BF),
            pltpu.SemaphoreType.DMA((2,)),
        ],
        input_output_aliases={0: 0, 1: 1},
        compiler_params=params(),
        cost_estimate=cost(1),
    )(grad, section, ta, own, ha)


IN_ORDER = Layout(major_to_minor=(0, 1, 2, 3))


def inward(values):
    return with_layout_constraint(jnp.transpose(values, (1, 2, 0, 3)), IN_ORDER)


def outward(values):
    return jnp.transpose(with_layout_constraint(values, IN_ORDER), (2, 0, 1, 3))


def send(values, axes, by):
    axes = axes.split()
    sizes = [lax.axis_size(a) for a in axes]
    if len(axes) == 1:
        pairs = [(i, (i + by) % sizes[0]) for i in range(sizes[0])]
    else:
        n, m = sizes
        pairs = [
            (i * m + j, (i + by) % n * m + (j + by) % m) for i in range(n) for j in range(m)
        ]
    return lax.ppermute(values, tuple(axes), pairs)


def per_device(
    tokens,
    regions_one,
    regions_three,
    gain_one,
    projection_one,
    outward_one,
    table_one,
    merge_gain_one,
    merge_weight_one,
    merge_gain_two,
    merge_weight_two,
    gain_three,
    projection_three,
    outward_three,
    table_three,
    cotangent,
):
    (early,) = arrange(early_kernel, ((2, 14),), tokens)
    ta_early = send(inward(early), "ta", -1)
    late, ha_late = arrange(late_kernel, ((2, 15), (4, 6)), tokens, cotangent)
    ha_late = send(ha_late, "ha", -1)
    ta_late = send(inward(late), "ta", -1)
    bias_one, bias_three, row_one, row_three, col_one, col_three = prepare(
        table_one, table_three, regions_one, regions_three
    )
    gain, merge_gain, seam = gain_one[None], merge_gain_one[None], merge_weight_one
    args = (gain, projection_one, outward_one, bias_one)
    (res_send, res_a), saved_a = front(False, (tokens, outward(ta_early)), *args, row_one, col_one)
    ha_late, res_send = lax.optimization_barrier((ha_late, res_send))
    dg_late = send(ha_late[:2], "ta", -1)
    row_send, *early_norm = merge_call(
        send_kernel, 0.5, [((4, 5, 28, 128), BF), ((256, 512), F32), ((256, 128), F32)], 4,
        res_send, merge_gain, seam,
    )
    row_next = send(row_send, "ha", -1)
    ta_late, res_a = lax.optimization_barrier((ta_late, res_a))
    ta_late = outward(ta_late)
    (res_b,), saved_b = front(True, (tokens, ta_late, ha_late, dg_late), *args, row_one, col_one)
    merged, *local_norm = merge_call(
        local_kernel, 0.1, [((576, 256), F32), ((576, 512), F32), ((576, 128), F32)], 9,
        res_a, res_b, merge_gain, seam,
    )
    row_next, merged = lax.optimization_barrier((row_next, merged))
    d_merged, d_30, d_send, sec_own, sec_ta, sec_ha = middle(
        merged, res_b, row_next, cotangent, ta_late, ha_late, dg_late,
        merge_gain, merge_gain_two[None], gain_three[None], row_three, col_three,
        merge_weight_one, merge_weight_two, projection_three, bias_three, outward_three,
    )
    d_prev = send(d_send, "ha", 1)
    d_a, d_b = merge_call(
        local_back_kernel, 1, [((4, 5, 28, 128), BF), ((4, 14, 28, 128), BF)], 9,
        d_merged, d_30, *local_norm, merge_gain, seam,
    )
    own_b, ta_b, ha_b = back(
        2, (d_b, sec_ta, sec_ha), gain, projection_one, outward_one, saved_b
    )
    d_prev, own_b = lax.optimization_barrier((d_prev, own_b))
    ta_b = send(inward(ta_b), "ta", 1)
    ha_b = send(ha_b, "ha", 1)
    d_3, d_10 = merge_call(
        receive_kernel, 0.5, [((4, 7, 28, 128), BF), ((4, 2, 28, 128), BF)], 4,
        d_prev, *early_norm, merge_gain, seam,
    )
    own_mid, ta_mid = back(1, (d_10, d_a), gain, projection_one, outward_one, saved_a)
    ta_mid = send(inward(ta_mid), "ta", 1)
    d_3, own_mid = lax.optimization_barrier((d_3, own_mid))
    own_a, ta_a = back(0, (d_3,), gain, projection_one, outward_one, saved_a)
    ta_b, ta_mid, ha_b, own_a = lax.optimization_barrier((ta_b, ta_mid, ha_b, own_a))
    ta_a = send(jnp.concatenate([inward(ta_a), inward(ha_b[2:])], 0), "ta", 1)
    grad, section = join(outward(ta_mid), outward(ta_b), own_mid, own_b, sec_own)
    ta_a, grad = lax.optimization_barrier((ta_a, grad))
    grad, section = join_last(grad, section, outward(ta_a), own_a, ha_b)
    return (jnp.transpose(section, (2, 0, 1, 3)), jnp.transpose(grad, (2, 0, 1, 3)))


def solution(mesh):
    tile = P(("col", "ta"), "ha", None, None)
    ids = P(("col", "ta"), "ha", None)
    in_specs = (tile, ids, ids) + (P(),) * 12 + (tile,)
    return jax.shard_map(
        per_device, mesh=mesh, in_specs=in_specs, out_specs=(tile, tile), check_vma=False
    )
```

```python
import functools

import jax
import jax.numpy as jnp
import numpy as np
from jax import lax
from jax.experimental import pallas as pl
from jax.experimental.layout import Layout, with_layout_constraint
from jax.experimental.pallas import tpu as pltpu
from jax.sharding import PartitionSpec as P

HEADS1 = 4
HEADS3 = 16
WT = 4
WS = 7
ST = 2
SS = 3
EPSILON = 1e-05
NREL = 1183
LOG2E = 1.4426950408889634
HEAD = 32
SCALE = HEAD**-0.5
ROWS = WT * WS * 8
LANES = 256
SPAN = 1280
GONE = -1e30
PER_STEP = 4
STEPS = 8 // PER_STEP
BF = jnp.bfloat16
F32 = jnp.float32


def dot(a, b):
    return jnp.dot(a, b, preferred_element_type=F32)


def dot_nt(a, b):
    return lax.dot_general(a, b, (((1,), (1,)), ((), ())), preferred_element_type=F32)


def params(limit=20):
    return pltpu.CompilerParams(vmem_limit_bytes=limit * 1024 * 1024)


def cost(us):
    return pl.CostEstimate(flops=int(us * 1.1e9), bytes_accessed=int(us * 1e6), transcendentals=0)


def normalise(x):
    centred = x - jnp.mean(x, -1, keepdims=True)
    rstd = lax.rsqrt(jnp.mean(centred * centred, -1, keepdims=True) + EPSILON)
    return centred * rstd, rstd


def normalise_back(grad, xhat, rstd):
    return rstd * (
        grad
        - jnp.mean(grad, -1, keepdims=True)
        - xhat * jnp.mean(grad * xhat, -1, keepdims=True)
    )


def head_rows(x, h):
    return x[HEAD * h : HEAD * (h + 1)]


def head_of_lane(shape):
    return lax.broadcasted_iota(jnp.int32, shape, 1) // HEAD


def by_head(x):
    lane = head_of_lane((1, 128))
    return jnp.concatenate([x * (lane == h).astype(F32).astype(BF) for h in range(4)], 0)


def pick_heads(stacked):
    lane = head_of_lane((ROWS, 128))
    got = stacked[:ROWS]
    for h in range(1, 4):
        got = jnp.where(lane == h, stacked[ROWS * h : ROWS * (h + 1)], got)
    return got


def lengthen(x):
    return jnp.concatenate([x, jnp.zeros((LANES - ROWS, x.shape[1]), x.dtype)], 0)


def region_mask(column, row):
    return jnp.where(jnp.concatenate([column, column], 1) == row, 0.0, GONE).astype(F32)


def attend_four(windows):
    scores = [dot(by_head(k), qT) for k, qT, _, _, _, _ in windows]
    results = []
    for s, (_, _, vT, mask, bias_at, keep_probs) in zip(scores, windows):
        outs, inverses = [], []
        for h in range(4):
            biased = s[ROWS * h : ROWS * (h + 1)] + (bias_at(h) + mask)
            peak = jnp.max(biased, 0, keepdims=True)
            probs = jnp.exp2(biased - peak).astype(BF)
            keep_probs(h, probs)
            extended = jnp.concatenate([head_rows(vT, h)[:, :ROWS], jnp.ones((16, ROWS), BF)], 0)
            out = dot(extended, probs)
            inverse = 1.0 / out[HEAD : HEAD + 1]
            outs.append(out[:HEAD] * inverse)
            inverses.append(inverse)
        results.append((jnp.concatenate(outs, 0), jnp.concatenate(inverses + inverses, 0)))
    return results


def attend_four_back(windows):
    first = []
    for v, qT, kT, oT, doT, inverse, probs_at in windows:
        scaled, deltas = [], []
        for h in range(4):
            part = head_rows(doT, h) * inverse[h : h + 1]
            deltas.append(jnp.sum(part * head_rows(oT, h), 0, keepdims=True))
            scaled.append(part)
        scaled = jnp.concatenate(scaled, 0).astype(BF)
        first.append((scaled, deltas, dot(by_head(v), scaled)))
    results = []
    for (scaled, deltas, dprobs), (v, qT, kT, oT, doT, inverse, probs_at) in zip(first, windows):
        probs = [probs_at(h) for h in range(4)]
        dscores = [
            (probs[h].astype(F32) * (dprobs[ROWS * h : ROWS * (h + 1)] - deltas[h])).astype(BF)
            for h in range(4)
        ]
        dv = pick_heads(dot_nt(jnp.concatenate(probs, 0), scaled))
        dk = pick_heads(dot_nt(jnp.concatenate(dscores, 0), qT))
        dqT = jnp.concatenate(
            [dot(head_rows(kT, h)[:, :ROWS], dscores[h]) for h in range(4)], 0
        )
        dq = (dqT * SCALE).astype(BF).T[:ROWS]
        results.append((dq, (dk * (1.0 / LOG2E)).astype(BF), dv.astype(BF)))
    return results


def lanes_of(shape):
    return lax.broadcasted_iota(jnp.int32, shape, 1)


def region_rows(ids, section):
    columns = ids.shape[1]
    count = columns // WS
    place = lax.broadcasted_iota(jnp.int32, (columns, LANES * count), 0)
    lane = lanes_of((columns, LANES * count))
    column = lane % 8
    real = (column < WS) & (lane % LANES < ROWS)
    if section == 3:
        column = jnp.where(column < 3, column + 4, column - 3)
    chosen = real & (place == lane // LANES * WS + column)
    spread = dot(ids.astype(F32).astype(BF), chosen.astype(F32).astype(BF))
    row = lax.broadcasted_iota(jnp.int32, spread.shape, 0)
    lane = lanes_of(spread.shape)
    real = (lane[:1] % 8 < WS) & (lane[:1] % LANES < ROWS)
    rows = []
    for hw in range(ids.shape[0] // (WT * WS)):
        mine = lane % LANES // 8 == row % 4 * WS + row // 4 - WS * hw
        inside = (row >= WT * WS * hw) & (row < WT * WS * (hw + 1))
        found = jnp.sum(jnp.where(mine & inside, spread, 0.0), 0, keepdims=True)
        found = jnp.where(real, found, -1.0)
        rows += [found[:, LANES * ww : LANES * (ww + 1)] for ww in range(count)]
    return rows


def region_columns(ids, section):
    columns = ids.shape[1]
    count = columns // WS
    source = ids.astype(F32).astype(BF)
    token = lax.broadcasted_iota(jnp.int32, (ROWS, ids.shape[0]), 0)
    place = lanes_of((ROWS, ids.shape[0]))
    column = lax.broadcasted_iota(jnp.int32, (ROWS, columns), 0) % 8
    lane = lanes_of((ROWS, columns))
    if section == 3:
        column = jnp.where(column < 3, column + 4, jnp.where(column == 7, 8, column - 3))
    ones = jnp.ones((columns, 128), BF)
    pad = lax.broadcasted_iota(jnp.int32, (ROWS, 128), 0) % 8 == 7
    found = []
    for hw in range(ids.shape[0] // (WT * WS)):
        chosen = place == (token // 8 % WS + WS * hw) * WT + token // 56
        picked = dot(chosen.astype(F32).astype(BF), source)
        for ww in range(count):
            mine = jnp.where(lane == WS * ww + column, picked, 0.0).astype(BF)
            found.append(jnp.where(pad, -1.0, dot(mine, ones)))
    return found


def prepare_kernel(
    t1_ref, t3_ref, s_ref, r1_ref, r3_ref, o1_ref, o3_ref, row1_ref, row3_ref, col1_ref, col3_ref,
    tab, spread
):
    tab[...] = jnp.zeros((24, SPAN), F32)
    tab[0:4, 0:NREL] = t1_ref[...] * LOG2E
    tab[8:24, 0:NREL] = t3_ref[...] * LOG2E
    slabs = []
    for dt in range(7):
        start = 169 * dt
        low = start // 128 * 128
        run = tab[:, low : low + 384]
        if start > low:
            run = pltpu.roll(run, 384 - (start - low), 1)
        slabs.append(run[:, :256])
    left = jnp.concatenate(slabs, 0)
    first = left.astype(BF)
    rest = left - first.astype(F32)
    second = rest.astype(BF)
    third = (rest - second.astype(F32)).astype(BF)
    chosen = s_ref[...]
    got = dot(first, chosen) + dot(second, chosen) + dot(third, chosen)
    lane16 = lanes_of((16, 128))
    for dt in range(7):
        for wj in range(8):
            part = got[24 * dt : 24 * dt + 24, 128 * wj : 128 * wj + 128]
            spread[dt, pl.ds(wj, 8, stride=8), :] = part[0:8]
            later = part[8:24]
            turned = jnp.where(lane16 % 8 < 3, pltpu.roll(later, 124, 1), pltpu.roll(later, 3, 1))
            spread[dt, pl.ds(64 + (7 if wj == 7 else (wj + 3) % 7), 16, stride=8), :] = turned
    for o_ref, heads, at in ((o1_ref, HEADS1, 0), (o3_ref, HEADS3, 64)):
        lane = lanes_of((heads * 8, 128))
        for tj in range(WT):
            for hj in range(WS):
                p0, p1, p2, p3 = (
                    pltpu.roll(
                        spread[ti - tj + 3, at : at + heads * 8, :], (ti * 56 - (6 - hj) * 8) % 128, 1
                    )
                    for ti in range(WT)
                )
                left = jnp.where(lane < 56, p0, jnp.where(lane < 112, p1, p2))
                right = jnp.where(lane < 40, p2, p3)
                row = (tj * WS + hj) * 8
                o_ref[:, row : row + 8, 0:128] = left.reshape(heads, 8, 128)
                o_ref[:, row : row + 8, 128:256] = right.reshape(heads, 8, 128)
    for i, found in enumerate(region_rows(r1_ref[...], 1)):
        row1_ref[i] = found
    row3_ref[...] = region_rows(r3_ref[...], 3)[0]
    for i, found in enumerate(region_columns(r1_ref[...], 1)):
        col1_ref[i] = found
    col3_ref[...] = region_columns(r3_ref[...], 3)[0]


def chooser():
    chosen = np.zeros((256, 1024), np.float32)
    for wj in range(WS):
        for dh in range(13):
            for wi in range(WS):
                chosen[dh * 13 + wi - wj + 6, wj * 128 + dh * 8 + wi] = 1.0
    return jnp.asarray(chosen, BF)


def by_height(ids):
    return jnp.transpose(ids, (1, 0, 2)).reshape(-1, ids.shape[2])


def prepare(table_one, table_three, regions_one, regions_three):
    return pl.pallas_call(
        prepare_kernel,
        out_shape=(
            jax.ShapeDtypeStruct((HEADS1, ROWS, LANES), F32),
            jax.ShapeDtypeStruct((HEADS3, ROWS, LANES), F32),
            jax.ShapeDtypeStruct((16, 1, LANES), F32),
            jax.ShapeDtypeStruct((1, LANES), F32),
            jax.ShapeDtypeStruct((16, ROWS, 128), F32),
            jax.ShapeDtypeStruct((ROWS, 128), F32),
        ),
        scratch_shapes=[pltpu.VMEM((24, SPAN), F32), pltpu.VMEM((7, 24 * 8, 128), F32)],
        compiler_params=params(),
        cost_estimate=cost(3),
    )(
        jnp.transpose(table_one),
        jnp.transpose(table_three),
        chooser(),
        by_height(regions_one),
        by_height(regions_three),
    )


def fold(values):
    return jnp.concatenate([values[..., 128 * g : 128 * g + 128] for g in range(4)], -2)


def unfold(values):
    return jnp.concatenate([values[..., 7 * g : 7 * g + 7, :] for g in range(4)], -1)


def early_kernel(tok_ref, early_ref):
    early_ref[...] = tok_ref[0:2, 3:17]


def late_kernel(tok_ref, cot_ref, late_ref, ha_ref, dg_ref):
    late_ref[:, 0:11] = tok_ref[0:2, 17:28]
    late_ref[:, 11:15] = fold(cot_ref[0:2, 3:7].astype(F32)).astype(BF)
    ha_ref[:, 0:3] = tok_ref[2:4, 0:3]
    ha_ref[:, 3:6] = fold(cot_ref[2:4, 0:3].astype(F32)).astype(BF)
    dg_ref[:, 0:3] = tok_ref[0:2, 0:3]
    dg_ref[:, 3:6] = fold(cot_ref[0:2, 0:3].astype(F32)).astype(BF)


def arrange(kernel, rows, *operands):
    return pl.pallas_call(
        kernel,
        out_shape=[jax.ShapeDtypeStruct((2, n, 28, 128), BF) for n in rows],
        compiler_params=params(8),
        cost_estimate=cost(0.3),
    )(*operands)


def put_rows(stage, frames, rows, values):
    values = values.astype(F32)
    stage[frames, rows, 0:28, :] = values
    stage[frames, rows, 28:36, :] = values[:, :, 0:8, :]


def cut_windows(stage, win):
    for hw in range(2):
        for ww in range(4):
            win[hw * 4 + ww] = stage[:, 7 * hw : 7 * hw + 7, 3 + 7 * ww : 11 + 7 * ww, :].reshape(
                ROWS, 128
            )


def join_windows(win, stage):
    for hw in range(2):
        for ww in range(4):
            stage[:, 7 * hw : 7 * hw + 7, 3 + 7 * ww : 11 + 7 * ww, :] = win[hw * 4 + ww].reshape(
                WT, WS, 8, 128
            )
    stage[:, :, 0:3, :] = stage[:, :, 28:31, :]


def front_kernel(late, *refs):
    n_in = 4 if late else 2
    pieces, refs = refs[:n_in], refs[n_in:]
    gain_ref, proj_ref, outw_ref, bias_ref, row_ref, col_ref = refs[:6]
    refs = refs[6:]
    n_out = 1 if late else 2
    outs, refs = refs[:n_out], refs[n_out:]
    xw_ref, kv_ref, t_ref, p_ref, o_ref, inv_ref, stage, win = refs
    own = pieces[0]
    if late:
        put_rows(stage, slice(0, 2), slice(0, 11), own[2:4, 17:28])
        put_rows(stage, slice(2, 4), slice(0, 11), pieces[1][:, 0:11])
        put_rows(stage, slice(0, 2), slice(11, 14), pieces[2][:, 0:3])
        put_rows(stage, slice(2, 4), slice(11, 14), pieces[3][:, 0:3])
    else:
        put_rows(stage, slice(0, 2), slice(0, 14), own[2:4, 3:17])
        put_rows(stage, slice(2, 4), slice(0, 14), pieces[1][...])
    cut_windows(stage, win)
    lax.fori_loop(
        0,
        STEPS,
        functools.partial(
            front_step, 8 * late, gain_ref, proj_ref, outw_ref, bias_ref, row_ref, col_ref,
            xw_ref, kv_ref, t_ref, p_ref, o_ref, inv_ref, win,
        ),
        0,
    )
    join_windows(win, stage)
    if late:
        outs[0][...] = stage[:, :, 0:28, :].astype(BF)
    else:
        outs[0][...] = stage[:, 0:9, 0:28, :].astype(BF)
        outs[1][...] = stage[:, 9:14, 0:28, :].astype(BF)


def front_step(
    first, gain_ref, proj_ref, outw_ref, bias_ref, row_ref, col_ref,
    xw_ref, kv_ref, t_ref, p_ref, o_ref, inv_ref, win, step, carry,
):
    xs, operands = [], []
    for u in range(PER_STEP):
        w = step * PER_STEP + u
        x = win[w]
        xs.append(x)
        xw_ref[w] = x.astype(BF)
        xhat, _ = normalise(x)
        packed = dot((xhat * gain_ref[...]).astype(BF), proj_ref[...])
        q = (packed[:, :128] * (SCALE * LOG2E)).astype(BF)
        kv = packed[:, 128:].astype(BF)
        kv_ref[w] = kv
        qT, kT, vT = (lengthen(part).T for part in (q, kv[:, :128], kv[:, 128:]))
        t_ref[w, :128] = qT
        t_ref[w, 128:] = kT

        def keep(h, probs, w=w):
            p_ref[w, h] = probs

        operands.append(
            (kv[:, :128], qT, vT, region_mask(col_ref[first + w], row_ref[first + w]), lambda h: bias_ref[h], keep)
        )
    for u, (oT, inverse) in enumerate(attend_four(operands)):
        w = step * PER_STEP + u
        oT = oT.astype(BF)
        o_ref[w] = oT
        inv_ref[w] = inverse
        mixed = dot(oT.T[:ROWS], outw_ref[...]).astype(BF).astype(F32)
        win[w] = xs[u] + mixed
    return carry


SAVED = (
    ((ROWS, 128), BF),
    ((ROWS, 256), BF),
    ((256, LANES), BF),
    ((4, ROWS, LANES), BF),
    ((128, LANES), BF),
    ((8, LANES), F32),
)


def front(late, pieces, gain, proj, outw, bias, row, column):
    consts = (gain, proj, outw, bias)
    shapes = [(4, 14, 28, 128)] if late else [(4, 9, 28, 128), (4, 5, 28, 128)]
    out = pl.pallas_call(
        functools.partial(front_kernel, late),
        out_shape=[jax.ShapeDtypeStruct(s, BF) for s in shapes]
        + [jax.ShapeDtypeStruct((8,) + s, d) for s, d in SAVED],
        scratch_shapes=[
            pltpu.VMEM((4, 14, 40, 128), F32),
            pltpu.VMEM((8, ROWS, 128), F32),
        ],
        compiler_params=params(),
        cost_estimate=cost(4.6),
    )(*pieces, *consts, row, column)
    return out[: len(shapes)], out[len(shapes) :]


def back_kernel(late, *refs):
    n_in = 3 if late else 2
    pieces, refs = refs[:n_in], refs[n_in:]
    gain_ref, proj_ref, outw_ref = refs[:3]
    xw_ref, kv_ref, t_ref, p_ref, o_ref, inv_ref = refs[3:9]
    refs = refs[9:]
    n_out = 3 if late else 2
    outs, refs = refs[:n_out], refs[n_out:]
    stage, win = refs
    if late:
        put_rows(stage, slice(0, 4), slice(0, 14), pieces[0][...])
        outs[1][:, 11:15] = pieces[1][:, 0:4]
        outs[2][0:2, 3:6] = pieces[2][...]
        outs[2][2:4, 3:6] = pieces[1][:, 4:7]
    else:
        put_rows(stage, slice(0, 4), slice(0, 9), pieces[0][...])
        put_rows(stage, slice(0, 4), slice(9, 14), pieces[1][...])
    cut_windows(stage, win)
    lax.fori_loop(
        0,
        STEPS,
        functools.partial(
            back_step, gain_ref, proj_ref, outw_ref,
            xw_ref, kv_ref, t_ref, p_ref, o_ref, inv_ref, win,
        ),
        0,
    )
    join_windows(win, stage)
    if late:
        outs[0][...] = stage[0:2, 0:11, 0:28, :].astype(BF)
        outs[1][:, 0:11] = stage[2:4, 0:11, 0:28, :].astype(BF)
        outs[2][:, 0:3] = stage[:, 11:14, 0:28, :].astype(BF)
    else:
        outs[0][...] = stage[0:2, :, 0:28, :].astype(BF)
        outs[1][...] = stage[2:4, :, 0:28, :].astype(BF)


def back_step(
    gain_ref, proj_ref, outw_ref, xw_ref, kv_ref, t_ref, p_ref, o_ref, inv_ref, win, step, carry
):
    drs, operands = [], []
    for u in range(PER_STEP):
        w = step * PER_STEP + u
        dr = win[w]
        drs.append(dr)
        operands.append(
            (
                kv_ref[w, :, 128:],
                t_ref[w, :128],
                t_ref[w, 128:],
                o_ref[w].astype(F32),
                dot_nt(outw_ref[...], lengthen(dr.astype(BF))),
                inv_ref[w],
                lambda h, w=w: p_ref[w, h],
            )
        )
    for u, (dq, dk, dv) in enumerate(attend_four_back(operands)):
        w = step * PER_STEP + u
        dpacked = jnp.concatenate([dq, dk, dv], 1)
        dn = dot_nt(dpacked, proj_ref[...])
        xhat, rstd = normalise(xw_ref[w].astype(F32))
        dx = normalise_back(dn * gain_ref[...], xhat, rstd)
        win[w] = drs[u] + dx
    return carry


def back(late, pieces, gain, proj, outw, saved):
    consts = (gain, proj, outw)
    if late:
        shapes = [(2, 11, 28, 128), (2, 15, 28, 128), (4, 6, 28, 128)]
    else:
        shapes = [(2, 14, 28, 128), (2, 14, 28, 128)]
    return pl.pallas_call(
        functools.partial(back_kernel, late),
        out_shape=[jax.ShapeDtypeStruct(s, BF) for s in shapes],
        scratch_shapes=[
            pltpu.VMEM((4, 14, 40, 128), F32),
            pltpu.VMEM((8, ROWS, 128), F32),
        ],
        compiler_params=params(),
        cost_estimate=cost(5.5),
    )(*pieces, *consts, *saved)


def merge_pairs(stage, gain_ref, weight):
    pairs = stage.shape[1]
    pieces = [
        stage[:, :, q % 2, pl.ds(q // 2, 16, stride=2), :].reshape(WT * pairs * 16, 128)
        for q in range(4)
    ]
    xhat, rstd = normalise(jnp.concatenate(pieces, 1))
    merged = dot((xhat * gain_ref[...]).astype(BF), weight).astype(BF).astype(F32)
    return merged, xhat, rstd


def merge_pairs_back(grad, xhat, rstd, gain_ref, weight, stage):
    pairs = stage.shape[1]
    dn = dot_nt(grad.astype(BF), weight)
    dg = normalise_back(dn * gain_ref[...], xhat, rstd)
    for q in range(4):
        stage[:, :, q % 2, pl.ds(q // 2, 16, stride=2), :] = dg[
            :, 128 * q : 128 * q + 128
        ].reshape(WT, pairs, 16, 128)


def put_pair_row(stage, at, values):
    stage[:, at // 2, at % 2, 0:28, :] = values.astype(F32)


def clear_pads(stage):
    stage[:, :, :, 28:32, :] = jnp.zeros((WT, stage.shape[1], 2, 4, 128), F32)


def pair_row(stage, at):
    return stage[:, at // 2, at % 2, 0:28, :].astype(BF)


def fold_merged(merged, pairs):
    halves = [
        merged[:, 128 * i : 128 * i + 128].reshape(WT, pairs, 16, 128)[:, :, 0:14] for i in range(2)
    ]
    return jnp.concatenate(halves, 2)


def unfold_merged(folded):
    pad = jnp.zeros(folded.shape[:2] + (2, 128), F32)
    halves = [
        jnp.concatenate([folded[:, :, 14 * i : 14 * i + 14], pad], 2).reshape(-1, 128)
        for i in range(2)
    ]
    return jnp.concatenate(halves, 1)


def send_kernel(res_ref, gain_ref, weight_ref, send_ref, xhat_ref, rstd_ref, stage):
    clear_pads(stage)
    for i in range(8):
        put_pair_row(stage, i, res_ref[:, 1 + i])
    merged, xhat, rstd = merge_pairs(stage, gain_ref, weight_ref[...])
    xhat_ref[...] = xhat
    rstd_ref[...] = jnp.broadcast_to(rstd, rstd_ref.shape)
    send_ref[:, 0:1] = res_ref[:, 0:1]
    send_ref[:, 1:5] = fold_merged(merged, 4).astype(BF)


def local_kernel(resA_ref, resB_ref, gain_ref, weight_ref, merged_ref, xhat_ref, rstd_ref, stage):
    clear_pads(stage)
    for i in range(5):
        put_pair_row(stage, i, resA_ref[:, i])
    for i in range(13):
        put_pair_row(stage, 5 + i, resB_ref[:, i])
    merged, xhat, rstd = merge_pairs(stage, gain_ref, weight_ref[...])
    xhat_ref[...] = xhat
    rstd_ref[...] = jnp.broadcast_to(rstd, rstd_ref.shape)
    merged_ref[...] = merged


def local_back_kernel(
    grad_ref, d30_ref, xhat_ref, rstd_ref, gain_ref, weight_ref, dA_ref, dB_ref, stage
):
    merge_pairs_back(
        grad_ref[...], xhat_ref[...], rstd_ref[:, 0:1], gain_ref, weight_ref[...], stage
    )
    for i in range(5):
        dA_ref[:, i] = pair_row(stage, i)
    for i in range(13):
        dB_ref[:, i] = pair_row(stage, 5 + i)
    dB_ref[:, 13] = d30_ref[...]


def receive_kernel(got_ref, xhat_ref, rstd_ref, gain_ref, weight_ref, d_ref, stage):
    grad = unfold_merged(got_ref[:, 1:5].astype(F32))
    merge_pairs_back(grad, xhat_ref[...], rstd_ref[:, 0:1], gain_ref, weight_ref[...], stage)
    d_ref[:, 0:1] = got_ref[:, 0:1]
    for i in range(8):
        d_ref[:, 1 + i] = pair_row(stage, i)


def merge_call(kernel, us, shapes, pairs, *operands):
    return pl.pallas_call(
        kernel,
        out_shape=[jax.ShapeDtypeStruct(shape, kind) for shape, kind in shapes],
        scratch_shapes=[pltpu.VMEM((WT, pairs, 2, 32, 128), F32)],
        compiler_params=params(),
        cost_estimate=cost(us),
    )(*operands)


def middle_kernel(
    merged_ref, resB_ref, next_ref, cot_ref, cta_ref, cha_ref, cdg_ref,
    mg1_ref, mg2_ref, g3_ref, row_ref, col_ref, mw1_hbm, mw2_hbm, p3_hbm, bias_hbm, ow3_hbm,
    dm_ref, d30_ref, dN_ref, so_ref, sta_ref, sha_ref,
    stage, stage2, xhat2, rstd2, cotw, k_s, v_s, qT_s, kT_s, vT_s, probs_s, oT_s, inv_s, doT_s, dqkv_s,
    mw1_ref, mw2_ref, p3_ref, bias_ref, ow3_ref, sems,
):
    fetches = [
        pltpu.make_async_copy(there, here, sems.at[i])
        for i, (there, here) in enumerate(
            (
                (mw1_hbm, mw1_ref),
                (mw2_hbm, mw2_ref),
                (p3_hbm, p3_ref),
                (bias_hbm, bias_ref),
                (ow3_hbm, ow3_ref),
            )
        )
    ]
    for fetch in fetches:
        fetch.start()
    cotw[...] = jnp.zeros((4, 7, 8, 512), F32)
    cotw[0:2, 0:4, 0:7, :] = cot_ref[2:4, 3:7].astype(F32)
    cotw[2:4, 0:4, 0:7, :] = unfold(cta_ref[:, 11:15].astype(F32))
    cotw[0:2, 4:7, 0:7, :] = unfold(cha_ref[:, 3:6].astype(F32))
    cotw[2:4, 4:7, 0:7, :] = unfold(cdg_ref[:, 3:6].astype(F32))

    def put_merged(first, count, values):
        for half in range(2):
            block = values[:, 128 * half : 128 * half + 128].reshape(WT, count, 16, 128)
            for i in range(count):
                stage2[half, :, (first + i) // 2, (first + i) % 2] = block[:, i]

    def take_merged(first, count):
        halves = [
            jnp.concatenate(
                [
                    stage2[half, :, (first + i) // 2, (first + i) % 2].reshape(WT, 1, 16, 128)
                    for i in range(count)
                ],
                1,
            ).reshape(WT * count * 16, 128)
            for half in range(2)
        ]
        return jnp.concatenate(halves, 1)

    put_merged(0, 9, merged_ref[...])
    put_merged(10, 4, unfold_merged(next_ref[:, 1:5].astype(F32)))
    clear_pads(stage)
    put_pair_row(stage, 0, resB_ref[:, 13])
    put_pair_row(stage, 1, next_ref[:, 0])
    fetches[0].wait()
    merged, xhat_seam, rstd_seam = merge_pairs(stage, mg1_ref, mw1_ref[...])
    put_merged(9, 1, merged)
    fetches[1].wait()
    pieces = [
        stage2[half, :, :, q % 2, pl.ds(q // 2, 8, stride=2), :].reshape(ROWS, 128)
        for q in range(4)
        for half in range(2)
    ]
    xhat, rstd = normalise(jnp.concatenate(pieces, 1))
    xhat2[...] = xhat
    rstd2[...] = jnp.broadcast_to(rstd, (ROWS, 128))
    merged_two = dot((xhat * mg2_ref[...]).astype(BF), mw2_ref[...]).astype(BF).astype(F32)
    xhat3, rstd3 = normalise(merged_two)
    n3 = (xhat3 * g3_ref[...]).astype(BF)
    fetches[2].wait()
    packed = [dot(n3, p3_ref[:, 512 * i : 512 * i + 512]) for i in range(3)]
    for g in range(4):
        q, k, v = (part[:, 128 * g : 128 * g + 128] for part in packed)
        q = lengthen((q * (SCALE * LOG2E)).astype(BF))
        k, v = k.astype(BF), v.astype(BF)
        k_s[g] = k
        v_s[g] = v
        qT_s[g] = q.T
        kT_s[g] = lengthen(k).T
        vT_s[g] = lengthen(v).T
    mask = region_mask(col_ref[...], row_ref[...])
    fetches[3].wait()

    operands = []
    for g in range(4):

        def keep(h, probs, g=g):
            probs_s[g * 4 + h] = probs

        operands.append((k_s[g], qT_s[g], vT_s[g], mask, lambda h, g=g: bias_ref[g * 4 + h], keep))
    for g, (oT, inverse) in enumerate(attend_four(operands)):
        oT_s[g] = oT
        inv_s[g] = inverse
    fetches[4].wait()
    att = jnp.concatenate([oT_s[g].astype(BF).T[:ROWS] for g in range(4)], 1)
    mixed = dot(att, ow3_ref[...]).astype(BF).astype(F32)
    section = (merged_two + mixed).reshape(4, 7, 8, 512)
    section = fold(section[:, :, 0:7])
    so_ref[...] = section[0:2, 0:4].astype(BF)
    sta_ref[...] = section[2:4].astype(BF)
    sha_ref[...] = section[0:2, 4:7].astype(BF)

    cot = cotw[...].reshape(ROWS, 512)
    cot_long = lengthen(cot.astype(BF))
    doT = dot_nt(ow3_ref[...], cot_long)
    for g in range(4):
        doT_s[g] = doT[128 * g : 128 * g + 128]

    operands = [
        (v_s[g], qT_s[g], kT_s[g], oT_s[g], doT_s[g], inv_s[g], lambda h, g=g: probs_s[g * 4 + h])
        for g in range(4)
    ]
    for g, (dq, dk, dv) in enumerate(attend_four_back(operands)):
        dqkv_s[g] = dq
        dqkv_s[4 + g] = dk
        dqkv_s[8 + g] = dv
    dpacked = jnp.concatenate([dqkv_s[i] for i in range(12)], 1)
    dn3 = dot_nt(dpacked, p3_ref[...])
    dm2 = cot + normalise_back(dn3 * g3_ref[...], xhat3, rstd3)
    dn2 = dot_nt(dm2.astype(BF), mw2_ref[...])
    dg2 = normalise_back(dn2 * mg2_ref[...], xhat2[...], rstd2[:, 0:1])
    for q in range(4):
        for half in range(2):
            at = 256 * q + 128 * half
            stage2[half, :, :, q % 2, pl.ds(q // 2, 8, stride=2), :] = dg2[:, at : at + 128].reshape(
                4, 7, 8, 128
            )

    dm_ref[...] = take_merged(0, 9)
    merge_pairs_back(take_merged(9, 1), xhat_seam, rstd_seam, mg1_ref, mw1_ref[...], stage)
    d30_ref[...] = pair_row(stage, 0)
    dN_ref[:, 0] = pair_row(stage, 1)
    dN_ref[:, 1:5] = fold_merged(take_merged(10, 4), 4).astype(BF)


def middle(*operands):
    shapes = [
        (4, 28, 128), (4, 5, 28, 128), (2, 4, 28, 128), (2, 7, 28, 128), (2, 3, 28, 128),
    ]
    return pl.pallas_call(
        middle_kernel,
        in_specs=[pl.BlockSpec(memory_space=pltpu.VMEM)] * 12
        + [pl.BlockSpec(memory_space=pl.ANY)] * 5,
        out_shape=[jax.ShapeDtypeStruct((576, 256), F32)]
        + [jax.ShapeDtypeStruct(s, BF) for s in shapes],
        scratch_shapes=[
            pltpu.VMEM((4, 1, 2, 32, 128), F32),
            pltpu.VMEM((2, 4, 7, 2, 16, 128), F32),
            pltpu.VMEM((ROWS, 1024), F32),
            pltpu.VMEM((ROWS, 128), F32),
            pltpu.VMEM((4, 7, 8, 512), F32),
            pltpu.VMEM((4, ROWS, 128), BF),
            pltpu.VMEM((4, ROWS, 128), BF),
            pltpu.VMEM((4, 128, LANES), BF),
            pltpu.VMEM((4, 128, LANES), BF),
            pltpu.VMEM((4, 128, LANES), BF),
            pltpu.VMEM((16, ROWS, LANES), BF),
            pltpu.VMEM((4, 128, LANES), F32),
            pltpu.VMEM((4, 8, LANES), F32),
            pltpu.VMEM((4, 128, LANES), F32),
            pltpu.VMEM((12, ROWS, 128), BF),
            pltpu.VMEM((512, 256), BF),
            pltpu.VMEM((1024, 512), BF),
            pltpu.VMEM((512, 1536), BF),
            pltpu.VMEM((HEADS3, ROWS, LANES), F32),
            pltpu.VMEM((512, 512), BF),
            pltpu.SemaphoreType.DMA((5,)),
        ],
        compiler_params=params(28),
        cost_estimate=cost(9),
    )(*operands)


def join_kernel(ta_ref, own_ref, so_ref, grad_ref, section_ref, wide, narrow):
    for t in range(WT):
        wide[:, pl.ds(t, 28, stride=4), :] = (ta_ref if t < 2 else own_ref)[t % 2, 0:11].astype(F32)
        low = (ta_ref[t, 11:15] if t < 2 else so_ref[t - 2]).astype(F32)
        for g in range(4):
            narrow[g, :, pl.ds(t, 7, stride=4), :] = low[:, 7 * g : 7 * g + 7]
    for i in range(11):
        grad_ref[17 + i] = wide[i].reshape(28, 4, 128).astype(BF)
    for i in range(4):
        row = jnp.concatenate([narrow[g, i] for g in range(4)], 1)
        section_ref[3 + i] = row.reshape(7, 4, 512).astype(BF)


JOINED = [
    jax.ShapeDtypeStruct((28, 28, 4, 128), BF),
    jax.ShapeDtypeStruct((7, 7, 4, 512), BF),
]


def join(ta, own, section_own):
    return pl.pallas_call(
        join_kernel,
        out_shape=JOINED,
        scratch_shapes=[pltpu.VMEM((11, 112, 128), F32), pltpu.VMEM((4, 4, 28, 128), F32)],
        compiler_params=params(),
        cost_estimate=cost(2),
    )(ta, own, section_own)


def last_kernel(
    grad_hbm, section_hbm, ta_ref, own_ref, dg_ref, ha_ref, grad_out, section_out,
    wide, narrow, rows, section_rows, sems,
):
    del grad_hbm, section_hbm
    for t in range(WT):
        corner = dg_ref if t < 2 else ha_ref
        wide[0:3, pl.ds(t, 28, stride=4), :] = corner[t % 2, 0:3].astype(F32)
        wide[3:17, pl.ds(t, 28, stride=4), :] = (ta_ref if t < 2 else own_ref)[t % 2].astype(F32)
        high = corner[t % 2, 3:6].astype(F32)
        for g in range(4):
            narrow[g, :, pl.ds(t, 7, stride=4), :] = high[:, 7 * g : 7 * g + 7]
    for i in range(17):
        rows[i] = wide[i].reshape(28, 4, 128).astype(BF)
    copy = pltpu.make_async_copy(rows, grad_out.at[0:17], sems.at[0])
    copy.start()
    for i in range(3):
        row = jnp.concatenate([narrow[g, i] for g in range(4)], 1)
        section_rows[i] = row.reshape(7, 4, 512).astype(BF)
    other = pltpu.make_async_copy(section_rows, section_out.at[0:3], sems.at[1])
    other.start()
    copy.wait()
    other.wait()


def join_last(grad, section, ta, own, dg, ha):
    return pl.pallas_call(
        last_kernel,
        in_specs=[pl.BlockSpec(memory_space=pl.ANY)] * 2
        + [pl.BlockSpec(memory_space=pltpu.VMEM)] * 4,
        out_specs=[pl.BlockSpec(memory_space=pl.ANY)] * 2,
        out_shape=JOINED,
        scratch_shapes=[
            pltpu.VMEM((17, 112, 128), F32),
            pltpu.VMEM((4, 3, 28, 128), F32),
            pltpu.VMEM((17, 28, 4, 128), BF),
            pltpu.VMEM((3, 7, 4, 512), BF),
            pltpu.SemaphoreType.DMA((2,)),
        ],
        input_output_aliases={0: 0, 1: 1},
        compiler_params=params(),
        cost_estimate=cost(1),
    )(grad, section, ta, own, dg, ha)


IN_ORDER = Layout(major_to_minor=(0, 1, 2, 3))


def inward(values):
    return with_layout_constraint(jnp.transpose(values, (1, 2, 0, 3)), IN_ORDER)


def outward(values):
    return jnp.transpose(with_layout_constraint(values, IN_ORDER), (2, 0, 1, 3))


def send(values, axes, by):
    axes = axes.split()
    sizes = [lax.axis_size(a) for a in axes]
    if len(axes) == 1:
        pairs = [(i, (i + by) % sizes[0]) for i in range(sizes[0])]
    else:
        n, m = sizes
        pairs = [
            (i * m + j, (i + by) % n * m + (j + by) % m) for i in range(n) for j in range(m)
        ]
    return lax.ppermute(values, tuple(axes), pairs)


def per_device(
    tokens,
    regions_one,
    regions_three,
    gain_one,
    projection_one,
    outward_one,
    table_one,
    merge_gain_one,
    merge_weight_one,
    merge_gain_two,
    merge_weight_two,
    gain_three,
    projection_three,
    outward_three,
    table_three,
    cotangent,
):
    (early,) = arrange(early_kernel, (14,), tokens)
    ta_early = send(inward(early), "ta", -1)
    late, ha_late, dg_late = arrange(late_kernel, (15, 6, 6), tokens, cotangent)
    ha_late = send(ha_late, "ha", -1)
    dg_late = send(dg_late, "ha ta", -1)
    ta_late = send(inward(late), "ta", -1)
    bias_one, bias_three, row_one, row_three, col_one, col_three = prepare(
        table_one, table_three, regions_one, regions_three
    )
    gain, merge_gain, seam = gain_one[None], merge_gain_one[None], merge_weight_one
    args = (gain, projection_one, outward_one, bias_one)
    (res_send, res_a), saved_a = front(False, (tokens, outward(ta_early)), *args, row_one, col_one)
    row_send, *early_norm = merge_call(
        send_kernel, 0.5, [((4, 5, 28, 128), BF), ((256, 512), F32), ((256, 128), F32)], 4,
        res_send, merge_gain, seam,
    )
    row_next = send(row_send, "ha", -1)
    ta_late, res_a = lax.optimization_barrier((ta_late, res_a))
    ta_late = outward(ta_late)
    (res_b,), saved_b = front(True, (tokens, ta_late, ha_late, dg_late), *args, row_one, col_one)
    merged, *local_norm = merge_call(
        local_kernel, 0.1, [((576, 256), F32), ((576, 512), F32), ((576, 128), F32)], 9,
        res_a, res_b, merge_gain, seam,
    )
    row_next, merged = lax.optimization_barrier((row_next, merged))
    d_merged, d_30, d_send, sec_own, sec_ta, sec_ha = middle(
        merged, res_b, row_next, cotangent, ta_late, ha_late, dg_late,
        merge_gain, merge_gain_two[None], gain_three[None], row_three, col_three,
        merge_weight_one, merge_weight_two, projection_three, bias_three, outward_three,
    )
    d_prev = send(d_send, "ha", 1)
    d_a, d_b = merge_call(
        local_back_kernel, 1, [((4, 5, 28, 128), BF), ((4, 14, 28, 128), BF)], 9,
        d_merged, d_30, *local_norm, merge_gain, seam,
    )
    own_b, ta_b, ha_b = back(
        True, (d_b, sec_ta, sec_ha), gain, projection_one, outward_one, saved_b
    )
    d_prev, own_b = lax.optimization_barrier((d_prev, own_b))
    ta_b = send(inward(ta_b), "ta", 1)
    ha_b = send(ha_b, "ha", 1)
    (d_first,) = merge_call(
        receive_kernel, 0.5, [((4, 9, 28, 128), BF)], 4, d_prev, *early_norm, merge_gain, seam
    )
    own_a, ta_a = back(False, (d_first, d_a), gain, projection_one, outward_one, saved_a)
    ta_b, ha_b, own_a = lax.optimization_barrier((ta_b, ha_b, own_a))
    ta_a = send(inward(ta_a), "ta", 1)
    dg_b = send(ha_b[2:], "ta", 1)
    grad, section = join(outward(ta_b), own_b, sec_own)
    ta_a, dg_b, grad = lax.optimization_barrier((ta_a, dg_b, grad))
    grad, section = join_last(grad, section, outward(ta_a), own_a, dg_b, ha_b)
    return (jnp.transpose(section, (2, 0, 1, 3)), jnp.transpose(grad, (2, 0, 1, 3)))


def solution(mesh):
    tile = P(("col", "ta"), "ha", None, None)
    ids = P(("col", "ta"), "ha", None)
    in_specs = (tile, ids, ids) + (P(),) * 12 + (tile,)
    return jax.shard_map(
        per_device, mesh=mesh, in_specs=in_specs, out_specs=(tile, tile), check_vma=False
    )
```

```python
import functools

import jax
import jax.numpy as jnp
import numpy as np
from jax import lax
from jax.experimental import pallas as pl
from jax.experimental.layout import Layout, with_layout_constraint
from jax.experimental.pallas import tpu as pltpu
from jax.sharding import PartitionSpec as P

HEADS1 = 4
HEADS3 = 16
WT = 4
WS = 7
ST = 2
SS = 3
EPSILON = 1e-05
NREL = 1183
LOG2E = 1.4426950408889634
HEAD = 32
SCALE = HEAD**-0.5
ROWS = WT * WS * 8
LANES = 256
SPAN = 1280
GONE = -1e30
PER_STEP = 4
STEPS = 8 // PER_STEP
BF = jnp.bfloat16
F32 = jnp.float32


def dot(a, b):
    return jnp.dot(a, b, preferred_element_type=F32)


def dot_nt(a, b):
    return lax.dot_general(a, b, (((1,), (1,)), ((), ())), preferred_element_type=F32)


def params(limit=20):
    return pltpu.CompilerParams(vmem_limit_bytes=limit * 1024 * 1024)


def cost(us):
    return pl.CostEstimate(flops=int(us * 1.1e9), bytes_accessed=int(us * 1e6), transcendentals=0)


def normalise(x):
    centred = x - jnp.mean(x, -1, keepdims=True)
    rstd = lax.rsqrt(jnp.mean(centred * centred, -1, keepdims=True) + EPSILON)
    return centred * rstd, rstd


def normalise_back(grad, xhat, rstd):
    return rstd * (
        grad
        - jnp.mean(grad, -1, keepdims=True)
        - xhat * jnp.mean(grad * xhat, -1, keepdims=True)
    )


def head_rows(x, h):
    return x[HEAD * h : HEAD * (h + 1)]


def head_of_lane(shape):
    return lax.broadcasted_iota(jnp.int32, shape, 1) // HEAD


def by_head(x):
    lane = head_of_lane((1, 128))
    return jnp.concatenate([x * (lane == h).astype(F32).astype(BF) for h in range(4)], 0)


def pick_heads(stacked):
    lane = head_of_lane((ROWS, 128))
    got = stacked[:ROWS]
    for h in range(1, 4):
        got = jnp.where(lane == h, stacked[ROWS * h : ROWS * (h + 1)], got)
    return got


def lengthen(x):
    return jnp.concatenate([x, jnp.zeros((LANES - ROWS, x.shape[1]), x.dtype)], 0)


def region_mask(column, row):
    return jnp.where(jnp.concatenate([column, column], 1) == row, 0.0, GONE).astype(F32)


def attend_four(windows):
    scores = [dot(by_head(k), qT) for k, qT, _, _, _, _ in windows]
    results = []
    for s, (_, _, vT, mask, bias_at, keep_probs) in zip(scores, windows):
        outs, inverses = [], []
        for h in range(4):
            biased = s[ROWS * h : ROWS * (h + 1)] + (bias_at(h) + mask)
            peak = jnp.max(biased, 0, keepdims=True)
            probs = jnp.exp2(biased - peak).astype(BF)
            keep_probs(h, probs)
            extended = jnp.concatenate([head_rows(vT, h)[:, :ROWS], jnp.ones((16, ROWS), BF)], 0)
            out = dot(extended, probs)
            inverse = 1.0 / out[HEAD : HEAD + 1]
            outs.append(out[:HEAD] * inverse)
            inverses.append(inverse)
        results.append((jnp.concatenate(outs, 0), jnp.concatenate(inverses + inverses, 0)))
    return results


def attend_four_back(windows):
    first = []
    for v, qT, kT, oT, doT, inverse, probs_at in windows:
        scaled, deltas = [], []
        for h in range(4):
            part = head_rows(doT, h) * inverse[h : h + 1]
            deltas.append(jnp.sum(part * head_rows(oT, h), 0, keepdims=True))
            scaled.append(part)
        scaled = jnp.concatenate(scaled, 0).astype(BF)
        first.append((scaled, deltas, dot(by_head(v), scaled)))
    results = []
    for (scaled, deltas, dprobs), (v, qT, kT, oT, doT, inverse, probs_at) in zip(first, windows):
        probs = [probs_at(h) for h in range(4)]
        dscores = [
            (probs[h].astype(F32) * (dprobs[ROWS * h : ROWS * (h + 1)] - deltas[h])).astype(BF)
            for h in range(4)
        ]
        dv = pick_heads(dot_nt(jnp.concatenate(probs, 0), scaled))
        dk = pick_heads(dot_nt(jnp.concatenate(dscores, 0), qT))
        dqT = jnp.concatenate(
            [dot(head_rows(kT, h)[:, :ROWS], dscores[h]) for h in range(4)], 0
        )
        dq = (dqT * SCALE).astype(BF).T[:ROWS]
        results.append((dq, (dk * (1.0 / LOG2E)).astype(BF), dv.astype(BF)))
    return results


def lanes_of(shape):
    return lax.broadcasted_iota(jnp.int32, shape, 1)


def region_rows(ids, section):
    columns = ids.shape[1]
    count = columns // WS
    place = lax.broadcasted_iota(jnp.int32, (columns, LANES * count), 0)
    lane = lanes_of((columns, LANES * count))
    column = lane % 8
    real = (column < WS) & (lane % LANES < ROWS)
    if section == 3:
        column = jnp.where(column < 3, column + 4, column - 3)
    chosen = real & (place == lane // LANES * WS + column)
    spread = dot(ids.astype(F32).astype(BF), chosen.astype(F32).astype(BF))
    row = lax.broadcasted_iota(jnp.int32, spread.shape, 0)
    lane = lanes_of(spread.shape)
    real = (lane[:1] % 8 < WS) & (lane[:1] % LANES < ROWS)
    rows = []
    for hw in range(ids.shape[0] // (WT * WS)):
        mine = lane % LANES // 8 == row % 4 * WS + row // 4 - WS * hw
        inside = (row >= WT * WS * hw) & (row < WT * WS * (hw + 1))
        found = jnp.sum(jnp.where(mine & inside, spread, 0.0), 0, keepdims=True)
        found = jnp.where(real, found, -1.0)
        rows += [found[:, LANES * ww : LANES * (ww + 1)] for ww in range(count)]
    return rows


def region_columns(ids, section):
    columns = ids.shape[1]
    count = columns // WS
    source = ids.astype(F32).astype(BF)
    token = lax.broadcasted_iota(jnp.int32, (ROWS, ids.shape[0]), 0)
    place = lanes_of((ROWS, ids.shape[0]))
    column = lax.broadcasted_iota(jnp.int32, (ROWS, columns), 0) % 8
    lane = lanes_of((ROWS, columns))
    if section == 3:
        column = jnp.where(column < 3, column + 4, jnp.where(column == 7, 8, column - 3))
    ones = jnp.ones((columns, 128), BF)
    pad = lax.broadcasted_iota(jnp.int32, (ROWS, 128), 0) % 8 == 7
    found = []
    for hw in range(ids.shape[0] // (WT * WS)):
        chosen = place == (token // 8 % WS + WS * hw) * WT + token // 56
        picked = dot(chosen.astype(F32).astype(BF), source)
        for ww in range(count):
            mine = jnp.where(lane == WS * ww + column, picked, 0.0).astype(BF)
            found.append(jnp.where(pad, -1.0, dot(mine, ones)))
    return found


def bias_rows(spread, at, heads, tj, hj):
    lane = lanes_of((heads * 8, 128))
    p0, p1, p2, p3 = (
        pltpu.roll(
            spread[ti - tj + 3, at : at + heads * 8, :], (ti * 56 - (6 - hj) * 8) % 128, 1
        )
        for ti in range(WT)
    )
    left = jnp.where(lane < 56, p0, jnp.where(lane < 112, p1, p2))
    right = jnp.where(lane < 40, p2, p3)
    return left.reshape(heads, 8, 128), right.reshape(heads, 8, 128)


def prepare_kernel(
    t1_ref, t3_ref, s_ref, r1_ref, r3_ref, o1_ref, spread, row1_ref, row3_ref, col1_ref, col3_ref, tab
):
    tab[...] = jnp.zeros((24, SPAN), F32)
    tab[0:4, 0:NREL] = t1_ref[...] * LOG2E
    tab[8:24, 0:NREL] = t3_ref[...] * LOG2E
    slabs = []
    for dt in range(7):
        start = 169 * dt
        low = start // 128 * 128
        run = tab[:, low : low + 384]
        if start > low:
            run = pltpu.roll(run, 384 - (start - low), 1)
        slabs.append(run[:, :256])
    left = jnp.concatenate(slabs, 0)
    first = left.astype(BF)
    rest = left - first.astype(F32)
    second = rest.astype(BF)
    third = (rest - second.astype(F32)).astype(BF)
    chosen = s_ref[...]
    got = dot(first, chosen) + dot(second, chosen) + dot(third, chosen)
    lane16 = lanes_of((16, 128))
    for dt in range(7):
        for wj in range(8):
            part = got[24 * dt : 24 * dt + 24, 128 * wj : 128 * wj + 128]
            spread[dt, pl.ds(wj, 8, stride=8), :] = part[0:8]
            later = part[8:24]
            turned = jnp.where(lane16 % 8 < 3, pltpu.roll(later, 124, 1), pltpu.roll(later, 3, 1))
            spread[dt, pl.ds(64 + (7 if wj == 7 else (wj + 3) % 7), 16, stride=8), :] = turned
    for tj in range(WT):
        for hj in range(WS):
            row = (tj * WS + hj) * 8
            left, right = bias_rows(spread, 0, HEADS1, tj, hj)
            o1_ref[:, row : row + 8, 0:128] = left
            o1_ref[:, row : row + 8, 128:256] = right
    for i, found in enumerate(region_rows(r1_ref[...], 1)):
        row1_ref[i] = found
    row3_ref[...] = region_rows(r3_ref[...], 3)[0]
    for i, found in enumerate(region_columns(r1_ref[...], 1)):
        col1_ref[i] = found
    col3_ref[...] = region_columns(r3_ref[...], 3)[0]


def chooser():
    chosen = np.zeros((256, 1024), np.float32)
    for wj in range(WS):
        for dh in range(13):
            for wi in range(WS):
                chosen[dh * 13 + wi - wj + 6, wj * 128 + dh * 8 + wi] = 1.0
    return jnp.asarray(chosen, BF)


def by_height(ids):
    return jnp.transpose(ids, (1, 0, 2)).reshape(-1, ids.shape[2])


def prepare(table_one, table_three, regions_one, regions_three):
    return pl.pallas_call(
        prepare_kernel,
        out_shape=(
            jax.ShapeDtypeStruct((HEADS1, ROWS, LANES), F32),
            jax.ShapeDtypeStruct((7, 24 * 8, 128), F32),
            jax.ShapeDtypeStruct((16, 1, LANES), F32),
            jax.ShapeDtypeStruct((1, LANES), F32),
            jax.ShapeDtypeStruct((16, ROWS, 128), F32),
            jax.ShapeDtypeStruct((ROWS, 128), F32),
        ),
        scratch_shapes=[pltpu.VMEM((24, SPAN), F32)],
        compiler_params=params(),
        cost_estimate=cost(1.5),
    )(
        jnp.transpose(table_one),
        jnp.transpose(table_three),
        chooser(),
        by_height(regions_one),
        by_height(regions_three),
    )


def fold(values):
    return jnp.concatenate([values[..., 128 * g : 128 * g + 128] for g in range(4)], -2)


def unfold(values):
    return jnp.concatenate([values[..., 7 * g : 7 * g + 7, :] for g in range(4)], -1)


def early_kernel(tok_ref, early_ref):
    early_ref[...] = tok_ref[0:2, 3:17]


def late_kernel(tok_ref, cot_ref, late_ref, ha_ref, dg_ref):
    late_ref[:, 0:11] = tok_ref[0:2, 17:28]
    late_ref[:, 11:15] = fold(cot_ref[0:2, 3:7].astype(F32)).astype(BF)
    ha_ref[:, 0:3] = tok_ref[2:4, 0:3]
    ha_ref[:, 3:6] = fold(cot_ref[2:4, 0:3].astype(F32)).astype(BF)
    dg_ref[:, 0:3] = tok_ref[0:2, 0:3]
    dg_ref[:, 3:6] = fold(cot_ref[0:2, 0:3].astype(F32)).astype(BF)


def arrange(kernel, rows, *operands):
    return pl.pallas_call(
        kernel,
        out_shape=[jax.ShapeDtypeStruct((2, n, 28, 128), BF) for n in rows],
        compiler_params=params(8),
        cost_estimate=cost(0.3),
    )(*operands)


def put_rows(stage, frames, rows, values):
    values = values.astype(F32)
    stage[frames, rows, 0:28, :] = values
    stage[frames, rows, 28:36, :] = values[:, :, 0:8, :]


def cut_windows(stage, win):
    for hw in range(2):
        for ww in range(4):
            win[hw * 4 + ww] = stage[:, 7 * hw : 7 * hw + 7, 3 + 7 * ww : 11 + 7 * ww, :].reshape(
                ROWS, 128
            )


def join_windows(win, stage):
    for hw in range(2):
        for ww in range(4):
            stage[:, 7 * hw : 7 * hw + 7, 3 + 7 * ww : 11 + 7 * ww, :] = win[hw * 4 + ww].reshape(
                WT, WS, 8, 128
            )
    stage[:, :, 0:3, :] = stage[:, :, 28:31, :]


def front_kernel(late, *refs):
    n_in = 4 if late else 2
    pieces, refs = refs[:n_in], refs[n_in:]
    gain_ref, proj_ref, outw_ref, bias_ref, spread_ref, row_ref, col_ref = refs[:7]
    refs = refs[7:]
    n_out = 1 if late else 2
    outs, refs = refs[:n_out], refs[n_out:]
    b3_ref, xw_ref, kv_ref, t_ref, p_ref, o_ref, inv_ref, stage, win = refs
    own = pieces[0]
    if late:
        put_rows(stage, slice(0, 2), slice(0, 11), own[2:4, 17:28])
        put_rows(stage, slice(2, 4), slice(0, 11), pieces[1][:, 0:11])
        put_rows(stage, slice(0, 2), slice(11, 14), pieces[2][:, 0:3])
        put_rows(stage, slice(2, 4), slice(11, 14), pieces[3][:, 0:3])
    else:
        put_rows(stage, slice(0, 2), slice(0, 14), own[2:4, 3:17])
        put_rows(stage, slice(2, 4), slice(0, 14), pieces[1][...])
    cut_windows(stage, win)
    lax.fori_loop(
        0,
        STEPS,
        functools.partial(
            front_step, late, gain_ref, proj_ref, outw_ref, bias_ref, spread_ref, row_ref, col_ref,
            b3_ref, xw_ref, kv_ref, t_ref, p_ref, o_ref, inv_ref, win,
        ),
        0,
    )
    join_windows(win, stage)
    if late:
        outs[0][...] = stage[:, :, 0:28, :].astype(BF)
    else:
        outs[0][...] = stage[:, 0:9, 0:28, :].astype(BF)
        outs[1][...] = stage[:, 9:14, 0:28, :].astype(BF)


def front_step(
    late, gain_ref, proj_ref, outw_ref, bias_ref, spread_ref, row_ref, col_ref,
    b3_ref, xw_ref, kv_ref, t_ref, p_ref, o_ref, inv_ref, win, step, carry,
):
    first = 8 * late
    for hj in range(WS):
        left, right = bias_rows(spread_ref, 64, HEADS3, 2 * late + step, hj)
        at = pl.ds(pl.multiple_of((step * WS + hj) * 8, 8), 8)
        b3_ref[:, at, 0:128] = left
        b3_ref[:, at, 128:256] = right
    xs, operands = [], []
    for u in range(PER_STEP):
        w = step * PER_STEP + u
        x = win[w]
        xs.append(x)
        xw_ref[w] = x.astype(BF)
        xhat, _ = normalise(x)
        packed = dot((xhat * gain_ref[...]).astype(BF), proj_ref[...])
        q = (packed[:, :128] * (SCALE * LOG2E)).astype(BF)
        kv = packed[:, 128:].astype(BF)
        kv_ref[w] = kv
        qT, kT, vT = (lengthen(part).T for part in (q, kv[:, :128], kv[:, 128:]))
        t_ref[w, :128] = qT
        t_ref[w, 128:] = kT

        def keep(h, probs, w=w):
            p_ref[w, h] = probs

        operands.append(
            (kv[:, :128], qT, vT, region_mask(col_ref[first + w], row_ref[first + w]), lambda h: bias_ref[h], keep)
        )
    for u, (oT, inverse) in enumerate(attend_four(operands)):
        w = step * PER_STEP + u
        oT = oT.astype(BF)
        o_ref[w] = oT
        inv_ref[w] = inverse
        mixed = dot(oT.T[:ROWS], outw_ref[...]).astype(BF).astype(F32)
        win[w] = xs[u] + mixed
    return carry


SAVED = (
    ((ROWS, 128), BF),
    ((ROWS, 256), BF),
    ((256, LANES), BF),
    ((4, ROWS, LANES), BF),
    ((128, LANES), BF),
    ((8, LANES), F32),
)


def front(late, pieces, gain, proj, outw, bias, spread, row, column):
    consts = (gain, proj, outw, bias, spread)
    shapes = [(4, 14, 28, 128)] if late else [(4, 9, 28, 128), (4, 5, 28, 128)]
    out = pl.pallas_call(
        functools.partial(front_kernel, late),
        out_shape=[jax.ShapeDtypeStruct(s, BF) for s in shapes]
        + [jax.ShapeDtypeStruct((HEADS3, ROWS // 2, LANES), F32)]
        + [jax.ShapeDtypeStruct((8,) + s, d) for s, d in SAVED],
        scratch_shapes=[
            pltpu.VMEM((4, 14, 40, 128), F32),
            pltpu.VMEM((8, ROWS, 128), F32),
        ],
        compiler_params=params(),
        cost_estimate=cost(4.6),
    )(*pieces, *consts, row, column)
    return out[: len(shapes) + 1], out[len(shapes) + 1 :]


def back_kernel(late, *refs):
    n_in = 3 if late else 2
    pieces, refs = refs[:n_in], refs[n_in:]
    gain_ref, proj_ref, outw_ref = refs[:3]
    xw_ref, kv_ref, t_ref, p_ref, o_ref, inv_ref = refs[3:9]
    refs = refs[9:]
    n_out = 3 if late else 2
    outs, refs = refs[:n_out], refs[n_out:]
    stage, win = refs
    if late:
        put_rows(stage, slice(0, 4), slice(0, 14), pieces[0][...])
        outs[1][:, 11:15] = pieces[1][:, 0:4]
        outs[2][0:2, 3:6] = pieces[2][...]
        outs[2][2:4, 3:6] = pieces[1][:, 4:7]
    else:
        put_rows(stage, slice(0, 4), slice(0, 9), pieces[0][...])
        put_rows(stage, slice(0, 4), slice(9, 14), pieces[1][...])
    cut_windows(stage, win)
    lax.fori_loop(
        0,
        STEPS,
        functools.partial(
            back_step, gain_ref, proj_ref, outw_ref,
            xw_ref, kv_ref, t_ref, p_ref, o_ref, inv_ref, win,
        ),
        0,
    )
    join_windows(win, stage)
    if late:
        outs[0][...] = stage[0:2, 0:11, 0:28, :].astype(BF)
        outs[1][:, 0:11] = stage[2:4, 0:11, 0:28, :].astype(BF)
        outs[2][:, 0:3] = stage[:, 11:14, 0:28, :].astype(BF)
    else:
        outs[0][...] = stage[0:2, :, 0:28, :].astype(BF)
        outs[1][...] = stage[2:4, :, 0:28, :].astype(BF)


def back_step(
    gain_ref, proj_ref, outw_ref, xw_ref, kv_ref, t_ref, p_ref, o_ref, inv_ref, win, step, carry
):
    drs, operands = [], []
    for u in range(PER_STEP):
        w = step * PER_STEP + u
        dr = win[w]
        drs.append(dr)
        operands.append(
            (
                kv_ref[w, :, 128:],
                t_ref[w, :128],
                t_ref[w, 128:],
                o_ref[w].astype(F32),
                dot_nt(outw_ref[...], lengthen(dr.astype(BF))),
                inv_ref[w],
                lambda h, w=w: p_ref[w, h],
            )
        )
    for u, (dq, dk, dv) in enumerate(attend_four_back(operands)):
        w = step * PER_STEP + u
        dpacked = jnp.concatenate([dq, dk, dv], 1)
        dn = dot_nt(dpacked, proj_ref[...])
        xhat, rstd = normalise(xw_ref[w].astype(F32))
        dx = normalise_back(dn * gain_ref[...], xhat, rstd)
        win[w] = drs[u] + dx
    return carry


def back(late, pieces, gain, proj, outw, saved):
    consts = (gain, proj, outw)
    if late:
        shapes = [(2, 11, 28, 128), (2, 15, 28, 128), (4, 6, 28, 128)]
    else:
        shapes = [(2, 14, 28, 128), (2, 14, 28, 128)]
    return pl.pallas_call(
        functools.partial(back_kernel, late),
        out_shape=[jax.ShapeDtypeStruct(s, BF) for s in shapes],
        scratch_shapes=[
            pltpu.VMEM((4, 14, 40, 128), F32),
            pltpu.VMEM((8, ROWS, 128), F32),
        ],
        compiler_params=params(),
        cost_estimate=cost(5.5),
    )(*pieces, *consts, *saved)


def merge_pairs(stage, gain_ref, weight):
    pairs = stage.shape[1]
    pieces = [
        stage[:, :, q % 2, pl.ds(q // 2, 16, stride=2), :].reshape(WT * pairs * 16, 128)
        for q in range(4)
    ]
    xhat, rstd = normalise(jnp.concatenate(pieces, 1))
    merged = dot((xhat * gain_ref[...]).astype(BF), weight).astype(BF).astype(F32)
    return merged, xhat, rstd


def merge_pairs_back(grad, xhat, rstd, gain_ref, weight, stage):
    pairs = stage.shape[1]
    dn = dot_nt(grad.astype(BF), weight)
    dg = normalise_back(dn * gain_ref[...], xhat, rstd)
    for q in range(4):
        stage[:, :, q % 2, pl.ds(q // 2, 16, stride=2), :] = dg[
            :, 128 * q : 128 * q + 128
        ].reshape(WT, pairs, 16, 128)


def put_pair_row(stage, at, values):
    stage[:, at // 2, at % 2, 0:28, :] = values.astype(F32)


def clear_pads(stage):
    stage[:, :, :, 28:32, :] = jnp.zeros((WT, stage.shape[1], 2, 4, 128), F32)


def pair_row(stage, at):
    return stage[:, at // 2, at % 2, 0:28, :].astype(BF)


def fold_merged(merged, pairs):
    halves = [
        merged[:, 128 * i : 128 * i + 128].reshape(WT, pairs, 16, 128)[:, :, 0:14] for i in range(2)
    ]
    return jnp.concatenate(halves, 2)


def unfold_merged(folded):
    pad = jnp.zeros(folded.shape[:2] + (2, 128), F32)
    halves = [
        jnp.concatenate([folded[:, :, 14 * i : 14 * i + 14], pad], 2).reshape(-1, 128)
        for i in range(2)
    ]
    return jnp.concatenate(halves, 1)


def send_kernel(res_ref, gain_ref, weight_ref, send_ref, xhat_ref, rstd_ref, stage):
    clear_pads(stage)
    for i in range(8):
        put_pair_row(stage, i, res_ref[:, 1 + i])
    merged, xhat, rstd = merge_pairs(stage, gain_ref, weight_ref[...])
    xhat_ref[...] = xhat
    rstd_ref[...] = jnp.broadcast_to(rstd, rstd_ref.shape)
    send_ref[:, 0:1] = res_ref[:, 0:1]
    send_ref[:, 1:5] = fold_merged(merged, 4).astype(BF)


def local_kernel(resA_ref, resB_ref, gain_ref, weight_ref, merged_ref, xhat_ref, rstd_ref, stage):
    clear_pads(stage)
    for i in range(5):
        put_pair_row(stage, i, resA_ref[:, i])
    for i in range(13):
        put_pair_row(stage, 5 + i, resB_ref[:, i])
    merged, xhat, rstd = merge_pairs(stage, gain_ref, weight_ref[...])
    xhat_ref[...] = xhat
    rstd_ref[...] = jnp.broadcast_to(rstd, rstd_ref.shape)
    merged_ref[...] = merged


def local_back_kernel(
    grad_ref, d30_ref, xhat_ref, rstd_ref, gain_ref, weight_ref, dA_ref, dB_ref, stage
):
    merge_pairs_back(
        grad_ref[...], xhat_ref[...], rstd_ref[:, 0:1], gain_ref, weight_ref[...], stage
    )
    for i in range(5):
        dA_ref[:, i] = pair_row(stage, i)
    for i in range(13):
        dB_ref[:, i] = pair_row(stage, 5 + i)
    dB_ref[:, 13] = d30_ref[...]


def receive_kernel(got_ref, xhat_ref, rstd_ref, gain_ref, weight_ref, d_ref, stage):
    grad = unfold_merged(got_ref[:, 1:5].astype(F32))
    merge_pairs_back(grad, xhat_ref[...], rstd_ref[:, 0:1], gain_ref, weight_ref[...], stage)
    d_ref[:, 0:1] = got_ref[:, 0:1]
    for i in range(8):
        d_ref[:, 1 + i] = pair_row(stage, i)


def merge_call(kernel, us, shapes, pairs, *operands):
    return pl.pallas_call(
        kernel,
        out_shape=[jax.ShapeDtypeStruct(shape, kind) for shape, kind in shapes],
        scratch_shapes=[pltpu.VMEM((WT, pairs, 2, 32, 128), F32)],
        compiler_params=params(),
        cost_estimate=cost(us),
    )(*operands)


def middle_kernel(
    merged_ref, resB_ref, next_ref, cot_ref, cta_ref, cha_ref, cdg_ref,
    mg1_ref, mg2_ref, g3_ref, row_ref, col_ref, mw1_hbm, mw2_hbm, p3_hbm, biasA_hbm, biasB_hbm, ow3_hbm,
    dm_ref, d30_ref, dN_ref, so_ref, sta_ref, sha_ref,
    stage, stage2, xhat2, rstd2, cotw, k_s, v_s, qT_s, kT_s, vT_s, probs_s, oT_s, inv_s, doT_s, dqkv_s,
    mw1_ref, mw2_ref, p3_ref, bias_ref, ow3_ref, sems,
):
    fetches = [
        pltpu.make_async_copy(there, here, sems.at[i])
        for i, (there, here) in enumerate(
            (
                (mw1_hbm, mw1_ref),
                (mw2_hbm, mw2_ref),
                (p3_hbm, p3_ref),
                (biasA_hbm, bias_ref.at[:, 0 : ROWS // 2]),
                (biasB_hbm, bias_ref.at[:, ROWS // 2 : ROWS]),
                (ow3_hbm, ow3_ref),
            )
        )
    ]
    for fetch in fetches:
        fetch.start()
    cotw[...] = jnp.zeros((4, 7, 8, 512), F32)
    cotw[0:2, 0:4, 0:7, :] = cot_ref[2:4, 3:7].astype(F32)
    cotw[2:4, 0:4, 0:7, :] = unfold(cta_ref[:, 11:15].astype(F32))
    cotw[0:2, 4:7, 0:7, :] = unfold(cha_ref[:, 3:6].astype(F32))
    cotw[2:4, 4:7, 0:7, :] = unfold(cdg_ref[:, 3:6].astype(F32))

    def put_merged(first, count, values):
        for half in range(2):
            block = values[:, 128 * half : 128 * half + 128].reshape(WT, count, 16, 128)
            for i in range(count):
                stage2[half, :, (first + i) // 2, (first + i) % 2] = block[:, i]

    def take_merged(first, count):
        halves = [
            jnp.concatenate(
                [
                    stage2[half, :, (first + i) // 2, (first + i) % 2].reshape(WT, 1, 16, 128)
                    for i in range(count)
                ],
                1,
            ).reshape(WT * count * 16, 128)
            for half in range(2)
        ]
        return jnp.concatenate(halves, 1)

    put_merged(0, 9, merged_ref[...])
    put_merged(10, 4, unfold_merged(next_ref[:, 1:5].astype(F32)))
    clear_pads(stage)
    put_pair_row(stage, 0, resB_ref[:, 13])
    put_pair_row(stage, 1, next_ref[:, 0])
    fetches[0].wait()
    merged, xhat_seam, rstd_seam = merge_pairs(stage, mg1_ref, mw1_ref[...])
    put_merged(9, 1, merged)
    fetches[1].wait()
    pieces = [
        stage2[half, :, :, q % 2, pl.ds(q // 2, 8, stride=2), :].reshape(ROWS, 128)
        for q in range(4)
        for half in range(2)
    ]
    xhat, rstd = normalise(jnp.concatenate(pieces, 1))
    xhat2[...] = xhat
    rstd2[...] = jnp.broadcast_to(rstd, (ROWS, 128))
    merged_two = dot((xhat * mg2_ref[...]).astype(BF), mw2_ref[...]).astype(BF).astype(F32)
    xhat3, rstd3 = normalise(merged_two)
    n3 = (xhat3 * g3_ref[...]).astype(BF)
    fetches[2].wait()
    packed = [dot(n3, p3_ref[:, 512 * i : 512 * i + 512]) for i in range(3)]
    for g in range(4):
        q, k, v = (part[:, 128 * g : 128 * g + 128] for part in packed)
        q = lengthen((q * (SCALE * LOG2E)).astype(BF))
        k, v = k.astype(BF), v.astype(BF)
        k_s[g] = k
        v_s[g] = v
        qT_s[g] = q.T
        kT_s[g] = lengthen(k).T
        vT_s[g] = lengthen(v).T
    mask = region_mask(col_ref[...], row_ref[...])
    fetches[3].wait()
    fetches[4].wait()

    operands = []
    for g in range(4):

        def keep(h, probs, g=g):
            probs_s[g * 4 + h] = probs

        operands.append((k_s[g], qT_s[g], vT_s[g], mask, lambda h, g=g: bias_ref[g * 4 + h], keep))
    for g, (oT, inverse) in enumerate(attend_four(operands)):
        oT_s[g] = oT
        inv_s[g] = inverse
    fetches[5].wait()
    att = jnp.concatenate([oT_s[g].astype(BF).T[:ROWS] for g in range(4)], 1)
    mixed = dot(att, ow3_ref[...]).astype(BF).astype(F32)
    section = (merged_two + mixed).reshape(4, 7, 8, 512)
    section = fold(section[:, :, 0:7])
    so_ref[...] = section[0:2, 0:4].astype(BF)
    sta_ref[...] = section[2:4].astype(BF)
    sha_ref[...] = section[0:2, 4:7].astype(BF)

    cot = cotw[...].reshape(ROWS, 512)
    cot_long = lengthen(cot.astype(BF))
    doT = dot_nt(ow3_ref[...], cot_long)
    for g in range(4):
        doT_s[g] = doT[128 * g : 128 * g + 128]

    operands = [
        (v_s[g], qT_s[g], kT_s[g], oT_s[g], doT_s[g], inv_s[g], lambda h, g=g: probs_s[g * 4 + h])
        for g in range(4)
    ]
    for g, (dq, dk, dv) in enumerate(attend_four_back(operands)):
        dqkv_s[g] = dq
        dqkv_s[4 + g] = dk
        dqkv_s[8 + g] = dv
    dpacked = jnp.concatenate([dqkv_s[i] for i in range(12)], 1)
    dn3 = dot_nt(dpacked, p3_ref[...])
    dm2 = cot + normalise_back(dn3 * g3_ref[...], xhat3, rstd3)
    dn2 = dot_nt(dm2.astype(BF), mw2_ref[...])
    dg2 = normalise_back(dn2 * mg2_ref[...], xhat2[...], rstd2[:, 0:1])
    for q in range(4):
        for half in range(2):
            at = 256 * q + 128 * half
            stage2[half, :, :, q % 2, pl.ds(q // 2, 8, stride=2), :] = dg2[:, at : at + 128].reshape(
                4, 7, 8, 128
            )

    dm_ref[...] = take_merged(0, 9)
    merge_pairs_back(take_merged(9, 1), xhat_seam, rstd_seam, mg1_ref, mw1_ref[...], stage)
    d30_ref[...] = pair_row(stage, 0)
    dN_ref[:, 0] = pair_row(stage, 1)
    dN_ref[:, 1:5] = fold_merged(take_merged(10, 4), 4).astype(BF)


def middle(*operands):
    shapes = [
        (4, 28, 128), (4, 5, 28, 128), (2, 4, 28, 128), (2, 7, 28, 128), (2, 3, 28, 128),
    ]
    return pl.pallas_call(
        middle_kernel,
        in_specs=[pl.BlockSpec(memory_space=pltpu.VMEM)] * 12
        + [pl.BlockSpec(memory_space=pl.ANY)] * 6,
        out_shape=[jax.ShapeDtypeStruct((576, 256), F32)]
        + [jax.ShapeDtypeStruct(s, BF) for s in shapes],
        scratch_shapes=[
            pltpu.VMEM((4, 1, 2, 32, 128), F32),
            pltpu.VMEM((2, 4, 7, 2, 16, 128), F32),
            pltpu.VMEM((ROWS, 1024), F32),
            pltpu.VMEM((ROWS, 128), F32),
            pltpu.VMEM((4, 7, 8, 512), F32),
            pltpu.VMEM((4, ROWS, 128), BF),
            pltpu.VMEM((4, ROWS, 128), BF),
            pltpu.VMEM((4, 128, LANES), BF),
            pltpu.VMEM((4, 128, LANES), BF),
            pltpu.VMEM((4, 128, LANES), BF),
            pltpu.VMEM((16, ROWS, LANES), BF),
            pltpu.VMEM((4, 128, LANES), F32),
            pltpu.VMEM((4, 8, LANES), F32),
            pltpu.VMEM((4, 128, LANES), F32),
            pltpu.VMEM((12, ROWS, 128), BF),
            pltpu.VMEM((512, 256), BF),
            pltpu.VMEM((1024, 512), BF),
            pltpu.VMEM((512, 1536), BF),
            pltpu.VMEM((HEADS3, ROWS, LANES), F32),
            pltpu.VMEM((512, 512), BF),
            pltpu.SemaphoreType.DMA((6,)),
        ],
        compiler_params=params(28),
        cost_estimate=cost(9),
    )(*operands)


def join_kernel(ta_ref, own_ref, so_ref, grad_ref, section_ref, wide, narrow):
    for t in range(WT):
        wide[:, pl.ds(t, 28, stride=4), :] = (ta_ref if t < 2 else own_ref)[t % 2, 0:11].astype(F32)
        low = (ta_ref[t, 11:15] if t < 2 else so_ref[t - 2]).astype(F32)
        for g in range(4):
            narrow[g, :, pl.ds(t, 7, stride=4), :] = low[:, 7 * g : 7 * g + 7]
    for i in range(11):
        grad_ref[17 + i] = wide[i].reshape(28, 4, 128).astype(BF)
    for i in range(4):
        row = jnp.concatenate([narrow[g, i] for g in range(4)], 1)
        section_ref[3 + i] = row.reshape(7, 4, 512).astype(BF)


JOINED = [
    jax.ShapeDtypeStruct((28, 28, 4, 128), BF),
    jax.ShapeDtypeStruct((7, 7, 4, 512), BF),
]


def join(ta, own, section_own):
    return pl.pallas_call(
        join_kernel,
        out_shape=JOINED,
        scratch_shapes=[pltpu.VMEM((11, 112, 128), F32), pltpu.VMEM((4, 4, 28, 128), F32)],
        compiler_params=params(),
        cost_estimate=cost(2),
    )(ta, own, section_own)


def last_kernel(
    grad_hbm, section_hbm, ta_ref, own_ref, dg_ref, ha_ref, grad_out, section_out,
    wide, narrow, rows, section_rows, sems,
):
    del grad_hbm, section_hbm
    for t in range(WT):
        corner = dg_ref if t < 2 else ha_ref
        wide[0:3, pl.ds(t, 28, stride=4), :] = corner[t % 2, 0:3].astype(F32)
        wide[3:17, pl.ds(t, 28, stride=4), :] = (ta_ref if t < 2 else own_ref)[t % 2].astype(F32)
        high = corner[t % 2, 3:6].astype(F32)
        for g in range(4):
            narrow[g, :, pl.ds(t, 7, stride=4), :] = high[:, 7 * g : 7 * g + 7]
    for i in range(17):
        rows[i] = wide[i].reshape(28, 4, 128).astype(BF)
    copy = pltpu.make_async_copy(rows, grad_out.at[0:17], sems.at[0])
    copy.start()
    for i in range(3):
        row = jnp.concatenate([narrow[g, i] for g in range(4)], 1)
        section_rows[i] = row.reshape(7, 4, 512).astype(BF)
    other = pltpu.make_async_copy(section_rows, section_out.at[0:3], sems.at[1])
    other.start()
    copy.wait()
    other.wait()


def join_last(grad, section, ta, own, dg, ha):
    return pl.pallas_call(
        last_kernel,
        in_specs=[pl.BlockSpec(memory_space=pl.ANY)] * 2
        + [pl.BlockSpec(memory_space=pltpu.VMEM)] * 4,
        out_specs=[pl.BlockSpec(memory_space=pl.ANY)] * 2,
        out_shape=JOINED,
        scratch_shapes=[
            pltpu.VMEM((17, 112, 128), F32),
            pltpu.VMEM((4, 3, 28, 128), F32),
            pltpu.VMEM((17, 28, 4, 128), BF),
            pltpu.VMEM((3, 7, 4, 512), BF),
            pltpu.SemaphoreType.DMA((2,)),
        ],
        input_output_aliases={0: 0, 1: 1},
        compiler_params=params(),
        cost_estimate=cost(1),
    )(grad, section, ta, own, dg, ha)


IN_ORDER = Layout(major_to_minor=(0, 1, 2, 3))


def inward(values):
    return with_layout_constraint(jnp.transpose(values, (1, 2, 0, 3)), IN_ORDER)


def outward(values):
    return jnp.transpose(with_layout_constraint(values, IN_ORDER), (2, 0, 1, 3))


def send(values, axes, by):
    axes = axes.split()
    sizes = [lax.axis_size(a) for a in axes]
    if len(axes) == 1:
        pairs = [(i, (i + by) % sizes[0]) for i in range(sizes[0])]
    else:
        n, m = sizes
        pairs = [
            (i * m + j, (i + by) % n * m + (j + by) % m) for i in range(n) for j in range(m)
        ]
    return lax.ppermute(values, tuple(axes), pairs)


def per_device(
    tokens,
    regions_one,
    regions_three,
    gain_one,
    projection_one,
    outward_one,
    table_one,
    merge_gain_one,
    merge_weight_one,
    merge_gain_two,
    merge_weight_two,
    gain_three,
    projection_three,
    outward_three,
    table_three,
    cotangent,
):
    (early,) = arrange(early_kernel, (14,), tokens)
    ta_early = send(inward(early), "ta", -1)
    late, ha_late, dg_late = arrange(late_kernel, (15, 6, 6), tokens, cotangent)
    ha_late = send(ha_late, "ha", -1)
    dg_late = send(dg_late, "ha ta", -1)
    ta_late = send(inward(late), "ta", -1)
    bias_one, spread, row_one, row_three, col_one, col_three = prepare(
        table_one, table_three, regions_one, regions_three
    )
    gain, merge_gain, seam = gain_one[None], merge_gain_one[None], merge_weight_one
    args = (gain, projection_one, outward_one, bias_one, spread)
    (res_send, res_a, bias_a), saved_a = front(False, (tokens, outward(ta_early)), *args, row_one, col_one)
    row_send, *early_norm = merge_call(
        send_kernel, 0.5, [((4, 5, 28, 128), BF), ((256, 512), F32), ((256, 128), F32)], 4,
        res_send, merge_gain, seam,
    )
    row_next = send(row_send, "ha", -1)
    ta_late, res_a = lax.optimization_barrier((ta_late, res_a))
    ta_late = outward(ta_late)
    (res_b, bias_b), saved_b = front(True, (tokens, ta_late, ha_late, dg_late), *args, row_one, col_one)
    merged, *local_norm = merge_call(
        local_kernel, 0.1, [((576, 256), F32), ((576, 512), F32), ((576, 128), F32)], 9,
        res_a, res_b, merge_gain, seam,
    )
    row_next, merged = lax.optimization_barrier((row_next, merged))
    d_merged, d_30, d_send, sec_own, sec_ta, sec_ha = middle(
        merged, res_b, row_next, cotangent, ta_late, ha_late, dg_late,
        merge_gain, merge_gain_two[None], gain_three[None], row_three, col_three,
        merge_weight_one, merge_weight_two, projection_three, bias_a, bias_b, outward_three,
    )
    d_prev = send(d_send, "ha", 1)
    d_a, d_b = merge_call(
        local_back_kernel, 1, [((4, 5, 28, 128), BF), ((4, 14, 28, 128), BF)], 9,
        d_merged, d_30, *local_norm, merge_gain, seam,
    )
    own_b, ta_b, ha_b = back(
        True, (d_b, sec_ta, sec_ha), gain, projection_one, outward_one, saved_b
    )
    d_prev, own_b = lax.optimization_barrier((d_prev, own_b))
    ta_b = send(inward(ta_b), "ta", 1)
    ha_b = send(ha_b, "ha", 1)
    (d_first,) = merge_call(
        receive_kernel, 0.5, [((4, 9, 28, 128), BF)], 4, d_prev, *early_norm, merge_gain, seam
    )
    own_a, ta_a = back(False, (d_first, d_a), gain, projection_one, outward_one, saved_a)
    ta_b, ha_b, own_a = lax.optimization_barrier((ta_b, ha_b, own_a))
    ta_a = send(inward(ta_a), "ta", 1)
    dg_b = send(ha_b[2:], "ta", 1)
    grad, section = join(outward(ta_b), own_b, sec_own)
    ta_a, dg_b, grad = lax.optimization_barrier((ta_a, dg_b, grad))
    grad, section = join_last(grad, section, outward(ta_a), own_a, dg_b, ha_b)
    return (jnp.transpose(section, (2, 0, 1, 3)), jnp.transpose(grad, (2, 0, 1, 3)))


def solution(mesh):
    tile = P(("col", "ta"), "ha", None, None)
    ids = P(("col", "ta"), "ha", None)
    in_specs = (tile, ids, ids) + (P(),) * 12 + (tile,)
    return jax.shard_map(
        per_device, mesh=mesh, in_specs=in_specs, out_specs=(tile, tile), check_vma=False
    )
```

```python
import functools

import jax
import jax.numpy as jnp
import numpy as np
from jax import lax
from jax.experimental import pallas as pl
from jax.experimental.layout import Layout, with_layout_constraint
from jax.experimental.pallas import tpu as pltpu
from jax.sharding import PartitionSpec as P

HEADS1 = 4
HEADS3 = 16
WT = 4
WS = 7
ST = 2
SS = 3
EPSILON = 1e-05
NREL = 1183
LOG2E = 1.4426950408889634
HEAD = 32
SCALE = HEAD**-0.5
ROWS = WT * WS * 8
LANES = 256
SPAN = 1280
GONE = -1e30
PER_STEP = 8
STEPS = 8 // PER_STEP
BF = jnp.bfloat16
F32 = jnp.float32


def dot(a, b):
    return jnp.dot(a, b, preferred_element_type=F32)


def dot_nt(a, b):
    return lax.dot_general(a, b, (((1,), (1,)), ((), ())), preferred_element_type=F32)


def params(limit=20):
    return pltpu.CompilerParams(vmem_limit_bytes=limit * 1024 * 1024)


def cost(us):
    return pl.CostEstimate(flops=int(us * 1.1e9), bytes_accessed=int(us * 1e6), transcendentals=0)


def normalise(x):
    centred = x - jnp.mean(x, -1, keepdims=True)
    rstd = lax.rsqrt(jnp.mean(centred * centred, -1, keepdims=True) + EPSILON)
    return centred * rstd, rstd


def normalise_back(grad, xhat, rstd):
    return rstd * (
        grad
        - jnp.mean(grad, -1, keepdims=True)
        - xhat * jnp.mean(grad * xhat, -1, keepdims=True)
    )


def head_rows(x, h):
    return x[HEAD * h : HEAD * (h + 1)]


def head_of_lane(shape):
    return lax.broadcasted_iota(jnp.int32, shape, 1) // HEAD


def by_head(x):
    lane = head_of_lane((1, 128))
    return jnp.concatenate([x * (lane == h).astype(F32).astype(BF) for h in range(4)], 0)


def pick_heads(stacked):
    lane = head_of_lane((ROWS, 128))
    got = stacked[:ROWS]
    for h in range(1, 4):
        got = jnp.where(lane == h, stacked[ROWS * h : ROWS * (h + 1)], got)
    return got


def lengthen(x):
    return jnp.concatenate([x, jnp.zeros((LANES - ROWS, x.shape[1]), x.dtype)], 0)


def region_mask(column, row):
    return jnp.where(jnp.concatenate([column, column], 1) == row, 0.0, GONE).astype(F32)


def attend_four(windows):
    scores = [dot(by_head(k), qT) for k, qT, _, _, _, _ in windows]
    results = []
    for s, (_, _, vT, mask, bias_at, keep_probs) in zip(scores, windows):
        outs, inverses = [], []
        for h in range(4):
            biased = s[ROWS * h : ROWS * (h + 1)] + (bias_at(h) + mask)
            peak = jnp.max(biased, 0, keepdims=True)
            probs = jnp.exp2(biased - peak).astype(BF)
            keep_probs(h, probs)
            extended = jnp.concatenate([head_rows(vT, h)[:, :ROWS], jnp.ones((16, ROWS), BF)], 0)
            out = dot(extended, probs)
            inverse = 1.0 / out[HEAD : HEAD + 1]
            outs.append(out[:HEAD] * inverse)
            inverses.append(inverse)
        results.append((jnp.concatenate(outs, 0), jnp.concatenate(inverses + inverses, 0)))
    return results


def attend_four_back(windows):
    first = []
    for v, qT, kT, oT, doT, inverse, probs_at in windows:
        scaled, deltas = [], []
        for h in range(4):
            part = head_rows(doT, h) * inverse[h : h + 1]
            deltas.append(jnp.sum(part * head_rows(oT, h), 0, keepdims=True))
            scaled.append(part)
        scaled = jnp.concatenate(scaled, 0).astype(BF)
        first.append((scaled, deltas, dot(by_head(v), scaled)))
    results = []
    for (scaled, deltas, dprobs), (v, qT, kT, oT, doT, inverse, probs_at) in zip(first, windows):
        probs = [probs_at(h) for h in range(4)]
        dscores = [
            (probs[h].astype(F32) * (dprobs[ROWS * h : ROWS * (h + 1)] - deltas[h])).astype(BF)
            for h in range(4)
        ]
        dv = pick_heads(dot_nt(jnp.concatenate(probs, 0), scaled))
        dk = pick_heads(dot_nt(jnp.concatenate(dscores, 0), qT))
        dqT = jnp.concatenate(
            [dot(head_rows(kT, h)[:, :ROWS], dscores[h]) for h in range(4)], 0
        )
        dq = (dqT * SCALE).astype(BF).T[:ROWS]
        results.append((dq, (dk * (1.0 / LOG2E)).astype(BF), dv.astype(BF)))
    return results


def lanes_of(shape):
    return lax.broadcasted_iota(jnp.int32, shape, 1)


def region_rows(ids, section):
    columns = ids.shape[1]
    count = columns // WS
    place = lax.broadcasted_iota(jnp.int32, (columns, LANES * count), 0)
    lane = lanes_of((columns, LANES * count))
    column = lane % 8
    real = (column < WS) & (lane % LANES < ROWS)
    if section == 3:
        column = jnp.where(column < 3, column + 4, column - 3)
    chosen = real & (place == lane // LANES * WS + column)
    spread = dot(ids.astype(F32).astype(BF), chosen.astype(F32).astype(BF))
    row = lax.broadcasted_iota(jnp.int32, spread.shape, 0)
    lane = lanes_of(spread.shape)
    real = (lane[:1] % 8 < WS) & (lane[:1] % LANES < ROWS)
    rows = []
    for hw in range(ids.shape[0] // (WT * WS)):
        mine = lane % LANES // 8 == row % 4 * WS + row // 4 - WS * hw
        inside = (row >= WT * WS * hw) & (row < WT * WS * (hw + 1))
        found = jnp.sum(jnp.where(mine & inside, spread, 0.0), 0, keepdims=True)
        found = jnp.where(real, found, -1.0)
        rows += [found[:, LANES * ww : LANES * (ww + 1)] for ww in range(count)]
    return rows


def region_columns(ids, section):
    columns = ids.shape[1]
    count = columns // WS
    source = ids.astype(F32).astype(BF)
    token = lax.broadcasted_iota(jnp.int32, (ROWS, ids.shape[0]), 0)
    place = lanes_of((ROWS, ids.shape[0]))
    column = lax.broadcasted_iota(jnp.int32, (ROWS, columns), 0) % 8
    lane = lanes_of((ROWS, columns))
    if section == 3:
        column = jnp.where(column < 3, column + 4, jnp.where(column == 7, 8, column - 3))
    ones = jnp.ones((columns, 128), BF)
    pad = lax.broadcasted_iota(jnp.int32, (ROWS, 128), 0) % 8 == 7
    found = []
    for hw in range(ids.shape[0] // (WT * WS)):
        chosen = place == (token // 8 % WS + WS * hw) * WT + token // 56
        picked = dot(chosen.astype(F32).astype(BF), source)
        for ww in range(count):
            mine = jnp.where(lane == WS * ww + column, picked, 0.0).astype(BF)
            found.append(jnp.where(pad, -1.0, dot(mine, ones)))
    return found


def bias_rows(spread, at, heads, tj, hj):
    lane = lanes_of((heads * 8, 128))
    p0, p1, p2, p3 = (
        pltpu.roll(
            spread[ti - tj + 3, at : at + heads * 8, :], (ti * 56 - (6 - hj) * 8) % 128, 1
        )
        for ti in range(WT)
    )
    left = jnp.where(lane < 56, p0, jnp.where(lane < 112, p1, p2))
    right = jnp.where(lane < 40, p2, p3)
    return left.reshape(heads, 8, 128), right.reshape(heads, 8, 128)


def prepare_kernel(
    t1_ref, t3_ref, s_ref, r1_ref, r3_ref, o1_ref, spread, row1_ref, row3_ref, col1_ref, col3_ref, tab
):
    tab[...] = jnp.zeros((24, SPAN), F32)
    tab[0:4, 0:NREL] = t1_ref[...] * LOG2E
    tab[8:24, 0:NREL] = t3_ref[...] * LOG2E
    slabs = []
    for dt in range(7):
        start = 169 * dt
        low = start // 128 * 128
        run = tab[:, low : low + 384]
        if start > low:
            run = pltpu.roll(run, 384 - (start - low), 1)
        slabs.append(run[:, :256])
    left = jnp.concatenate(slabs, 0)
    first = left.astype(BF)
    rest = left - first.astype(F32)
    second = rest.astype(BF)
    third = (rest - second.astype(F32)).astype(BF)
    chosen = s_ref[...]
    got = dot(first, chosen) + dot(second, chosen) + dot(third, chosen)
    lane16 = lanes_of((16, 128))
    for dt in range(7):
        for wj in range(8):
            part = got[24 * dt : 24 * dt + 24, 128 * wj : 128 * wj + 128]
            spread[dt, pl.ds(wj, 8, stride=8), :] = part[0:8]
            later = part[8:24]
            turned = jnp.where(lane16 % 8 < 3, pltpu.roll(later, 124, 1), pltpu.roll(later, 3, 1))
            spread[dt, pl.ds(64 + (7 if wj == 7 else (wj + 3) % 7), 16, stride=8), :] = turned
    for tj in range(WT):
        for hj in range(WS):
            row = (tj * WS + hj) * 8
            left, right = bias_rows(spread, 0, HEADS1, tj, hj)
            o1_ref[:, row : row + 8, 0:128] = left
            o1_ref[:, row : row + 8, 128:256] = right
    for i, found in enumerate(region_rows(r1_ref[...], 1)):
        row1_ref[i] = found
    row3_ref[...] = region_rows(r3_ref[...], 3)[0]
    for i, found in enumerate(region_columns(r1_ref[...], 1)):
        col1_ref[i] = found
    col3_ref[...] = region_columns(r3_ref[...], 3)[0]


def chooser():
    chosen = np.zeros((256, 1024), np.float32)
    for wj in range(WS):
        for dh in range(13):
            for wi in range(WS):
                chosen[dh * 13 + wi - wj + 6, wj * 128 + dh * 8 + wi] = 1.0
    return jnp.asarray(chosen, BF)


def by_height(ids):
    return jnp.transpose(ids, (1, 0, 2)).reshape(-1, ids.shape[2])


def prepare(table_one, table_three, regions_one, regions_three):
    return pl.pallas_call(
        prepare_kernel,
        out_shape=(
            jax.ShapeDtypeStruct((HEADS1, ROWS, LANES), F32),
            jax.ShapeDtypeStruct((7, 24 * 8, 128), F32),
            jax.ShapeDtypeStruct((16, 1, LANES), F32),
            jax.ShapeDtypeStruct((1, LANES), F32),
            jax.ShapeDtypeStruct((16, ROWS, 128), F32),
            jax.ShapeDtypeStruct((ROWS, 128), F32),
        ),
        scratch_shapes=[pltpu.VMEM((24, SPAN), F32)],
        compiler_params=params(),
        cost_estimate=cost(1.5),
    )(
        jnp.transpose(table_one),
        jnp.transpose(table_three),
        chooser(),
        by_height(regions_one),
        by_height(regions_three),
    )


def fold(values):
    return jnp.concatenate([values[..., 128 * g : 128 * g + 128] for g in range(4)], -2)


def unfold(values):
    return jnp.concatenate([values[..., 7 * g : 7 * g + 7, :] for g in range(4)], -1)


def early_kernel(tok_ref, early_ref):
    early_ref[...] = tok_ref[0:2, 3:17]


def late_kernel(tok_ref, cot_ref, late_ref, ha_ref, dg_ref):
    late_ref[:, 0:11] = tok_ref[0:2, 17:28]
    late_ref[:, 11:15] = fold(cot_ref[0:2, 3:7].astype(F32)).astype(BF)
    ha_ref[:, 0:3] = tok_ref[2:4, 0:3]
    ha_ref[:, 3:6] = fold(cot_ref[2:4, 0:3].astype(F32)).astype(BF)
    dg_ref[:, 0:3] = tok_ref[0:2, 0:3]
    dg_ref[:, 3:6] = fold(cot_ref[0:2, 0:3].astype(F32)).astype(BF)


def arrange(kernel, rows, *operands):
    return pl.pallas_call(
        kernel,
        out_shape=[jax.ShapeDtypeStruct((2, n, 28, 128), BF) for n in rows],
        compiler_params=params(8),
        cost_estimate=cost(0.3),
    )(*operands)


def put_rows(stage, frames, rows, values):
    values = values.astype(F32)
    stage[frames, rows, 0:28, :] = values
    stage[frames, rows, 28:36, :] = values[:, :, 0:8, :]


def cut_windows(stage, win):
    for hw in range(2):
        for ww in range(4):
            win[hw * 4 + ww] = stage[:, 7 * hw : 7 * hw + 7, 3 + 7 * ww : 11 + 7 * ww, :].reshape(
                ROWS, 128
            )


def join_windows(win, stage):
    for hw in range(2):
        for ww in range(4):
            stage[:, 7 * hw : 7 * hw + 7, 3 + 7 * ww : 11 + 7 * ww, :] = win[hw * 4 + ww].reshape(
                WT, WS, 8, 128
            )
    stage[:, :, 0:3, :] = stage[:, :, 28:31, :]


def front_kernel(late, *refs):
    n_in = 4 if late else 2
    pieces, refs = refs[:n_in], refs[n_in:]
    gain_ref, proj_ref, outw_ref, bias_ref, spread_ref, row_ref, col_ref = refs[:7]
    refs = refs[7:]
    n_out = 1 if late else 2
    outs, refs = refs[:n_out], refs[n_out:]
    b3_ref, xw_ref, kv_ref, t_ref, p_ref, o_ref, inv_ref, stage, win = refs
    own = pieces[0]
    if late:
        put_rows(stage, slice(0, 2), slice(0, 11), own[2:4, 17:28])
        put_rows(stage, slice(2, 4), slice(0, 11), pieces[1][:, 0:11])
        put_rows(stage, slice(0, 2), slice(11, 14), pieces[2][:, 0:3])
        put_rows(stage, slice(2, 4), slice(11, 14), pieces[3][:, 0:3])
    else:
        put_rows(stage, slice(0, 2), slice(0, 14), own[2:4, 3:17])
        put_rows(stage, slice(2, 4), slice(0, 14), pieces[1][...])
    cut_windows(stage, win)
    lax.fori_loop(
        0,
        STEPS,
        functools.partial(
            front_step, late, gain_ref, proj_ref, outw_ref, bias_ref, spread_ref, row_ref, col_ref,
            b3_ref, xw_ref, kv_ref, t_ref, p_ref, o_ref, inv_ref, win,
        ),
        0,
    )
    join_windows(win, stage)
    if late:
        outs[0][...] = stage[:, :, 0:28, :].astype(BF)
    else:
        outs[0][...] = stage[:, 0:9, 0:28, :].astype(BF)
        outs[1][...] = stage[:, 9:14, 0:28, :].astype(BF)


def front_step(
    late, gain_ref, proj_ref, outw_ref, bias_ref, spread_ref, row_ref, col_ref,
    b3_ref, xw_ref, kv_ref, t_ref, p_ref, o_ref, inv_ref, win, step, carry,
):
    first = 8 * late
    for i in range(2 // STEPS):
        tj = step * (2 // STEPS) + i
        for hj in range(WS):
            left, right = bias_rows(spread_ref, 64, HEADS3, 2 * late + tj, hj)
            at = pl.ds(pl.multiple_of((tj * WS + hj) * 8, 8), 8)
            b3_ref[:, at, 0:128] = left
            b3_ref[:, at, 128:256] = right
    xs, operands = [], []
    for u in range(PER_STEP):
        w = step * PER_STEP + u
        x = win[w]
        xs.append(x)
        xw_ref[w] = x.astype(BF)
        xhat, _ = normalise(x)
        packed = dot((xhat * gain_ref[...]).astype(BF), proj_ref[...])
        q = (packed[:, :128] * (SCALE * LOG2E)).astype(BF)
        kv = packed[:, 128:].astype(BF)
        kv_ref[w] = kv
        qT, kT, vT = (lengthen(part).T for part in (q, kv[:, :128], kv[:, 128:]))
        t_ref[w, :128] = qT
        t_ref[w, 128:] = kT

        def keep(h, probs, w=w):
            p_ref[w, h] = probs

        operands.append(
            (kv[:, :128], qT, vT, region_mask(col_ref[first + w], row_ref[first + w]), lambda h: bias_ref[h], keep)
        )
    for u, (oT, inverse) in enumerate(attend_four(operands)):
        w = step * PER_STEP + u
        oT = oT.astype(BF)
        o_ref[w] = oT
        inv_ref[w] = inverse
        mixed = dot(oT.T[:ROWS], outw_ref[...]).astype(BF).astype(F32)
        win[w] = xs[u] + mixed
    return carry


SAVED = (
    ((ROWS, 128), BF),
    ((ROWS, 256), BF),
    ((256, LANES), BF),
    ((4, ROWS, LANES), BF),
    ((128, LANES), BF),
    ((8, LANES), F32),
)


def front(late, pieces, gain, proj, outw, bias, spread, row, column):
    consts = (gain, proj, outw, bias, spread)
    shapes = [(4, 14, 28, 128)] if late else [(4, 9, 28, 128), (4, 5, 28, 128)]
    out = pl.pallas_call(
        functools.partial(front_kernel, late),
        out_shape=[jax.ShapeDtypeStruct(s, BF) for s in shapes]
        + [jax.ShapeDtypeStruct((HEADS3, ROWS // 2, LANES), F32)]
        + [jax.ShapeDtypeStruct((8,) + s, d) for s, d in SAVED],
        scratch_shapes=[
            pltpu.VMEM((4, 14, 40, 128), F32),
            pltpu.VMEM((8, ROWS, 128), F32),
        ],
        compiler_params=params(),
        cost_estimate=cost(4.6),
    )(*pieces, *consts, row, column)
    return out[: len(shapes) + 1], out[len(shapes) + 1 :]


def back_kernel(late, *refs):
    n_in = 3 if late else 2
    pieces, refs = refs[:n_in], refs[n_in:]
    gain_ref, proj_ref, outw_ref = refs[:3]
    xw_ref, kv_ref, t_ref, p_ref, o_ref, inv_ref = refs[3:9]
    refs = refs[9:]
    n_out = 3 if late else 2
    outs, refs = refs[:n_out], refs[n_out:]
    stage, win = refs
    if late:
        put_rows(stage, slice(0, 4), slice(0, 14), pieces[0][...])
        outs[1][:, 11:15] = pieces[1][:, 0:4]
        outs[2][0:2, 3:6] = pieces[2][...]
        outs[2][2:4, 3:6] = pieces[1][:, 4:7]
    else:
        put_rows(stage, slice(0, 4), slice(0, 9), pieces[0][...])
        put_rows(stage, slice(0, 4), slice(9, 14), pieces[1][...])
    cut_windows(stage, win)
    lax.fori_loop(
        0,
        STEPS,
        functools.partial(
            back_step, gain_ref, proj_ref, outw_ref,
            xw_ref, kv_ref, t_ref, p_ref, o_ref, inv_ref, win,
        ),
        0,
    )
    join_windows(win, stage)
    if late:
        outs[0][...] = stage[0:2, 0:11, 0:28, :].astype(BF)
        outs[1][:, 0:11] = stage[2:4, 0:11, 0:28, :].astype(BF)
        outs[2][:, 0:3] = stage[:, 11:14, 0:28, :].astype(BF)
    else:
        outs[0][...] = stage[0:2, :, 0:28, :].astype(BF)
        outs[1][...] = stage[2:4, :, 0:28, :].astype(BF)


def back_step(
    gain_ref, proj_ref, outw_ref, xw_ref, kv_ref, t_ref, p_ref, o_ref, inv_ref, win, step, carry
):
    drs, operands = [], []
    for u in range(PER_STEP):
        w = step * PER_STEP + u
        dr = win[w]
        drs.append(dr)
        operands.append(
            (
                kv_ref[w, :, 128:],
                t_ref[w, :128],
                t_ref[w, 128:],
                o_ref[w].astype(F32),
                dot_nt(outw_ref[...], lengthen(dr.astype(BF))),
                inv_ref[w],
                lambda h, w=w: p_ref[w, h],
            )
        )
    for u, (dq, dk, dv) in enumerate(attend_four_back(operands)):
        w = step * PER_STEP + u
        dpacked = jnp.concatenate([dq, dk, dv], 1)
        dn = dot_nt(dpacked, proj_ref[...])
        xhat, rstd = normalise(xw_ref[w].astype(F32))
        dx = normalise_back(dn * gain_ref[...], xhat, rstd)
        win[w] = drs[u] + dx
    return carry


def back(late, pieces, gain, proj, outw, saved):
    consts = (gain, proj, outw)
    if late:
        shapes = [(2, 11, 28, 128), (2, 15, 28, 128), (4, 6, 28, 128)]
    else:
        shapes = [(2, 14, 28, 128), (2, 14, 28, 128)]
    return pl.pallas_call(
        functools.partial(back_kernel, late),
        out_shape=[jax.ShapeDtypeStruct(s, BF) for s in shapes],
        scratch_shapes=[
            pltpu.VMEM((4, 14, 40, 128), F32),
            pltpu.VMEM((8, ROWS, 128), F32),
        ],
        compiler_params=params(),
        cost_estimate=cost(5.5),
    )(*pieces, *consts, *saved)


def merge_pairs(stage, gain_ref, weight):
    pairs = stage.shape[1]
    pieces = [
        stage[:, :, q % 2, pl.ds(q // 2, 16, stride=2), :].reshape(WT * pairs * 16, 128)
        for q in range(4)
    ]
    xhat, rstd = normalise(jnp.concatenate(pieces, 1))
    merged = dot((xhat * gain_ref[...]).astype(BF), weight).astype(BF).astype(F32)
    return merged, xhat, rstd


def merge_pairs_back(grad, xhat, rstd, gain_ref, weight, stage):
    pairs = stage.shape[1]
    dn = dot_nt(grad.astype(BF), weight)
    dg = normalise_back(dn * gain_ref[...], xhat, rstd)
    for q in range(4):
        stage[:, :, q % 2, pl.ds(q // 2, 16, stride=2), :] = dg[
            :, 128 * q : 128 * q + 128
        ].reshape(WT, pairs, 16, 128)


def put_pair_row(stage, at, values):
    stage[:, at // 2, at % 2, 0:28, :] = values.astype(F32)


def clear_pads(stage):
    stage[:, :, :, 28:32, :] = jnp.zeros((WT, stage.shape[1], 2, 4, 128), F32)


def pair_row(stage, at):
    return stage[:, at // 2, at % 2, 0:28, :].astype(BF)


def fold_merged(merged, pairs):
    halves = [
        merged[:, 128 * i : 128 * i + 128].reshape(WT, pairs, 16, 128)[:, :, 0:14] for i in range(2)
    ]
    return jnp.concatenate(halves, 2)


def unfold_merged(folded):
    pad = jnp.zeros(folded.shape[:2] + (2, 128), F32)
    halves = [
        jnp.concatenate([folded[:, :, 14 * i : 14 * i + 14], pad], 2).reshape(-1, 128)
        for i in range(2)
    ]
    return jnp.concatenate(halves, 1)


def send_kernel(res_ref, gain_ref, weight_ref, send_ref, xhat_ref, rstd_ref, stage):
    clear_pads(stage)
    for i in range(8):
        put_pair_row(stage, i, res_ref[:, 1 + i])
    merged, xhat, rstd = merge_pairs(stage, gain_ref, weight_ref[...])
    xhat_ref[...] = xhat
    rstd_ref[...] = jnp.broadcast_to(rstd, rstd_ref.shape)
    send_ref[:, 0:1] = res_ref[:, 0:1]
    send_ref[:, 1:5] = fold_merged(merged, 4).astype(BF)


def local_kernel(resA_ref, resB_ref, gain_ref, weight_ref, merged_ref, xhat_ref, rstd_ref, stage):
    clear_pads(stage)
    for i in range(5):
        put_pair_row(stage, i, resA_ref[:, i])
    for i in range(13):
        put_pair_row(stage, 5 + i, resB_ref[:, i])
    merged, xhat, rstd = merge_pairs(stage, gain_ref, weight_ref[...])
    xhat_ref[...] = xhat
    rstd_ref[...] = jnp.broadcast_to(rstd, rstd_ref.shape)
    merged_ref[...] = merged


def local_back_kernel(
    grad_ref, d30_ref, xhat_ref, rstd_ref, gain_ref, weight_ref, dA_ref, dB_ref, stage
):
    merge_pairs_back(
        grad_ref[...], xhat_ref[...], rstd_ref[:, 0:1], gain_ref, weight_ref[...], stage
    )
    for i in range(5):
        dA_ref[:, i] = pair_row(stage, i)
    for i in range(13):
        dB_ref[:, i] = pair_row(stage, 5 + i)
    dB_ref[:, 13] = d30_ref[...]


def receive_kernel(got_ref, xhat_ref, rstd_ref, gain_ref, weight_ref, d_ref, stage):
    grad = unfold_merged(got_ref[:, 1:5].astype(F32))
    merge_pairs_back(grad, xhat_ref[...], rstd_ref[:, 0:1], gain_ref, weight_ref[...], stage)
    d_ref[:, 0:1] = got_ref[:, 0:1]
    for i in range(8):
        d_ref[:, 1 + i] = pair_row(stage, i)


def merge_call(kernel, us, shapes, pairs, *operands):
    return pl.pallas_call(
        kernel,
        out_shape=[jax.ShapeDtypeStruct(shape, kind) for shape, kind in shapes],
        scratch_shapes=[pltpu.VMEM((WT, pairs, 2, 32, 128), F32)],
        compiler_params=params(),
        cost_estimate=cost(us),
    )(*operands)


def middle_kernel(
    merged_ref, resB_ref, next_ref, cot_ref, cta_ref, cha_ref, cdg_ref,
    mg1_ref, mg2_ref, g3_ref, row_ref, col_ref, mw1_hbm, mw2_hbm, p3_hbm, biasA_hbm, biasB_hbm, ow3_hbm,
    dm_ref, d30_ref, dN_ref, so_ref, sta_ref, sha_ref,
    stage, stage2, xhat2, rstd2, cotw, k_s, v_s, qT_s, kT_s, vT_s, probs_s, oT_s, inv_s, doT_s, dqkv_s,
    mw1_ref, mw2_ref, p3_ref, bias_ref, ow3_ref, sems,
):
    fetches = [
        pltpu.make_async_copy(there, here, sems.at[i])
        for i, (there, here) in enumerate(
            (
                (ow3_hbm, ow3_ref),
                (mw1_hbm, mw1_ref),
                (mw2_hbm, mw2_ref),
                (p3_hbm, p3_ref),
                (biasA_hbm, bias_ref.at[:, 0 : ROWS // 2]),
                (biasB_hbm, bias_ref.at[:, ROWS // 2 : ROWS]),
            )
        )
    ]
    for fetch in fetches:
        fetch.start()
    cotw[...] = jnp.zeros((4, 7, 8, 512), F32)
    cotw[0:2, 0:4, 0:7, :] = cot_ref[2:4, 3:7].astype(F32)
    cotw[2:4, 0:4, 0:7, :] = unfold(cta_ref[:, 11:15].astype(F32))
    cotw[0:2, 4:7, 0:7, :] = unfold(cha_ref[:, 3:6].astype(F32))
    cotw[2:4, 4:7, 0:7, :] = unfold(cdg_ref[:, 3:6].astype(F32))

    fetches[0].wait()
    cot = cotw[...].reshape(ROWS, 512)
    cot_long = lengthen(cot.astype(BF))
    doT = dot_nt(ow3_ref[...], cot_long)
    for g in range(4):
        doT_s[g] = doT[128 * g : 128 * g + 128]

    def put_merged(first, count, values):
        for half in range(2):
            block = values[:, 128 * half : 128 * half + 128].reshape(WT, count, 16, 128)
            for i in range(count):
                stage2[half, :, (first + i) // 2, (first + i) % 2] = block[:, i]

    def take_merged(first, count):
        halves = [
            jnp.concatenate(
                [
                    stage2[half, :, (first + i) // 2, (first + i) % 2].reshape(WT, 1, 16, 128)
                    for i in range(count)
                ],
                1,
            ).reshape(WT * count * 16, 128)
            for half in range(2)
        ]
        return jnp.concatenate(halves, 1)

    put_merged(0, 9, merged_ref[...])
    put_merged(10, 4, unfold_merged(next_ref[:, 1:5].astype(F32)))
    clear_pads(stage)
    put_pair_row(stage, 0, resB_ref[:, 13])
    put_pair_row(stage, 1, next_ref[:, 0])
    fetches[1].wait()
    merged, xhat_seam, rstd_seam = merge_pairs(stage, mg1_ref, mw1_ref[...])
    put_merged(9, 1, merged)
    fetches[2].wait()
    pieces = [
        stage2[half, :, :, q % 2, pl.ds(q // 2, 8, stride=2), :].reshape(ROWS, 128)
        for q in range(4)
        for half in range(2)
    ]
    xhat, rstd = normalise(jnp.concatenate(pieces, 1))
    xhat2[...] = xhat
    rstd2[...] = jnp.broadcast_to(rstd, (ROWS, 128))
    merged_two = dot((xhat * mg2_ref[...]).astype(BF), mw2_ref[...]).astype(BF).astype(F32)
    xhat3, rstd3 = normalise(merged_two)
    n3 = (xhat3 * g3_ref[...]).astype(BF)
    fetches[3].wait()
    packed = [dot(n3, p3_ref[:, 512 * i : 512 * i + 512]) for i in range(3)]
    for g in range(4):
        q, k, v = (part[:, 128 * g : 128 * g + 128] for part in packed)
        q = lengthen((q * (SCALE * LOG2E)).astype(BF))
        k, v = k.astype(BF), v.astype(BF)
        k_s[g] = k
        v_s[g] = v
        qT_s[g] = q.T
        kT_s[g] = lengthen(k).T
        vT_s[g] = lengthen(v).T
    mask = region_mask(col_ref[...], row_ref[...])
    fetches[4].wait()
    fetches[5].wait()

    operands = []
    for g in range(4):

        def keep(h, probs, g=g):
            probs_s[g * 4 + h] = probs

        operands.append((k_s[g], qT_s[g], vT_s[g], mask, lambda h, g=g: bias_ref[g * 4 + h], keep))
    for g, (oT, inverse) in enumerate(attend_four(operands)):
        oT_s[g] = oT
        inv_s[g] = inverse
    att = jnp.concatenate([oT_s[g].astype(BF).T[:ROWS] for g in range(4)], 1)
    mixed = dot(att, ow3_ref[...]).astype(BF).astype(F32)
    section = (merged_two + mixed).reshape(4, 7, 8, 512)
    section = fold(section[:, :, 0:7])
    so_ref[...] = section[0:2, 0:4].astype(BF)
    sta_ref[...] = section[2:4].astype(BF)
    sha_ref[...] = section[0:2, 4:7].astype(BF)


    operands = [
        (v_s[g], qT_s[g], kT_s[g], oT_s[g], doT_s[g], inv_s[g], lambda h, g=g: probs_s[g * 4 + h])
        for g in range(4)
    ]
    for g, (dq, dk, dv) in enumerate(attend_four_back(operands)):
        dqkv_s[g] = dq
        dqkv_s[4 + g] = dk
        dqkv_s[8 + g] = dv
    dpacked = jnp.concatenate([dqkv_s[i] for i in range(12)], 1)
    dn3 = dot_nt(dpacked, p3_ref[...])
    dm2 = cot + normalise_back(dn3 * g3_ref[...], xhat3, rstd3)
    dn2 = dot_nt(dm2.astype(BF), mw2_ref[...])
    dg2 = normalise_back(dn2 * mg2_ref[...], xhat2[...], rstd2[:, 0:1])
    for q in range(4):
        for half in range(2):
            at = 256 * q + 128 * half
            stage2[half, :, :, q % 2, pl.ds(q // 2, 8, stride=2), :] = dg2[:, at : at + 128].reshape(
                4, 7, 8, 128
            )

    dm_ref[...] = take_merged(0, 9)
    merge_pairs_back(take_merged(9, 1), xhat_seam, rstd_seam, mg1_ref, mw1_ref[...], stage)
    d30_ref[...] = pair_row(stage, 0)
    dN_ref[:, 0] = pair_row(stage, 1)
    dN_ref[:, 1:5] = fold_merged(take_merged(10, 4), 4).astype(BF)


def middle(*operands):
    shapes = [
        (4, 28, 128), (4, 5, 28, 128), (2, 4, 28, 128), (2, 7, 28, 128), (2, 3, 28, 128),
    ]
    return pl.pallas_call(
        middle_kernel,
        in_specs=[pl.BlockSpec(memory_space=pltpu.VMEM)] * 12
        + [pl.BlockSpec(memory_space=pl.ANY)] * 6,
        out_shape=[jax.ShapeDtypeStruct((576, 256), F32)]
        + [jax.ShapeDtypeStruct(s, BF) for s in shapes],
        scratch_shapes=[
            pltpu.VMEM((4, 1, 2, 32, 128), F32),
            pltpu.VMEM((2, 4, 7, 2, 16, 128), F32),
            pltpu.VMEM((ROWS, 1024), F32),
            pltpu.VMEM((ROWS, 128), F32),
            pltpu.VMEM((4, 7, 8, 512), F32),
            pltpu.VMEM((4, ROWS, 128), BF),
            pltpu.VMEM((4, ROWS, 128), BF),
            pltpu.VMEM((4, 128, LANES), BF),
            pltpu.VMEM((4, 128, LANES), BF),
            pltpu.VMEM((4, 128, LANES), BF),
            pltpu.VMEM((16, ROWS, LANES), BF),
            pltpu.VMEM((4, 128, LANES), F32),
            pltpu.VMEM((4, 8, LANES), F32),
            pltpu.VMEM((4, 128, LANES), F32),
            pltpu.VMEM((12, ROWS, 128), BF),
            pltpu.VMEM((512, 256), BF),
            pltpu.VMEM((1024, 512), BF),
            pltpu.VMEM((512, 1536), BF),
            pltpu.VMEM((HEADS3, ROWS, LANES), F32),
            pltpu.VMEM((512, 512), BF),
            pltpu.SemaphoreType.DMA((6,)),
        ],
        compiler_params=params(28),
        cost_estimate=cost(9),
    )(*operands)


def join_kernel(ta_ref, own_ref, so_ref, grad_ref, section_ref, wide, narrow):
    for t in range(WT):
        wide[:, pl.ds(t, 28, stride=4), :] = (ta_ref if t < 2 else own_ref)[t % 2, 0:11].astype(F32)
        low = (ta_ref[t, 11:15] if t < 2 else so_ref[t - 2]).astype(F32)
        for g in range(4):
            narrow[g, :, pl.ds(t, 7, stride=4), :] = low[:, 7 * g : 7 * g + 7]
    for i in range(11):
        grad_ref[17 + i] = wide[i].reshape(28, 4, 128).astype(BF)
    for i in range(4):
        row = jnp.concatenate([narrow[g, i] for g in range(4)], 1)
        section_ref[3 + i] = row.reshape(7, 4, 512).astype(BF)


JOINED = [
    jax.ShapeDtypeStruct((28, 28, 4, 128), BF),
    jax.ShapeDtypeStruct((7, 7, 4, 512), BF),
]


def join(ta, own, section_own):
    return pl.pallas_call(
        join_kernel,
        out_shape=JOINED,
        scratch_shapes=[pltpu.VMEM((11, 112, 128), F32), pltpu.VMEM((4, 4, 28, 128), F32)],
        compiler_params=params(),
        cost_estimate=cost(2),
    )(ta, own, section_own)


def last_kernel(
    grad_hbm, section_hbm, ta_ref, own_ref, dg_ref, ha_ref, grad_out, section_out,
    wide, narrow, rows, section_rows, sems,
):
    del grad_hbm, section_hbm
    for t in range(WT):
        corner = dg_ref if t < 2 else ha_ref
        wide[0:3, pl.ds(t, 28, stride=4), :] = corner[t % 2, 0:3].astype(F32)
        wide[3:17, pl.ds(t, 28, stride=4), :] = (ta_ref if t < 2 else own_ref)[t % 2].astype(F32)
        high = corner[t % 2, 3:6].astype(F32)
        for g in range(4):
            narrow[g, :, pl.ds(t, 7, stride=4), :] = high[:, 7 * g : 7 * g + 7]
    for i in range(17):
        rows[i] = wide[i].reshape(28, 4, 128).astype(BF)
    copy = pltpu.make_async_copy(rows, grad_out.at[0:17], sems.at[0])
    copy.start()
    for i in range(3):
        row = jnp.concatenate([narrow[g, i] for g in range(4)], 1)
        section_rows[i] = row.reshape(7, 4, 512).astype(BF)
    other = pltpu.make_async_copy(section_rows, section_out.at[0:3], sems.at[1])
    other.start()
    copy.wait()
    other.wait()


def join_last(grad, section, ta, own, dg, ha):
    return pl.pallas_call(
        last_kernel,
        in_specs=[pl.BlockSpec(memory_space=pl.ANY)] * 2
        + [pl.BlockSpec(memory_space=pltpu.VMEM)] * 4,
        out_specs=[pl.BlockSpec(memory_space=pl.ANY)] * 2,
        out_shape=JOINED,
        scratch_shapes=[
            pltpu.VMEM((17, 112, 128), F32),
            pltpu.VMEM((4, 3, 28, 128), F32),
            pltpu.VMEM((17, 28, 4, 128), BF),
            pltpu.VMEM((3, 7, 4, 512), BF),
            pltpu.SemaphoreType.DMA((2,)),
        ],
        input_output_aliases={0: 0, 1: 1},
        compiler_params=params(),
        cost_estimate=cost(1),
    )(grad, section, ta, own, dg, ha)


IN_ORDER = Layout(major_to_minor=(0, 1, 2, 3))


def inward(values):
    return with_layout_constraint(jnp.transpose(values, (1, 2, 0, 3)), IN_ORDER)


def outward(values):
    return jnp.transpose(with_layout_constraint(values, IN_ORDER), (2, 0, 1, 3))


def send(values, axes, by):
    axes = axes.split()
    sizes = [lax.axis_size(a) for a in axes]
    if len(axes) == 1:
        pairs = [(i, (i + by) % sizes[0]) for i in range(sizes[0])]
    else:
        n, m = sizes
        pairs = [
            (i * m + j, (i + by) % n * m + (j + by) % m) for i in range(n) for j in range(m)
        ]
    return lax.ppermute(values, tuple(axes), pairs)


def per_device(
    tokens,
    regions_one,
    regions_three,
    gain_one,
    projection_one,
    outward_one,
    table_one,
    merge_gain_one,
    merge_weight_one,
    merge_gain_two,
    merge_weight_two,
    gain_three,
    projection_three,
    outward_three,
    table_three,
    cotangent,
):
    (early,) = arrange(early_kernel, (14,), tokens)
    ta_early = send(inward(early), "ta", -1)
    late, ha_late, dg_late = arrange(late_kernel, (15, 6, 6), tokens, cotangent)
    ha_late = send(ha_late, "ha", -1)
    dg_late = send(dg_late, "ha ta", -1)
    ta_late = send(inward(late), "ta", -1)
    bias_one, spread, row_one, row_three, col_one, col_three = prepare(
        table_one, table_three, regions_one, regions_three
    )
    gain, merge_gain, seam = gain_one[None], merge_gain_one[None], merge_weight_one
    args = (gain, projection_one, outward_one, bias_one, spread)
    (res_send, res_a, bias_a), saved_a = front(False, (tokens, outward(ta_early)), *args, row_one, col_one)
    row_send, *early_norm = merge_call(
        send_kernel, 0.5, [((4, 5, 28, 128), BF), ((256, 512), F32), ((256, 128), F32)], 4,
        res_send, merge_gain, seam,
    )
    row_next = send(row_send, "ha", -1)
    ta_late, res_a = lax.optimization_barrier((ta_late, res_a))
    ta_late = outward(ta_late)
    (res_b, bias_b), saved_b = front(True, (tokens, ta_late, ha_late, dg_late), *args, row_one, col_one)
    merged, *local_norm = merge_call(
        local_kernel, 0.1, [((576, 256), F32), ((576, 512), F32), ((576, 128), F32)], 9,
        res_a, res_b, merge_gain, seam,
    )
    row_next, merged = lax.optimization_barrier((row_next, merged))
    d_merged, d_30, d_send, sec_own, sec_ta, sec_ha = middle(
        merged, res_b, row_next, cotangent, ta_late, ha_late, dg_late,
        merge_gain, merge_gain_two[None], gain_three[None], row_three, col_three,
        merge_weight_one, merge_weight_two, projection_three, bias_a, bias_b, outward_three,
    )
    d_prev = send(d_send, "ha", 1)
    d_a, d_b = merge_call(
        local_back_kernel, 1, [((4, 5, 28, 128), BF), ((4, 14, 28, 128), BF)], 9,
        d_merged, d_30, *local_norm, merge_gain, seam,
    )
    own_b, ta_b, ha_b = back(
        True, (d_b, sec_ta, sec_ha), gain, projection_one, outward_one, saved_b
    )
    d_prev, own_b = lax.optimization_barrier((d_prev, own_b))
    ta_b = send(inward(ta_b), "ta", 1)
    ha_b = send(ha_b, "ha", 1)
    (d_first,) = merge_call(
        receive_kernel, 0.5, [((4, 9, 28, 128), BF)], 4, d_prev, *early_norm, merge_gain, seam
    )
    own_a, ta_a = back(False, (d_first, d_a), gain, projection_one, outward_one, saved_a)
    ta_b, ha_b, own_a = lax.optimization_barrier((ta_b, ha_b, own_a))
    ta_a = send(inward(ta_a), "ta", 1)
    dg_b = send(ha_b[2:], "ta", 1)
    grad, section = join(outward(ta_b), own_b, sec_own)
    ta_a, dg_b, grad = lax.optimization_barrier((ta_a, dg_b, grad))
    grad, section = join_last(grad, section, outward(ta_a), own_a, dg_b, ha_b)
    return (jnp.transpose(section, (2, 0, 1, 3)), jnp.transpose(grad, (2, 0, 1, 3)))


def solution(mesh):
    tile = P(("col", "ta"), "ha", None, None)
    ids = P(("col", "ta"), "ha", None)
    in_specs = (tile, ids, ids) + (P(),) * 12 + (tile,)
    return jax.shard_map(
        per_device, mesh=mesh, in_specs=in_specs, out_specs=(tile, tile), check_vma=False
    )
```

```python
import functools

import jax
import jax.numpy as jnp
import numpy as np
from jax import lax
from jax.experimental import pallas as pl
from jax.experimental.layout import Layout, with_layout_constraint
from jax.experimental.pallas import tpu as pltpu
from jax.sharding import PartitionSpec as P

HEADS1 = 4
HEADS3 = 16
WT = 4
WS = 7
ST = 2
SS = 3
EPSILON = 1e-05
NREL = 1183
LOG2E = 1.4426950408889634
HEAD = 32
SCALE = HEAD**-0.5
ROWS = WT * WS * 8
LANES = 256
SPAN = 1280
GONE = -1e30
PER_STEP = 8
STEPS = 8 // PER_STEP
BF = jnp.bfloat16
F32 = jnp.float32


def dot(a, b):
    return jnp.dot(a, b, preferred_element_type=F32)


def dot_nt(a, b):
    return lax.dot_general(a, b, (((1,), (1,)), ((), ())), preferred_element_type=F32)


def params(limit=20):
    return pltpu.CompilerParams(vmem_limit_bytes=limit * 1024 * 1024)


def cost(us):
    return pl.CostEstimate(flops=int(us * 1.1e9), bytes_accessed=int(us * 1e6), transcendentals=0)


def normalise(x):
    centred = x - jnp.mean(x, -1, keepdims=True)
    rstd = lax.rsqrt(jnp.mean(centred * centred, -1, keepdims=True) + EPSILON)
    return centred * rstd, rstd


def normalise_back(grad, xhat, rstd):
    return rstd * (
        grad
        - jnp.mean(grad, -1, keepdims=True)
        - xhat * jnp.mean(grad * xhat, -1, keepdims=True)
    )


def head_rows(x, h):
    return x[HEAD * h : HEAD * (h + 1)]


def head_of_lane(shape):
    return lax.broadcasted_iota(jnp.int32, shape, 1) // HEAD


def by_head(x):
    lane = head_of_lane((1, 128))
    return jnp.concatenate([x * (lane == h).astype(F32).astype(BF) for h in range(4)], 0)


def pick_heads(stacked):
    lane = head_of_lane((ROWS, 128))
    got = stacked[:ROWS]
    for h in range(1, 4):
        got = jnp.where(lane == h, stacked[ROWS * h : ROWS * (h + 1)], got)
    return got


def lengthen(x):
    return jnp.concatenate([x, jnp.zeros((LANES - ROWS, x.shape[1]), x.dtype)], 0)


def region_mask(column, row):
    return jnp.where(jnp.concatenate([column, column], 1) == row, 0.0, GONE).astype(F32)


def stagger(pending):
    pending, active = list(pending), []
    while pending or active:
        if pending:
            active.append(pending.pop(0))
        active = [g for g in active if next(g, "end") is None]


def attend_four(k, qT, vT, mask, bias_at, keep_probs):
    scores = dot(by_head(k), qT)
    yield
    outs, inverses = [], []
    for h in range(4):
        biased = scores[ROWS * h : ROWS * (h + 1)] + (bias_at(h) + mask)
        peak = jnp.max(biased, 0, keepdims=True)
        probs = jnp.exp2(biased - peak).astype(BF)
        keep_probs(h, probs)
        extended = jnp.concatenate([head_rows(vT, h)[:, :ROWS], jnp.ones((16, ROWS), BF)], 0)
        out = dot(extended, probs)
        inverse = 1.0 / out[HEAD : HEAD + 1]
        outs.append(out[:HEAD] * inverse)
        inverses.append(inverse)
    yield
    return jnp.concatenate(outs, 0), jnp.concatenate(inverses + inverses, 0)


def attend_four_back(v, qT, kT, oT, doT, inverse, probs_at):
    scaled, deltas = [], []
    for h in range(4):
        part = head_rows(doT, h) * inverse[h : h + 1]
        deltas.append(jnp.sum(part * head_rows(oT, h), 0, keepdims=True))
        scaled.append(part)
    scaled = jnp.concatenate(scaled, 0).astype(BF)
    dprobs = dot(by_head(v), scaled)
    yield
    probs = [probs_at(h) for h in range(4)]
    dscores = [
        (probs[h].astype(F32) * (dprobs[ROWS * h : ROWS * (h + 1)] - deltas[h])).astype(BF)
        for h in range(4)
    ]
    dv = pick_heads(dot_nt(jnp.concatenate(probs, 0), scaled))
    yield
    dk = pick_heads(dot_nt(jnp.concatenate(dscores, 0), qT))
    dqT = jnp.concatenate([dot(head_rows(kT, h)[:, :ROWS], dscores[h]) for h in range(4)], 0)
    yield
    dq = (dqT * SCALE).astype(BF).T[:ROWS]
    return dq, (dk * (1.0 / LOG2E)).astype(BF), dv.astype(BF)


def lanes_of(shape):
    return lax.broadcasted_iota(jnp.int32, shape, 1)


def region_rows(ids, section):
    columns = ids.shape[1]
    count = columns // WS
    place = lax.broadcasted_iota(jnp.int32, (columns, LANES * count), 0)
    lane = lanes_of((columns, LANES * count))
    column = lane % 8
    real = (column < WS) & (lane % LANES < ROWS)
    if section == 3:
        column = jnp.where(column < 3, column + 4, column - 3)
    chosen = real & (place == lane // LANES * WS + column)
    spread = dot(ids.astype(F32).astype(BF), chosen.astype(F32).astype(BF))
    row = lax.broadcasted_iota(jnp.int32, spread.shape, 0)
    lane = lanes_of(spread.shape)
    real = (lane[:1] % 8 < WS) & (lane[:1] % LANES < ROWS)
    rows = []
    for hw in range(ids.shape[0] // (WT * WS)):
        mine = lane % LANES // 8 == row % 4 * WS + row // 4 - WS * hw
        inside = (row >= WT * WS * hw) & (row < WT * WS * (hw + 1))
        found = jnp.sum(jnp.where(mine & inside, spread, 0.0), 0, keepdims=True)
        found = jnp.where(real, found, -1.0)
        rows += [found[:, LANES * ww : LANES * (ww + 1)] for ww in range(count)]
    return rows


def region_columns(ids, section):
    columns = ids.shape[1]
    count = columns // WS
    source = ids.astype(F32).astype(BF)
    token = lax.broadcasted_iota(jnp.int32, (ROWS, ids.shape[0]), 0)
    place = lanes_of((ROWS, ids.shape[0]))
    column = lax.broadcasted_iota(jnp.int32, (ROWS, columns), 0) % 8
    lane = lanes_of((ROWS, columns))
    if section == 3:
        column = jnp.where(column < 3, column + 4, jnp.where(column == 7, 8, column - 3))
    ones = jnp.ones((columns, 128), BF)
    pad = lax.broadcasted_iota(jnp.int32, (ROWS, 128), 0) % 8 == 7
    found = []
    for hw in range(ids.shape[0] // (WT * WS)):
        chosen = place == (token // 8 % WS + WS * hw) * WT + token // 56
        picked = dot(chosen.astype(F32).astype(BF), source)
        for ww in range(count):
            mine = jnp.where(lane == WS * ww + column, picked, 0.0).astype(BF)
            found.append(jnp.where(pad, -1.0, dot(mine, ones)))
    return found


def bias_rows(spread, at, heads, tj, hj):
    lane = lanes_of((heads * 8, 128))
    p0, p1, p2, p3 = (
        pltpu.roll(
            spread[ti - tj + 3, at : at + heads * 8, :], (ti * 56 - (6 - hj) * 8) % 128, 1
        )
        for ti in range(WT)
    )
    left = jnp.where(lane < 56, p0, jnp.where(lane < 112, p1, p2))
    right = jnp.where(lane < 40, p2, p3)
    return left.reshape(heads, 8, 128), right.reshape(heads, 8, 128)


def prepare_kernel(
    t1_ref, t3_ref, s_ref, r1_ref, r3_ref, o1_ref, spread, row1_ref, row3_ref, col1_ref, col3_ref, tab
):
    tab[...] = jnp.zeros((24, SPAN), F32)
    tab[0:4, 0:NREL] = t1_ref[...] * LOG2E
    tab[8:24, 0:NREL] = t3_ref[...] * LOG2E
    slabs = []
    for dt in range(7):
        start = 169 * dt
        low = start // 128 * 128
        run = tab[:, low : low + 384]
        if start > low:
            run = pltpu.roll(run, 384 - (start - low), 1)
        slabs.append(run[:, :256])
    left = jnp.concatenate(slabs, 0)
    first = left.astype(BF)
    rest = left - first.astype(F32)
    second = rest.astype(BF)
    third = (rest - second.astype(F32)).astype(BF)
    chosen = s_ref[...]
    got = dot(first, chosen) + dot(second, chosen) + dot(third, chosen)
    lane16 = lanes_of((16, 128))
    for dt in range(7):
        for wj in range(8):
            part = got[24 * dt : 24 * dt + 24, 128 * wj : 128 * wj + 128]
            spread[dt, pl.ds(wj, 8, stride=8), :] = part[0:8]
            later = part[8:24]
            turned = jnp.where(lane16 % 8 < 3, pltpu.roll(later, 124, 1), pltpu.roll(later, 3, 1))
            spread[dt, pl.ds(64 + (7 if wj == 7 else (wj + 3) % 7), 16, stride=8), :] = turned
    for tj in range(WT):
        for hj in range(WS):
            row = (tj * WS + hj) * 8
            left, right = bias_rows(spread, 0, HEADS1, tj, hj)
            o1_ref[:, row : row + 8, 0:128] = left
            o1_ref[:, row : row + 8, 128:256] = right
    for i, found in enumerate(region_rows(r1_ref[...], 1)):
        row1_ref[i] = found
    row3_ref[...] = region_rows(r3_ref[...], 3)[0]
    for i, found in enumerate(region_columns(r1_ref[...], 1)):
        col1_ref[i] = found
    col3_ref[...] = region_columns(r3_ref[...], 3)[0]


def chooser():
    chosen = np.zeros((256, 1024), np.float32)
    for wj in range(WS):
        for dh in range(13):
            for wi in range(WS):
                chosen[dh * 13 + wi - wj + 6, wj * 128 + dh * 8 + wi] = 1.0
    return jnp.asarray(chosen, BF)


def by_height(ids):
    return jnp.transpose(ids, (1, 0, 2)).reshape(-1, ids.shape[2])


def prepare(table_one, table_three, regions_one, regions_three):
    return pl.pallas_call(
        prepare_kernel,
        out_shape=(
            jax.ShapeDtypeStruct((HEADS1, ROWS, LANES), F32),
            jax.ShapeDtypeStruct((7, 24 * 8, 128), F32),
            jax.ShapeDtypeStruct((16, 1, LANES), F32),
            jax.ShapeDtypeStruct((1, LANES), F32),
            jax.ShapeDtypeStruct((16, ROWS, 128), F32),
            jax.ShapeDtypeStruct((ROWS, 128), F32),
        ),
        scratch_shapes=[pltpu.VMEM((24, SPAN), F32)],
        compiler_params=params(),
        cost_estimate=cost(1.5),
    )(
        jnp.transpose(table_one),
        jnp.transpose(table_three),
        chooser(),
        by_height(regions_one),
        by_height(regions_three),
    )


def fold(values):
    return jnp.concatenate([values[..., 128 * g : 128 * g + 128] for g in range(4)], -2)


def unfold(values):
    return jnp.concatenate([values[..., 7 * g : 7 * g + 7, :] for g in range(4)], -1)


def early_kernel(tok_ref, early_ref):
    early_ref[...] = tok_ref[0:2, 3:17]


def late_kernel(tok_ref, cot_ref, late_ref, ha_ref, dg_ref):
    late_ref[:, 0:11] = tok_ref[0:2, 17:28]
    late_ref[:, 11:15] = fold(cot_ref[0:2, 3:7].astype(F32)).astype(BF)
    ha_ref[:, 0:3] = tok_ref[2:4, 0:3]
    ha_ref[:, 3:6] = fold(cot_ref[2:4, 0:3].astype(F32)).astype(BF)
    dg_ref[:, 0:3] = tok_ref[0:2, 0:3]
    dg_ref[:, 3:6] = fold(cot_ref[0:2, 0:3].astype(F32)).astype(BF)


def arrange(kernel, rows, *operands):
    return pl.pallas_call(
        kernel,
        out_shape=[jax.ShapeDtypeStruct((2, n, 28, 128), BF) for n in rows],
        compiler_params=params(8),
        cost_estimate=cost(0.3),
    )(*operands)


def put_rows(stage, frames, rows, values):
    values = values.astype(F32)
    stage[frames, rows, 0:28, :] = values
    stage[frames, rows, 28:36, :] = values[:, :, 0:8, :]


def cut_windows(stage, win):
    for hw in range(2):
        for ww in range(4):
            win[hw * 4 + ww] = stage[:, 7 * hw : 7 * hw + 7, 3 + 7 * ww : 11 + 7 * ww, :].reshape(
                ROWS, 128
            )


def join_windows(win, stage):
    for hw in range(2):
        for ww in range(4):
            stage[:, 7 * hw : 7 * hw + 7, 3 + 7 * ww : 11 + 7 * ww, :] = win[hw * 4 + ww].reshape(
                WT, WS, 8, 128
            )
    stage[:, :, 0:3, :] = stage[:, :, 28:31, :]


def front_kernel(late, *refs):
    n_in = 4 if late else 2
    pieces, refs = refs[:n_in], refs[n_in:]
    gain_ref, proj_ref, outw_ref, bias_ref, spread_ref, row_ref, col_ref = refs[:7]
    refs = refs[7:]
    n_out = 1 if late else 2
    outs, refs = refs[:n_out], refs[n_out:]
    b3_ref, xw_ref, kv_ref, t_ref, p_ref, o_ref, inv_ref, stage, win = refs
    own = pieces[0]
    if late:
        put_rows(stage, slice(0, 2), slice(0, 11), own[2:4, 17:28])
        put_rows(stage, slice(2, 4), slice(0, 11), pieces[1][:, 0:11])
        put_rows(stage, slice(0, 2), slice(11, 14), pieces[2][:, 0:3])
        put_rows(stage, slice(2, 4), slice(11, 14), pieces[3][:, 0:3])
    else:
        put_rows(stage, slice(0, 2), slice(0, 14), own[2:4, 3:17])
        put_rows(stage, slice(2, 4), slice(0, 14), pieces[1][...])
    cut_windows(stage, win)
    lax.fori_loop(
        0,
        STEPS,
        functools.partial(
            front_step, late, gain_ref, proj_ref, outw_ref, bias_ref, spread_ref, row_ref, col_ref,
            b3_ref, xw_ref, kv_ref, t_ref, p_ref, o_ref, inv_ref, win,
        ),
        0,
    )
    join_windows(win, stage)
    if late:
        outs[0][...] = stage[:, :, 0:28, :].astype(BF)
    else:
        outs[0][...] = stage[:, 0:9, 0:28, :].astype(BF)
        outs[1][...] = stage[:, 9:14, 0:28, :].astype(BF)


def front_step(
    late, gain_ref, proj_ref, outw_ref, bias_ref, spread_ref, row_ref, col_ref,
    b3_ref, xw_ref, kv_ref, t_ref, p_ref, o_ref, inv_ref, win, step, carry,
):
    first = 8 * late
    for i in range(2 // STEPS):
        tj = step * (2 // STEPS) + i
        for hj in range(WS):
            left, right = bias_rows(spread_ref, 64, HEADS3, 2 * late + tj, hj)
            at = pl.ds(pl.multiple_of((tj * WS + hj) * 8, 8), 8)
            b3_ref[:, at, 0:128] = left
            b3_ref[:, at, 128:256] = right

    def window(w):
        x = win[w]
        xw_ref[w] = x.astype(BF)
        xhat, _ = normalise(x)
        packed = dot((xhat * gain_ref[...]).astype(BF), proj_ref[...])
        q = (packed[:, :128] * (SCALE * LOG2E)).astype(BF)
        kv = packed[:, 128:].astype(BF)
        kv_ref[w] = kv
        qT, kT, vT = (lengthen(part).T for part in (q, kv[:, :128], kv[:, 128:]))
        t_ref[w, :128] = qT
        t_ref[w, 128:] = kT

        def keep(h, probs):
            p_ref[w, h] = probs

        mask = region_mask(col_ref[first + w], row_ref[first + w])
        yield
        oT, inverse = yield from attend_four(
            kv[:, :128], qT, vT, mask, lambda h: bias_ref[h], keep
        )
        oT = oT.astype(BF)
        o_ref[w] = oT
        inv_ref[w] = inverse
        mixed = dot(oT.T[:ROWS], outw_ref[...]).astype(BF).astype(F32)
        win[w] = x + mixed

    stagger(window(step * PER_STEP + u) for u in range(PER_STEP))
    return carry


SAVED = (
    ((ROWS, 128), BF),
    ((ROWS, 256), BF),
    ((256, LANES), BF),
    ((4, ROWS, LANES), BF),
    ((128, LANES), BF),
    ((8, LANES), F32),
)


def front(late, pieces, gain, proj, outw, bias, spread, row, column):
    consts = (gain, proj, outw, bias, spread)
    shapes = [(4, 14, 28, 128)] if late else [(4, 9, 28, 128), (4, 5, 28, 128)]
    out = pl.pallas_call(
        functools.partial(front_kernel, late),
        out_shape=[jax.ShapeDtypeStruct(s, BF) for s in shapes]
        + [jax.ShapeDtypeStruct((HEADS3, ROWS // 2, LANES), F32)]
        + [jax.ShapeDtypeStruct((8,) + s, d) for s, d in SAVED],
        scratch_shapes=[
            pltpu.VMEM((4, 14, 40, 128), F32),
            pltpu.VMEM((8, ROWS, 128), F32),
        ],
        compiler_params=params(),
        cost_estimate=cost(4.6),
    )(*pieces, *consts, row, column)
    return out[: len(shapes) + 1], out[len(shapes) + 1 :]


def back_kernel(late, *refs):
    n_in = 3 if late else 2
    pieces, refs = refs[:n_in], refs[n_in:]
    gain_ref, proj_ref, outw_ref = refs[:3]
    xw_ref, kv_ref, t_ref, p_ref, o_ref, inv_ref = refs[3:9]
    refs = refs[9:]
    n_out = 3 if late else 2
    outs, refs = refs[:n_out], refs[n_out:]
    stage, win = refs
    if late:
        put_rows(stage, slice(0, 4), slice(0, 14), pieces[0][...])
        outs[1][:, 11:15] = pieces[1][:, 0:4]
        outs[2][0:2, 3:6] = pieces[2][...]
        outs[2][2:4, 3:6] = pieces[1][:, 4:7]
    else:
        put_rows(stage, slice(0, 4), slice(0, 9), pieces[0][...])
        put_rows(stage, slice(0, 4), slice(9, 14), pieces[1][...])
    cut_windows(stage, win)
    lax.fori_loop(
        0,
        STEPS,
        functools.partial(
            back_step, gain_ref, proj_ref, outw_ref,
            xw_ref, kv_ref, t_ref, p_ref, o_ref, inv_ref, win,
        ),
        0,
    )
    join_windows(win, stage)
    if late:
        outs[0][...] = stage[0:2, 0:11, 0:28, :].astype(BF)
        outs[1][:, 0:11] = stage[2:4, 0:11, 0:28, :].astype(BF)
        outs[2][:, 0:3] = stage[:, 11:14, 0:28, :].astype(BF)
    else:
        outs[0][...] = stage[0:2, :, 0:28, :].astype(BF)
        outs[1][...] = stage[2:4, :, 0:28, :].astype(BF)


def back_step(
    gain_ref, proj_ref, outw_ref, xw_ref, kv_ref, t_ref, p_ref, o_ref, inv_ref, win, step, carry
):
    def window(w):
        dr = win[w]
        doT = dot_nt(outw_ref[...], lengthen(dr.astype(BF)))
        yield
        dq, dk, dv = yield from attend_four_back(
            kv_ref[w, :, 128:], t_ref[w, :128], t_ref[w, 128:], o_ref[w].astype(F32), doT,
            inv_ref[w], lambda h: p_ref[w, h],
        )
        dn = dot_nt(jnp.concatenate([dq, dk, dv], 1), proj_ref[...])
        yield
        xhat, rstd = normalise(xw_ref[w].astype(F32))
        win[w] = dr + normalise_back(dn * gain_ref[...], xhat, rstd)

    stagger(window(step * PER_STEP + u) for u in range(PER_STEP))
    return carry


def back(late, pieces, gain, proj, outw, saved):
    consts = (gain, proj, outw)
    if late:
        shapes = [(2, 11, 28, 128), (2, 15, 28, 128), (4, 6, 28, 128)]
    else:
        shapes = [(2, 14, 28, 128), (2, 14, 28, 128)]
    return pl.pallas_call(
        functools.partial(back_kernel, late),
        out_shape=[jax.ShapeDtypeStruct(s, BF) for s in shapes],
        scratch_shapes=[
            pltpu.VMEM((4, 14, 40, 128), F32),
            pltpu.VMEM((8, ROWS, 128), F32),
        ],
        compiler_params=params(),
        cost_estimate=cost(5.5),
    )(*pieces, *consts, *saved)


def merge_pairs(stage, gain_ref, weight):
    pairs = stage.shape[1]
    pieces = [
        stage[:, :, q % 2, pl.ds(q // 2, 16, stride=2), :].reshape(WT * pairs * 16, 128)
        for q in range(4)
    ]
    xhat, rstd = normalise(jnp.concatenate(pieces, 1))
    merged = dot((xhat * gain_ref[...]).astype(BF), weight).astype(BF).astype(F32)
    return merged, xhat, rstd


def merge_pairs_back(grad, xhat, rstd, gain_ref, weight, stage):
    pairs = stage.shape[1]
    dn = dot_nt(grad.astype(BF), weight)
    dg = normalise_back(dn * gain_ref[...], xhat, rstd)
    for q in range(4):
        stage[:, :, q % 2, pl.ds(q // 2, 16, stride=2), :] = dg[
            :, 128 * q : 128 * q + 128
        ].reshape(WT, pairs, 16, 128)


def put_pair_row(stage, at, values):
    stage[:, at // 2, at % 2, 0:28, :] = values.astype(F32)


def clear_pads(stage):
    stage[:, :, :, 28:32, :] = jnp.zeros((WT, stage.shape[1], 2, 4, 128), F32)


def pair_row(stage, at):
    return stage[:, at // 2, at % 2, 0:28, :].astype(BF)


def fold_merged(merged, pairs):
    halves = [
        merged[:, 128 * i : 128 * i + 128].reshape(WT, pairs, 16, 128)[:, :, 0:14] for i in range(2)
    ]
    return jnp.concatenate(halves, 2)


def unfold_merged(folded):
    pad = jnp.zeros(folded.shape[:2] + (2, 128), F32)
    halves = [
        jnp.concatenate([folded[:, :, 14 * i : 14 * i + 14], pad], 2).reshape(-1, 128)
        for i in range(2)
    ]
    return jnp.concatenate(halves, 1)


def send_kernel(res_ref, gain_ref, weight_ref, send_ref, xhat_ref, rstd_ref, stage):
    clear_pads(stage)
    for i in range(8):
        put_pair_row(stage, i, res_ref[:, 1 + i])
    merged, xhat, rstd = merge_pairs(stage, gain_ref, weight_ref[...])
    xhat_ref[...] = xhat
    rstd_ref[...] = jnp.broadcast_to(rstd, rstd_ref.shape)
    send_ref[:, 0:1] = res_ref[:, 0:1]
    send_ref[:, 1:5] = fold_merged(merged, 4).astype(BF)


def local_kernel(resA_ref, resB_ref, gain_ref, weight_ref, merged_ref, xhat_ref, rstd_ref, stage):
    clear_pads(stage)
    for i in range(5):
        put_pair_row(stage, i, resA_ref[:, i])
    for i in range(13):
        put_pair_row(stage, 5 + i, resB_ref[:, i])
    merged, xhat, rstd = merge_pairs(stage, gain_ref, weight_ref[...])
    xhat_ref[...] = xhat
    rstd_ref[...] = jnp.broadcast_to(rstd, rstd_ref.shape)
    merged_ref[...] = merged


def local_back_kernel(
    grad_ref, d30_ref, xhat_ref, rstd_ref, gain_ref, weight_ref, dA_ref, dB_ref, stage
):
    merge_pairs_back(
        grad_ref[...], xhat_ref[...], rstd_ref[:, 0:1], gain_ref, weight_ref[...], stage
    )
    for i in range(5):
        dA_ref[:, i] = pair_row(stage, i)
    for i in range(13):
        dB_ref[:, i] = pair_row(stage, 5 + i)
    dB_ref[:, 13] = d30_ref[...]


def receive_kernel(got_ref, xhat_ref, rstd_ref, gain_ref, weight_ref, d_ref, stage):
    grad = unfold_merged(got_ref[:, 1:5].astype(F32))
    merge_pairs_back(grad, xhat_ref[...], rstd_ref[:, 0:1], gain_ref, weight_ref[...], stage)
    d_ref[:, 0:1] = got_ref[:, 0:1]
    for i in range(8):
        d_ref[:, 1 + i] = pair_row(stage, i)


def merge_call(kernel, us, shapes, pairs, *operands):
    return pl.pallas_call(
        kernel,
        out_shape=[jax.ShapeDtypeStruct(shape, kind) for shape, kind in shapes],
        scratch_shapes=[pltpu.VMEM((WT, pairs, 2, 32, 128), F32)],
        compiler_params=params(),
        cost_estimate=cost(us),
    )(*operands)


def middle_kernel(
    merged_ref, resB_ref, next_ref, cot_ref, cta_ref, cha_ref, cdg_ref,
    mg1_ref, mg2_ref, g3_ref, row_ref, col_ref, mw1_hbm, mw2_hbm, p3_hbm, biasA_hbm, biasB_hbm, ow3_hbm,
    dm_ref, d30_ref, dN_ref, so_ref, sta_ref, sha_ref,
    stage, stage2, xhat2, rstd2, cotw, k_s, v_s, qT_s, kT_s, vT_s, probs_s, oT_s, inv_s, doT_s, dqkv_s,
    mw1_ref, mw2_ref, p3_ref, bias_ref, ow3_ref, sems,
):
    fetches = [
        pltpu.make_async_copy(there, here, sems.at[i])
        for i, (there, here) in enumerate(
            (
                (mw1_hbm, mw1_ref),
                (mw2_hbm, mw2_ref),
                (p3_hbm, p3_ref),
                (biasA_hbm, bias_ref.at[:, 0 : ROWS // 2]),
                (biasB_hbm, bias_ref.at[:, ROWS // 2 : ROWS]),
                (ow3_hbm, ow3_ref),
            )
        )
    ]
    for fetch in fetches:
        fetch.start()
    cotw[...] = jnp.zeros((4, 7, 8, 512), F32)
    cotw[0:2, 0:4, 0:7, :] = cot_ref[2:4, 3:7].astype(F32)
    cotw[2:4, 0:4, 0:7, :] = unfold(cta_ref[:, 11:15].astype(F32))
    cotw[0:2, 4:7, 0:7, :] = unfold(cha_ref[:, 3:6].astype(F32))
    cotw[2:4, 4:7, 0:7, :] = unfold(cdg_ref[:, 3:6].astype(F32))

    def put_merged(first, count, values):
        for half in range(2):
            block = values[:, 128 * half : 128 * half + 128].reshape(WT, count, 16, 128)
            for i in range(count):
                stage2[half, :, (first + i) // 2, (first + i) % 2] = block[:, i]

    def take_merged(first, count):
        halves = [
            jnp.concatenate(
                [
                    stage2[half, :, (first + i) // 2, (first + i) % 2].reshape(WT, 1, 16, 128)
                    for i in range(count)
                ],
                1,
            ).reshape(WT * count * 16, 128)
            for half in range(2)
        ]
        return jnp.concatenate(halves, 1)

    put_merged(0, 9, merged_ref[...])
    put_merged(10, 4, unfold_merged(next_ref[:, 1:5].astype(F32)))
    clear_pads(stage)
    put_pair_row(stage, 0, resB_ref[:, 13])
    put_pair_row(stage, 1, next_ref[:, 0])
    fetches[0].wait()
    merged, xhat_seam, rstd_seam = merge_pairs(stage, mg1_ref, mw1_ref[...])
    put_merged(9, 1, merged)
    fetches[1].wait()
    pieces = [
        stage2[half, :, :, q % 2, pl.ds(q // 2, 8, stride=2), :].reshape(ROWS, 128)
        for q in range(4)
        for half in range(2)
    ]
    xhat, rstd = normalise(jnp.concatenate(pieces, 1))
    xhat2[...] = xhat
    rstd2[...] = jnp.broadcast_to(rstd, (ROWS, 128))
    merged_two = dot((xhat * mg2_ref[...]).astype(BF), mw2_ref[...]).astype(BF).astype(F32)
    xhat3, rstd3 = normalise(merged_two)
    n3 = (xhat3 * g3_ref[...]).astype(BF)
    fetches[2].wait()
    packed = [dot(n3, p3_ref[:, 512 * i : 512 * i + 512]) for i in range(3)]
    mask = region_mask(col_ref[...], row_ref[...])
    fetches[3].wait()
    fetches[4].wait()

    def group(g):
        q, k, v = (part[:, 128 * g : 128 * g + 128] for part in packed)
        q = lengthen((q * (SCALE * LOG2E)).astype(BF))
        k, v = k.astype(BF), v.astype(BF)
        k_s[g] = k
        v_s[g] = v
        qT, vT = q.T, lengthen(v).T
        qT_s[g] = qT
        kT_s[g] = lengthen(k).T

        def keep(h, probs):
            probs_s[g * 4 + h] = probs

        yield
        oT_s[g], inv_s[g] = yield from attend_four(
            k, qT, vT, mask, lambda h: bias_ref[g * 4 + h], keep
        )

    stagger(group(g) for g in range(4))
    fetches[5].wait()
    att = jnp.concatenate([oT_s[g].astype(BF).T[:ROWS] for g in range(4)], 1)
    mixed = dot(att, ow3_ref[...]).astype(BF).astype(F32)
    section = (merged_two + mixed).reshape(4, 7, 8, 512)
    section = fold(section[:, :, 0:7])
    so_ref[...] = section[0:2, 0:4].astype(BF)
    sta_ref[...] = section[2:4].astype(BF)
    sha_ref[...] = section[0:2, 4:7].astype(BF)

    cot = cotw[...].reshape(ROWS, 512)
    cot_long = lengthen(cot.astype(BF))
    doT = dot_nt(ow3_ref[...], cot_long)
    for g in range(4):
        doT_s[g] = doT[128 * g : 128 * g + 128]

    def group_back(g):
        dqkv_s[g], dqkv_s[4 + g], dqkv_s[8 + g] = yield from attend_four_back(
            v_s[g], qT_s[g], kT_s[g], oT_s[g], doT_s[g], inv_s[g], lambda h: probs_s[g * 4 + h]
        )

    stagger(group_back(g) for g in range(4))
    dpacked = jnp.concatenate([dqkv_s[i] for i in range(12)], 1)
    dn3 = dot_nt(dpacked, p3_ref[...])
    dm2 = cot + normalise_back(dn3 * g3_ref[...], xhat3, rstd3)
    dn2 = dot_nt(dm2.astype(BF), mw2_ref[...])
    dg2 = normalise_back(dn2 * mg2_ref[...], xhat2[...], rstd2[:, 0:1])
    for q in range(4):
        for half in range(2):
            at = 256 * q + 128 * half
            stage2[half, :, :, q % 2, pl.ds(q // 2, 8, stride=2), :] = dg2[:, at : at + 128].reshape(
                4, 7, 8, 128
            )

    dm_ref[...] = take_merged(0, 9)
    merge_pairs_back(take_merged(9, 1), xhat_seam, rstd_seam, mg1_ref, mw1_ref[...], stage)
    d30_ref[...] = pair_row(stage, 0)
    dN_ref[:, 0] = pair_row(stage, 1)
    dN_ref[:, 1:5] = fold_merged(take_merged(10, 4), 4).astype(BF)


def middle(*operands):
    shapes = [
        (4, 28, 128), (4, 5, 28, 128), (2, 4, 28, 128), (2, 7, 28, 128), (2, 3, 28, 128),
    ]
    return pl.pallas_call(
        middle_kernel,
        in_specs=[pl.BlockSpec(memory_space=pltpu.VMEM)] * 12
        + [pl.BlockSpec(memory_space=pl.ANY)] * 6,
        out_shape=[jax.ShapeDtypeStruct((576, 256), F32)]
        + [jax.ShapeDtypeStruct(s, BF) for s in shapes],
        scratch_shapes=[
            pltpu.VMEM((4, 1, 2, 32, 128), F32),
            pltpu.VMEM((2, 4, 7, 2, 16, 128), F32),
            pltpu.VMEM((ROWS, 1024), F32),
            pltpu.VMEM((ROWS, 128), F32),
            pltpu.VMEM((4, 7, 8, 512), F32),
            pltpu.VMEM((4, ROWS, 128), BF),
            pltpu.VMEM((4, ROWS, 128), BF),
            pltpu.VMEM((4, 128, LANES), BF),
            pltpu.VMEM((4, 128, LANES), BF),
            pltpu.VMEM((4, 128, LANES), BF),
            pltpu.VMEM((16, ROWS, LANES), BF),
            pltpu.VMEM((4, 128, LANES), F32),
            pltpu.VMEM((4, 8, LANES), F32),
            pltpu.VMEM((4, 128, LANES), F32),
            pltpu.VMEM((12, ROWS, 128), BF),
            pltpu.VMEM((512, 256), BF),
            pltpu.VMEM((1024, 512), BF),
            pltpu.VMEM((512, 1536), BF),
            pltpu.VMEM((HEADS3, ROWS, LANES), F32),
            pltpu.VMEM((512, 512), BF),
            pltpu.SemaphoreType.DMA((6,)),
        ],
        compiler_params=params(28),
        cost_estimate=cost(9),
    )(*operands)


def join_kernel(ta_ref, own_ref, so_ref, grad_ref, section_ref, wide, narrow):
    for t in range(WT):
        wide[:, pl.ds(t, 28, stride=4), :] = (ta_ref if t < 2 else own_ref)[t % 2, 0:11].astype(F32)
        low = (ta_ref[t, 11:15] if t < 2 else so_ref[t - 2]).astype(F32)
        for g in range(4):
            narrow[g, :, pl.ds(t, 7, stride=4), :] = low[:, 7 * g : 7 * g + 7]
    for i in range(11):
        grad_ref[17 + i] = wide[i].reshape(28, 4, 128).astype(BF)
    for i in range(4):
        row = jnp.concatenate([narrow[g, i] for g in range(4)], 1)
        section_ref[3 + i] = row.reshape(7, 4, 512).astype(BF)


JOINED = [
    jax.ShapeDtypeStruct((28, 28, 4, 128), BF),
    jax.ShapeDtypeStruct((7, 7, 4, 512), BF),
]


def join(ta, own, section_own):
    return pl.pallas_call(
        join_kernel,
        out_shape=JOINED,
        scratch_shapes=[pltpu.VMEM((11, 112, 128), F32), pltpu.VMEM((4, 4, 28, 128), F32)],
        compiler_params=params(),
        cost_estimate=cost(2),
    )(ta, own, section_own)


def last_kernel(
    grad_hbm, section_hbm, ta_ref, own_ref, dg_ref, ha_ref, grad_out, section_out,
    wide, narrow, rows, section_rows, sems,
):
    del grad_hbm, section_hbm
    for t in range(WT):
        corner = dg_ref if t < 2 else ha_ref
        wide[0:3, pl.ds(t, 28, stride=4), :] = corner[t % 2, 0:3].astype(F32)
        wide[3:17, pl.ds(t, 28, stride=4), :] = (ta_ref if t < 2 else own_ref)[t % 2].astype(F32)
        high = corner[t % 2, 3:6].astype(F32)
        for g in range(4):
            narrow[g, :, pl.ds(t, 7, stride=4), :] = high[:, 7 * g : 7 * g + 7]
    for i in range(17):
        rows[i] = wide[i].reshape(28, 4, 128).astype(BF)
    copy = pltpu.make_async_copy(rows, grad_out.at[0:17], sems.at[0])
    copy.start()
    for i in range(3):
        row = jnp.concatenate([narrow[g, i] for g in range(4)], 1)
        section_rows[i] = row.reshape(7, 4, 512).astype(BF)
    other = pltpu.make_async_copy(section_rows, section_out.at[0:3], sems.at[1])
    other.start()
    copy.wait()
    other.wait()


def join_last(grad, section, ta, own, dg, ha):
    return pl.pallas_call(
        last_kernel,
        in_specs=[pl.BlockSpec(memory_space=pl.ANY)] * 2
        + [pl.BlockSpec(memory_space=pltpu.VMEM)] * 4,
        out_specs=[pl.BlockSpec(memory_space=pl.ANY)] * 2,
        out_shape=JOINED,
        scratch_shapes=[
            pltpu.VMEM((17, 112, 128), F32),
            pltpu.VMEM((4, 3, 28, 128), F32),
            pltpu.VMEM((17, 28, 4, 128), BF),
            pltpu.VMEM((3, 7, 4, 512), BF),
            pltpu.SemaphoreType.DMA((2,)),
        ],
        input_output_aliases={0: 0, 1: 1},
        compiler_params=params(),
        cost_estimate=cost(1),
    )(grad, section, ta, own, dg, ha)


IN_ORDER = Layout(major_to_minor=(0, 1, 2, 3))


def inward(values):
    return with_layout_constraint(jnp.transpose(values, (1, 2, 0, 3)), IN_ORDER)


def outward(values):
    return jnp.transpose(with_layout_constraint(values, IN_ORDER), (2, 0, 1, 3))


def send(values, axes, by):
    axes = axes.split()
    sizes = [lax.axis_size(a) for a in axes]
    if len(axes) == 1:
        pairs = [(i, (i + by) % sizes[0]) for i in range(sizes[0])]
    else:
        n, m = sizes
        pairs = [
            (i * m + j, (i + by) % n * m + (j + by) % m) for i in range(n) for j in range(m)
        ]
    return lax.ppermute(values, tuple(axes), pairs)


def per_device(
    tokens,
    regions_one,
    regions_three,
    gain_one,
    projection_one,
    outward_one,
    table_one,
    merge_gain_one,
    merge_weight_one,
    merge_gain_two,
    merge_weight_two,
    gain_three,
    projection_three,
    outward_three,
    table_three,
    cotangent,
):
    (early,) = arrange(early_kernel, (14,), tokens)
    ta_early = send(inward(early), "ta", -1)
    late, ha_late, dg_late = arrange(late_kernel, (15, 6, 6), tokens, cotangent)
    ha_late = send(ha_late, "ha", -1)
    dg_late = send(dg_late, "ha ta", -1)
    ta_late = send(inward(late), "ta", -1)
    bias_one, spread, row_one, row_three, col_one, col_three = prepare(
        table_one, table_three, regions_one, regions_three
    )
    gain, merge_gain, seam = gain_one[None], merge_gain_one[None], merge_weight_one
    args = (gain, projection_one, outward_one, bias_one, spread)
    (res_send, res_a, bias_a), saved_a = front(False, (tokens, outward(ta_early)), *args, row_one, col_one)
    row_send, *early_norm = merge_call(
        send_kernel, 0.5, [((4, 5, 28, 128), BF), ((256, 512), F32), ((256, 128), F32)], 4,
        res_send, merge_gain, seam,
    )
    row_next = send(row_send, "ha", -1)
    ta_late, res_a = lax.optimization_barrier((ta_late, res_a))
    ta_late = outward(ta_late)
    (res_b, bias_b), saved_b = front(True, (tokens, ta_late, ha_late, dg_late), *args, row_one, col_one)
    merged, *local_norm = merge_call(
        local_kernel, 0.1, [((576, 256), F32), ((576, 512), F32), ((576, 128), F32)], 9,
        res_a, res_b, merge_gain, seam,
    )
    row_next, merged = lax.optimization_barrier((row_next, merged))
    d_merged, d_30, d_send, sec_own, sec_ta, sec_ha = middle(
        merged, res_b, row_next, cotangent, ta_late, ha_late, dg_late,
        merge_gain, merge_gain_two[None], gain_three[None], row_three, col_three,
        merge_weight_one, merge_weight_two, projection_three, bias_a, bias_b, outward_three,
    )
    d_prev = send(d_send, "ha", 1)
    d_a, d_b = merge_call(
        local_back_kernel, 1, [((4, 5, 28, 128), BF), ((4, 14, 28, 128), BF)], 9,
        d_merged, d_30, *local_norm, merge_gain, seam,
    )
    own_b, ta_b, ha_b = back(
        True, (d_b, sec_ta, sec_ha), gain, projection_one, outward_one, saved_b
    )
    d_prev, own_b = lax.optimization_barrier((d_prev, own_b))
    ta_b = send(inward(ta_b), "ta", 1)
    ha_b = send(ha_b, "ha", 1)
    (d_first,) = merge_call(
        receive_kernel, 0.5, [((4, 9, 28, 128), BF)], 4, d_prev, *early_norm, merge_gain, seam
    )
    own_a, ta_a = back(False, (d_first, d_a), gain, projection_one, outward_one, saved_a)
    ta_b, ha_b, own_a = lax.optimization_barrier((ta_b, ha_b, own_a))
    ta_a = send(inward(ta_a), "ta", 1)
    dg_b = send(ha_b[2:], "ta", 1)
    grad, section = join(outward(ta_b), own_b, sec_own)
    ta_a, dg_b, grad = lax.optimization_barrier((ta_a, dg_b, grad))
    grad, section = join_last(grad, section, outward(ta_a), own_a, dg_b, ha_b)
    return (jnp.transpose(section, (2, 0, 1, 3)), jnp.transpose(grad, (2, 0, 1, 3)))


def solution(mesh):
    tile = P(("col", "ta"), "ha", None, None)
    ids = P(("col", "ta"), "ha", None)
    in_specs = (tile, ids, ids) + (P(),) * 12 + (tile,)
    return jax.shard_map(
        per_device, mesh=mesh, in_specs=in_specs, out_specs=(tile, tile), check_vma=False
    )
```

```python
import functools

import jax
import jax.numpy as jnp
import numpy as np
from jax import lax
from jax.experimental import pallas as pl
from jax.experimental.layout import Layout, with_layout_constraint
from jax.experimental.pallas import tpu as pltpu
from jax.sharding import PartitionSpec as P

HEADS1 = 4
HEADS3 = 16
WT = 4
WS = 7
ST = 2
SS = 3
EPSILON = 1e-05
NREL = 1183
LOG2E = 1.4426950408889634
HEAD = 32
SCALE = HEAD**-0.5
ROWS = WT * WS * 8
LANES = 256
SPAN = 1280
GONE = -1e30
PER_STEP = 8
STEPS = 8 // PER_STEP
BF = jnp.bfloat16
F32 = jnp.float32


def dot(a, b):
    return jnp.dot(a, b, preferred_element_type=F32)


def dot_nt(a, b):
    return lax.dot_general(a, b, (((1,), (1,)), ((), ())), preferred_element_type=F32)


def params(limit=20):
    return pltpu.CompilerParams(vmem_limit_bytes=limit * 1024 * 1024)


def cost(us):
    return pl.CostEstimate(flops=int(us * 1.1e9), bytes_accessed=int(us * 1e6), transcendentals=0)


def normalise(x):
    centred = x - jnp.mean(x, -1, keepdims=True)
    rstd = lax.rsqrt(jnp.mean(centred * centred, -1, keepdims=True) + EPSILON)
    return centred * rstd, rstd


def normalise_back(grad, xhat, rstd):
    return rstd * (
        grad
        - jnp.mean(grad, -1, keepdims=True)
        - xhat * jnp.mean(grad * xhat, -1, keepdims=True)
    )


def head_rows(x, h):
    return x[HEAD * h : HEAD * (h + 1)]


def head_of_lane(shape):
    return lax.broadcasted_iota(jnp.int32, shape, 1) // HEAD


def by_head(x):
    lane = head_of_lane((1, 128))
    return jnp.concatenate([x * (lane == h).astype(F32).astype(BF) for h in range(4)], 0)


def pick_heads(stacked):
    lane = head_of_lane((ROWS, 128))
    got = stacked[:ROWS]
    for h in range(1, 4):
        got = jnp.where(lane == h, stacked[ROWS * h : ROWS * (h + 1)], got)
    return got


def lengthen(x):
    return jnp.concatenate([x, jnp.zeros((LANES - ROWS, x.shape[1]), x.dtype)], 0)


def region_mask(column, row):
    return jnp.where(jnp.concatenate([column, column], 1) == row, 0.0, GONE).astype(F32)


def stagger(pending):
    pending, active = list(pending), []
    while pending or active:
        if pending:
            active.append(pending.pop(0))
        active = [g for g in active if next(g, "end") is None]


def attend_four(windows, beside=()):
    scores = [dot(by_head(k), qT) for k, qT, _, _, _, _ in windows]
    results = []
    beside = list(beside)
    share = -(-len(beside) // len(windows))
    for s, (_, _, vT, mask, bias_at, keep_probs) in zip(scores, windows):
        for emit in beside[:share]:
            emit()
        beside = beside[share:]
        outs, inverses = [], []
        for h in range(4):
            biased = s[ROWS * h : ROWS * (h + 1)] + (bias_at(h) + mask)
            peak = jnp.max(biased, 0, keepdims=True)
            probs = jnp.exp2(biased - peak).astype(BF)
            keep_probs(h, probs)
            extended = jnp.concatenate([head_rows(vT, h)[:, :ROWS], jnp.ones((16, ROWS), BF)], 0)
            out = dot(extended, probs)
            inverse = 1.0 / out[HEAD : HEAD + 1]
            outs.append(out[:HEAD] * inverse)
            inverses.append(inverse)
        results.append((jnp.concatenate(outs, 0), jnp.concatenate(inverses + inverses, 0)))
    return results


def attend_four_back(v, qT, kT, oT, doT, inverse, probs_at):
    scaled, deltas = [], []
    for h in range(4):
        part = head_rows(doT, h) * inverse[h : h + 1]
        deltas.append(jnp.sum(part * head_rows(oT, h), 0, keepdims=True))
        scaled.append(part)
    scaled = jnp.concatenate(scaled, 0).astype(BF)
    dprobs = dot(by_head(v), scaled)
    yield
    probs = [probs_at(h) for h in range(4)]
    dscores = [
        (probs[h].astype(F32) * (dprobs[ROWS * h : ROWS * (h + 1)] - deltas[h])).astype(BF)
        for h in range(4)
    ]
    dv = pick_heads(dot_nt(jnp.concatenate(probs, 0), scaled))
    yield
    dk = pick_heads(dot_nt(jnp.concatenate(dscores, 0), qT))
    dqT = jnp.concatenate([dot(head_rows(kT, h)[:, :ROWS], dscores[h]) for h in range(4)], 0)
    yield
    dq = (dqT * SCALE).astype(BF).T[:ROWS]
    return dq, (dk * (1.0 / LOG2E)).astype(BF), dv.astype(BF)


def lanes_of(shape):
    return lax.broadcasted_iota(jnp.int32, shape, 1)


def region_rows(ids, section):
    columns = ids.shape[1]
    count = columns // WS
    place = lax.broadcasted_iota(jnp.int32, (columns, LANES * count), 0)
    lane = lanes_of((columns, LANES * count))
    column = lane % 8
    real = (column < WS) & (lane % LANES < ROWS)
    if section == 3:
        column = jnp.where(column < 3, column + 4, column - 3)
    chosen = real & (place == lane // LANES * WS + column)
    spread = dot(ids.astype(F32).astype(BF), chosen.astype(F32).astype(BF))
    row = lax.broadcasted_iota(jnp.int32, spread.shape, 0)
    lane = lanes_of(spread.shape)
    real = (lane[:1] % 8 < WS) & (lane[:1] % LANES < ROWS)
    rows = []
    for hw in range(ids.shape[0] // (WT * WS)):
        mine = lane % LANES // 8 == row % 4 * WS + row // 4 - WS * hw
        inside = (row >= WT * WS * hw) & (row < WT * WS * (hw + 1))
        found = jnp.sum(jnp.where(mine & inside, spread, 0.0), 0, keepdims=True)
        found = jnp.where(real, found, -1.0)
        rows += [found[:, LANES * ww : LANES * (ww + 1)] for ww in range(count)]
    return rows


def region_columns(ids, section):
    columns = ids.shape[1]
    count = columns // WS
    source = ids.astype(F32).astype(BF)
    token = lax.broadcasted_iota(jnp.int32, (ROWS, ids.shape[0]), 0)
    place = lanes_of((ROWS, ids.shape[0]))
    column = lax.broadcasted_iota(jnp.int32, (ROWS, columns), 0) % 8
    lane = lanes_of((ROWS, columns))
    if section == 3:
        column = jnp.where(column < 3, column + 4, jnp.where(column == 7, 8, column - 3))
    ones = jnp.ones((columns, 128), BF)
    pad = lax.broadcasted_iota(jnp.int32, (ROWS, 128), 0) % 8 == 7
    found = []
    for hw in range(ids.shape[0] // (WT * WS)):
        chosen = place == (token // 8 % WS + WS * hw) * WT + token // 56
        picked = dot(chosen.astype(F32).astype(BF), source)
        for ww in range(count):
            mine = jnp.where(lane == WS * ww + column, picked, 0.0).astype(BF)
            found.append(jnp.where(pad, -1.0, dot(mine, ones)))
    return found


def bias_rows(spread, at, heads, tj, hj):
    lane = lanes_of((heads * 8, 128))
    p0, p1, p2, p3 = (
        pltpu.roll(
            spread[ti - tj + 3, at : at + heads * 8, :], (ti * 56 - (6 - hj) * 8) % 128, 1
        )
        for ti in range(WT)
    )
    left = jnp.where(lane < 56, p0, jnp.where(lane < 112, p1, p2))
    right = jnp.where(lane < 40, p2, p3)
    return left.reshape(heads, 8, 128), right.reshape(heads, 8, 128)


def prepare_kernel(
    t1_ref, t3_ref, s_ref, r1_ref, r3_ref, o1_ref, spread, row1_ref, row3_ref, col1_ref, col3_ref, tab
):
    tab[...] = jnp.zeros((24, SPAN), F32)
    tab[0:4, 0:NREL] = t1_ref[...] * LOG2E
    tab[8:24, 0:NREL] = t3_ref[...] * LOG2E
    slabs = []
    for dt in range(7):
        start = 169 * dt
        low = start // 128 * 128
        run = tab[:, low : low + 384]
        if start > low:
            run = pltpu.roll(run, 384 - (start - low), 1)
        slabs.append(run[:, :256])
    left = jnp.concatenate(slabs, 0)
    first = left.astype(BF)
    rest = left - first.astype(F32)
    second = rest.astype(BF)
    third = (rest - second.astype(F32)).astype(BF)
    chosen = s_ref[...]
    got = dot(first, chosen) + dot(second, chosen) + dot(third, chosen)
    lane16 = lanes_of((16, 128))
    for dt in range(7):
        for wj in range(8):
            part = got[24 * dt : 24 * dt + 24, 128 * wj : 128 * wj + 128]
            spread[dt, pl.ds(wj, 8, stride=8), :] = part[0:8]
            later = part[8:24]
            turned = jnp.where(lane16 % 8 < 3, pltpu.roll(later, 124, 1), pltpu.roll(later, 3, 1))
            spread[dt, pl.ds(64 + (7 if wj == 7 else (wj + 3) % 7), 16, stride=8), :] = turned
    for tj in range(WT):
        for hj in range(WS):
            row = (tj * WS + hj) * 8
            left, right = bias_rows(spread, 0, HEADS1, tj, hj)
            o1_ref[:, row : row + 8, 0:128] = left
            o1_ref[:, row : row + 8, 128:256] = right
    for i, found in enumerate(region_rows(r1_ref[...], 1)):
        row1_ref[i] = found
    row3_ref[...] = region_rows(r3_ref[...], 3)[0]
    for i, found in enumerate(region_columns(r1_ref[...], 1)):
        col1_ref[i] = found
    col3_ref[...] = region_columns(r3_ref[...], 3)[0]


def chooser():
    chosen = np.zeros((256, 1024), np.float32)
    for wj in range(WS):
        for dh in range(13):
            for wi in range(WS):
                chosen[dh * 13 + wi - wj + 6, wj * 128 + dh * 8 + wi] = 1.0
    return jnp.asarray(chosen, BF)


def by_height(ids):
    return jnp.transpose(ids, (1, 0, 2)).reshape(-1, ids.shape[2])


def prepare(table_one, table_three, regions_one, regions_three):
    return pl.pallas_call(
        prepare_kernel,
        out_shape=(
            jax.ShapeDtypeStruct((HEADS1, ROWS, LANES), F32),
            jax.ShapeDtypeStruct((7, 24 * 8, 128), F32),
            jax.ShapeDtypeStruct((16, 1, LANES), F32),
            jax.ShapeDtypeStruct((1, LANES), F32),
            jax.ShapeDtypeStruct((16, ROWS, 128), F32),
            jax.ShapeDtypeStruct((ROWS, 128), F32),
        ),
        scratch_shapes=[pltpu.VMEM((24, SPAN), F32)],
        compiler_params=params(),
        cost_estimate=cost(1.5),
    )(
        jnp.transpose(table_one),
        jnp.transpose(table_three),
        chooser(),
        by_height(regions_one),
        by_height(regions_three),
    )


def fold(values):
    return jnp.concatenate([values[..., 128 * g : 128 * g + 128] for g in range(4)], -2)


def unfold(values):
    return jnp.concatenate([values[..., 7 * g : 7 * g + 7, :] for g in range(4)], -1)


def early_kernel(tok_ref, early_ref):
    early_ref[...] = tok_ref[0:2, 3:17]


def late_kernel(tok_ref, cot_ref, late_ref, ha_ref, dg_ref):
    late_ref[:, 0:11] = tok_ref[0:2, 17:28]
    late_ref[:, 11:15] = fold(cot_ref[0:2, 3:7].astype(F32)).astype(BF)
    ha_ref[:, 0:3] = tok_ref[2:4, 0:3]
    ha_ref[:, 3:6] = fold(cot_ref[2:4, 0:3].astype(F32)).astype(BF)
    dg_ref[:, 0:3] = tok_ref[0:2, 0:3]
    dg_ref[:, 3:6] = fold(cot_ref[0:2, 0:3].astype(F32)).astype(BF)


def arrange(kernel, rows, *operands):
    return pl.pallas_call(
        kernel,
        out_shape=[jax.ShapeDtypeStruct((2, n, 28, 128), BF) for n in rows],
        compiler_params=params(8),
        cost_estimate=cost(0.3),
    )(*operands)


def put_rows(stage, frames, rows, values):
    values = values.astype(F32)
    stage[frames, rows, 0:28, :] = values
    stage[frames, rows, 28:36, :] = values[:, :, 0:8, :]


def cut_windows(stage, win):
    for hw in range(2):
        for ww in range(4):
            win[hw * 4 + ww] = stage[:, 7 * hw : 7 * hw + 7, 3 + 7 * ww : 11 + 7 * ww, :].reshape(
                ROWS, 128
            )


def join_windows(win, stage):
    for hw in range(2):
        for ww in range(4):
            stage[:, 7 * hw : 7 * hw + 7, 3 + 7 * ww : 11 + 7 * ww, :] = win[hw * 4 + ww].reshape(
                WT, WS, 8, 128
            )
    stage[:, :, 0:3, :] = stage[:, :, 28:31, :]


def front_kernel(late, *refs):
    n_in = 4 if late else 2
    pieces, refs = refs[:n_in], refs[n_in:]
    gain_ref, proj_ref, outw_ref, bias_ref, spread_ref, row_ref, col_ref = refs[:7]
    refs = refs[7:]
    n_out = 1 if late else 2
    outs, refs = refs[:n_out], refs[n_out:]
    b3_ref, xw_ref, kv_ref, t_ref, p_ref, o_ref, inv_ref, stage, win = refs
    own = pieces[0]
    if late:
        put_rows(stage, slice(0, 2), slice(0, 11), own[2:4, 17:28])
        put_rows(stage, slice(2, 4), slice(0, 11), pieces[1][:, 0:11])
        put_rows(stage, slice(0, 2), slice(11, 14), pieces[2][:, 0:3])
        put_rows(stage, slice(2, 4), slice(11, 14), pieces[3][:, 0:3])
    else:
        put_rows(stage, slice(0, 2), slice(0, 14), own[2:4, 3:17])
        put_rows(stage, slice(2, 4), slice(0, 14), pieces[1][...])
    cut_windows(stage, win)
    lax.fori_loop(
        0,
        STEPS,
        functools.partial(
            front_step, late, gain_ref, proj_ref, outw_ref, bias_ref, spread_ref, row_ref, col_ref,
            b3_ref, xw_ref, kv_ref, t_ref, p_ref, o_ref, inv_ref, win,
        ),
        0,
    )
    join_windows(win, stage)
    if late:
        outs[0][...] = stage[:, :, 0:28, :].astype(BF)
    else:
        outs[0][...] = stage[:, 0:9, 0:28, :].astype(BF)
        outs[1][...] = stage[:, 9:14, 0:28, :].astype(BF)


def front_step(
    late, gain_ref, proj_ref, outw_ref, bias_ref, spread_ref, row_ref, col_ref,
    b3_ref, xw_ref, kv_ref, t_ref, p_ref, o_ref, inv_ref, win, step, carry,
):
    first = 8 * late
    def block(tj, hj):
        def emit():
            left, right = bias_rows(spread_ref, 64, HEADS3, 2 * late + tj, hj)
            at = pl.ds(pl.multiple_of((tj * WS + hj) * 8, 8), 8)
            b3_ref[:, at, 0:128] = left
            b3_ref[:, at, 128:256] = right

        return emit

    count = 2 // STEPS
    blocks = [block(step * count + i, hj) for i in range(count) for hj in range(WS)]
    xs, operands = [], []
    for u in range(PER_STEP):
        w = step * PER_STEP + u
        x = win[w]
        xs.append(x)
        xw_ref[w] = x.astype(BF)
        xhat, _ = normalise(x)
        packed = dot((xhat * gain_ref[...]).astype(BF), proj_ref[...])
        q = (packed[:, :128] * (SCALE * LOG2E)).astype(BF)
        kv = packed[:, 128:].astype(BF)
        kv_ref[w] = kv
        qT, kT, vT = (lengthen(part).T for part in (q, kv[:, :128], kv[:, 128:]))
        t_ref[w, :128] = qT
        t_ref[w, 128:] = kT

        def keep(h, probs, w=w):
            p_ref[w, h] = probs

        operands.append(
            (kv[:, :128], qT, vT, region_mask(col_ref[first + w], row_ref[first + w]), lambda h: bias_ref[h], keep)
        )
    for u, (oT, inverse) in enumerate(attend_four(operands, blocks)):
        w = step * PER_STEP + u
        oT = oT.astype(BF)
        o_ref[w] = oT
        inv_ref[w] = inverse
        mixed = dot(oT.T[:ROWS], outw_ref[...]).astype(BF).astype(F32)
        win[w] = xs[u] + mixed
    return carry


SAVED = (
    ((ROWS, 128), BF),
    ((ROWS, 256), BF),
    ((256, LANES), BF),
    ((4, ROWS, LANES), BF),
    ((128, LANES), BF),
    ((8, LANES), F32),
)


def front(late, pieces, gain, proj, outw, bias, spread, row, column):
    consts = (gain, proj, outw, bias, spread)
    shapes = [(4, 14, 28, 128)] if late else [(4, 9, 28, 128), (4, 5, 28, 128)]
    out = pl.pallas_call(
        functools.partial(front_kernel, late),
        out_shape=[jax.ShapeDtypeStruct(s, BF) for s in shapes]
        + [jax.ShapeDtypeStruct((HEADS3, ROWS // 2, LANES), F32)]
        + [jax.ShapeDtypeStruct((8,) + s, d) for s, d in SAVED],
        scratch_shapes=[
            pltpu.VMEM((4, 14, 40, 128), F32),
            pltpu.VMEM((8, ROWS, 128), F32),
        ],
        compiler_params=params(),
        cost_estimate=cost(4.6),
    )(*pieces, *consts, row, column)
    return out[: len(shapes) + 1], out[len(shapes) + 1 :]


def back_kernel(late, *refs):
    n_in = 3 if late else 2
    pieces, refs = refs[:n_in], refs[n_in:]
    gain_ref, proj_ref, outw_ref = refs[:3]
    xw_ref, kv_ref, t_ref, p_ref, o_ref, inv_ref = refs[3:9]
    refs = refs[9:]
    n_out = 3 if late else 2
    outs, refs = refs[:n_out], refs[n_out:]
    stage, win = refs
    if late:
        put_rows(stage, slice(0, 4), slice(0, 14), pieces[0][...])
        outs[1][:, 11:15] = pieces[1][:, 0:4]
        outs[2][0:2, 3:6] = pieces[2][...]
        outs[2][2:4, 3:6] = pieces[1][:, 4:7]
    else:
        put_rows(stage, slice(0, 4), slice(0, 9), pieces[0][...])
        put_rows(stage, slice(0, 4), slice(9, 14), pieces[1][...])
    cut_windows(stage, win)
    lax.fori_loop(
        0,
        STEPS,
        functools.partial(
            back_step, gain_ref, proj_ref, outw_ref,
            xw_ref, kv_ref, t_ref, p_ref, o_ref, inv_ref, win,
        ),
        0,
    )
    join_windows(win, stage)
    if late:
        outs[0][...] = stage[0:2, 0:11, 0:28, :].astype(BF)
        outs[1][:, 0:11] = stage[2:4, 0:11, 0:28, :].astype(BF)
        outs[2][:, 0:3] = stage[:, 11:14, 0:28, :].astype(BF)
    else:
        outs[0][...] = stage[0:2, :, 0:28, :].astype(BF)
        outs[1][...] = stage[2:4, :, 0:28, :].astype(BF)


def back_step(
    gain_ref, proj_ref, outw_ref, xw_ref, kv_ref, t_ref, p_ref, o_ref, inv_ref, win, step, carry
):
    def window(w):
        dr = win[w]
        doT = dot_nt(outw_ref[...], lengthen(dr.astype(BF)))
        yield
        dq, dk, dv = yield from attend_four_back(
            kv_ref[w, :, 128:], t_ref[w, :128], t_ref[w, 128:], o_ref[w].astype(F32), doT,
            inv_ref[w], lambda h: p_ref[w, h],
        )
        dn = dot_nt(jnp.concatenate([dq, dk, dv], 1), proj_ref[...])
        yield
        xhat, rstd = normalise(xw_ref[w].astype(F32))
        win[w] = dr + normalise_back(dn * gain_ref[...], xhat, rstd)

    stagger(window(step * PER_STEP + u) for u in range(PER_STEP))
    return carry


def back(late, pieces, gain, proj, outw, saved):
    consts = (gain, proj, outw)
    if late:
        shapes = [(2, 11, 28, 128), (2, 15, 28, 128), (4, 6, 28, 128)]
    else:
        shapes = [(2, 14, 28, 128), (2, 14, 28, 128)]
    return pl.pallas_call(
        functools.partial(back_kernel, late),
        out_shape=[jax.ShapeDtypeStruct(s, BF) for s in shapes],
        scratch_shapes=[
            pltpu.VMEM((4, 14, 40, 128), F32),
            pltpu.VMEM((8, ROWS, 128), F32),
        ],
        compiler_params=params(),
        cost_estimate=cost(5.5),
    )(*pieces, *consts, *saved)


def merge_pairs(stage, gain_ref, weight):
    pairs = stage.shape[1]
    pieces = [
        stage[:, :, q % 2, pl.ds(q // 2, 16, stride=2), :].reshape(WT * pairs * 16, 128)
        for q in range(4)
    ]
    xhat, rstd = normalise(jnp.concatenate(pieces, 1))
    merged = dot((xhat * gain_ref[...]).astype(BF), weight).astype(BF).astype(F32)
    return merged, xhat, rstd


def merge_pairs_back(grad, xhat, rstd, gain_ref, weight, stage):
    pairs = stage.shape[1]
    dn = dot_nt(grad.astype(BF), weight)
    dg = normalise_back(dn * gain_ref[...], xhat, rstd)
    for q in range(4):
        stage[:, :, q % 2, pl.ds(q // 2, 16, stride=2), :] = dg[
            :, 128 * q : 128 * q + 128
        ].reshape(WT, pairs, 16, 128)


def put_pair_row(stage, at, values):
    stage[:, at // 2, at % 2, 0:28, :] = values.astype(F32)


def clear_pads(stage):
    stage[:, :, :, 28:32, :] = jnp.zeros((WT, stage.shape[1], 2, 4, 128), F32)


def pair_row(stage, at):
    return stage[:, at // 2, at % 2, 0:28, :].astype(BF)


def fold_merged(merged, pairs):
    halves = [
        merged[:, 128 * i : 128 * i + 128].reshape(WT, pairs, 16, 128)[:, :, 0:14] for i in range(2)
    ]
    return jnp.concatenate(halves, 2)


def unfold_merged(folded):
    pad = jnp.zeros(folded.shape[:2] + (2, 128), F32)
    halves = [
        jnp.concatenate([folded[:, :, 14 * i : 14 * i + 14], pad], 2).reshape(-1, 128)
        for i in range(2)
    ]
    return jnp.concatenate(halves, 1)


def send_kernel(res_ref, gain_ref, weight_ref, send_ref, xhat_ref, rstd_ref, stage):
    clear_pads(stage)
    for i in range(8):
        put_pair_row(stage, i, res_ref[:, 1 + i])
    merged, xhat, rstd = merge_pairs(stage, gain_ref, weight_ref[...])
    xhat_ref[...] = xhat
    rstd_ref[...] = jnp.broadcast_to(rstd, rstd_ref.shape)
    send_ref[:, 0:1] = res_ref[:, 0:1]
    send_ref[:, 1:5] = fold_merged(merged, 4).astype(BF)


def local_kernel(resA_ref, resB_ref, gain_ref, weight_ref, merged_ref, xhat_ref, rstd_ref, stage):
    clear_pads(stage)
    for i in range(5):
        put_pair_row(stage, i, resA_ref[:, i])
    for i in range(13):
        put_pair_row(stage, 5 + i, resB_ref[:, i])
    merged, xhat, rstd = merge_pairs(stage, gain_ref, weight_ref[...])
    xhat_ref[...] = xhat
    rstd_ref[...] = jnp.broadcast_to(rstd, rstd_ref.shape)
    merged_ref[...] = merged


def local_back_kernel(
    grad_ref, d30_ref, xhat_ref, rstd_ref, gain_ref, weight_ref, dA_ref, dB_ref, stage
):
    merge_pairs_back(
        grad_ref[...], xhat_ref[...], rstd_ref[:, 0:1], gain_ref, weight_ref[...], stage
    )
    for i in range(5):
        dA_ref[:, i] = pair_row(stage, i)
    for i in range(13):
        dB_ref[:, i] = pair_row(stage, 5 + i)
    dB_ref[:, 13] = d30_ref[...]


def receive_kernel(got_ref, xhat_ref, rstd_ref, gain_ref, weight_ref, d_ref, stage):
    grad = unfold_merged(got_ref[:, 1:5].astype(F32))
    merge_pairs_back(grad, xhat_ref[...], rstd_ref[:, 0:1], gain_ref, weight_ref[...], stage)
    d_ref[:, 0:1] = got_ref[:, 0:1]
    for i in range(8):
        d_ref[:, 1 + i] = pair_row(stage, i)


def merge_call(kernel, us, shapes, pairs, *operands):
    return pl.pallas_call(
        kernel,
        out_shape=[jax.ShapeDtypeStruct(shape, kind) for shape, kind in shapes],
        scratch_shapes=[pltpu.VMEM((WT, pairs, 2, 32, 128), F32)],
        compiler_params=params(),
        cost_estimate=cost(us),
    )(*operands)


def middle_kernel(
    merged_ref, resB_ref, next_ref, cot_ref, cta_ref, cha_ref, cdg_ref,
    mg1_ref, mg2_ref, g3_ref, row_ref, col_ref, mw1_hbm, mw2_hbm, p3_hbm, biasA_hbm, biasB_hbm, ow3_hbm,
    dm_ref, d30_ref, dN_ref, so_ref, sta_ref, sha_ref,
    stage, stage2, xhat2, rstd2, cotw, k_s, v_s, qT_s, kT_s, vT_s, probs_s, oT_s, inv_s, doT_s, dqkv_s,
    mw1_ref, mw2_ref, p3_ref, bias_ref, ow3_ref, sems,
):
    fetches = [
        pltpu.make_async_copy(there, here, sems.at[i])
        for i, (there, here) in enumerate(
            (
                (mw1_hbm, mw1_ref),
                (mw2_hbm, mw2_ref),
                (p3_hbm, p3_ref),
                (biasA_hbm, bias_ref.at[:, 0 : ROWS // 2]),
                (biasB_hbm, bias_ref.at[:, ROWS // 2 : ROWS]),
                (ow3_hbm, ow3_ref),
            )
        )
    ]
    for fetch in fetches:
        fetch.start()
    cotw[...] = jnp.zeros((4, 7, 8, 512), F32)
    cotw[0:2, 0:4, 0:7, :] = cot_ref[2:4, 3:7].astype(F32)
    cotw[2:4, 0:4, 0:7, :] = unfold(cta_ref[:, 11:15].astype(F32))
    cotw[0:2, 4:7, 0:7, :] = unfold(cha_ref[:, 3:6].astype(F32))
    cotw[2:4, 4:7, 0:7, :] = unfold(cdg_ref[:, 3:6].astype(F32))

    def put_merged(first, count, values):
        for half in range(2):
            block = values[:, 128 * half : 128 * half + 128].reshape(WT, count, 16, 128)
            for i in range(count):
                stage2[half, :, (first + i) // 2, (first + i) % 2] = block[:, i]

    def take_merged(first, count):
        halves = [
            jnp.concatenate(
                [
                    stage2[half, :, (first + i) // 2, (first + i) % 2].reshape(WT, 1, 16, 128)
                    for i in range(count)
                ],
                1,
            ).reshape(WT * count * 16, 128)
            for half in range(2)
        ]
        return jnp.concatenate(halves, 1)

    put_merged(0, 9, merged_ref[...])
    put_merged(10, 4, unfold_merged(next_ref[:, 1:5].astype(F32)))
    clear_pads(stage)
    put_pair_row(stage, 0, resB_ref[:, 13])
    put_pair_row(stage, 1, next_ref[:, 0])
    fetches[0].wait()
    merged, xhat_seam, rstd_seam = merge_pairs(stage, mg1_ref, mw1_ref[...])
    put_merged(9, 1, merged)
    fetches[1].wait()
    pieces = [
        stage2[half, :, :, q % 2, pl.ds(q // 2, 8, stride=2), :].reshape(ROWS, 128)
        for q in range(4)
        for half in range(2)
    ]
    xhat, rstd = normalise(jnp.concatenate(pieces, 1))
    xhat2[...] = xhat
    rstd2[...] = jnp.broadcast_to(rstd, (ROWS, 128))
    merged_two = dot((xhat * mg2_ref[...]).astype(BF), mw2_ref[...]).astype(BF).astype(F32)
    xhat3, rstd3 = normalise(merged_two)
    n3 = (xhat3 * g3_ref[...]).astype(BF)
    fetches[2].wait()
    packed = [dot(n3, p3_ref[:, 512 * i : 512 * i + 512]) for i in range(3)]
    for g in range(4):
        q, k, v = (part[:, 128 * g : 128 * g + 128] for part in packed)
        q = lengthen((q * (SCALE * LOG2E)).astype(BF))
        k, v = k.astype(BF), v.astype(BF)
        k_s[g] = k
        v_s[g] = v
        qT_s[g] = q.T
        kT_s[g] = lengthen(k).T
        vT_s[g] = lengthen(v).T
    mask = region_mask(col_ref[...], row_ref[...])
    fetches[3].wait()
    fetches[4].wait()

    operands = []
    for g in range(4):

        def keep(h, probs, g=g):
            probs_s[g * 4 + h] = probs

        operands.append((k_s[g], qT_s[g], vT_s[g], mask, lambda h, g=g: bias_ref[g * 4 + h], keep))
    for g, (oT, inverse) in enumerate(attend_four(operands)):
        oT_s[g] = oT
        inv_s[g] = inverse
    fetches[5].wait()
    att = jnp.concatenate([oT_s[g].astype(BF).T[:ROWS] for g in range(4)], 1)
    mixed = dot(att, ow3_ref[...]).astype(BF).astype(F32)
    section = (merged_two + mixed).reshape(4, 7, 8, 512)
    section = fold(section[:, :, 0:7])
    so_ref[...] = section[0:2, 0:4].astype(BF)
    sta_ref[...] = section[2:4].astype(BF)
    sha_ref[...] = section[0:2, 4:7].astype(BF)

    cot = cotw[...].reshape(ROWS, 512)
    cot_long = lengthen(cot.astype(BF))
    doT = dot_nt(ow3_ref[...], cot_long)
    for g in range(4):
        doT_s[g] = doT[128 * g : 128 * g + 128]

    def group_back(g):
        dqkv_s[g], dqkv_s[4 + g], dqkv_s[8 + g] = yield from attend_four_back(
            v_s[g], qT_s[g], kT_s[g], oT_s[g], doT_s[g], inv_s[g], lambda h: probs_s[g * 4 + h]
        )

    stagger(group_back(g) for g in range(4))
    dpacked = jnp.concatenate([dqkv_s[i] for i in range(12)], 1)
    dn3 = dot_nt(dpacked, p3_ref[...])
    dm2 = cot + normalise_back(dn3 * g3_ref[...], xhat3, rstd3)
    dn2 = dot_nt(dm2.astype(BF), mw2_ref[...])
    dg2 = normalise_back(dn2 * mg2_ref[...], xhat2[...], rstd2[:, 0:1])
    for q in range(4):
        for half in range(2):
            at = 256 * q + 128 * half
            stage2[half, :, :, q % 2, pl.ds(q // 2, 8, stride=2), :] = dg2[:, at : at + 128].reshape(
                4, 7, 8, 128
            )

    dm_ref[...] = take_merged(0, 9)
    merge_pairs_back(take_merged(9, 1), xhat_seam, rstd_seam, mg1_ref, mw1_ref[...], stage)
    d30_ref[...] = pair_row(stage, 0)
    dN_ref[:, 0] = pair_row(stage, 1)
    dN_ref[:, 1:5] = fold_merged(take_merged(10, 4), 4).astype(BF)


def middle(*operands):
    shapes = [
        (4, 28, 128), (4, 5, 28, 128), (2, 4, 28, 128), (2, 7, 28, 128), (2, 3, 28, 128),
    ]
    return pl.pallas_call(
        middle_kernel,
        in_specs=[pl.BlockSpec(memory_space=pltpu.VMEM)] * 12
        + [pl.BlockSpec(memory_space=pl.ANY)] * 6,
        out_shape=[jax.ShapeDtypeStruct((576, 256), F32)]
        + [jax.ShapeDtypeStruct(s, BF) for s in shapes],
        scratch_shapes=[
            pltpu.VMEM((4, 1, 2, 32, 128), F32),
            pltpu.VMEM((2, 4, 7, 2, 16, 128), F32),
            pltpu.VMEM((ROWS, 1024), F32),
            pltpu.VMEM((ROWS, 128), F32),
            pltpu.VMEM((4, 7, 8, 512), F32),
            pltpu.VMEM((4, ROWS, 128), BF),
            pltpu.VMEM((4, ROWS, 128), BF),
            pltpu.VMEM((4, 128, LANES), BF),
            pltpu.VMEM((4, 128, LANES), BF),
            pltpu.VMEM((4, 128, LANES), BF),
            pltpu.VMEM((16, ROWS, LANES), BF),
            pltpu.VMEM((4, 128, LANES), F32),
            pltpu.VMEM((4, 8, LANES), F32),
            pltpu.VMEM((4, 128, LANES), F32),
            pltpu.VMEM((12, ROWS, 128), BF),
            pltpu.VMEM((512, 256), BF),
            pltpu.VMEM((1024, 512), BF),
            pltpu.VMEM((512, 1536), BF),
            pltpu.VMEM((HEADS3, ROWS, LANES), F32),
            pltpu.VMEM((512, 512), BF),
            pltpu.SemaphoreType.DMA((6,)),
        ],
        compiler_params=params(28),
        cost_estimate=cost(9),
    )(*operands)


def join_kernel(ta_ref, own_ref, so_ref, grad_ref, section_ref, wide, narrow):
    for t in range(WT):
        wide[:, pl.ds(t, 28, stride=4), :] = (ta_ref if t < 2 else own_ref)[t % 2, 0:11].astype(F32)
        low = (ta_ref[t, 11:15] if t < 2 else so_ref[t - 2]).astype(F32)
        for g in range(4):
            narrow[g, :, pl.ds(t, 7, stride=4), :] = low[:, 7 * g : 7 * g + 7]
    for i in range(11):
        grad_ref[17 + i] = wide[i].reshape(28, 4, 128).astype(BF)
    for i in range(4):
        row = jnp.concatenate([narrow[g, i] for g in range(4)], 1)
        section_ref[3 + i] = row.reshape(7, 4, 512).astype(BF)


JOINED = [
    jax.ShapeDtypeStruct((28, 28, 4, 128), BF),
    jax.ShapeDtypeStruct((7, 7, 4, 512), BF),
]


def join(ta, own, section_own):
    return pl.pallas_call(
        join_kernel,
        out_shape=JOINED,
        scratch_shapes=[pltpu.VMEM((11, 112, 128), F32), pltpu.VMEM((4, 4, 28, 128), F32)],
        compiler_params=params(),
        cost_estimate=cost(2),
    )(ta, own, section_own)


def last_kernel(
    grad_hbm, section_hbm, ta_ref, own_ref, dg_ref, ha_ref, grad_out, section_out,
    wide, narrow, rows, section_rows, sems,
):
    del grad_hbm, section_hbm
    for t in range(WT):
        corner = dg_ref if t < 2 else ha_ref
        wide[0:3, pl.ds(t, 28, stride=4), :] = corner[t % 2, 0:3].astype(F32)
        wide[3:17, pl.ds(t, 28, stride=4), :] = (ta_ref if t < 2 else own_ref)[t % 2].astype(F32)
        high = corner[t % 2, 3:6].astype(F32)
        for g in range(4):
            narrow[g, :, pl.ds(t, 7, stride=4), :] = high[:, 7 * g : 7 * g + 7]
    for i in range(17):
        rows[i] = wide[i].reshape(28, 4, 128).astype(BF)
    copy = pltpu.make_async_copy(rows, grad_out.at[0:17], sems.at[0])
    copy.start()
    for i in range(3):
        row = jnp.concatenate([narrow[g, i] for g in range(4)], 1)
        section_rows[i] = row.reshape(7, 4, 512).astype(BF)
    other = pltpu.make_async_copy(section_rows, section_out.at[0:3], sems.at[1])
    other.start()
    copy.wait()
    other.wait()


def join_last(grad, section, ta, own, dg, ha):
    return pl.pallas_call(
        last_kernel,
        in_specs=[pl.BlockSpec(memory_space=pl.ANY)] * 2
        + [pl.BlockSpec(memory_space=pltpu.VMEM)] * 4,
        out_specs=[pl.BlockSpec(memory_space=pl.ANY)] * 2,
        out_shape=JOINED,
        scratch_shapes=[
            pltpu.VMEM((17, 112, 128), F32),
            pltpu.VMEM((4, 3, 28, 128), F32),
            pltpu.VMEM((17, 28, 4, 128), BF),
            pltpu.VMEM((3, 7, 4, 512), BF),
            pltpu.SemaphoreType.DMA((2,)),
        ],
        input_output_aliases={0: 0, 1: 1},
        compiler_params=params(),
        cost_estimate=cost(1),
    )(grad, section, ta, own, dg, ha)


IN_ORDER = Layout(major_to_minor=(0, 1, 2, 3))


def inward(values):
    return with_layout_constraint(jnp.transpose(values, (1, 2, 0, 3)), IN_ORDER)


def outward(values):
    return jnp.transpose(with_layout_constraint(values, IN_ORDER), (2, 0, 1, 3))


def send(values, axes, by):
    axes = axes.split()
    sizes = [lax.axis_size(a) for a in axes]
    if len(axes) == 1:
        pairs = [(i, (i + by) % sizes[0]) for i in range(sizes[0])]
    else:
        n, m = sizes
        pairs = [
            (i * m + j, (i + by) % n * m + (j + by) % m) for i in range(n) for j in range(m)
        ]
    return lax.ppermute(values, tuple(axes), pairs)


def per_device(
    tokens,
    regions_one,
    regions_three,
    gain_one,
    projection_one,
    outward_one,
    table_one,
    merge_gain_one,
    merge_weight_one,
    merge_gain_two,
    merge_weight_two,
    gain_three,
    projection_three,
    outward_three,
    table_three,
    cotangent,
):
    (early,) = arrange(early_kernel, (14,), tokens)
    ta_early = send(inward(early), "ta", -1)
    late, ha_late, dg_late = arrange(late_kernel, (15, 6, 6), tokens, cotangent)
    ha_late = send(ha_late, "ha", -1)
    dg_late = send(dg_late, "ha ta", -1)
    ta_late = send(inward(late), "ta", -1)
    bias_one, spread, row_one, row_three, col_one, col_three = prepare(
        table_one, table_three, regions_one, regions_three
    )
    gain, merge_gain, seam = gain_one[None], merge_gain_one[None], merge_weight_one
    args = (gain, projection_one, outward_one, bias_one, spread)
    (res_send, res_a, bias_a), saved_a = front(False, (tokens, outward(ta_early)), *args, row_one, col_one)
    row_send, *early_norm = merge_call(
        send_kernel, 0.5, [((4, 5, 28, 128), BF), ((256, 512), F32), ((256, 128), F32)], 4,
        res_send, merge_gain, seam,
    )
    row_next = send(row_send, "ha", -1)
    ta_late, res_a = lax.optimization_barrier((ta_late, res_a))
    ta_late = outward(ta_late)
    (res_b, bias_b), saved_b = front(True, (tokens, ta_late, ha_late, dg_late), *args, row_one, col_one)
    merged, *local_norm = merge_call(
        local_kernel, 0.1, [((576, 256), F32), ((576, 512), F32), ((576, 128), F32)], 9,
        res_a, res_b, merge_gain, seam,
    )
    row_next, merged = lax.optimization_barrier((row_next, merged))
    d_merged, d_30, d_send, sec_own, sec_ta, sec_ha = middle(
        merged, res_b, row_next, cotangent, ta_late, ha_late, dg_late,
        merge_gain, merge_gain_two[None], gain_three[None], row_three, col_three,
        merge_weight_one, merge_weight_two, projection_three, bias_a, bias_b, outward_three,
    )
    d_prev = send(d_send, "ha", 1)
    d_a, d_b = merge_call(
        local_back_kernel, 1, [((4, 5, 28, 128), BF), ((4, 14, 28, 128), BF)], 9,
        d_merged, d_30, *local_norm, merge_gain, seam,
    )
    own_b, ta_b, ha_b = back(
        True, (d_b, sec_ta, sec_ha), gain, projection_one, outward_one, saved_b
    )
    d_prev, own_b = lax.optimization_barrier((d_prev, own_b))
    ta_b = send(inward(ta_b), "ta", 1)
    ha_b = send(ha_b, "ha", 1)
    (d_first,) = merge_call(
        receive_kernel, 0.5, [((4, 9, 28, 128), BF)], 4, d_prev, *early_norm, merge_gain, seam
    )
    own_a, ta_a = back(False, (d_first, d_a), gain, projection_one, outward_one, saved_a)
    ta_b, ha_b, own_a = lax.optimization_barrier((ta_b, ha_b, own_a))
    ta_a = send(inward(ta_a), "ta", 1)
    dg_b = send(ha_b[2:], "ta", 1)
    grad, section = join(outward(ta_b), own_b, sec_own)
    ta_a, dg_b, grad = lax.optimization_barrier((ta_a, dg_b, grad))
    grad, section = join_last(grad, section, outward(ta_a), own_a, dg_b, ha_b)
    return (jnp.transpose(section, (2, 0, 1, 3)), jnp.transpose(grad, (2, 0, 1, 3)))


def solution(mesh):
    tile = P(("col", "ta"), "ha", None, None)
    ids = P(("col", "ta"), "ha", None)
    in_specs = (tile, ids, ids) + (P(),) * 12 + (tile,)
    return jax.shard_map(
        per_device, mesh=mesh, in_specs=in_specs, out_specs=(tile, tile), check_vma=False
    )
```

```python
import functools

import jax
import jax.numpy as jnp
import numpy as np
from jax import lax
from jax.experimental import pallas as pl
from jax.experimental.layout import Layout, with_layout_constraint
from jax.experimental.pallas import tpu as pltpu
from jax.sharding import PartitionSpec as P

HEADS1 = 4
HEADS3 = 16
WT = 4
WS = 7
ST = 2
SS = 3
EPSILON = 1e-05
NREL = 1183
LOG2E = 1.4426950408889634
HEAD = 32
SCALE = HEAD**-0.5
ROWS = WT * WS * 8
LANES = 256
SPAN = 1280
GONE = -1e30
PER_STEP = 8
STEPS = 8 // PER_STEP
BF = jnp.bfloat16
F32 = jnp.float32


def dot(a, b):
    return jnp.dot(a, b, preferred_element_type=F32)


def dot_nt(a, b):
    return lax.dot_general(a, b, (((1,), (1,)), ((), ())), preferred_element_type=F32)


def params(limit=20):
    return pltpu.CompilerParams(vmem_limit_bytes=limit * 1024 * 1024)


def cost(us):
    return pl.CostEstimate(flops=int(us * 1.1e9), bytes_accessed=int(us * 1e6), transcendentals=0)


def normalise(x):
    centred = x - jnp.mean(x, -1, keepdims=True)
    rstd = lax.rsqrt(jnp.mean(centred * centred, -1, keepdims=True) + EPSILON)
    return centred * rstd, rstd


def normalise_back(grad, xhat, rstd):
    return rstd * (
        grad
        - jnp.mean(grad, -1, keepdims=True)
        - xhat * jnp.mean(grad * xhat, -1, keepdims=True)
    )


def head_rows(x, h):
    return x[HEAD * h : HEAD * (h + 1)]


def head_of_lane(shape):
    return lax.broadcasted_iota(jnp.int32, shape, 1) // HEAD


def by_head(x):
    lane = head_of_lane((1, 128))
    return jnp.concatenate([x * (lane == h).astype(F32).astype(BF) for h in range(4)], 0)


def pick_heads(stacked):
    lane = head_of_lane((ROWS, 128))
    got = stacked[:ROWS]
    for h in range(1, 4):
        got = jnp.where(lane == h, stacked[ROWS * h : ROWS * (h + 1)], got)
    return got


def lengthen(x):
    return jnp.concatenate([x, jnp.zeros((LANES - ROWS, x.shape[1]), x.dtype)], 0)


def region_mask(column, row):
    return jnp.where(jnp.concatenate([column, column], 1) == row, 0.0, GONE).astype(F32)


def stagger(pending):
    pending, active = list(pending), []
    while pending or active:
        if pending:
            active.append(pending.pop(0))
        active = [g for g in active if next(g, "end") is None]


def attend_four(windows, beside=()):
    scores = [dot(by_head(k), qT) for k, qT, _, _, _, _ in windows]
    results = []
    beside = list(beside)
    share = -(-len(beside) // len(windows))
    for s, (_, _, vT, mask, bias_at, keep_probs) in zip(scores, windows):
        for emit in beside[:share]:
            emit()
        beside = beside[share:]
        outs, inverses = [], []
        for h in range(4):
            biased = s[ROWS * h : ROWS * (h + 1)] + (bias_at(h) + mask)
            peak = jnp.max(biased, 0, keepdims=True)
            probs = jnp.exp2(biased - peak).astype(BF)
            keep_probs(h, probs)
            extended = jnp.concatenate([head_rows(vT, h)[:, :ROWS], jnp.ones((16, ROWS), BF)], 0)
            out = dot(extended, probs)
            inverse = 1.0 / out[HEAD : HEAD + 1]
            outs.append(out[:HEAD] * inverse)
            inverses.append(inverse)
        results.append((jnp.concatenate(outs, 0), jnp.concatenate(inverses + inverses, 0)))
    return results


def attend_four_back(v, qT, kT, oT, doT, inverse, probs_at):
    scaled, deltas = [], []
    for h in range(4):
        part = head_rows(doT, h) * inverse[h : h + 1]
        deltas.append(jnp.sum(part * head_rows(oT, h), 0, keepdims=True))
        scaled.append(part)
    scaled = jnp.concatenate(scaled, 0).astype(BF)
    dprobs = dot(by_head(v), scaled)
    yield
    probs = [probs_at(h) for h in range(4)]
    dscores = [
        (probs[h].astype(F32) * (dprobs[ROWS * h : ROWS * (h + 1)] - deltas[h])).astype(BF)
        for h in range(4)
    ]
    dv = pick_heads(dot_nt(jnp.concatenate(probs, 0), scaled))
    yield
    dk = pick_heads(dot_nt(jnp.concatenate(dscores, 0), qT))
    dqT = jnp.concatenate([dot(head_rows(kT, h)[:, :ROWS], dscores[h]) for h in range(4)], 0)
    yield
    dq = (dqT * SCALE).astype(BF).T[:ROWS]
    return dq, (dk * (1.0 / LOG2E)).astype(BF), dv.astype(BF)


def lanes_of(shape):
    return lax.broadcasted_iota(jnp.int32, shape, 1)


def region_rows(ids, section):
    columns = ids.shape[1]
    count = columns // WS
    place = lax.broadcasted_iota(jnp.int32, (columns, LANES * count), 0)
    lane = lanes_of((columns, LANES * count))
    column = lane % 8
    real = (column < WS) & (lane % LANES < ROWS)
    if section == 3:
        column = jnp.where(column < 3, column + 4, column - 3)
    chosen = real & (place == lane // LANES * WS + column)
    spread = dot(ids.astype(F32).astype(BF), chosen.astype(F32).astype(BF))
    row = lax.broadcasted_iota(jnp.int32, spread.shape, 0)
    lane = lanes_of(spread.shape)
    real = (lane[:1] % 8 < WS) & (lane[:1] % LANES < ROWS)
    rows = []
    for hw in range(ids.shape[0] // (WT * WS)):
        mine = lane % LANES // 8 == row % 4 * WS + row // 4 - WS * hw
        inside = (row >= WT * WS * hw) & (row < WT * WS * (hw + 1))
        found = jnp.sum(jnp.where(mine & inside, spread, 0.0), 0, keepdims=True)
        found = jnp.where(real, found, -1.0)
        rows += [found[:, LANES * ww : LANES * (ww + 1)] for ww in range(count)]
    return rows


def region_columns(ids, section):
    columns = ids.shape[1]
    count = columns // WS
    source = ids.astype(F32).astype(BF)
    token = lax.broadcasted_iota(jnp.int32, (ROWS, ids.shape[0]), 0)
    place = lanes_of((ROWS, ids.shape[0]))
    column = lax.broadcasted_iota(jnp.int32, (ROWS, columns), 0) % 8
    lane = lanes_of((ROWS, columns))
    if section == 3:
        column = jnp.where(column < 3, column + 4, jnp.where(column == 7, 8, column - 3))
    ones = jnp.ones((columns, 128), BF)
    pad = lax.broadcasted_iota(jnp.int32, (ROWS, 128), 0) % 8 == 7
    found = []
    for hw in range(ids.shape[0] // (WT * WS)):
        chosen = place == (token // 8 % WS + WS * hw) * WT + token // 56
        picked = dot(chosen.astype(F32).astype(BF), source)
        for ww in range(count):
            mine = jnp.where(lane == WS * ww + column, picked, 0.0).astype(BF)
            found.append(jnp.where(pad, -1.0, dot(mine, ones)))
    return found


def bias_rows(spread, at, heads, tj, hj):
    lane = lanes_of((heads * 8, 128))
    p0, p1, p2, p3 = (
        pltpu.roll(
            spread[ti - tj + 3, at : at + heads * 8, :], (ti * 56 - (6 - hj) * 8) % 128, 1
        )
        for ti in range(WT)
    )
    left = jnp.where(lane < 56, p0, jnp.where(lane < 112, p1, p2))
    right = jnp.where(lane < 40, p2, p3)
    return left.reshape(heads, 8, 128), right.reshape(heads, 8, 128)


def prepare_kernel(
    t1_ref, t3_ref, s_ref, r1_ref, r3_ref, o1_ref, spread, row1_ref, row3_ref, col1_ref, col3_ref, tab
):
    tab[...] = jnp.zeros((24, SPAN), F32)
    tab[0:4, 0:NREL] = t1_ref[...] * LOG2E
    tab[8:24, 0:NREL] = t3_ref[...] * LOG2E
    slabs = []
    for dt in range(7):
        start = 169 * dt
        low = start // 128 * 128
        run = tab[:, low : low + 384]
        if start > low:
            run = pltpu.roll(run, 384 - (start - low), 1)
        slabs.append(run[:, :256])
    left = jnp.concatenate(slabs, 0)
    first = left.astype(BF)
    rest = left - first.astype(F32)
    second = rest.astype(BF)
    third = (rest - second.astype(F32)).astype(BF)
    chosen = s_ref[...]
    got = dot(first, chosen) + dot(second, chosen) + dot(third, chosen)
    lane16 = lanes_of((16, 128))
    for dt in range(7):
        for wj in range(8):
            part = got[24 * dt : 24 * dt + 24, 128 * wj : 128 * wj + 128]
            spread[dt, pl.ds(wj, 8, stride=8), :] = part[0:8]
            later = part[8:24]
            turned = jnp.where(lane16 % 8 < 3, pltpu.roll(later, 124, 1), pltpu.roll(later, 3, 1))
            spread[dt, pl.ds(64 + (7 if wj == 7 else (wj + 3) % 7), 16, stride=8), :] = turned
    for tj in range(WT):
        for hj in range(WS):
            row = (tj * WS + hj) * 8
            left, right = bias_rows(spread, 0, HEADS1, tj, hj)
            o1_ref[:, row : row + 8, 0:128] = left
            o1_ref[:, row : row + 8, 128:256] = right
    for i, found in enumerate(region_rows(r1_ref[...], 1)):
        row1_ref[i] = found
    row3_ref[...] = region_rows(r3_ref[...], 3)[0]
    for i, found in enumerate(region_columns(r1_ref[...], 1)):
        col1_ref[i] = found
    col3_ref[...] = region_columns(r3_ref[...], 3)[0]


def chooser():
    chosen = np.zeros((256, 1024), np.float32)
    for wj in range(WS):
        for dh in range(13):
            for wi in range(WS):
                chosen[dh * 13 + wi - wj + 6, wj * 128 + dh * 8 + wi] = 1.0
    return jnp.asarray(chosen, BF)


def by_height(ids):
    return jnp.transpose(ids, (1, 0, 2)).reshape(-1, ids.shape[2])


def prepare(table_one, table_three, regions_one, regions_three):
    return pl.pallas_call(
        prepare_kernel,
        out_shape=(
            jax.ShapeDtypeStruct((HEADS1, ROWS, LANES), F32),
            jax.ShapeDtypeStruct((7, 24 * 8, 128), F32),
            jax.ShapeDtypeStruct((16, 1, LANES), F32),
            jax.ShapeDtypeStruct((1, LANES), F32),
            jax.ShapeDtypeStruct((16, ROWS, 128), F32),
            jax.ShapeDtypeStruct((ROWS, 128), F32),
        ),
        scratch_shapes=[pltpu.VMEM((24, SPAN), F32)],
        compiler_params=params(),
        cost_estimate=cost(1.5),
    )(
        jnp.transpose(table_one),
        jnp.transpose(table_three),
        chooser(),
        by_height(regions_one),
        by_height(regions_three),
    )


def fold(values):
    return jnp.concatenate([values[..., 128 * g : 128 * g + 128] for g in range(4)], -2)


def unfold(values):
    return jnp.concatenate([values[..., 7 * g : 7 * g + 7, :] for g in range(4)], -1)


def early_kernel(tok_ref, early_ref):
    early_ref[...] = tok_ref[0:2, 3:17]


def late_kernel(tok_ref, cot_ref, late_ref, ha_ref, dg_ref):
    late_ref[:, 0:11] = tok_ref[0:2, 17:28]
    late_ref[:, 11:15] = fold(cot_ref[0:2, 3:7].astype(F32)).astype(BF)
    ha_ref[:, 0:3] = tok_ref[2:4, 0:3]
    ha_ref[:, 3:6] = fold(cot_ref[2:4, 0:3].astype(F32)).astype(BF)
    dg_ref[:, 0:3] = tok_ref[0:2, 0:3]
    dg_ref[:, 3:6] = fold(cot_ref[0:2, 0:3].astype(F32)).astype(BF)


def arrange(kernel, rows, *operands):
    return pl.pallas_call(
        kernel,
        out_shape=[jax.ShapeDtypeStruct((2, n, 28, 128), BF) for n in rows],
        compiler_params=params(8),
        cost_estimate=cost(0.3),
    )(*operands)


def put_rows(stage, frames, rows, values):
    values = values.astype(F32)
    stage[frames, rows, 0:28, :] = values
    stage[frames, rows, 28:36, :] = values[:, :, 0:8, :]


def cut_windows(stage, win):
    for hw in range(2):
        for ww in range(4):
            win[hw * 4 + ww] = stage[:, 7 * hw : 7 * hw + 7, 3 + 7 * ww : 11 + 7 * ww, :].reshape(
                ROWS, 128
            )


def join_windows(win, stage):
    for hw in range(2):
        for ww in range(4):
            stage[:, 7 * hw : 7 * hw + 7, 3 + 7 * ww : 11 + 7 * ww, :] = win[hw * 4 + ww].reshape(
                WT, WS, 8, 128
            )
    stage[:, :, 0:3, :] = stage[:, :, 28:31, :]


def front_kernel(late, *refs):
    n_in = 4 if late else 2
    pieces, refs = refs[:n_in], refs[n_in:]
    gain_ref, proj_ref, outw_ref, bias_ref, spread_ref, row_ref, col_ref = refs[:7]
    refs = refs[7:]
    n_out = 1 if late else 2
    outs, refs = refs[:n_out], refs[n_out:]
    b3_ref, xw_ref, kv_ref, t_ref, p_ref, o_ref, inv_ref, stage, win = refs
    own = pieces[0]
    if late:
        put_rows(stage, slice(0, 2), slice(0, 11), own[2:4, 17:28])
        put_rows(stage, slice(2, 4), slice(0, 11), pieces[1][:, 0:11])
        put_rows(stage, slice(0, 2), slice(11, 14), pieces[2][:, 0:3])
        put_rows(stage, slice(2, 4), slice(11, 14), pieces[3][:, 0:3])
    else:
        put_rows(stage, slice(0, 2), slice(0, 14), own[2:4, 3:17])
        put_rows(stage, slice(2, 4), slice(0, 14), pieces[1][...])
    cut_windows(stage, win)
    lax.fori_loop(
        0,
        STEPS,
        functools.partial(
            front_step, late, gain_ref, proj_ref, outw_ref, bias_ref, spread_ref, row_ref, col_ref,
            b3_ref, xw_ref, kv_ref, t_ref, p_ref, o_ref, inv_ref, win,
        ),
        0,
    )
    join_windows(win, stage)
    if late:
        outs[0][...] = stage[:, :, 0:28, :].astype(BF)
    else:
        outs[0][...] = stage[:, 0:9, 0:28, :].astype(BF)
        outs[1][...] = stage[:, 9:14, 0:28, :].astype(BF)


def front_step(
    late, gain_ref, proj_ref, outw_ref, bias_ref, spread_ref, row_ref, col_ref,
    b3_ref, xw_ref, kv_ref, t_ref, p_ref, o_ref, inv_ref, win, step, carry,
):
    first = 8 * late
    def block(tj, hj):
        def emit():
            left, right = bias_rows(spread_ref, 64, HEADS3, 2 * late + tj, hj)
            at = pl.ds(pl.multiple_of((tj * WS + hj) * 8, 8), 8)
            b3_ref[:, at, 0:128] = left
            b3_ref[:, at, 128:256] = right

        return emit

    count = 2 // STEPS
    blocks = [block(step * count + i, hj) for i in range(count) for hj in range(WS)]
    xs, operands = [], []
    for u in range(PER_STEP):
        w = step * PER_STEP + u
        x = win[w]
        xs.append(x)
        xw_ref[w] = x.astype(BF)
        xhat, _ = normalise(x)
        packed = dot((xhat * gain_ref[...]).astype(BF), proj_ref[...])
        q = (packed[:, :128] * (SCALE * LOG2E)).astype(BF)
        kv = packed[:, 128:].astype(BF)
        kv_ref[w] = kv
        qT, kT, vT = (lengthen(part).T for part in (q, kv[:, :128], kv[:, 128:]))
        t_ref[w, :128] = qT
        t_ref[w, 128:] = kT

        def keep(h, probs, w=w):
            p_ref[w, h] = probs

        operands.append(
            (kv[:, :128], qT, vT, region_mask(col_ref[first + w], row_ref[first + w]), lambda h: bias_ref[h], keep)
        )
    for u, (oT, inverse) in enumerate(attend_four(operands, blocks)):
        w = step * PER_STEP + u
        oT = oT.astype(BF)
        o_ref[w] = oT
        inv_ref[w] = inverse
        mixed = dot(oT.T[:ROWS], outw_ref[...]).astype(BF).astype(F32)
        win[w] = xs[u] + mixed
    return carry


SAVED = (
    ((ROWS, 128), BF),
    ((ROWS, 256), BF),
    ((256, LANES), BF),
    ((4, ROWS, LANES), BF),
    ((128, LANES), BF),
    ((8, LANES), F32),
)


def front(late, pieces, gain, proj, outw, bias, spread, row, column):
    consts = (gain, proj, outw, bias, spread)
    shapes = [(4, 14, 28, 128)] if late else [(4, 9, 28, 128), (4, 5, 28, 128)]
    out = pl.pallas_call(
        functools.partial(front_kernel, late),
        out_shape=[jax.ShapeDtypeStruct(s, BF) for s in shapes]
        + [jax.ShapeDtypeStruct((HEADS3, ROWS // 2, LANES), F32)]
        + [jax.ShapeDtypeStruct((8,) + s, d) for s, d in SAVED],
        scratch_shapes=[
            pltpu.VMEM((4, 14, 40, 128), F32),
            pltpu.VMEM((8, ROWS, 128), F32),
        ],
        compiler_params=params(),
        cost_estimate=cost(4.6),
    )(*pieces, *consts, row, column)
    return out[: len(shapes) + 1], out[len(shapes) + 1 :]


def back_kernel(late, *refs):
    n_in = 3 if late else 2
    pieces, refs = refs[:n_in], refs[n_in:]
    gain_ref, proj_ref, outw_ref = refs[:3]
    xw_ref, kv_ref, t_ref, p_ref, o_ref, inv_ref = refs[3:9]
    refs = refs[9:]
    n_out = 3 if late else 2
    outs, refs = refs[:n_out], refs[n_out:]
    stage, win = refs
    if late:
        put_rows(stage, slice(0, 4), slice(0, 14), pieces[0][...])
        outs[1][:, 11:15] = pieces[1][:, 0:4]
        outs[2][0:2, 3:6] = pieces[2][...]
        outs[2][2:4, 3:6] = pieces[1][:, 4:7]
    else:
        put_rows(stage, slice(0, 4), slice(0, 9), pieces[0][...])
        put_rows(stage, slice(0, 4), slice(9, 14), pieces[1][...])
    cut_windows(stage, win)
    lax.fori_loop(
        0,
        STEPS,
        functools.partial(
            back_step, gain_ref, proj_ref, outw_ref,
            xw_ref, kv_ref, t_ref, p_ref, o_ref, inv_ref, win,
        ),
        0,
    )
    join_windows(win, stage)
    if late:
        outs[0][...] = stage[0:2, 0:11, 0:28, :].astype(BF)
        outs[1][:, 0:11] = stage[2:4, 0:11, 0:28, :].astype(BF)
        outs[2][:, 0:3] = stage[:, 11:14, 0:28, :].astype(BF)
    else:
        outs[0][...] = stage[0:2, :, 0:28, :].astype(BF)
        outs[1][...] = stage[2:4, :, 0:28, :].astype(BF)


def back_step(
    gain_ref, proj_ref, outw_ref, xw_ref, kv_ref, t_ref, p_ref, o_ref, inv_ref, win, step, carry
):
    def window(w):
        dr = win[w]
        doT = dot_nt(outw_ref[...], lengthen(dr.astype(BF)))
        yield
        dq, dk, dv = yield from attend_four_back(
            kv_ref[w, :, 128:], t_ref[w, :128], t_ref[w, 128:], o_ref[w].astype(F32), doT,
            inv_ref[w], lambda h: p_ref[w, h],
        )
        dn = dot_nt(jnp.concatenate([dq, dk, dv], 1), proj_ref[...])
        yield
        xhat, rstd = normalise(xw_ref[w].astype(F32))
        win[w] = dr + normalise_back(dn * gain_ref[...], xhat, rstd)

    stagger(window(step * PER_STEP + u) for u in range(PER_STEP))
    return carry


def back(late, pieces, gain, proj, outw, saved):
    consts = (gain, proj, outw)
    if late:
        shapes = [(2, 11, 28, 128), (2, 15, 28, 128), (4, 6, 28, 128)]
    else:
        shapes = [(2, 14, 28, 128), (2, 14, 28, 128)]
    return pl.pallas_call(
        functools.partial(back_kernel, late),
        out_shape=[jax.ShapeDtypeStruct(s, BF) for s in shapes],
        scratch_shapes=[
            pltpu.VMEM((4, 14, 40, 128), F32),
            pltpu.VMEM((8, ROWS, 128), F32),
        ],
        compiler_params=params(),
        cost_estimate=cost(5.5),
    )(*pieces, *consts, *saved)


def merge_pairs(stage, gain_ref, weight):
    pairs = stage.shape[1]
    pieces = [
        stage[:, :, q % 2, pl.ds(q // 2, 16, stride=2), :].reshape(WT * pairs * 16, 128)
        for q in range(4)
    ]
    xhat, rstd = normalise(jnp.concatenate(pieces, 1))
    merged = dot((xhat * gain_ref[...]).astype(BF), weight).astype(BF).astype(F32)
    return merged, xhat, rstd


def merge_pairs_back(grad, xhat, rstd, gain_ref, weight, stage):
    pairs = stage.shape[1]
    dn = dot_nt(grad.astype(BF), weight)
    dg = normalise_back(dn * gain_ref[...], xhat, rstd)
    for q in range(4):
        stage[:, :, q % 2, pl.ds(q // 2, 16, stride=2), :] = dg[
            :, 128 * q : 128 * q + 128
        ].reshape(WT, pairs, 16, 128)


def put_pair_row(stage, at, values):
    stage[:, at // 2, at % 2, 0:28, :] = values.astype(F32)


def clear_pads(stage):
    stage[:, :, :, 28:32, :] = jnp.zeros((WT, stage.shape[1], 2, 4, 128), F32)


def pair_row(stage, at):
    return stage[:, at // 2, at % 2, 0:28, :].astype(BF)


def fold_merged(merged, pairs):
    halves = [
        merged[:, 128 * i : 128 * i + 128].reshape(WT, pairs, 16, 128)[:, :, 0:14] for i in range(2)
    ]
    return jnp.concatenate(halves, 2)


def unfold_merged(folded):
    pad = jnp.zeros(folded.shape[:2] + (2, 128), F32)
    halves = [
        jnp.concatenate([folded[:, :, 14 * i : 14 * i + 14], pad], 2).reshape(-1, 128)
        for i in range(2)
    ]
    return jnp.concatenate(halves, 1)


def send_kernel(res_ref, gain_ref, weight_ref, send_ref, xhat_ref, rstd_ref, stage):
    clear_pads(stage)
    for i in range(8):
        put_pair_row(stage, i, res_ref[:, 1 + i])
    merged, xhat, rstd = merge_pairs(stage, gain_ref, weight_ref[...])
    xhat_ref[...] = xhat
    rstd_ref[...] = jnp.broadcast_to(rstd, rstd_ref.shape)
    send_ref[:, 0:1] = res_ref[:, 0:1]
    send_ref[:, 1:5] = fold_merged(merged, 4).astype(BF)


def local_kernel(resA_ref, resB_ref, gain_ref, weight_ref, merged_ref, xhat_ref, rstd_ref, stage):
    clear_pads(stage)
    for i in range(5):
        put_pair_row(stage, i, resA_ref[:, i])
    for i in range(13):
        put_pair_row(stage, 5 + i, resB_ref[:, i])
    merged, xhat, rstd = merge_pairs(stage, gain_ref, weight_ref[...])
    xhat_ref[...] = xhat
    rstd_ref[...] = jnp.broadcast_to(rstd, rstd_ref.shape)
    merged_ref[...] = merged


def local_back_kernel(
    grad_ref, d30_ref, xhat_ref, rstd_ref, gain_ref, weight_ref, dA_ref, dB_ref, stage
):
    merge_pairs_back(
        grad_ref[...], xhat_ref[...], rstd_ref[:, 0:1], gain_ref, weight_ref[...], stage
    )
    for i in range(5):
        dA_ref[:, i] = pair_row(stage, i)
    for i in range(13):
        dB_ref[:, i] = pair_row(stage, 5 + i)
    dB_ref[:, 13] = d30_ref[...]


def receive_kernel(got_ref, xhat_ref, rstd_ref, gain_ref, weight_ref, d_ref, stage):
    grad = unfold_merged(got_ref[:, 1:5].astype(F32))
    merge_pairs_back(grad, xhat_ref[...], rstd_ref[:, 0:1], gain_ref, weight_ref[...], stage)
    d_ref[:, 0:1] = got_ref[:, 0:1]
    for i in range(8):
        d_ref[:, 1 + i] = pair_row(stage, i)


def merge_call(kernel, us, shapes, pairs, *operands):
    return pl.pallas_call(
        kernel,
        out_shape=[jax.ShapeDtypeStruct(shape, kind) for shape, kind in shapes],
        scratch_shapes=[pltpu.VMEM((WT, pairs, 2, 32, 128), F32)],
        compiler_params=params(),
        cost_estimate=cost(us),
    )(*operands)


def middle_kernel(
    merged_ref, resB_ref, next_ref, cot_ref, cta_ref, cha_ref, cdg_ref,
    mg1_ref, mg2_ref, g3_ref, row_ref, col_ref, mw1_ref, mw2_ref, p3_ref, biasA_ref, biasB_ref, ow3_ref,
    dm_ref, d30_ref, dN_ref, so_ref, sta_ref, sha_ref,
    stage, stage2, xhat2, rstd2, cotw, k_s, v_s, qT_s, kT_s, vT_s, probs_s, oT_s, inv_s, doT_s, dqkv_s,
):
    cotw[...] = jnp.zeros((4, 7, 8, 512), F32)
    cotw[0:2, 0:4, 0:7, :] = cot_ref[2:4, 3:7].astype(F32)
    cotw[2:4, 0:4, 0:7, :] = unfold(cta_ref[:, 11:15].astype(F32))
    cotw[0:2, 4:7, 0:7, :] = unfold(cha_ref[:, 3:6].astype(F32))
    cotw[2:4, 4:7, 0:7, :] = unfold(cdg_ref[:, 3:6].astype(F32))

    def put_merged(first, count, values):
        for half in range(2):
            block = values[:, 128 * half : 128 * half + 128].reshape(WT, count, 16, 128)
            for i in range(count):
                stage2[half, :, (first + i) // 2, (first + i) % 2] = block[:, i]

    def take_merged(first, count):
        halves = [
            jnp.concatenate(
                [
                    stage2[half, :, (first + i) // 2, (first + i) % 2].reshape(WT, 1, 16, 128)
                    for i in range(count)
                ],
                1,
            ).reshape(WT * count * 16, 128)
            for half in range(2)
        ]
        return jnp.concatenate(halves, 1)

    put_merged(0, 9, merged_ref[...])
    put_merged(10, 4, unfold_merged(next_ref[:, 1:5].astype(F32)))
    clear_pads(stage)
    put_pair_row(stage, 0, resB_ref[:, 13])
    put_pair_row(stage, 1, next_ref[:, 0])
    merged, xhat_seam, rstd_seam = merge_pairs(stage, mg1_ref, mw1_ref[...])
    put_merged(9, 1, merged)
    pieces = [
        stage2[half, :, :, q % 2, pl.ds(q // 2, 8, stride=2), :].reshape(ROWS, 128)
        for q in range(4)
        for half in range(2)
    ]
    xhat, rstd = normalise(jnp.concatenate(pieces, 1))
    xhat2[...] = xhat
    rstd2[...] = jnp.broadcast_to(rstd, (ROWS, 128))
    merged_two = dot((xhat * mg2_ref[...]).astype(BF), mw2_ref[...]).astype(BF).astype(F32)
    xhat3, rstd3 = normalise(merged_two)
    n3 = (xhat3 * g3_ref[...]).astype(BF)
    packed = [dot(n3, p3_ref[:, 512 * i : 512 * i + 512]) for i in range(3)]
    for g in range(4):
        q, k, v = (part[:, 128 * g : 128 * g + 128] for part in packed)
        q = lengthen((q * (SCALE * LOG2E)).astype(BF))
        k, v = k.astype(BF), v.astype(BF)
        k_s[g] = k
        v_s[g] = v
        qT_s[g] = q.T
        kT_s[g] = lengthen(k).T
        vT_s[g] = lengthen(v).T

    def bias_at(head):
        return jnp.concatenate([biasA_ref[head], biasB_ref[head]], 0)

    mask = region_mask(col_ref[...], row_ref[...])

    operands = []
    for g in range(4):

        def keep(h, probs, g=g):
            probs_s[g * 4 + h] = probs

        operands.append((k_s[g], qT_s[g], vT_s[g], mask, lambda h, g=g: bias_at(g * 4 + h), keep))
    for g, (oT, inverse) in enumerate(attend_four(operands)):
        oT_s[g] = oT
        inv_s[g] = inverse
    att = jnp.concatenate([oT_s[g].astype(BF).T[:ROWS] for g in range(4)], 1)
    mixed = dot(att, ow3_ref[...]).astype(BF).astype(F32)
    section = (merged_two + mixed).reshape(4, 7, 8, 512)
    section = fold(section[:, :, 0:7])
    so_ref[...] = section[0:2, 0:4].astype(BF)
    sta_ref[...] = section[2:4].astype(BF)
    sha_ref[...] = section[0:2, 4:7].astype(BF)

    cot = cotw[...].reshape(ROWS, 512)
    cot_long = lengthen(cot.astype(BF))
    doT = dot_nt(ow3_ref[...], cot_long)
    for g in range(4):
        doT_s[g] = doT[128 * g : 128 * g + 128]

    def group_back(g):
        dqkv_s[g], dqkv_s[4 + g], dqkv_s[8 + g] = yield from attend_four_back(
            v_s[g], qT_s[g], kT_s[g], oT_s[g], doT_s[g], inv_s[g], lambda h: probs_s[g * 4 + h]
        )

    stagger(group_back(g) for g in range(4))
    dpacked = jnp.concatenate([dqkv_s[i] for i in range(12)], 1)
    dn3 = dot_nt(dpacked, p3_ref[...])
    dm2 = cot + normalise_back(dn3 * g3_ref[...], xhat3, rstd3)
    dn2 = dot_nt(dm2.astype(BF), mw2_ref[...])
    dg2 = normalise_back(dn2 * mg2_ref[...], xhat2[...], rstd2[:, 0:1])
    for q in range(4):
        for half in range(2):
            at = 256 * q + 128 * half
            stage2[half, :, :, q % 2, pl.ds(q // 2, 8, stride=2), :] = dg2[:, at : at + 128].reshape(
                4, 7, 8, 128
            )

    dm_ref[...] = take_merged(0, 9)
    merge_pairs_back(take_merged(9, 1), xhat_seam, rstd_seam, mg1_ref, mw1_ref[...], stage)
    d30_ref[...] = pair_row(stage, 0)
    dN_ref[:, 0] = pair_row(stage, 1)
    dN_ref[:, 1:5] = fold_merged(take_merged(10, 4), 4).astype(BF)


def middle(*operands):
    shapes = [
        (4, 28, 128), (4, 5, 28, 128), (2, 4, 28, 128), (2, 7, 28, 128), (2, 3, 28, 128),
    ]
    return pl.pallas_call(
        middle_kernel,
        out_shape=[jax.ShapeDtypeStruct((576, 256), F32)]
        + [jax.ShapeDtypeStruct(s, BF) for s in shapes],
        scratch_shapes=[
            pltpu.VMEM((4, 1, 2, 32, 128), F32),
            pltpu.VMEM((2, 4, 7, 2, 16, 128), F32),
            pltpu.VMEM((ROWS, 1024), F32),
            pltpu.VMEM((ROWS, 128), F32),
            pltpu.VMEM((4, 7, 8, 512), F32),
            pltpu.VMEM((4, ROWS, 128), BF),
            pltpu.VMEM((4, ROWS, 128), BF),
            pltpu.VMEM((4, 128, LANES), BF),
            pltpu.VMEM((4, 128, LANES), BF),
            pltpu.VMEM((4, 128, LANES), BF),
            pltpu.VMEM((16, ROWS, LANES), BF),
            pltpu.VMEM((4, 128, LANES), F32),
            pltpu.VMEM((4, 8, LANES), F32),
            pltpu.VMEM((4, 128, LANES), F32),
            pltpu.VMEM((12, ROWS, 128), BF),
        ],
        compiler_params=params(24),
        cost_estimate=cost(9),
    )(*operands)


def join_kernel(ta_ref, own_ref, so_ref, grad_ref, section_ref, wide, narrow):
    for t in range(WT):
        wide[:, pl.ds(t, 28, stride=4), :] = (ta_ref if t < 2 else own_ref)[t % 2, 0:11].astype(F32)
        low = (ta_ref[t, 11:15] if t < 2 else so_ref[t - 2]).astype(F32)
        for g in range(4):
            narrow[g, :, pl.ds(t, 7, stride=4), :] = low[:, 7 * g : 7 * g + 7]
    for i in range(11):
        grad_ref[17 + i] = wide[i].reshape(28, 4, 128).astype(BF)
    for i in range(4):
        row = jnp.concatenate([narrow[g, i] for g in range(4)], 1)
        section_ref[3 + i] = row.reshape(7, 4, 512).astype(BF)


JOINED = [
    jax.ShapeDtypeStruct((28, 28, 4, 128), BF),
    jax.ShapeDtypeStruct((7, 7, 4, 512), BF),
]


def join(ta, own, section_own):
    return pl.pallas_call(
        join_kernel,
        out_shape=JOINED,
        scratch_shapes=[pltpu.VMEM((11, 112, 128), F32), pltpu.VMEM((4, 4, 28, 128), F32)],
        compiler_params=params(),
        cost_estimate=cost(2),
    )(ta, own, section_own)


def last_kernel(
    grad_hbm, section_hbm, ta_ref, own_ref, dg_ref, ha_ref, grad_out, section_out,
    wide, narrow, rows, section_rows, sems,
):
    del grad_hbm, section_hbm
    for t in range(WT):
        corner = dg_ref if t < 2 else ha_ref
        wide[0:3, pl.ds(t, 28, stride=4), :] = corner[t % 2, 0:3].astype(F32)
        wide[3:17, pl.ds(t, 28, stride=4), :] = (ta_ref if t < 2 else own_ref)[t % 2].astype(F32)
        high = corner[t % 2, 3:6].astype(F32)
        for g in range(4):
            narrow[g, :, pl.ds(t, 7, stride=4), :] = high[:, 7 * g : 7 * g + 7]
    for i in range(17):
        rows[i] = wide[i].reshape(28, 4, 128).astype(BF)
    copy = pltpu.make_async_copy(rows, grad_out.at[0:17], sems.at[0])
    copy.start()
    for i in range(3):
        row = jnp.concatenate([narrow[g, i] for g in range(4)], 1)
        section_rows[i] = row.reshape(7, 4, 512).astype(BF)
    other = pltpu.make_async_copy(section_rows, section_out.at[0:3], sems.at[1])
    other.start()
    copy.wait()
    other.wait()


def join_last(grad, section, ta, own, dg, ha):
    return pl.pallas_call(
        last_kernel,
        in_specs=[pl.BlockSpec(memory_space=pl.ANY)] * 2
        + [pl.BlockSpec(memory_space=pltpu.VMEM)] * 4,
        out_specs=[pl.BlockSpec(memory_space=pl.ANY)] * 2,
        out_shape=JOINED,
        scratch_shapes=[
            pltpu.VMEM((17, 112, 128), F32),
            pltpu.VMEM((4, 3, 28, 128), F32),
            pltpu.VMEM((17, 28, 4, 128), BF),
            pltpu.VMEM((3, 7, 4, 512), BF),
            pltpu.SemaphoreType.DMA((2,)),
        ],
        input_output_aliases={0: 0, 1: 1},
        compiler_params=params(),
        cost_estimate=cost(1),
    )(grad, section, ta, own, dg, ha)


IN_ORDER = Layout(major_to_minor=(0, 1, 2, 3))


def inward(values):
    return with_layout_constraint(jnp.transpose(values, (1, 2, 0, 3)), IN_ORDER)


def outward(values):
    return jnp.transpose(with_layout_constraint(values, IN_ORDER), (2, 0, 1, 3))


def send(values, axes, by):
    axes = axes.split()
    sizes = [lax.axis_size(a) for a in axes]
    if len(axes) == 1:
        pairs = [(i, (i + by) % sizes[0]) for i in range(sizes[0])]
    else:
        n, m = sizes
        pairs = [
            (i * m + j, (i + by) % n * m + (j + by) % m) for i in range(n) for j in range(m)
        ]
    return lax.ppermute(values, tuple(axes), pairs)


def per_device(
    tokens,
    regions_one,
    regions_three,
    gain_one,
    projection_one,
    outward_one,
    table_one,
    merge_gain_one,
    merge_weight_one,
    merge_gain_two,
    merge_weight_two,
    gain_three,
    projection_three,
    outward_three,
    table_three,
    cotangent,
):
    (early,) = arrange(early_kernel, (14,), tokens)
    ta_early = send(inward(early), "ta", -1)
    late, ha_late, dg_late = arrange(late_kernel, (15, 6, 6), tokens, cotangent)
    ha_late = send(ha_late, "ha", -1)
    dg_late = send(dg_late, "ha ta", -1)
    ta_late = send(inward(late), "ta", -1)
    bias_one, spread, row_one, row_three, col_one, col_three = prepare(
        table_one, table_three, regions_one, regions_three
    )
    gain, merge_gain, seam = gain_one[None], merge_gain_one[None], merge_weight_one
    args = (gain, projection_one, outward_one, bias_one, spread)
    (res_send, res_a, bias_a), saved_a = front(False, (tokens, outward(ta_early)), *args, row_one, col_one)
    row_send, *early_norm = merge_call(
        send_kernel, 0.5, [((4, 5, 28, 128), BF), ((256, 512), F32), ((256, 128), F32)], 4,
        res_send, merge_gain, seam,
    )
    row_next = send(row_send, "ha", -1)
    ta_late, res_a = lax.optimization_barrier((ta_late, res_a))
    ta_late = outward(ta_late)
    (res_b, bias_b), saved_b = front(True, (tokens, ta_late, ha_late, dg_late), *args, row_one, col_one)
    merged, *local_norm = merge_call(
        local_kernel, 0.1, [((576, 256), F32), ((576, 512), F32), ((576, 128), F32)], 9,
        res_a, res_b, merge_gain, seam,
    )
    row_next, merged = lax.optimization_barrier((row_next, merged))
    d_merged, d_30, d_send, sec_own, sec_ta, sec_ha = middle(
        merged, res_b, row_next, cotangent, ta_late, ha_late, dg_late,
        merge_gain, merge_gain_two[None], gain_three[None], row_three, col_three,
        merge_weight_one, merge_weight_two, projection_three, bias_a, bias_b, outward_three,
    )
    d_prev = send(d_send, "ha", 1)
    d_a, d_b = merge_call(
        local_back_kernel, 1, [((4, 5, 28, 128), BF), ((4, 14, 28, 128), BF)], 9,
        d_merged, d_30, *local_norm, merge_gain, seam,
    )
    own_b, ta_b, ha_b = back(
        True, (d_b, sec_ta, sec_ha), gain, projection_one, outward_one, saved_b
    )
    d_prev, own_b = lax.optimization_barrier((d_prev, own_b))
    ta_b = send(inward(ta_b), "ta", 1)
    ha_b = send(ha_b, "ha", 1)
    (d_first,) = merge_call(
        receive_kernel, 0.5, [((4, 9, 28, 128), BF)], 4, d_prev, *early_norm, merge_gain, seam
    )
    own_a, ta_a = back(False, (d_first, d_a), gain, projection_one, outward_one, saved_a)
    ta_b, ha_b, own_a = lax.optimization_barrier((ta_b, ha_b, own_a))
    ta_a = send(inward(ta_a), "ta", 1)
    dg_b = send(ha_b[2:], "ta", 1)
    grad, section = join(outward(ta_b), own_b, sec_own)
    ta_a, dg_b, grad = lax.optimization_barrier((ta_a, dg_b, grad))
    grad, section = join_last(grad, section, outward(ta_a), own_a, dg_b, ha_b)
    return (jnp.transpose(section, (2, 0, 1, 3)), jnp.transpose(grad, (2, 0, 1, 3)))


def solution(mesh):
    tile = P(("col", "ta"), "ha", None, None)
    ids = P(("col", "ta"), "ha", None)
    in_specs = (tile, ids, ids) + (P(),) * 12 + (tile,)
    return jax.shard_map(
        per_device, mesh=mesh, in_specs=in_specs, out_specs=(tile, tile), check_vma=False
    )
```

```python
import functools

import jax
import jax.numpy as jnp
import numpy as np
from jax import lax
from jax.experimental import pallas as pl
from jax.experimental.layout import Layout, with_layout_constraint
from jax.experimental.pallas import tpu as pltpu
from jax.sharding import PartitionSpec as P

HEADS1 = 4
HEADS3 = 16
WT = 4
WS = 7
ST = 2
SS = 3
EPSILON = 1e-05
NREL = 1183
LOG2E = 1.4426950408889634
HEAD = 32
SCALE = HEAD**-0.5
ROWS = WT * WS * 8
LANES = 256
SPAN = 1280
GONE = -1e30
PER_STEP = 8
STEPS = 8 // PER_STEP
BF = jnp.bfloat16
F32 = jnp.float32


def dot(a, b):
    return jnp.dot(a, b, preferred_element_type=F32)


def dot_nt(a, b):
    return lax.dot_general(a, b, (((1,), (1,)), ((), ())), preferred_element_type=F32)


def params(limit=20):
    return pltpu.CompilerParams(vmem_limit_bytes=limit * 1024 * 1024)


def cost(us):
    return pl.CostEstimate(flops=int(us * 1.1e9), bytes_accessed=int(us * 1e6), transcendentals=0)


def normalise(x):
    centred = x - jnp.mean(x, -1, keepdims=True)
    rstd = lax.rsqrt(jnp.mean(centred * centred, -1, keepdims=True) + EPSILON)
    return centred * rstd, rstd


def normalise_back(grad, xhat, rstd):
    return rstd * (
        grad
        - jnp.mean(grad, -1, keepdims=True)
        - xhat * jnp.mean(grad * xhat, -1, keepdims=True)
    )


def head_rows(x, h):
    return x[HEAD * h : HEAD * (h + 1)]


def head_of_lane(shape):
    return lax.broadcasted_iota(jnp.int32, shape, 1) // HEAD


def by_head(x):
    lane = head_of_lane((1, 128))
    return jnp.concatenate([x * (lane == h).astype(F32).astype(BF) for h in range(4)], 0)


def pick_heads(stacked):
    lane = head_of_lane((ROWS, 128))
    got = stacked[:ROWS]
    for h in range(1, 4):
        got = jnp.where(lane == h, stacked[ROWS * h : ROWS * (h + 1)], got)
    return got


def lengthen(x):
    return jnp.concatenate([x, jnp.zeros((LANES - ROWS, x.shape[1]), x.dtype)], 0)


def region_mask(column, row):
    return jnp.where(jnp.concatenate([column, column], 1) == row, 0.0, GONE).astype(F32)


def lockstep(active):
    active = list(active)
    while active:
        active = [g for g in active if next(g, "end") is None]


def attend_four(windows, beside=()):
    scores = [dot(by_head(k), qT) for k, qT, _, _, _, _ in windows]
    results = []
    beside = list(beside)
    share = -(-len(beside) // len(windows))
    for s, (_, _, vT, mask, bias_at, keep_probs) in zip(scores, windows):
        for emit in beside[:share]:
            emit()
        beside = beside[share:]
        outs, inverses = [], []
        for h in range(4):
            biased = s[ROWS * h : ROWS * (h + 1)] + (bias_at(h) + mask)
            peak = jnp.max(biased, 0, keepdims=True)
            probs = jnp.exp2(biased - peak).astype(BF)
            keep_probs(h, probs)
            extended = jnp.concatenate([head_rows(vT, h)[:, :ROWS], jnp.ones((16, ROWS), BF)], 0)
            out = dot(extended, probs)
            inverse = 1.0 / out[HEAD : HEAD + 1]
            outs.append(out[:HEAD] * inverse)
            inverses.append(inverse)
        results.append((jnp.concatenate(outs, 0), jnp.concatenate(inverses + inverses, 0)))
    return results


def attend_four_back(v, qT, kT, oT, doT, inverse, probs_at):
    scaled, deltas = [], []
    for h in range(4):
        part = head_rows(doT, h) * inverse[h : h + 1]
        deltas.append(jnp.sum(part * head_rows(oT, h), 0, keepdims=True))
        scaled.append(part)
    scaled = jnp.concatenate(scaled, 0).astype(BF)
    dprobs = dot(by_head(v), scaled)
    yield
    probs = [probs_at(h) for h in range(4)]
    dscores = [
        (probs[h].astype(F32) * (dprobs[ROWS * h : ROWS * (h + 1)] - deltas[h])).astype(BF)
        for h in range(4)
    ]
    dv = pick_heads(dot_nt(jnp.concatenate(probs, 0), scaled))
    yield
    dk = pick_heads(dot_nt(jnp.concatenate(dscores, 0), qT))
    dqT = jnp.concatenate([dot(head_rows(kT, h)[:, :ROWS], dscores[h]) for h in range(4)], 0)
    yield
    dq = (dqT * SCALE).astype(BF).T[:ROWS]
    return dq, (dk * (1.0 / LOG2E)).astype(BF), dv.astype(BF)


def lanes_of(shape):
    return lax.broadcasted_iota(jnp.int32, shape, 1)


def region_rows(ids, section):
    columns = ids.shape[1]
    count = columns // WS
    place = lax.broadcasted_iota(jnp.int32, (columns, LANES * count), 0)
    lane = lanes_of((columns, LANES * count))
    column = lane % 8
    real = (column < WS) & (lane % LANES < ROWS)
    if section == 3:
        column = jnp.where(column < 3, column + 4, column - 3)
    chosen = real & (place == lane // LANES * WS + column)
    spread = dot(ids.astype(F32).astype(BF), chosen.astype(F32).astype(BF))
    row = lax.broadcasted_iota(jnp.int32, spread.shape, 0)
    lane = lanes_of(spread.shape)
    real = (lane[:1] % 8 < WS) & (lane[:1] % LANES < ROWS)
    rows = []
    for hw in range(ids.shape[0] // (WT * WS)):
        mine = lane % LANES // 8 == row % 4 * WS + row // 4 - WS * hw
        inside = (row >= WT * WS * hw) & (row < WT * WS * (hw + 1))
        found = jnp.sum(jnp.where(mine & inside, spread, 0.0), 0, keepdims=True)
        found = jnp.where(real, found, -1.0)
        rows += [found[:, LANES * ww : LANES * (ww + 1)] for ww in range(count)]
    return rows


def region_columns(ids, section):
    columns = ids.shape[1]
    count = columns // WS
    source = ids.astype(F32).astype(BF)
    token = lax.broadcasted_iota(jnp.int32, (ROWS, ids.shape[0]), 0)
    place = lanes_of((ROWS, ids.shape[0]))
    column = lax.broadcasted_iota(jnp.int32, (ROWS, columns), 0) % 8
    lane = lanes_of((ROWS, columns))
    if section == 3:
        column = jnp.where(column < 3, column + 4, jnp.where(column == 7, 8, column - 3))
    ones = jnp.ones((columns, 128), BF)
    pad = lax.broadcasted_iota(jnp.int32, (ROWS, 128), 0) % 8 == 7
    found = []
    for hw in range(ids.shape[0] // (WT * WS)):
        chosen = place == (token // 8 % WS + WS * hw) * WT + token // 56
        picked = dot(chosen.astype(F32).astype(BF), source)
        for ww in range(count):
            mine = jnp.where(lane == WS * ww + column, picked, 0.0).astype(BF)
            found.append(jnp.where(pad, -1.0, dot(mine, ones)))
    return found


def bias_rows(spread, at, heads, tj, hj):
    lane = lanes_of((heads * 8, 128))
    p0, p1, p2, p3 = (
        pltpu.roll(
            spread[ti - tj + 3, at : at + heads * 8, :], (ti * 56 - (6 - hj) * 8) % 128, 1
        )
        for ti in range(WT)
    )
    left = jnp.where(lane < 56, p0, jnp.where(lane < 112, p1, p2))
    right = jnp.where(lane < 40, p2, p3)
    return left.reshape(heads, 8, 128), right.reshape(heads, 8, 128)


def prepare_kernel(
    t1_ref, t3_ref, s_ref, r1_ref, r3_ref, o1_ref, spread, row1_ref, row3_ref, col1_ref, col3_ref, tab
):
    tab[...] = jnp.zeros((24, SPAN), F32)
    tab[0:4, 0:NREL] = t1_ref[...] * LOG2E
    tab[8:24, 0:NREL] = t3_ref[...] * LOG2E
    slabs = []
    for dt in range(7):
        start = 169 * dt
        low = start // 128 * 128
        run = tab[:, low : low + 384]
        if start > low:
            run = pltpu.roll(run, 384 - (start - low), 1)
        slabs.append(run[:, :256])
    left = jnp.concatenate(slabs, 0)
    first = left.astype(BF)
    rest = left - first.astype(F32)
    second = rest.astype(BF)
    third = (rest - second.astype(F32)).astype(BF)
    chosen = s_ref[...]
    got = dot(first, chosen) + dot(second, chosen) + dot(third, chosen)
    lane16 = lanes_of((16, 128))
    for dt in range(7):
        for wj in range(8):
            part = got[24 * dt : 24 * dt + 24, 128 * wj : 128 * wj + 128]
            spread[dt, pl.ds(wj, 8, stride=8), :] = part[0:8]
            later = part[8:24]
            turned = jnp.where(lane16 % 8 < 3, pltpu.roll(later, 124, 1), pltpu.roll(later, 3, 1))
            spread[dt, pl.ds(64 + (7 if wj == 7 else (wj + 3) % 7), 16, stride=8), :] = turned
    for tj in range(WT):
        for hj in range(WS):
            row = (tj * WS + hj) * 8
            left, right = bias_rows(spread, 0, HEADS1, tj, hj)
            o1_ref[:, row : row + 8, 0:128] = left
            o1_ref[:, row : row + 8, 128:256] = right
    for i, found in enumerate(region_rows(r1_ref[...], 1)):
        row1_ref[i] = found
    row3_ref[...] = region_rows(r3_ref[...], 3)[0]
    for i, found in enumerate(region_columns(r1_ref[...], 1)):
        col1_ref[i] = found
    col3_ref[...] = region_columns(r3_ref[...], 3)[0]


def chooser():
    chosen = np.zeros((256, 1024), np.float32)
    for wj in range(WS):
        for dh in range(13):
            for wi in range(WS):
                chosen[dh * 13 + wi - wj + 6, wj * 128 + dh * 8 + wi] = 1.0
    return jnp.asarray(chosen, BF)


def by_height(ids):
    return jnp.transpose(ids, (1, 0, 2)).reshape(-1, ids.shape[2])


def prepare(table_one, table_three, regions_one, regions_three):
    return pl.pallas_call(
        prepare_kernel,
        out_shape=(
            jax.ShapeDtypeStruct((HEADS1, ROWS, LANES), F32),
            jax.ShapeDtypeStruct((7, 24 * 8, 128), F32),
            jax.ShapeDtypeStruct((16, 1, LANES), F32),
            jax.ShapeDtypeStruct((1, LANES), F32),
            jax.ShapeDtypeStruct((16, ROWS, 128), F32),
            jax.ShapeDtypeStruct((ROWS, 128), F32),
        ),
        scratch_shapes=[pltpu.VMEM((24, SPAN), F32)],
        compiler_params=params(),
        cost_estimate=cost(1.5),
    )(
        jnp.transpose(table_one),
        jnp.transpose(table_three),
        chooser(),
        by_height(regions_one),
        by_height(regions_three),
    )


def fold(values):
    return jnp.concatenate([values[..., 128 * g : 128 * g + 128] for g in range(4)], -2)


def unfold(values):
    return jnp.concatenate([values[..., 7 * g : 7 * g + 7, :] for g in range(4)], -1)


def early_kernel(tok_ref, early_ref):
    early_ref[...] = tok_ref[0:2, 3:17]


def late_kernel(tok_ref, cot_ref, late_ref, ha_ref, dg_ref):
    late_ref[:, 0:11] = tok_ref[0:2, 17:28]
    late_ref[:, 11:15] = fold(cot_ref[0:2, 3:7].astype(F32)).astype(BF)
    ha_ref[:, 0:3] = tok_ref[2:4, 0:3]
    ha_ref[:, 3:6] = fold(cot_ref[2:4, 0:3].astype(F32)).astype(BF)
    dg_ref[:, 0:3] = tok_ref[0:2, 0:3]
    dg_ref[:, 3:6] = fold(cot_ref[0:2, 0:3].astype(F32)).astype(BF)


def arrange(kernel, rows, *operands):
    return pl.pallas_call(
        kernel,
        out_shape=[jax.ShapeDtypeStruct((2, n, 28, 128), BF) for n in rows],
        compiler_params=params(8),
        cost_estimate=cost(0.3),
    )(*operands)


def put_rows(stage, frames, rows, values):
    values = values.astype(F32)
    stage[frames, rows, 0:28, :] = values
    stage[frames, rows, 28:36, :] = values[:, :, 0:8, :]


def cut_windows(stage, win):
    for hw in range(2):
        for ww in range(4):
            win[hw * 4 + ww] = stage[:, 7 * hw : 7 * hw + 7, 3 + 7 * ww : 11 + 7 * ww, :].reshape(
                ROWS, 128
            )


def join_windows(win, stage):
    for hw in range(2):
        for ww in range(4):
            stage[:, 7 * hw : 7 * hw + 7, 3 + 7 * ww : 11 + 7 * ww, :] = win[hw * 4 + ww].reshape(
                WT, WS, 8, 128
            )
    stage[:, :, 0:3, :] = stage[:, :, 28:31, :]


def front_kernel(late, *refs):
    n_in = 4 if late else 2
    pieces, refs = refs[:n_in], refs[n_in:]
    gain_ref, proj_ref, outw_ref, bias_ref, spread_ref, row_ref, col_ref = refs[:7]
    refs = refs[7:]
    n_out = 1 if late else 2
    outs, refs = refs[:n_out], refs[n_out:]
    b3_ref, xw_ref, kv_ref, t_ref, p_ref, o_ref, inv_ref, stage, win = refs
    own = pieces[0]
    if late:
        put_rows(stage, slice(0, 2), slice(0, 11), own[2:4, 17:28])
        put_rows(stage, slice(2, 4), slice(0, 11), pieces[1][:, 0:11])
        put_rows(stage, slice(0, 2), slice(11, 14), pieces[2][:, 0:3])
        put_rows(stage, slice(2, 4), slice(11, 14), pieces[3][:, 0:3])
    else:
        put_rows(stage, slice(0, 2), slice(0, 14), own[2:4, 3:17])
        put_rows(stage, slice(2, 4), slice(0, 14), pieces[1][...])
    cut_windows(stage, win)
    lax.fori_loop(
        0,
        STEPS,
        functools.partial(
            front_step, late, gain_ref, proj_ref, outw_ref, bias_ref, spread_ref, row_ref, col_ref,
            b3_ref, xw_ref, kv_ref, t_ref, p_ref, o_ref, inv_ref, win,
        ),
        0,
    )
    join_windows(win, stage)
    if late:
        outs[0][...] = stage[:, :, 0:28, :].astype(BF)
    else:
        outs[0][...] = stage[:, 0:9, 0:28, :].astype(BF)
        outs[1][...] = stage[:, 9:14, 0:28, :].astype(BF)


def front_step(
    late, gain_ref, proj_ref, outw_ref, bias_ref, spread_ref, row_ref, col_ref,
    b3_ref, xw_ref, kv_ref, t_ref, p_ref, o_ref, inv_ref, win, step, carry,
):
    first = 8 * late
    def block(tj, hj):
        def emit():
            left, right = bias_rows(spread_ref, 64, HEADS3, 2 * late + tj, hj)
            at = pl.ds(pl.multiple_of((tj * WS + hj) * 8, 8), 8)
            b3_ref[:, at, 0:128] = left
            b3_ref[:, at, 128:256] = right

        return emit

    count = 2 // STEPS
    blocks = [block(step * count + i, hj) for i in range(count) for hj in range(WS)]
    xs, operands = [], []
    for u in range(PER_STEP):
        w = step * PER_STEP + u
        x = win[w]
        xs.append(x)
        xw_ref[w] = x.astype(BF)
        xhat, _ = normalise(x)
        packed = dot((xhat * gain_ref[...]).astype(BF), proj_ref[...])
        q = (packed[:, :128] * (SCALE * LOG2E)).astype(BF)
        kv = packed[:, 128:].astype(BF)
        kv_ref[w] = kv
        qT, kT, vT = (lengthen(part).T for part in (q, kv[:, :128], kv[:, 128:]))
        t_ref[w, :128] = qT
        t_ref[w, 128:] = kT

        def keep(h, probs, w=w):
            p_ref[w, h] = probs

        operands.append(
            (kv[:, :128], qT, vT, region_mask(col_ref[first + w], row_ref[first + w]), lambda h: bias_ref[h], keep)
        )
    for u, (oT, inverse) in enumerate(attend_four(operands, blocks)):
        w = step * PER_STEP + u
        oT = oT.astype(BF)
        o_ref[w] = oT
        inv_ref[w] = inverse
        mixed = dot(oT.T[:ROWS], outw_ref[...]).astype(BF).astype(F32)
        win[w] = xs[u] + mixed
    return carry


SAVED = (
    ((ROWS, 128), BF),
    ((ROWS, 256), BF),
    ((256, LANES), BF),
    ((4, ROWS, LANES), BF),
    ((128, LANES), BF),
    ((8, LANES), F32),
)


def front(late, pieces, gain, proj, outw, bias, spread, row, column):
    consts = (gain, proj, outw, bias, spread)
    shapes = [(4, 14, 28, 128)] if late else [(4, 9, 28, 128), (4, 5, 28, 128)]
    out = pl.pallas_call(
        functools.partial(front_kernel, late),
        out_shape=[jax.ShapeDtypeStruct(s, BF) for s in shapes]
        + [jax.ShapeDtypeStruct((HEADS3, ROWS // 2, LANES), F32)]
        + [jax.ShapeDtypeStruct((8,) + s, d) for s, d in SAVED],
        scratch_shapes=[
            pltpu.VMEM((4, 14, 40, 128), F32),
            pltpu.VMEM((8, ROWS, 128), F32),
        ],
        compiler_params=params(),
        cost_estimate=cost(4.6),
    )(*pieces, *consts, row, column)
    return out[: len(shapes) + 1], out[len(shapes) + 1 :]


def back_kernel(late, *refs):
    n_in = 3 if late else 2
    pieces, refs = refs[:n_in], refs[n_in:]
    gain_ref, proj_ref, outw_ref = refs[:3]
    xw_ref, kv_ref, t_ref, p_ref, o_ref, inv_ref = refs[3:9]
    refs = refs[9:]
    n_out = 3 if late else 2
    outs, refs = refs[:n_out], refs[n_out:]
    stage, win = refs
    if late:
        put_rows(stage, slice(0, 4), slice(0, 14), pieces[0][...])
        outs[1][:, 11:15] = pieces[1][:, 0:4]
        outs[2][0:2, 3:6] = pieces[2][...]
        outs[2][2:4, 3:6] = pieces[1][:, 4:7]
    else:
        put_rows(stage, slice(0, 4), slice(0, 9), pieces[0][...])
        put_rows(stage, slice(0, 4), slice(9, 14), pieces[1][...])
    cut_windows(stage, win)
    lax.fori_loop(
        0,
        STEPS,
        functools.partial(
            back_step, gain_ref, proj_ref, outw_ref,
            xw_ref, kv_ref, t_ref, p_ref, o_ref, inv_ref, win,
        ),
        0,
    )
    join_windows(win, stage)
    if late:
        outs[0][...] = stage[0:2, 0:11, 0:28, :].astype(BF)
        outs[1][:, 0:11] = stage[2:4, 0:11, 0:28, :].astype(BF)
        outs[2][:, 0:3] = stage[:, 11:14, 0:28, :].astype(BF)
    else:
        outs[0][...] = stage[0:2, :, 0:28, :].astype(BF)
        outs[1][...] = stage[2:4, :, 0:28, :].astype(BF)


def back_step(
    gain_ref, proj_ref, outw_ref, xw_ref, kv_ref, t_ref, p_ref, o_ref, inv_ref, win, step, carry
):
    def window(w):
        dr = win[w]
        doT = dot_nt(outw_ref[...], lengthen(dr.astype(BF)))
        yield
        dq, dk, dv = yield from attend_four_back(
            kv_ref[w, :, 128:], t_ref[w, :128], t_ref[w, 128:], o_ref[w].astype(F32), doT,
            inv_ref[w], lambda h: p_ref[w, h],
        )
        dn = dot_nt(jnp.concatenate([dq, dk, dv], 1), proj_ref[...])
        yield
        xhat, rstd = normalise(xw_ref[w].astype(F32))
        win[w] = dr + normalise_back(dn * gain_ref[...], xhat, rstd)

    lockstep(window(step * PER_STEP + u) for u in range(PER_STEP))
    return carry


def back(late, pieces, gain, proj, outw, saved):
    consts = (gain, proj, outw)
    if late:
        shapes = [(2, 11, 28, 128), (2, 15, 28, 128), (4, 6, 28, 128)]
    else:
        shapes = [(2, 14, 28, 128), (2, 14, 28, 128)]
    return pl.pallas_call(
        functools.partial(back_kernel, late),
        out_shape=[jax.ShapeDtypeStruct(s, BF) for s in shapes],
        scratch_shapes=[
            pltpu.VMEM((4, 14, 40, 128), F32),
            pltpu.VMEM((8, ROWS, 128), F32),
        ],
        compiler_params=params(),
        cost_estimate=cost(5.5),
    )(*pieces, *consts, *saved)


def merge_pairs(stage, gain_ref, weight):
    pairs = stage.shape[1]
    pieces = [
        stage[:, :, q % 2, pl.ds(q // 2, 16, stride=2), :].reshape(WT * pairs * 16, 128)
        for q in range(4)
    ]
    xhat, rstd = normalise(jnp.concatenate(pieces, 1))
    merged = dot((xhat * gain_ref[...]).astype(BF), weight).astype(BF).astype(F32)
    return merged, xhat, rstd


def merge_pairs_back(grad, xhat, rstd, gain_ref, weight, stage):
    pairs = stage.shape[1]
    dn = dot_nt(grad.astype(BF), weight)
    dg = normalise_back(dn * gain_ref[...], xhat, rstd)
    for q in range(4):
        stage[:, :, q % 2, pl.ds(q // 2, 16, stride=2), :] = dg[
            :, 128 * q : 128 * q + 128
        ].reshape(WT, pairs, 16, 128)


def put_pair_row(stage, at, values):
    stage[:, at // 2, at % 2, 0:28, :] = values.astype(F32)


def clear_pads(stage):
    stage[:, :, :, 28:32, :] = jnp.zeros((WT, stage.shape[1], 2, 4, 128), F32)


def pair_row(stage, at):
    return stage[:, at // 2, at % 2, 0:28, :].astype(BF)


def fold_merged(merged, pairs):
    halves = [
        merged[:, 128 * i : 128 * i + 128].reshape(WT, pairs, 16, 128)[:, :, 0:14] for i in range(2)
    ]
    return jnp.concatenate(halves, 2)


def unfold_merged(folded):
    pad = jnp.zeros(folded.shape[:2] + (2, 128), F32)
    halves = [
        jnp.concatenate([folded[:, :, 14 * i : 14 * i + 14], pad], 2).reshape(-1, 128)
        for i in range(2)
    ]
    return jnp.concatenate(halves, 1)


def send_kernel(res_ref, gain_ref, weight_ref, send_ref, xhat_ref, rstd_ref, stage):
    clear_pads(stage)
    for i in range(8):
        put_pair_row(stage, i, res_ref[:, 1 + i])
    merged, xhat, rstd = merge_pairs(stage, gain_ref, weight_ref[...])
    xhat_ref[...] = xhat
    rstd_ref[...] = jnp.broadcast_to(rstd, rstd_ref.shape)
    send_ref[:, 0:1] = res_ref[:, 0:1]
    send_ref[:, 1:5] = fold_merged(merged, 4).astype(BF)


def local_kernel(resA_ref, resB_ref, gain_ref, weight_ref, merged_ref, xhat_ref, rstd_ref, stage):
    clear_pads(stage)
    for i in range(5):
        put_pair_row(stage, i, resA_ref[:, i])
    for i in range(13):
        put_pair_row(stage, 5 + i, resB_ref[:, i])
    merged, xhat, rstd = merge_pairs(stage, gain_ref, weight_ref[...])
    xhat_ref[...] = xhat
    rstd_ref[...] = jnp.broadcast_to(rstd, rstd_ref.shape)
    merged_ref[...] = merged


def local_back_kernel(
    grad_ref, d30_ref, xhat_ref, rstd_ref, gain_ref, weight_ref, dA_ref, dB_ref, stage
):
    merge_pairs_back(
        grad_ref[...], xhat_ref[...], rstd_ref[:, 0:1], gain_ref, weight_ref[...], stage
    )
    for i in range(5):
        dA_ref[:, i] = pair_row(stage, i)
    for i in range(13):
        dB_ref[:, i] = pair_row(stage, 5 + i)
    dB_ref[:, 13] = d30_ref[...]


def receive_kernel(got_ref, xhat_ref, rstd_ref, gain_ref, weight_ref, d_ref, stage):
    grad = unfold_merged(got_ref[:, 1:5].astype(F32))
    merge_pairs_back(grad, xhat_ref[...], rstd_ref[:, 0:1], gain_ref, weight_ref[...], stage)
    d_ref[:, 0:1] = got_ref[:, 0:1]
    for i in range(8):
        d_ref[:, 1 + i] = pair_row(stage, i)


def merge_call(kernel, us, shapes, pairs, *operands):
    return pl.pallas_call(
        kernel,
        out_shape=[jax.ShapeDtypeStruct(shape, kind) for shape, kind in shapes],
        scratch_shapes=[pltpu.VMEM((WT, pairs, 2, 32, 128), F32)],
        compiler_params=params(),
        cost_estimate=cost(us),
    )(*operands)


def middle_kernel(
    merged_ref, resB_ref, next_ref, cot_ref, cta_ref, cha_ref, cdg_ref,
    mg1_ref, mg2_ref, g3_ref, row_ref, col_ref, mw1_ref, mw2_ref, p3_ref, biasA_ref, biasB_ref, ow3_ref,
    dm_ref, d30_ref, dN_ref, so_ref, sta_ref, sha_ref,
    stage, stage2, xhat2, rstd2, cotw, k_s, v_s, qT_s, kT_s, vT_s, probs_s, oT_s, inv_s, doT_s, dqkv_s,
):
    cotw[...] = jnp.zeros((4, 7, 8, 512), F32)
    cotw[0:2, 0:4, 0:7, :] = cot_ref[2:4, 3:7].astype(F32)
    cotw[2:4, 0:4, 0:7, :] = unfold(cta_ref[:, 11:15].astype(F32))
    cotw[0:2, 4:7, 0:7, :] = unfold(cha_ref[:, 3:6].astype(F32))
    cotw[2:4, 4:7, 0:7, :] = unfold(cdg_ref[:, 3:6].astype(F32))

    def put_merged(first, count, values):
        for half in range(2):
            block = values[:, 128 * half : 128 * half + 128].reshape(WT, count, 16, 128)
            for i in range(count):
                stage2[half, :, (first + i) // 2, (first + i) % 2] = block[:, i]

    def take_merged(first, count):
        halves = [
            jnp.concatenate(
                [
                    stage2[half, :, (first + i) // 2, (first + i) % 2].reshape(WT, 1, 16, 128)
                    for i in range(count)
                ],
                1,
            ).reshape(WT * count * 16, 128)
            for half in range(2)
        ]
        return jnp.concatenate(halves, 1)

    put_merged(0, 9, merged_ref[...])
    put_merged(10, 4, unfold_merged(next_ref[:, 1:5].astype(F32)))
    clear_pads(stage)
    put_pair_row(stage, 0, resB_ref[:, 13])
    put_pair_row(stage, 1, next_ref[:, 0])
    merged, xhat_seam, rstd_seam = merge_pairs(stage, mg1_ref, mw1_ref[...])
    put_merged(9, 1, merged)
    pieces = [
        stage2[half, :, :, q % 2, pl.ds(q // 2, 8, stride=2), :].reshape(ROWS, 128)
        for q in range(4)
        for half in range(2)
    ]
    xhat, rstd = normalise(jnp.concatenate(pieces, 1))
    xhat2[...] = xhat
    rstd2[...] = jnp.broadcast_to(rstd, (ROWS, 128))
    merged_two = dot((xhat * mg2_ref[...]).astype(BF), mw2_ref[...]).astype(BF).astype(F32)
    xhat3, rstd3 = normalise(merged_two)
    n3 = (xhat3 * g3_ref[...]).astype(BF)
    packed = [dot(n3, p3_ref[:, 512 * i : 512 * i + 512]) for i in range(3)]
    for g in range(4):
        q, k, v = (part[:, 128 * g : 128 * g + 128] for part in packed)
        q = lengthen((q * (SCALE * LOG2E)).astype(BF))
        k, v = k.astype(BF), v.astype(BF)
        k_s[g] = k
        v_s[g] = v
        qT_s[g] = q.T
        kT_s[g] = lengthen(k).T
        vT_s[g] = lengthen(v).T

    def bias_at(head):
        return jnp.concatenate([biasA_ref[head], biasB_ref[head]], 0)

    mask = region_mask(col_ref[...], row_ref[...])

    operands = []
    for g in range(4):

        def keep(h, probs, g=g):
            probs_s[g * 4 + h] = probs

        operands.append((k_s[g], qT_s[g], vT_s[g], mask, lambda h, g=g: bias_at(g * 4 + h), keep))
    for g, (oT, inverse) in enumerate(attend_four(operands)):
        oT_s[g] = oT
        inv_s[g] = inverse
    att = jnp.concatenate([oT_s[g].astype(BF).T[:ROWS] for g in range(4)], 1)
    mixed = dot(att, ow3_ref[...]).astype(BF).astype(F32)
    section = (merged_two + mixed).reshape(4, 7, 8, 512)
    section = fold(section[:, :, 0:7])
    so_ref[...] = section[0:2, 0:4].astype(BF)
    sta_ref[...] = section[2:4].astype(BF)
    sha_ref[...] = section[0:2, 4:7].astype(BF)

    cot = cotw[...].reshape(ROWS, 512)
    cot_long = lengthen(cot.astype(BF))
    doT = dot_nt(ow3_ref[...], cot_long)
    for g in range(4):
        doT_s[g] = doT[128 * g : 128 * g + 128]

    def group_back(g):
        dqkv_s[g], dqkv_s[4 + g], dqkv_s[8 + g] = yield from attend_four_back(
            v_s[g], qT_s[g], kT_s[g], oT_s[g], doT_s[g], inv_s[g], lambda h: probs_s[g * 4 + h]
        )

    lockstep(group_back(g) for g in range(4))
    dpacked = jnp.concatenate([dqkv_s[i] for i in range(12)], 1)
    dn3 = dot_nt(dpacked, p3_ref[...])
    dm2 = cot + normalise_back(dn3 * g3_ref[...], xhat3, rstd3)
    dn2 = dot_nt(dm2.astype(BF), mw2_ref[...])
    dg2 = normalise_back(dn2 * mg2_ref[...], xhat2[...], rstd2[:, 0:1])
    for q in range(4):
        for half in range(2):
            at = 256 * q + 128 * half
            stage2[half, :, :, q % 2, pl.ds(q // 2, 8, stride=2), :] = dg2[:, at : at + 128].reshape(
                4, 7, 8, 128
            )

    dm_ref[...] = take_merged(0, 9)
    merge_pairs_back(take_merged(9, 1), xhat_seam, rstd_seam, mg1_ref, mw1_ref[...], stage)
    d30_ref[...] = pair_row(stage, 0)
    dN_ref[:, 0] = pair_row(stage, 1)
    dN_ref[:, 1:5] = fold_merged(take_merged(10, 4), 4).astype(BF)


def middle(*operands):
    shapes = [
        (4, 28, 128), (4, 5, 28, 128), (2, 4, 28, 128), (2, 7, 28, 128), (2, 3, 28, 128),
    ]
    return pl.pallas_call(
        middle_kernel,
        out_shape=[jax.ShapeDtypeStruct((576, 256), F32)]
        + [jax.ShapeDtypeStruct(s, BF) for s in shapes],
        scratch_shapes=[
            pltpu.VMEM((4, 1, 2, 32, 128), F32),
            pltpu.VMEM((2, 4, 7, 2, 16, 128), F32),
            pltpu.VMEM((ROWS, 1024), F32),
            pltpu.VMEM((ROWS, 128), F32),
            pltpu.VMEM((4, 7, 8, 512), F32),
            pltpu.VMEM((4, ROWS, 128), BF),
            pltpu.VMEM((4, ROWS, 128), BF),
            pltpu.VMEM((4, 128, LANES), BF),
            pltpu.VMEM((4, 128, LANES), BF),
            pltpu.VMEM((4, 128, LANES), BF),
            pltpu.VMEM((16, ROWS, LANES), BF),
            pltpu.VMEM((4, 128, LANES), F32),
            pltpu.VMEM((4, 8, LANES), F32),
            pltpu.VMEM((4, 128, LANES), F32),
            pltpu.VMEM((12, ROWS, 128), BF),
        ],
        compiler_params=params(24),
        cost_estimate=cost(9),
    )(*operands)


def join_kernel(ta_ref, own_ref, so_ref, grad_ref, section_ref, wide, narrow):
    for t in range(WT):
        wide[:, pl.ds(t, 28, stride=4), :] = (ta_ref if t < 2 else own_ref)[t % 2, 0:11].astype(F32)
        low = (ta_ref[t, 11:15] if t < 2 else so_ref[t - 2]).astype(F32)
        for g in range(4):
            narrow[g, :, pl.ds(t, 7, stride=4), :] = low[:, 7 * g : 7 * g + 7]
    for i in range(11):
        grad_ref[17 + i] = wide[i].reshape(28, 4, 128).astype(BF)
    for i in range(4):
        row = jnp.concatenate([narrow[g, i] for g in range(4)], 1)
        section_ref[3 + i] = row.reshape(7, 4, 512).astype(BF)


JOINED = [
    jax.ShapeDtypeStruct((28, 28, 4, 128), BF),
    jax.ShapeDtypeStruct((7, 7, 4, 512), BF),
]


def join(ta, own, section_own):
    return pl.pallas_call(
        join_kernel,
        out_shape=JOINED,
        scratch_shapes=[pltpu.VMEM((11, 112, 128), F32), pltpu.VMEM((4, 4, 28, 128), F32)],
        compiler_params=params(),
        cost_estimate=cost(2),
    )(ta, own, section_own)


def last_kernel(
    grad_hbm, section_hbm, ta_ref, own_ref, dg_ref, ha_ref, grad_out, section_out,
    wide, narrow, rows, section_rows, sems,
):
    del grad_hbm, section_hbm
    for t in range(WT):
        corner = dg_ref if t < 2 else ha_ref
        wide[0:3, pl.ds(t, 28, stride=4), :] = corner[t % 2, 0:3].astype(F32)
        wide[3:17, pl.ds(t, 28, stride=4), :] = (ta_ref if t < 2 else own_ref)[t % 2].astype(F32)
        high = corner[t % 2, 3:6].astype(F32)
        for g in range(4):
            narrow[g, :, pl.ds(t, 7, stride=4), :] = high[:, 7 * g : 7 * g + 7]
    for i in range(8):
        rows[i] = wide[i].reshape(28, 4, 128).astype(BF)
    start = pltpu.make_async_copy(rows.at[0:8], grad_out.at[0:8], sems.at[2])
    start.start()
    for i in range(8, 17):
        rows[i] = wide[i].reshape(28, 4, 128).astype(BF)
    copy = pltpu.make_async_copy(rows.at[8:17], grad_out.at[8:17], sems.at[0])
    copy.start()
    for i in range(3):
        row = jnp.concatenate([narrow[g, i] for g in range(4)], 1)
        section_rows[i] = row.reshape(7, 4, 512).astype(BF)
    other = pltpu.make_async_copy(section_rows, section_out.at[0:3], sems.at[1])
    other.start()
    start.wait()
    copy.wait()
    other.wait()


def join_last(grad, section, ta, own, dg, ha):
    return pl.pallas_call(
        last_kernel,
        in_specs=[pl.BlockSpec(memory_space=pl.ANY)] * 2
        + [pl.BlockSpec(memory_space=pltpu.VMEM)] * 4,
        out_specs=[pl.BlockSpec(memory_space=pl.ANY)] * 2,
        out_shape=JOINED,
        scratch_shapes=[
            pltpu.VMEM((17, 112, 128), F32),
            pltpu.VMEM((4, 3, 28, 128), F32),
            pltpu.VMEM((17, 28, 4, 128), BF),
            pltpu.VMEM((3, 7, 4, 512), BF),
            pltpu.SemaphoreType.DMA((3,)),
        ],
        input_output_aliases={0: 0, 1: 1},
        compiler_params=params(),
        cost_estimate=cost(1),
    )(grad, section, ta, own, dg, ha)


IN_ORDER = Layout(major_to_minor=(0, 1, 2, 3))


def inward(values):
    return with_layout_constraint(jnp.transpose(values, (1, 2, 0, 3)), IN_ORDER)


def outward(values):
    return jnp.transpose(with_layout_constraint(values, IN_ORDER), (2, 0, 1, 3))


def send(values, axes, by):
    axes = axes.split()
    sizes = [lax.axis_size(a) for a in axes]
    if len(axes) == 1:
        pairs = [(i, (i + by) % sizes[0]) for i in range(sizes[0])]
    else:
        n, m = sizes
        pairs = [
            (i * m + j, (i + by) % n * m + (j + by) % m) for i in range(n) for j in range(m)
        ]
    return lax.ppermute(values, tuple(axes), pairs)


def per_device(
    tokens,
    regions_one,
    regions_three,
    gain_one,
    projection_one,
    outward_one,
    table_one,
    merge_gain_one,
    merge_weight_one,
    merge_gain_two,
    merge_weight_two,
    gain_three,
    projection_three,
    outward_three,
    table_three,
    cotangent,
):
    (early,) = arrange(early_kernel, (14,), tokens)
    ta_early = send(inward(early), "ta", -1)
    late, ha_late, dg_late = arrange(late_kernel, (15, 6, 6), tokens, cotangent)
    ha_late = send(ha_late, "ha", -1)
    dg_late = send(dg_late, "ha ta", -1)
    ta_late = send(inward(late), "ta", -1)
    bias_one, spread, row_one, row_three, col_one, col_three = prepare(
        table_one, table_three, regions_one, regions_three
    )
    gain, merge_gain, seam = gain_one[None], merge_gain_one[None], merge_weight_one
    args = (gain, projection_one, outward_one, bias_one, spread)
    (res_send, res_a, bias_a), saved_a = front(False, (tokens, outward(ta_early)), *args, row_one, col_one)
    row_send, *early_norm = merge_call(
        send_kernel, 0.5, [((4, 5, 28, 128), BF), ((256, 512), F32), ((256, 128), F32)], 4,
        res_send, merge_gain, seam,
    )
    row_next = send(row_send, "ha", -1)
    ta_late, res_a = lax.optimization_barrier((ta_late, res_a))
    ta_late = outward(ta_late)
    (res_b, bias_b), saved_b = front(True, (tokens, ta_late, ha_late, dg_late), *args, row_one, col_one)
    merged, *local_norm = merge_call(
        local_kernel, 0.1, [((576, 256), F32), ((576, 512), F32), ((576, 128), F32)], 9,
        res_a, res_b, merge_gain, seam,
    )
    row_next, merged = lax.optimization_barrier((row_next, merged))
    d_merged, d_30, d_send, sec_own, sec_ta, sec_ha = middle(
        merged, res_b, row_next, cotangent, ta_late, ha_late, dg_late,
        merge_gain, merge_gain_two[None], gain_three[None], row_three, col_three,
        merge_weight_one, merge_weight_two, projection_three, bias_a, bias_b, outward_three,
    )
    d_prev = send(d_send, "ha", 1)
    d_a, d_b = merge_call(
        local_back_kernel, 1, [((4, 5, 28, 128), BF), ((4, 14, 28, 128), BF)], 9,
        d_merged, d_30, *local_norm, merge_gain, seam,
    )
    own_b, ta_b, ha_b = back(
        True, (d_b, sec_ta, sec_ha), gain, projection_one, outward_one, saved_b
    )
    d_prev, own_b = lax.optimization_barrier((d_prev, own_b))
    ta_b = send(inward(ta_b), "ta", 1)
    ha_b = send(ha_b, "ha", 1)
    (d_first,) = merge_call(
        receive_kernel, 0.5, [((4, 9, 28, 128), BF)], 4, d_prev, *early_norm, merge_gain, seam
    )
    own_a, ta_a = back(False, (d_first, d_a), gain, projection_one, outward_one, saved_a)
    ta_b, ha_b, own_a = lax.optimization_barrier((ta_b, ha_b, own_a))
    ta_a = send(inward(ta_a), "ta", 1)
    dg_b = send(ha_b[2:], "ta", 1)
    grad, section = join(outward(ta_b), own_b, sec_own)
    ta_a, dg_b, grad = lax.optimization_barrier((ta_a, dg_b, grad))
    grad, section = join_last(grad, section, outward(ta_a), own_a, dg_b, ha_b)
    return (jnp.transpose(section, (2, 0, 1, 3)), jnp.transpose(grad, (2, 0, 1, 3)))


def solution(mesh):
    tile = P(("col", "ta"), "ha", None, None)
    ids = P(("col", "ta"), "ha", None)
    in_specs = (tile, ids, ids) + (P(),) * 12 + (tile,)
    return jax.shard_map(
        per_device, mesh=mesh, in_specs=in_specs, out_specs=(tile, tile), check_vma=False
    )
```

```python
import functools

import jax
import jax.numpy as jnp
import numpy as np
from jax import lax
from jax.experimental import pallas as pl
from jax.experimental.layout import Layout, with_layout_constraint
from jax.experimental.pallas import tpu as pltpu
from jax.sharding import PartitionSpec as P

HEADS1 = 4
HEADS3 = 16
WT = 4
WS = 7
ST = 2
SS = 3
EPSILON = 1e-05
NREL = 1183
WIDTH = 28
LOG2E = 1.4426950408889634
HEAD = 32
SCALE = HEAD**-0.5
ROWS = WT * WS * 8
LANES = 256
SPAN = 1280
GONE = -1e30
PER_STEP = 8
STEPS = 8 // PER_STEP
BF = jnp.bfloat16
F32 = jnp.float32


def dot(a, b):
    return jnp.dot(a, b, preferred_element_type=F32)


def dot_nt(a, b):
    return lax.dot_general(a, b, (((1,), (1,)), ((), ())), preferred_element_type=F32)


def params(limit=20):
    return pltpu.CompilerParams(vmem_limit_bytes=limit * 1024 * 1024)


def cost(us):
    return pl.CostEstimate(flops=int(us * 1.1e9), bytes_accessed=int(us * 1e6), transcendentals=0)


def normalise(x):
    centred = x - jnp.mean(x, -1, keepdims=True)
    rstd = lax.rsqrt(jnp.mean(centred * centred, -1, keepdims=True) + EPSILON)
    return centred * rstd, rstd


def normalise_back(grad, xhat, rstd):
    return rstd * (
        grad
        - jnp.mean(grad, -1, keepdims=True)
        - xhat * jnp.mean(grad * xhat, -1, keepdims=True)
    )


def head_rows(x, h):
    return x[HEAD * h : HEAD * (h + 1)]


def head_of_lane(shape):
    return lax.broadcasted_iota(jnp.int32, shape, 1) // HEAD


def by_head(x):
    lane = head_of_lane((1, 128))
    return jnp.concatenate([x * (lane == h).astype(F32).astype(BF) for h in range(4)], 0)


def pick_heads(stacked):
    lane = head_of_lane((ROWS, 128))
    got = stacked[:ROWS]
    for h in range(1, 4):
        got = jnp.where(lane == h, stacked[ROWS * h : ROWS * (h + 1)], got)
    return got


def lengthen(x):
    return jnp.concatenate([x, jnp.zeros((LANES - ROWS, x.shape[1]), x.dtype)], 0)


def region_mask(column, row):
    return jnp.where(jnp.concatenate([column, column], 1) == row, 0.0, GONE).astype(F32)


def lockstep(active):
    active = list(active)
    while active:
        active = [g for g in active if next(g, "end") is None]


def attend_four(windows, beside=()):
    scores = [dot(by_head(k), qT) for k, qT, _, _, _, _ in windows]
    results = []
    beside = list(beside)
    share = -(-len(beside) // len(windows))
    for s, (_, _, vT, mask, bias_at, keep_probs) in zip(scores, windows):
        for emit in beside[:share]:
            emit()
        beside = beside[share:]
        outs, inverses = [], []
        for h in range(4):
            biased = s[ROWS * h : ROWS * (h + 1)] + (bias_at(h) + mask)
            peak = jnp.max(biased, 0, keepdims=True)
            probs = jnp.exp2(biased - peak).astype(BF)
            keep_probs(h, probs)
            extended = jnp.concatenate([head_rows(vT, h)[:, :ROWS], jnp.ones((16, ROWS), BF)], 0)
            out = dot(extended, probs)
            inverse = 1.0 / out[HEAD : HEAD + 1]
            outs.append(out[:HEAD] * inverse)
            inverses.append(inverse)
        results.append((jnp.concatenate(outs, 0), jnp.concatenate(inverses + inverses, 0)))
    return results


def attend_four_back(v, qT, kT, oT, doT, inverse, probs_at):
    scaled, deltas = [], []
    for h in range(4):
        part = head_rows(doT, h) * inverse[h : h + 1]
        deltas.append(jnp.sum(part * head_rows(oT, h), 0, keepdims=True))
        scaled.append(part)
    scaled = jnp.concatenate(scaled, 0).astype(BF)
    dprobs = dot(by_head(v), scaled)
    yield
    probs = [probs_at(h) for h in range(4)]
    dscores = [
        (probs[h].astype(F32) * (dprobs[ROWS * h : ROWS * (h + 1)] - deltas[h])).astype(BF)
        for h in range(4)
    ]
    dv = pick_heads(dot_nt(jnp.concatenate(probs, 0), scaled))
    yield
    dk = pick_heads(dot_nt(jnp.concatenate(dscores, 0), qT))
    dqT = jnp.concatenate([dot(head_rows(kT, h)[:, :ROWS], dscores[h]) for h in range(4)], 0)
    yield
    dq = (dqT * SCALE).astype(BF).T[:ROWS]
    return dq, (dk * (1.0 / LOG2E)).astype(BF), dv.astype(BF)


def lanes_of(shape):
    return lax.broadcasted_iota(jnp.int32, shape, 1)


def region_rows(ids, section, place_of):
    columns = ids.shape[1]
    count = columns // WS
    place = lax.broadcasted_iota(jnp.int32, (columns, LANES * count), 0)
    lane = lanes_of((columns, LANES * count))
    column = lane % 8
    real = (column < WS) & (lane % LANES < ROWS)
    if section == 3:
        column = jnp.where(column < 3, column + 4, column - 3)
    chosen = real & (place == lane // LANES * WS + column)
    spread = dot(ids.astype(F32).astype(BF), chosen.astype(F32).astype(BF))
    lane = lanes_of((1, LANES))
    real = (lane % 8 < WS) & (lane < ROWS)
    rows = []
    for hw in range(ids.shape[0] // (WT * WS)):
        mine = place_of == float(hw)
        for ww in range(count):
            part = jnp.where(mine, spread[:, LANES * ww : LANES * (ww + 1)], 0.0)
            rows.append(jnp.where(real, jnp.sum(part, 0, keepdims=True), -1.0))
    return rows


def id_places():
    places = np.full((WIDTH * WT, LANES), -1.0, np.float32)
    for row in range(WIDTH * WT):
        height, frame = row // WT, row % WT
        at = (frame * WS + height % WS) * 8
        places[row, at : at + 8] = height // WS
    return jnp.asarray(places)


def region_columns(ids, section):
    columns = ids.shape[1]
    count = columns // WS
    source = ids.astype(F32).astype(BF)
    token = lax.broadcasted_iota(jnp.int32, (ROWS, ids.shape[0]), 0)
    place = lanes_of((ROWS, ids.shape[0]))
    column = lax.broadcasted_iota(jnp.int32, (ROWS, columns), 0) % 8
    lane = lanes_of((ROWS, columns))
    if section == 3:
        column = jnp.where(column < 3, column + 4, jnp.where(column == 7, 8, column - 3))
    ones = jnp.ones((columns, 128), BF)
    ahead = lane - column
    wanted = token // 8 % WS * WT + token // 56
    pad = lax.broadcasted_iota(jnp.int32, (ROWS, 128), 0) % 8 == 7
    found = []
    for hw in range(ids.shape[0] // (WT * WS)):
        chosen = place - WS * WT * hw == wanted
        picked = dot(chosen.astype(F32).astype(BF), source)
        for ww in range(count):
            mine = jnp.where(ahead == WS * ww, picked, 0.0).astype(BF)
            found.append(jnp.where(pad, -1.0, dot(mine, ones)))
    return found


def bias_rows(spread, at, heads, tj, hj):
    lane = lanes_of((heads * 8, 128))
    p0, p1, p2, p3 = (
        pltpu.roll(
            spread[ti - tj + 3, at : at + heads * 8, :], (ti * 56 - (6 - hj) * 8) % 128, 1
        )
        for ti in range(WT)
    )
    left = jnp.where(lane < 56, p0, jnp.where(lane < 112, p1, p2))
    right = jnp.where(lane < 40, p2, p3)
    return left.reshape(heads, 8, 128), right.reshape(heads, 8, 128)


def prepare_kernel(
    t1_ref, t3_ref, s_ref, r1_ref, r3_ref, place_ref, o1_ref, spread, row1_ref, row3_ref, col1_ref, col3_ref, tab
):
    tab[...] = jnp.zeros((24, SPAN), F32)
    tab[0:4, 0:NREL] = t1_ref[...] * LOG2E
    tab[8:24, 0:NREL] = t3_ref[...] * LOG2E
    slabs = []
    for dt in range(7):
        start = 169 * dt
        low = start // 128 * 128
        run = tab[:, low : low + 384]
        if start > low:
            run = pltpu.roll(run, 384 - (start - low), 1)
        slabs.append(run[:, :256])
    left = jnp.concatenate(slabs, 0)
    first = left.astype(BF)
    rest = left - first.astype(F32)
    second = rest.astype(BF)
    third = (rest - second.astype(F32)).astype(BF)
    chosen = s_ref[...]
    got = dot(first, chosen) + dot(second, chosen) + dot(third, chosen)
    lane16 = lanes_of((16, 128))
    for dt in range(7):
        for wj in range(8):
            part = got[24 * dt : 24 * dt + 24, 128 * wj : 128 * wj + 128]
            spread[dt, pl.ds(wj, 8, stride=8), :] = part[0:8]
            later = part[8:24]
            turned = jnp.where(lane16 % 8 < 3, pltpu.roll(later, 124, 1), pltpu.roll(later, 3, 1))
            spread[dt, pl.ds(64 + (7 if wj == 7 else (wj + 3) % 7), 16, stride=8), :] = turned
    for tj in range(WT):
        for hj in range(WS):
            row = (tj * WS + hj) * 8
            left, right = bias_rows(spread, 0, HEADS1, tj, hj)
            o1_ref[:, row : row + 8, 0:128] = left
            o1_ref[:, row : row + 8, 128:256] = right
    for i, found in enumerate(region_rows(r1_ref[...], 1, place_ref[...])):
        row1_ref[i] = found
    row3_ref[...] = region_rows(r3_ref[...], 3, place_ref[0 : WT * WS])[0]
    for i, found in enumerate(region_columns(r1_ref[...], 1)):
        col1_ref[i] = found
    col3_ref[...] = region_columns(r3_ref[...], 3)[0]


def chooser():
    chosen = np.zeros((256, 1024), np.float32)
    for wj in range(WS):
        for dh in range(13):
            for wi in range(WS):
                chosen[dh * 13 + wi - wj + 6, wj * 128 + dh * 8 + wi] = 1.0
    return jnp.asarray(chosen, BF)


def by_height(ids):
    return jnp.transpose(ids, (1, 0, 2)).reshape(-1, ids.shape[2])


def prepare(table_one, table_three, regions_one, regions_three):
    return pl.pallas_call(
        prepare_kernel,
        out_shape=(
            jax.ShapeDtypeStruct((HEADS1, ROWS, LANES), F32),
            jax.ShapeDtypeStruct((7, 24 * 8, 128), F32),
            jax.ShapeDtypeStruct((16, 1, LANES), F32),
            jax.ShapeDtypeStruct((1, LANES), F32),
            jax.ShapeDtypeStruct((16, ROWS, 128), F32),
            jax.ShapeDtypeStruct((ROWS, 128), F32),
        ),
        scratch_shapes=[pltpu.VMEM((24, SPAN), F32)],
        compiler_params=params(),
        cost_estimate=cost(1.5),
    )(
        jnp.transpose(table_one),
        jnp.transpose(table_three),
        chooser(),
        by_height(regions_one),
        by_height(regions_three),
        id_places(),
    )


def fold(values):
    return jnp.concatenate([values[..., 128 * g : 128 * g + 128] for g in range(4)], -2)


def unfold(values):
    return jnp.concatenate([values[..., 7 * g : 7 * g + 7, :] for g in range(4)], -1)


def early_kernel(tok_ref, early_ref):
    early_ref[...] = tok_ref[0:2, 3:17]


def late_kernel(tok_ref, cot_ref, late_ref, ha_ref, dg_ref):
    late_ref[:, 0:11] = tok_ref[0:2, 17:28]
    late_ref[:, 11:15] = fold(cot_ref[0:2, 3:7].astype(F32)).astype(BF)
    ha_ref[:, 0:3] = tok_ref[2:4, 0:3]
    ha_ref[:, 3:6] = fold(cot_ref[2:4, 0:3].astype(F32)).astype(BF)
    dg_ref[:, 0:3] = tok_ref[0:2, 0:3]
    dg_ref[:, 3:6] = fold(cot_ref[0:2, 0:3].astype(F32)).astype(BF)


def arrange(kernel, rows, *operands):
    return pl.pallas_call(
        kernel,
        out_shape=[jax.ShapeDtypeStruct((2, n, 28, 128), BF) for n in rows],
        compiler_params=params(8),
        cost_estimate=cost(0.3),
    )(*operands)


def put_rows(stage, frames, rows, values):
    values = values.astype(F32)
    stage[frames, rows, 0:28, :] = values
    stage[frames, rows, 28:36, :] = values[:, :, 0:8, :]


def cut_windows(stage, win):
    for hw in range(2):
        for ww in range(4):
            win[hw * 4 + ww] = stage[:, 7 * hw : 7 * hw + 7, 3 + 7 * ww : 11 + 7 * ww, :].reshape(
                ROWS, 128
            )


def join_windows(win, stage):
    for hw in range(2):
        for ww in range(4):
            stage[:, 7 * hw : 7 * hw + 7, 3 + 7 * ww : 11 + 7 * ww, :] = win[hw * 4 + ww].reshape(
                WT, WS, 8, 128
            )
    stage[:, :, 0:3, :] = stage[:, :, 28:31, :]


def front_kernel(late, *refs):
    n_in = 4 if late else 2
    pieces, refs = refs[:n_in], refs[n_in:]
    gain_ref, proj_ref, outw_ref, bias_ref, spread_ref, row_ref, col_ref = refs[:7]
    refs = refs[7:]
    n_out = 1 if late else 2
    outs, refs = refs[:n_out], refs[n_out:]
    b3_ref, xw_ref, kv_ref, t_ref, p_ref, o_ref, inv_ref, stage, win = refs
    own = pieces[0]
    if late:
        put_rows(stage, slice(0, 2), slice(0, 11), own[2:4, 17:28])
        put_rows(stage, slice(2, 4), slice(0, 11), pieces[1][:, 0:11])
        put_rows(stage, slice(0, 2), slice(11, 14), pieces[2][:, 0:3])
        put_rows(stage, slice(2, 4), slice(11, 14), pieces[3][:, 0:3])
    else:
        put_rows(stage, slice(0, 2), slice(0, 14), own[2:4, 3:17])
        put_rows(stage, slice(2, 4), slice(0, 14), pieces[1][...])
    cut_windows(stage, win)
    lax.fori_loop(
        0,
        STEPS,
        functools.partial(
            front_step, late, gain_ref, proj_ref, outw_ref, bias_ref, spread_ref, row_ref, col_ref,
            b3_ref, xw_ref, kv_ref, t_ref, p_ref, o_ref, inv_ref, win,
        ),
        0,
    )
    join_windows(win, stage)
    if late:
        outs[0][...] = stage[:, :, 0:28, :].astype(BF)
    else:
        outs[0][...] = stage[:, 0:9, 0:28, :].astype(BF)
        outs[1][...] = stage[:, 9:14, 0:28, :].astype(BF)


def front_step(
    late, gain_ref, proj_ref, outw_ref, bias_ref, spread_ref, row_ref, col_ref,
    b3_ref, xw_ref, kv_ref, t_ref, p_ref, o_ref, inv_ref, win, step, carry,
):
    first = 8 * late
    def block(tj, hj):
        def emit():
            left, right = bias_rows(spread_ref, 64, HEADS3, 2 * late + tj, hj)
            at = pl.ds(pl.multiple_of((tj * WS + hj) * 8, 8), 8)
            b3_ref[:, at, 0:128] = left
            b3_ref[:, at, 128:256] = right

        return emit

    count = 2 // STEPS
    blocks = [block(step * count + i, hj) for i in range(count) for hj in range(WS)]
    xs, operands = [], []
    for u in range(PER_STEP):
        w = step * PER_STEP + u
        x = win[w]
        xs.append(x)
        xw_ref[w] = x.astype(BF)
        xhat, _ = normalise(x)
        packed = dot((xhat * gain_ref[...]).astype(BF), proj_ref[...])
        q = (packed[:, :128] * (SCALE * LOG2E)).astype(BF)
        kv = packed[:, 128:].astype(BF)
        kv_ref[w] = kv
        qT, kT, vT = (lengthen(part).T for part in (q, kv[:, :128], kv[:, 128:]))
        t_ref[w, :128] = qT
        t_ref[w, 128:] = kT

        def keep(h, probs, w=w):
            p_ref[w, h] = probs

        operands.append(
            (kv[:, :128], qT, vT, region_mask(col_ref[first + w], row_ref[first + w]), lambda h: bias_ref[h], keep)
        )
    for u, (oT, inverse) in enumerate(attend_four(operands, blocks)):
        w = step * PER_STEP + u
        oT = oT.astype(BF)
        o_ref[w] = oT
        inv_ref[w] = inverse
        mixed = dot(oT.T[:ROWS], outw_ref[...]).astype(BF).astype(F32)
        win[w] = xs[u] + mixed
    return carry


SAVED = (
    ((ROWS, 128), BF),
    ((ROWS, 256), BF),
    ((256, LANES), BF),
    ((4, ROWS, LANES), BF),
    ((128, LANES), BF),
    ((8, LANES), F32),
)


def front(late, pieces, gain, proj, outw, bias, spread, row, column):
    consts = (gain, proj, outw, bias, spread)
    shapes = [(4, 14, 28, 128)] if late else [(4, 9, 28, 128), (4, 5, 28, 128)]
    out = pl.pallas_call(
        functools.partial(front_kernel, late),
        out_shape=[jax.ShapeDtypeStruct(s, BF) for s in shapes]
        + [jax.ShapeDtypeStruct((HEADS3, ROWS // 2, LANES), F32)]
        + [jax.ShapeDtypeStruct((8,) + s, d) for s, d in SAVED],
        scratch_shapes=[
            pltpu.VMEM((4, 14, 40, 128), F32),
            pltpu.VMEM((8, ROWS, 128), F32),
        ],
        compiler_params=params(),
        cost_estimate=cost(4.6),
    )(*pieces, *consts, row, column)
    return out[: len(shapes) + 1], out[len(shapes) + 1 :]


def back_kernel(late, *refs):
    n_in = 3 if late else 2
    pieces, refs = refs[:n_in], refs[n_in:]
    gain_ref, proj_ref, outw_ref = refs[:3]
    xw_ref, kv_ref, t_ref, p_ref, o_ref, inv_ref = refs[3:9]
    refs = refs[9:]
    n_out = 3 if late else 2
    outs, refs = refs[:n_out], refs[n_out:]
    stage, win = refs
    if late:
        put_rows(stage, slice(0, 4), slice(0, 14), pieces[0][...])
        outs[1][:, 11:15] = pieces[1][:, 0:4]
        outs[2][0:2, 3:6] = pieces[2][...]
        outs[2][2:4, 3:6] = pieces[1][:, 4:7]
    else:
        put_rows(stage, slice(0, 4), slice(0, 9), pieces[0][...])
        put_rows(stage, slice(0, 4), slice(9, 14), pieces[1][...])
    cut_windows(stage, win)
    lax.fori_loop(
        0,
        STEPS,
        functools.partial(
            back_step, gain_ref, proj_ref, outw_ref,
            xw_ref, kv_ref, t_ref, p_ref, o_ref, inv_ref, win,
        ),
        0,
    )
    join_windows(win, stage)
    if late:
        outs[0][...] = stage[0:2, 0:11, 0:28, :].astype(BF)
        outs[1][:, 0:11] = stage[2:4, 0:11, 0:28, :].astype(BF)
        outs[2][:, 0:3] = stage[:, 11:14, 0:28, :].astype(BF)
    else:
        outs[0][...] = stage[0:2, :, 0:28, :].astype(BF)
        outs[1][...] = stage[2:4, :, 0:28, :].astype(BF)


def back_step(
    gain_ref, proj_ref, outw_ref, xw_ref, kv_ref, t_ref, p_ref, o_ref, inv_ref, win, step, carry
):
    def window(w):
        dr = win[w]
        doT = dot_nt(outw_ref[...], lengthen(dr.astype(BF)))
        yield
        dq, dk, dv = yield from attend_four_back(
            kv_ref[w, :, 128:], t_ref[w, :128], t_ref[w, 128:], o_ref[w].astype(F32), doT,
            inv_ref[w], lambda h: p_ref[w, h],
        )
        dn = dot_nt(jnp.concatenate([dq, dk, dv], 1), proj_ref[...])
        yield
        xhat, rstd = normalise(xw_ref[w].astype(F32))
        win[w] = dr + normalise_back(dn * gain_ref[...], xhat, rstd)

    lockstep(window(step * PER_STEP + u) for u in range(PER_STEP))
    return carry


def back(late, pieces, gain, proj, outw, saved):
    consts = (gain, proj, outw)
    if late:
        shapes = [(2, 11, 28, 128), (2, 15, 28, 128), (4, 6, 28, 128)]
    else:
        shapes = [(2, 14, 28, 128), (2, 14, 28, 128)]
    return pl.pallas_call(
        functools.partial(back_kernel, late),
        out_shape=[jax.ShapeDtypeStruct(s, BF) for s in shapes],
        scratch_shapes=[
            pltpu.VMEM((4, 14, 40, 128), F32),
            pltpu.VMEM((8, ROWS, 128), F32),
        ],
        compiler_params=params(),
        cost_estimate=cost(5.5),
    )(*pieces, *consts, *saved)


def merge_pairs(stage, gain_ref, weight):
    pairs = stage.shape[1]
    pieces = [
        stage[:, :, q % 2, pl.ds(q // 2, 16, stride=2), :].reshape(WT * pairs * 16, 128)
        for q in range(4)
    ]
    xhat, rstd = normalise(jnp.concatenate(pieces, 1))
    merged = dot((xhat * gain_ref[...]).astype(BF), weight).astype(BF).astype(F32)
    return merged, xhat, rstd


def merge_pairs_back(grad, xhat, rstd, gain_ref, weight, stage):
    pairs = stage.shape[1]
    dn = dot_nt(grad.astype(BF), weight)
    dg = normalise_back(dn * gain_ref[...], xhat, rstd)
    for q in range(4):
        stage[:, :, q % 2, pl.ds(q // 2, 16, stride=2), :] = dg[
            :, 128 * q : 128 * q + 128
        ].reshape(WT, pairs, 16, 128)


def put_pair_row(stage, at, values):
    stage[:, at // 2, at % 2, 0:28, :] = values.astype(F32)


def clear_pads(stage):
    stage[:, :, :, 28:32, :] = jnp.zeros((WT, stage.shape[1], 2, 4, 128), F32)


def pair_row(stage, at):
    return stage[:, at // 2, at % 2, 0:28, :].astype(BF)


def fold_merged(merged, pairs):
    halves = [
        merged[:, 128 * i : 128 * i + 128].reshape(WT, pairs, 16, 128)[:, :, 0:14] for i in range(2)
    ]
    return jnp.concatenate(halves, 2)


def unfold_merged(folded):
    pad = jnp.zeros(folded.shape[:2] + (2, 128), F32)
    halves = [
        jnp.concatenate([folded[:, :, 14 * i : 14 * i + 14], pad], 2).reshape(-1, 128)
        for i in range(2)
    ]
    return jnp.concatenate(halves, 1)


def send_kernel(res_ref, gain_ref, weight_ref, send_ref, xhat_ref, rstd_ref, stage):
    clear_pads(stage)
    for i in range(8):
        put_pair_row(stage, i, res_ref[:, 1 + i])
    merged, xhat, rstd = merge_pairs(stage, gain_ref, weight_ref[...])
    xhat_ref[...] = xhat
    rstd_ref[...] = jnp.broadcast_to(rstd, rstd_ref.shape)
    send_ref[:, 0:1] = res_ref[:, 0:1]
    send_ref[:, 1:5] = fold_merged(merged, 4).astype(BF)


def local_kernel(resA_ref, resB_ref, gain_ref, weight_ref, merged_ref, xhat_ref, rstd_ref, stage):
    clear_pads(stage)
    for i in range(5):
        put_pair_row(stage, i, resA_ref[:, i])
    for i in range(13):
        put_pair_row(stage, 5 + i, resB_ref[:, i])
    merged, xhat, rstd = merge_pairs(stage, gain_ref, weight_ref[...])
    xhat_ref[...] = xhat
    rstd_ref[...] = jnp.broadcast_to(rstd, rstd_ref.shape)
    merged_ref[...] = merged


def local_back_kernel(
    grad_ref, d30_ref, xhat_ref, rstd_ref, gain_ref, weight_ref, dA_ref, dB_ref, stage
):
    merge_pairs_back(
        grad_ref[...], xhat_ref[...], rstd_ref[:, 0:1], gain_ref, weight_ref[...], stage
    )
    for i in range(5):
        dA_ref[:, i] = pair_row(stage, i)
    for i in range(13):
        dB_ref[:, i] = pair_row(stage, 5 + i)
    dB_ref[:, 13] = d30_ref[...]


def receive_kernel(got_ref, xhat_ref, rstd_ref, gain_ref, weight_ref, d_ref, stage):
    grad = unfold_merged(got_ref[:, 1:5].astype(F32))
    merge_pairs_back(grad, xhat_ref[...], rstd_ref[:, 0:1], gain_ref, weight_ref[...], stage)
    d_ref[:, 0:1] = got_ref[:, 0:1]
    for i in range(8):
        d_ref[:, 1 + i] = pair_row(stage, i)


def merge_call(kernel, us, shapes, pairs, *operands):
    return pl.pallas_call(
        kernel,
        out_shape=[jax.ShapeDtypeStruct(shape, kind) for shape, kind in shapes],
        scratch_shapes=[pltpu.VMEM((WT, pairs, 2, 32, 128), F32)],
        compiler_params=params(),
        cost_estimate=cost(us),
    )(*operands)


def middle_kernel(
    merged_ref, resB_ref, next_ref, cot_ref, cta_ref, cha_ref, cdg_ref,
    mg1_ref, mg2_ref, g3_ref, row_ref, col_ref, mw1_ref, mw2_ref, p3_ref, biasA_ref, biasB_ref, ow3_ref,
    dm_ref, d30_ref, dN_ref, so_ref, sta_ref, sha_ref,
    stage, stage2, xhat2, rstd2, cotw, k_s, v_s, qT_s, kT_s, vT_s, probs_s, oT_s, inv_s, doT_s, dqkv_s,
):
    cotw[...] = jnp.zeros((4, 7, 8, 512), F32)
    cotw[0:2, 0:4, 0:7, :] = cot_ref[2:4, 3:7].astype(F32)
    cotw[2:4, 0:4, 0:7, :] = unfold(cta_ref[:, 11:15].astype(F32))
    cotw[0:2, 4:7, 0:7, :] = unfold(cha_ref[:, 3:6].astype(F32))
    cotw[2:4, 4:7, 0:7, :] = unfold(cdg_ref[:, 3:6].astype(F32))

    def put_merged(first, count, values):
        for half in range(2):
            block = values[:, 128 * half : 128 * half + 128].reshape(WT, count, 16, 128)
            for i in range(count):
                stage2[half, :, (first + i) // 2, (first + i) % 2] = block[:, i]

    def take_merged(first, count):
        halves = [
            jnp.concatenate(
                [
                    stage2[half, :, (first + i) // 2, (first + i) % 2].reshape(WT, 1, 16, 128)
                    for i in range(count)
                ],
                1,
            ).reshape(WT * count * 16, 128)
            for half in range(2)
        ]
        return jnp.concatenate(halves, 1)

    put_merged(0, 9, merged_ref[...])
    put_merged(10, 4, unfold_merged(next_ref[:, 1:5].astype(F32)))
    clear_pads(stage)
    put_pair_row(stage, 0, resB_ref[:, 13])
    put_pair_row(stage, 1, next_ref[:, 0])
    merged, xhat_seam, rstd_seam = merge_pairs(stage, mg1_ref, mw1_ref[...])
    put_merged(9, 1, merged)
    pieces = [
        stage2[half, :, :, q % 2, pl.ds(q // 2, 8, stride=2), :].reshape(ROWS, 128)
        for q in range(4)
        for half in range(2)
    ]
    xhat, rstd = normalise(jnp.concatenate(pieces, 1))
    xhat2[...] = xhat
    rstd2[...] = jnp.broadcast_to(rstd, (ROWS, 128))
    merged_two = dot((xhat * mg2_ref[...]).astype(BF), mw2_ref[...]).astype(BF).astype(F32)
    xhat3, rstd3 = normalise(merged_two)
    n3 = (xhat3 * g3_ref[...]).astype(BF)
    packed = [dot(n3, p3_ref[:, 512 * i : 512 * i + 512]) for i in range(3)]
    for g in range(4):
        q, k, v = (part[:, 128 * g : 128 * g + 128] for part in packed)
        q = lengthen((q * (SCALE * LOG2E)).astype(BF))
        k, v = k.astype(BF), v.astype(BF)
        k_s[g] = k
        v_s[g] = v
        qT_s[g] = q.T
        kT_s[g] = lengthen(k).T
        vT_s[g] = lengthen(v).T

    def bias_at(head):
        return jnp.concatenate([biasA_ref[head], biasB_ref[head]], 0)

    mask = region_mask(col_ref[...], row_ref[...])

    operands = []
    for g in range(4):

        def keep(h, probs, g=g):
            probs_s[g * 4 + h] = probs

        operands.append((k_s[g], qT_s[g], vT_s[g], mask, lambda h, g=g: bias_at(g * 4 + h), keep))
    for g, (oT, inverse) in enumerate(attend_four(operands)):
        oT_s[g] = oT
        inv_s[g] = inverse
    att = jnp.concatenate([oT_s[g].astype(BF).T[:ROWS] for g in range(4)], 1)
    mixed = dot(att, ow3_ref[...]).astype(BF).astype(F32)
    section = (merged_two + mixed).reshape(4, 7, 8, 512)
    section = fold(section[:, :, 0:7])
    so_ref[...] = section[0:2, 0:4].astype(BF)
    sta_ref[...] = section[2:4].astype(BF)
    sha_ref[...] = section[0:2, 4:7].astype(BF)

    cot = cotw[...].reshape(ROWS, 512)
    cot_long = lengthen(cot.astype(BF))
    doT = dot_nt(ow3_ref[...], cot_long)
    for g in range(4):
        doT_s[g] = doT[128 * g : 128 * g + 128]

    def group_back(g):
        dqkv_s[g], dqkv_s[4 + g], dqkv_s[8 + g] = yield from attend_four_back(
            v_s[g], qT_s[g], kT_s[g], oT_s[g], doT_s[g], inv_s[g], lambda h: probs_s[g * 4 + h]
        )

    lockstep(group_back(g) for g in range(4))
    dpacked = jnp.concatenate([dqkv_s[i] for i in range(12)], 1)
    dn3 = dot_nt(dpacked, p3_ref[...])
    dm2 = cot + normalise_back(dn3 * g3_ref[...], xhat3, rstd3)
    dn2 = dot_nt(dm2.astype(BF), mw2_ref[...])
    dg2 = normalise_back(dn2 * mg2_ref[...], xhat2[...], rstd2[:, 0:1])
    for q in range(4):
        for half in range(2):
            at = 256 * q + 128 * half
            stage2[half, :, :, q % 2, pl.ds(q // 2, 8, stride=2), :] = dg2[:, at : at + 128].reshape(
                4, 7, 8, 128
            )

    dm_ref[...] = take_merged(0, 9)
    merge_pairs_back(take_merged(9, 1), xhat_seam, rstd_seam, mg1_ref, mw1_ref[...], stage)
    d30_ref[...] = pair_row(stage, 0)
    dN_ref[:, 0] = pair_row(stage, 1)
    dN_ref[:, 1:5] = fold_merged(take_merged(10, 4), 4).astype(BF)


def middle(*operands):
    shapes = [
        (4, 28, 128), (4, 5, 28, 128), (2, 4, 28, 128), (2, 7, 28, 128), (2, 3, 28, 128),
    ]
    return pl.pallas_call(
        middle_kernel,
        out_shape=[jax.ShapeDtypeStruct((576, 256), F32)]
        + [jax.ShapeDtypeStruct(s, BF) for s in shapes],
        scratch_shapes=[
            pltpu.VMEM((4, 1, 2, 32, 128), F32),
            pltpu.VMEM((2, 4, 7, 2, 16, 128), F32),
            pltpu.VMEM((ROWS, 1024), F32),
            pltpu.VMEM((ROWS, 128), F32),
            pltpu.VMEM((4, 7, 8, 512), F32),
            pltpu.VMEM((4, ROWS, 128), BF),
            pltpu.VMEM((4, ROWS, 128), BF),
            pltpu.VMEM((4, 128, LANES), BF),
            pltpu.VMEM((4, 128, LANES), BF),
            pltpu.VMEM((4, 128, LANES), BF),
            pltpu.VMEM((16, ROWS, LANES), BF),
            pltpu.VMEM((4, 128, LANES), F32),
            pltpu.VMEM((4, 8, LANES), F32),
            pltpu.VMEM((4, 128, LANES), F32),
            pltpu.VMEM((12, ROWS, 128), BF),
        ],
        compiler_params=params(24),
        cost_estimate=cost(9),
    )(*operands)


def join_kernel(ta_ref, own_ref, so_ref, grad_ref, section_ref, wide, narrow):
    for t in range(WT):
        wide[:, pl.ds(t, 28, stride=4), :] = (ta_ref if t < 2 else own_ref)[t % 2, 0:11].astype(F32)
        low = (ta_ref[t, 11:15] if t < 2 else so_ref[t - 2]).astype(F32)
        for g in range(4):
            narrow[g, :, pl.ds(t, 7, stride=4), :] = low[:, 7 * g : 7 * g + 7]
    for i in range(11):
        grad_ref[17 + i] = wide[i].reshape(28, 4, 128).astype(BF)
    for i in range(4):
        row = jnp.concatenate([narrow[g, i] for g in range(4)], 1)
        section_ref[3 + i] = row.reshape(7, 4, 512).astype(BF)


JOINED = [
    jax.ShapeDtypeStruct((28, 28, 4, 128), BF),
    jax.ShapeDtypeStruct((7, 7, 4, 512), BF),
]


def join(ta, own, section_own):
    return pl.pallas_call(
        join_kernel,
        out_shape=JOINED,
        scratch_shapes=[pltpu.VMEM((11, 112, 128), F32), pltpu.VMEM((4, 4, 28, 128), F32)],
        compiler_params=params(),
        cost_estimate=cost(2),
    )(ta, own, section_own)


def last_kernel(
    grad_hbm, section_hbm, ta_ref, own_ref, dg_ref, ha_ref, grad_out, section_out,
    wide, narrow, rows, section_rows, sems,
):
    del grad_hbm, section_hbm
    for t in range(WT):
        corner = dg_ref if t < 2 else ha_ref
        wide[0:3, pl.ds(t, 28, stride=4), :] = corner[t % 2, 0:3].astype(F32)
        wide[3:17, pl.ds(t, 28, stride=4), :] = (ta_ref if t < 2 else own_ref)[t % 2].astype(F32)
        high = corner[t % 2, 3:6].astype(F32)
        for g in range(4):
            narrow[g, :, pl.ds(t, 7, stride=4), :] = high[:, 7 * g : 7 * g + 7]
    for i in range(8):
        rows[i] = wide[i].reshape(28, 4, 128).astype(BF)
    start = pltpu.make_async_copy(rows.at[0:8], grad_out.at[0:8], sems.at[2])
    start.start()
    for i in range(8, 17):
        rows[i] = wide[i].reshape(28, 4, 128).astype(BF)
    copy = pltpu.make_async_copy(rows.at[8:17], grad_out.at[8:17], sems.at[0])
    copy.start()
    for i in range(3):
        row = jnp.concatenate([narrow[g, i] for g in range(4)], 1)
        section_rows[i] = row.reshape(7, 4, 512).astype(BF)
    other = pltpu.make_async_copy(section_rows, section_out.at[0:3], sems.at[1])
    other.start()
    start.wait()
    copy.wait()
    other.wait()


def join_last(grad, section, ta, own, dg, ha):
    return pl.pallas_call(
        last_kernel,
        in_specs=[pl.BlockSpec(memory_space=pl.ANY)] * 2
        + [pl.BlockSpec(memory_space=pltpu.VMEM)] * 4,
        out_specs=[pl.BlockSpec(memory_space=pl.ANY)] * 2,
        out_shape=JOINED,
        scratch_shapes=[
            pltpu.VMEM((17, 112, 128), F32),
            pltpu.VMEM((4, 3, 28, 128), F32),
            pltpu.VMEM((17, 28, 4, 128), BF),
            pltpu.VMEM((3, 7, 4, 512), BF),
            pltpu.SemaphoreType.DMA((3,)),
        ],
        input_output_aliases={0: 0, 1: 1},
        compiler_params=params(),
        cost_estimate=cost(1),
    )(grad, section, ta, own, dg, ha)


IN_ORDER = Layout(major_to_minor=(0, 1, 2, 3))


def inward(values):
    return with_layout_constraint(jnp.transpose(values, (1, 2, 0, 3)), IN_ORDER)


def outward(values):
    return jnp.transpose(with_layout_constraint(values, IN_ORDER), (2, 0, 1, 3))


def send(values, axes, by):
    axes = axes.split()
    sizes = [lax.axis_size(a) for a in axes]
    if len(axes) == 1:
        pairs = [(i, (i + by) % sizes[0]) for i in range(sizes[0])]
    else:
        n, m = sizes
        pairs = [
            (i * m + j, (i + by) % n * m + (j + by) % m) for i in range(n) for j in range(m)
        ]
    return lax.ppermute(values, tuple(axes), pairs)


def per_device(
    tokens,
    regions_one,
    regions_three,
    gain_one,
    projection_one,
    outward_one,
    table_one,
    merge_gain_one,
    merge_weight_one,
    merge_gain_two,
    merge_weight_two,
    gain_three,
    projection_three,
    outward_three,
    table_three,
    cotangent,
):
    (early,) = arrange(early_kernel, (14,), tokens)
    ta_early = send(inward(early), "ta", -1)
    late, ha_late, dg_late = arrange(late_kernel, (15, 6, 6), tokens, cotangent)
    ha_late = send(ha_late, "ha", -1)
    dg_late = send(dg_late, "ha ta", -1)
    ta_late = send(inward(late), "ta", -1)
    bias_one, spread, row_one, row_three, col_one, col_three = prepare(
        table_one, table_three, regions_one, regions_three
    )
    gain, merge_gain, seam = gain_one[None], merge_gain_one[None], merge_weight_one
    args = (gain, projection_one, outward_one, bias_one, spread)
    (res_send, res_a, bias_a), saved_a = front(False, (tokens, outward(ta_early)), *args, row_one, col_one)
    row_send, *early_norm = merge_call(
        send_kernel, 0.5, [((4, 5, 28, 128), BF), ((256, 512), F32), ((256, 128), F32)], 4,
        res_send, merge_gain, seam,
    )
    row_next = send(row_send, "ha", -1)
    ta_late, res_a = lax.optimization_barrier((ta_late, res_a))
    ta_late = outward(ta_late)
    (res_b, bias_b), saved_b = front(True, (tokens, ta_late, ha_late, dg_late), *args, row_one, col_one)
    merged, *local_norm = merge_call(
        local_kernel, 0.1, [((576, 256), F32), ((576, 512), F32), ((576, 128), F32)], 9,
        res_a, res_b, merge_gain, seam,
    )
    row_next, merged = lax.optimization_barrier((row_next, merged))
    d_merged, d_30, d_send, sec_own, sec_ta, sec_ha = middle(
        merged, res_b, row_next, cotangent, ta_late, ha_late, dg_late,
        merge_gain, merge_gain_two[None], gain_three[None], row_three, col_three,
        merge_weight_one, merge_weight_two, projection_three, bias_a, bias_b, outward_three,
    )
    d_prev = send(d_send, "ha", 1)
    d_a, d_b = merge_call(
        local_back_kernel, 1, [((4, 5, 28, 128), BF), ((4, 14, 28, 128), BF)], 9,
        d_merged, d_30, *local_norm, merge_gain, seam,
    )
    own_b, ta_b, ha_b = back(
        True, (d_b, sec_ta, sec_ha), gain, projection_one, outward_one, saved_b
    )
    d_prev, own_b = lax.optimization_barrier((d_prev, own_b))
    ta_b = send(inward(ta_b), "ta", 1)
    ha_b = send(ha_b, "ha", 1)
    (d_first,) = merge_call(
        receive_kernel, 0.5, [((4, 9, 28, 128), BF)], 4, d_prev, *early_norm, merge_gain, seam
    )
    own_a, ta_a = back(False, (d_first, d_a), gain, projection_one, outward_one, saved_a)
    ta_b, ha_b, own_a = lax.optimization_barrier((ta_b, ha_b, own_a))
    ta_a = send(inward(ta_a), "ta", 1)
    dg_b = send(ha_b[2:], "ta", 1)
    grad, section = join(outward(ta_b), own_b, sec_own)
    ta_a, dg_b, grad = lax.optimization_barrier((ta_a, dg_b, grad))
    grad, section = join_last(grad, section, outward(ta_a), own_a, dg_b, ha_b)
    return (jnp.transpose(section, (2, 0, 1, 3)), jnp.transpose(grad, (2, 0, 1, 3)))


def solution(mesh):
    tile = P(("col", "ta"), "ha", None, None)
    ids = P(("col", "ta"), "ha", None)
    in_specs = (tile, ids, ids) + (P(),) * 12 + (tile,)
    return jax.shard_map(
        per_device, mesh=mesh, in_specs=in_specs, out_specs=(tile, tile), check_vma=False
    )
```

```python
import functools

import jax
import jax.numpy as jnp
import numpy as np
from jax import lax
from jax.experimental import pallas as pl
from jax.experimental.layout import Layout, with_layout_constraint
from jax.experimental.pallas import tpu as pltpu
from jax.sharding import PartitionSpec as P

HEADS1 = 4
HEADS3 = 16
WT = 4
WS = 7
ST = 2
SS = 3
EPSILON = 1e-05
NREL = 1183
LOG2E = 1.4426950408889634
HEAD = 32
SCALE = HEAD**-0.5
ROWS = WT * WS * 8
LANES = 256
SPAN = 1280
GONE = -1e30
PER_STEP = 8
STEPS = 8 // PER_STEP
BF = jnp.bfloat16
F32 = jnp.float32


def dot(a, b):
    return jnp.dot(a, b, preferred_element_type=F32)


def dot_nt(a, b):
    return lax.dot_general(a, b, (((1,), (1,)), ((), ())), preferred_element_type=F32)


def params(limit=20):
    return pltpu.CompilerParams(vmem_limit_bytes=limit * 1024 * 1024)


def cost(us):
    return pl.CostEstimate(flops=int(us * 1.1e9), bytes_accessed=int(us * 1e6), transcendentals=0)


def normalise(x):
    centred = x - jnp.mean(x, -1, keepdims=True)
    rstd = lax.rsqrt(jnp.mean(centred * centred, -1, keepdims=True) + EPSILON)
    return centred * rstd, rstd


def normalise_back(grad, xhat, rstd):
    return rstd * (
        grad
        - jnp.mean(grad, -1, keepdims=True)
        - xhat * jnp.mean(grad * xhat, -1, keepdims=True)
    )


def head_rows(x, h):
    return x[HEAD * h : HEAD * (h + 1)]


def head_of_lane(shape):
    return lax.broadcasted_iota(jnp.int32, shape, 1) // HEAD


def by_head(x):
    lane = head_of_lane((1, 128))
    return jnp.concatenate([x * (lane == h).astype(F32).astype(BF) for h in range(4)], 0)


def pick_heads(stacked):
    lane = head_of_lane((ROWS, 128))
    got = stacked[:ROWS]
    for h in range(1, 4):
        got = jnp.where(lane == h, stacked[ROWS * h : ROWS * (h + 1)], got)
    return got


def lengthen(x):
    return jnp.concatenate([x, jnp.zeros((LANES - ROWS, x.shape[1]), x.dtype)], 0)


def region_mask(column, row):
    return jnp.where(jnp.concatenate([column, column], 1) == row, 0.0, GONE).astype(F32)


def lockstep(active):
    active = list(active)
    while active:
        active = [g for g in active if next(g, "end") is None]


def attend_four(windows, beside=()):
    scores = [dot(by_head(k), qT) for k, qT, _, _, _, _ in windows]
    results = []
    beside = list(beside)
    share = -(-len(beside) // len(windows))
    for s, (_, _, vT, mask, bias_at, keep_probs) in zip(scores, windows):
        for emit in beside[:share]:
            emit()
        beside = beside[share:]
        outs, inverses = [], []
        for h in range(4):
            biased = s[ROWS * h : ROWS * (h + 1)] + (bias_at(h) + mask)
            peak = jnp.max(biased, 0, keepdims=True)
            probs = jnp.exp2(biased - peak).astype(BF)
            keep_probs(h, probs)
            extended = jnp.concatenate([head_rows(vT, h)[:, :ROWS], jnp.ones((16, ROWS), BF)], 0)
            out = dot(extended, probs)
            inverse = 1.0 / out[HEAD : HEAD + 1]
            outs.append(out[:HEAD] * inverse)
            inverses.append(inverse)
        results.append((jnp.concatenate(outs, 0), jnp.concatenate(inverses + inverses, 0)))
    return results


def attend_four_back(v, qT, kT, oT, doT, inverse, probs_at):
    scaled, deltas = [], []
    for h in range(4):
        part = head_rows(doT, h) * inverse[h : h + 1]
        deltas.append(jnp.sum(part * head_rows(oT, h), 0, keepdims=True))
        scaled.append(part)
    scaled = jnp.concatenate(scaled, 0).astype(BF)
    dprobs = dot(by_head(v), scaled)
    yield
    probs = [probs_at(h) for h in range(4)]
    dscores = [
        (probs[h].astype(F32) * (dprobs[ROWS * h : ROWS * (h + 1)] - deltas[h])).astype(BF)
        for h in range(4)
    ]
    dv = pick_heads(dot_nt(jnp.concatenate(probs, 0), scaled))
    yield
    dk = pick_heads(dot_nt(jnp.concatenate(dscores, 0), qT))
    dqT = jnp.concatenate([dot(head_rows(kT, h)[:, :ROWS], dscores[h]) for h in range(4)], 0)
    yield
    dq = (dqT * SCALE).astype(BF).T[:ROWS]
    return dq, (dk * (1.0 / LOG2E)).astype(BF), dv.astype(BF)


def lanes_of(shape):
    return lax.broadcasted_iota(jnp.int32, shape, 1)


def region_rows(ids, section):
    columns = ids.shape[1]
    count = columns // WS
    place = lax.broadcasted_iota(jnp.int32, (columns, LANES * count), 0)
    lane = lanes_of((columns, LANES * count))
    column = lane % 8
    real = (column < WS) & (lane % LANES < ROWS)
    if section == 3:
        column = jnp.where(column < 3, column + 4, column - 3)
    chosen = real & (place == lane // LANES * WS + column)
    spread = dot(ids.astype(F32).astype(BF), chosen.astype(F32).astype(BF))
    row = lax.broadcasted_iota(jnp.int32, spread.shape, 0)
    lane = lanes_of(spread.shape)
    real = (lane[:1] % 8 < WS) & (lane[:1] % LANES < ROWS)
    rows = []
    for hw in range(ids.shape[0] // (WT * WS)):
        mine = lane % LANES // 8 == row % 4 * WS + row // 4 - WS * hw
        inside = (row >= WT * WS * hw) & (row < WT * WS * (hw + 1))
        found = jnp.sum(jnp.where(mine & inside, spread, 0.0), 0, keepdims=True)
        found = jnp.where(real, found, -1.0)
        rows += [found[:, LANES * ww : LANES * (ww + 1)] for ww in range(count)]
    return rows


def region_columns(ids, section):
    columns = ids.shape[1]
    count = columns // WS
    source = ids.astype(F32).astype(BF)
    token = lax.broadcasted_iota(jnp.int32, (ROWS, ids.shape[0]), 0)
    place = lanes_of((ROWS, ids.shape[0]))
    column = lax.broadcasted_iota(jnp.int32, (ROWS, columns), 0) % 8
    lane = lanes_of((ROWS, columns))
    if section == 3:
        column = jnp.where(column < 3, column + 4, jnp.where(column == 7, 8, column - 3))
    ones = jnp.ones((columns, 128), BF)
    pad = lax.broadcasted_iota(jnp.int32, (ROWS, 128), 0) % 8 == 7
    found = []
    for hw in range(ids.shape[0] // (WT * WS)):
        chosen = place == (token // 8 % WS + WS * hw) * WT + token // 56
        picked = dot(chosen.astype(F32).astype(BF), source)
        for ww in range(count):
            mine = jnp.where(lane == WS * ww + column, picked, 0.0).astype(BF)
            found.append(jnp.where(pad, -1.0, dot(mine, ones)))
    return found


def bias_rows(spread, at, heads, tj, hj):
    lane = lanes_of((heads * 8, 128))
    p0, p1, p2, p3 = (
        pltpu.roll(
            spread[ti - tj + 3, at : at + heads * 8, :], (ti * 56 - (6 - hj) * 8) % 128, 1
        )
        for ti in range(WT)
    )
    left = jnp.where(lane < 56, p0, jnp.where(lane < 112, p1, p2))
    right = jnp.where(lane < 40, p2, p3)
    return left.reshape(heads, 8, 128), right.reshape(heads, 8, 128)


def prepare_kernel(
    t1_ref, t3_ref, s_ref, r1_ref, r3_ref, o1_ref, spread, row1_ref, row3_ref, col1_ref, col3_ref, tab
):
    tab[...] = jnp.zeros((24, SPAN), F32)
    tab[0:4, 0:NREL] = t1_ref[...] * LOG2E
    tab[8:24, 0:NREL] = t3_ref[...] * LOG2E
    slabs = []
    for dt in range(7):
        start = 169 * dt
        low = start // 128 * 128
        run = tab[:, low : low + 384]
        if start > low:
            run = pltpu.roll(run, 384 - (start - low), 1)
        slabs.append(run[:, :256])
    left = jnp.concatenate(slabs, 0)
    first = left.astype(BF)
    rest = left - first.astype(F32)
    second = rest.astype(BF)
    third = (rest - second.astype(F32)).astype(BF)
    chosen = s_ref[...]
    got = dot(first, chosen) + dot(second, chosen) + dot(third, chosen)
    lane16 = lanes_of((16, 128))
    for dt in range(7):
        for wj in range(8):
            part = got[24 * dt : 24 * dt + 24, 128 * wj : 128 * wj + 128]
            spread[dt, pl.ds(wj, 8, stride=8), :] = part[0:8]
            later = part[8:24]
            turned = jnp.where(lane16 % 8 < 3, pltpu.roll(later, 124, 1), pltpu.roll(later, 3, 1))
            spread[dt, pl.ds(64 + (7 if wj == 7 else (wj + 3) % 7), 16, stride=8), :] = turned
    for tj in range(WT):
        for hj in range(WS):
            row = (tj * WS + hj) * 8
            left, right = bias_rows(spread, 0, HEADS1, tj, hj)
            o1_ref[:, row : row + 8, 0:128] = left
            o1_ref[:, row : row + 8, 128:256] = right
    for i, found in enumerate(region_rows(r1_ref[...], 1)):
        row1_ref[i] = found
    row3_ref[...] = region_rows(r3_ref[...], 3)[0]
    for i, found in enumerate(region_columns(r1_ref[...], 1)):
        col1_ref[i] = found
    col3_ref[...] = region_columns(r3_ref[...], 3)[0]


def chooser():
    chosen = np.zeros((256, 1024), np.float32)
    for wj in range(WS):
        for dh in range(13):
            for wi in range(WS):
                chosen[dh * 13 + wi - wj + 6, wj * 128 + dh * 8 + wi] = 1.0
    return jnp.asarray(chosen, BF)


def by_height(ids):
    return jnp.transpose(ids, (1, 0, 2)).reshape(-1, ids.shape[2])


def prepare(table_one, table_three, regions_one, regions_three):
    return pl.pallas_call(
        prepare_kernel,
        out_shape=(
            jax.ShapeDtypeStruct((HEADS1, ROWS, LANES), F32),
            jax.ShapeDtypeStruct((7, 25 * 8, 128), F32),
            jax.ShapeDtypeStruct((16, 1, LANES), F32),
            jax.ShapeDtypeStruct((1, LANES), F32),
            jax.ShapeDtypeStruct((16, ROWS, 128), F32),
            jax.ShapeDtypeStruct((ROWS, 128), F32),
        ),
        scratch_shapes=[pltpu.VMEM((24, SPAN), F32)],
        compiler_params=params(),
        cost_estimate=cost(1.5),
    )(
        jnp.transpose(table_one),
        jnp.transpose(table_three),
        chooser(),
        by_height(regions_one),
        by_height(regions_three),
    )


def fold(values):
    return jnp.concatenate([values[..., 128 * g : 128 * g + 128] for g in range(4)], -2)


def unfold(values):
    return jnp.concatenate([values[..., 7 * g : 7 * g + 7, :] for g in range(4)], -1)


def early_kernel(tok_ref, early_ref):
    early_ref[...] = tok_ref[0:2, 3:17]


def late_kernel(tok_ref, cot_ref, late_ref, ha_ref, dg_ref):
    late_ref[:, 0:11] = tok_ref[0:2, 17:28]
    late_ref[:, 11:15] = fold(cot_ref[0:2, 3:7].astype(F32)).astype(BF)
    ha_ref[:, 0:3] = tok_ref[2:4, 0:3]
    ha_ref[:, 3:6] = fold(cot_ref[2:4, 0:3].astype(F32)).astype(BF)
    dg_ref[:, 0:3] = tok_ref[0:2, 0:3]
    dg_ref[:, 3:6] = fold(cot_ref[0:2, 0:3].astype(F32)).astype(BF)


def arrange(kernel, rows, *operands):
    return pl.pallas_call(
        kernel,
        out_shape=[jax.ShapeDtypeStruct((2, n, 28, 128), BF) for n in rows],
        compiler_params=params(8),
        cost_estimate=cost(0.3),
    )(*operands)


def put_rows(stage, frames, rows, values):
    values = values.astype(F32)
    stage[frames, rows, 0:28, :] = values
    stage[frames, rows, 28:36, :] = values[:, :, 0:8, :]


def cut_windows(stage, win):
    for hw in range(2):
        for ww in range(4):
            win[hw * 4 + ww] = stage[:, 7 * hw : 7 * hw + 7, 3 + 7 * ww : 11 + 7 * ww, :].reshape(
                ROWS, 128
            )


def join_windows(win, stage):
    for hw in range(2):
        for ww in range(4):
            stage[:, 7 * hw : 7 * hw + 7, 3 + 7 * ww : 11 + 7 * ww, :] = win[hw * 4 + ww].reshape(
                WT, WS, 8, 128
            )
    stage[:, :, 0:3, :] = stage[:, :, 28:31, :]


def front_kernel(late, *refs):
    n_in = 4 if late else 2
    pieces, refs = refs[:n_in], refs[n_in:]
    gain_ref, proj_ref, outw_ref, bias_ref, spread_ref, row_ref, col_ref = refs[:7]
    refs = refs[7:]
    n_out = 1 if late else 2
    outs, refs = refs[:n_out], refs[n_out:]
    b3_ref, xw_ref, kv_ref, t_ref, p_ref, o_ref, inv_ref, stage, win = refs
    own = pieces[0]
    if late:
        put_rows(stage, slice(0, 2), slice(0, 11), own[2:4, 17:28])
        put_rows(stage, slice(2, 4), slice(0, 11), pieces[1][:, 0:11])
        put_rows(stage, slice(0, 2), slice(11, 14), pieces[2][:, 0:3])
        put_rows(stage, slice(2, 4), slice(11, 14), pieces[3][:, 0:3])
    else:
        put_rows(stage, slice(0, 2), slice(0, 14), own[2:4, 3:17])
        put_rows(stage, slice(2, 4), slice(0, 14), pieces[1][...])
    cut_windows(stage, win)
    lax.fori_loop(
        0,
        STEPS,
        functools.partial(
            front_step, late, gain_ref, proj_ref, outw_ref, bias_ref, spread_ref, row_ref, col_ref,
            b3_ref, xw_ref, kv_ref, t_ref, p_ref, o_ref, inv_ref, win,
        ),
        0,
    )
    join_windows(win, stage)
    if late:
        outs[0][...] = stage[:, :, 0:28, :].astype(BF)
    else:
        outs[0][...] = stage[:, 0:9, 0:28, :].astype(BF)
        outs[1][...] = stage[:, 9:14, 0:28, :].astype(BF)


def front_step(
    late, gain_ref, proj_ref, outw_ref, bias_ref, spread_ref, row_ref, col_ref,
    b3_ref, xw_ref, kv_ref, t_ref, p_ref, o_ref, inv_ref, win, step, carry,
):
    first = 8 * late
    def block(tj, hj):
        def emit():
            left, right = bias_rows(spread_ref, 64, HEADS3, 2 * late + tj, hj)
            at = pl.ds(pl.multiple_of((tj * WS + hj) * 8, 8), 8)
            b3_ref[:, at, 0:128] = left
            b3_ref[:, at, 128:256] = right

        return emit

    count = 2 // STEPS
    blocks = [block(step * count + i, hj) for i in range(count) for hj in range(WS)]
    xs, operands = [], []
    for u in range(PER_STEP):
        w = step * PER_STEP + u
        x = win[w]
        xs.append(x)
        xw_ref[w] = x.astype(BF)
        xhat, _ = normalise(x)
        packed = dot((xhat * gain_ref[...]).astype(BF), proj_ref[...])
        q = (packed[:, :128] * (SCALE * LOG2E)).astype(BF)
        kv = packed[:, 128:].astype(BF)
        kv_ref[w] = kv
        qT, kT, vT = (lengthen(part).T for part in (q, kv[:, :128], kv[:, 128:]))
        t_ref[w, :128] = qT
        t_ref[w, 128:] = kT

        def keep(h, probs, w=w):
            p_ref[w, h] = probs

        operands.append(
            (kv[:, :128], qT, vT, region_mask(col_ref[first + w], row_ref[first + w]), lambda h: bias_ref[h], keep)
        )
    for u, (oT, inverse) in enumerate(attend_four(operands, blocks)):
        w = step * PER_STEP + u
        oT = oT.astype(BF)
        o_ref[w] = oT
        inv_ref[w] = inverse
        mixed = dot(oT.T[:ROWS], outw_ref[...]).astype(BF).astype(F32)
        win[w] = xs[u] + mixed
    return carry


SAVED = (
    ((ROWS, 128), BF),
    ((ROWS, 256), BF),
    ((256, LANES), BF),
    ((4, ROWS, LANES), BF),
    ((128, LANES), BF),
    ((8, LANES), F32),
)


def front(late, pieces, gain, proj, outw, bias, spread, row, column):
    consts = (gain, proj, outw, bias, spread)
    shapes = [(4, 14, 28, 128)] if late else [(4, 9, 28, 128), (4, 5, 28, 128)]
    out = pl.pallas_call(
        functools.partial(front_kernel, late),
        out_shape=[jax.ShapeDtypeStruct(s, BF) for s in shapes]
        + [jax.ShapeDtypeStruct((HEADS3, ROWS // 2, LANES), F32)]
        + [jax.ShapeDtypeStruct((8,) + s, d) for s, d in SAVED],
        scratch_shapes=[
            pltpu.VMEM((4, 14, 40, 128), F32),
            pltpu.VMEM((8, ROWS, 128), F32),
        ],
        compiler_params=params(),
        cost_estimate=cost(4.6),
    )(*pieces, *consts, row, column)
    return out[: len(shapes) + 1], out[len(shapes) + 1 :]


def back_kernel(late, *refs):
    n_in = 3 if late else 2
    pieces, refs = refs[:n_in], refs[n_in:]
    gain_ref, proj_ref, outw_ref = refs[:3]
    xw_ref, kv_ref, t_ref, p_ref, o_ref, inv_ref = refs[3:9]
    refs = refs[9:]
    n_out = 3 if late else 2
    outs, refs = refs[:n_out], refs[n_out:]
    stage, win = refs
    if late:
        put_rows(stage, slice(0, 4), slice(0, 14), pieces[0][...])
        outs[1][:, 11:15] = pieces[1][:, 0:4]
        outs[2][0:2, 3:6] = pieces[2][...]
        outs[2][2:4, 3:6] = pieces[1][:, 4:7]
    else:
        put_rows(stage, slice(0, 4), slice(0, 9), pieces[0][...])
        put_rows(stage, slice(0, 4), slice(9, 14), pieces[1][...])
    cut_windows(stage, win)
    lax.fori_loop(
        0,
        STEPS,
        functools.partial(
            back_step, gain_ref, proj_ref, outw_ref,
            xw_ref, kv_ref, t_ref, p_ref, o_ref, inv_ref, win,
        ),
        0,
    )
    join_windows(win, stage)
    if late:
        outs[0][...] = stage[0:2, 0:11, 0:28, :].astype(BF)
        outs[1][:, 0:11] = stage[2:4, 0:11, 0:28, :].astype(BF)
        outs[2][:, 0:3] = stage[:, 11:14, 0:28, :].astype(BF)
    else:
        outs[0][...] = stage[0:2, :, 0:28, :].astype(BF)
        outs[1][...] = stage[2:4, :, 0:28, :].astype(BF)


def back_step(
    gain_ref, proj_ref, outw_ref, xw_ref, kv_ref, t_ref, p_ref, o_ref, inv_ref, win, step, carry
):
    def window(w):
        dr = win[w]
        doT = dot_nt(outw_ref[...], lengthen(dr.astype(BF)))
        yield
        dq, dk, dv = yield from attend_four_back(
            kv_ref[w, :, 128:], t_ref[w, :128], t_ref[w, 128:], o_ref[w].astype(F32), doT,
            inv_ref[w], lambda h: p_ref[w, h],
        )
        dn = dot_nt(jnp.concatenate([dq, dk, dv], 1), proj_ref[...])
        yield
        xhat, rstd = normalise(xw_ref[w].astype(F32))
        win[w] = dr + normalise_back(dn * gain_ref[...], xhat, rstd)

    lockstep(window(step * PER_STEP + u) for u in range(PER_STEP))
    return carry


def back(late, pieces, gain, proj, outw, saved):
    consts = (gain, proj, outw)
    if late:
        shapes = [(2, 11, 28, 128), (2, 15, 28, 128), (4, 6, 28, 128)]
    else:
        shapes = [(2, 14, 28, 128), (2, 14, 28, 128)]
    return pl.pallas_call(
        functools.partial(back_kernel, late),
        out_shape=[jax.ShapeDtypeStruct(s, BF) for s in shapes],
        scratch_shapes=[
            pltpu.VMEM((4, 14, 40, 128), F32),
            pltpu.VMEM((8, ROWS, 128), F32),
        ],
        compiler_params=params(),
        cost_estimate=cost(5.5),
    )(*pieces, *consts, *saved)


def merge_pairs(stage, gain_ref, weight):
    pairs = stage.shape[1]
    pieces = [
        stage[:, :, q % 2, pl.ds(q // 2, 16, stride=2), :].reshape(WT * pairs * 16, 128)
        for q in range(4)
    ]
    xhat, rstd = normalise(jnp.concatenate(pieces, 1))
    merged = dot((xhat * gain_ref[...]).astype(BF), weight).astype(BF).astype(F32)
    return merged, xhat, rstd


def merge_pairs_back(grad, xhat, rstd, gain_ref, weight, stage):
    pairs = stage.shape[1]
    dn = dot_nt(grad.astype(BF), weight)
    dg = normalise_back(dn * gain_ref[...], xhat, rstd)
    for q in range(4):
        stage[:, :, q % 2, pl.ds(q // 2, 16, stride=2), :] = dg[
            :, 128 * q : 128 * q + 128
        ].reshape(WT, pairs, 16, 128)


def put_pair_row(stage, at, values):
    stage[:, at // 2, at % 2, 0:28, :] = values.astype(F32)


def clear_pads(stage):
    stage[:, :, :, 28:32, :] = jnp.zeros((WT, stage.shape[1], 2, 4, 128), F32)


def pair_row(stage, at):
    return stage[:, at // 2, at % 2, 0:28, :].astype(BF)


def fold_merged(merged, pairs):
    halves = [
        merged[:, 128 * i : 128 * i + 128].reshape(WT, pairs, 16, 128)[:, :, 0:14] for i in range(2)
    ]
    return jnp.concatenate(halves, 2)


def unfold_merged(folded):
    pad = jnp.zeros(folded.shape[:2] + (2, 128), F32)
    halves = [
        jnp.concatenate([folded[:, :, 14 * i : 14 * i + 14], pad], 2).reshape(-1, 128)
        for i in range(2)
    ]
    return jnp.concatenate(halves, 1)


def send_kernel(res_ref, gain_ref, weight_ref, send_ref, xhat_ref, rstd_ref, stage):
    clear_pads(stage)
    for i in range(8):
        put_pair_row(stage, i, res_ref[:, 1 + i])
    merged, xhat, rstd = merge_pairs(stage, gain_ref, weight_ref[...])
    xhat_ref[...] = xhat
    rstd_ref[...] = jnp.broadcast_to(rstd, rstd_ref.shape)
    send_ref[:, 0:1] = res_ref[:, 0:1]
    send_ref[:, 1:5] = fold_merged(merged, 4).astype(BF)


def local_kernel(resA_ref, resB_ref, gain_ref, weight_ref, merged_ref, xhat_ref, rstd_ref, stage):
    clear_pads(stage)
    for i in range(5):
        put_pair_row(stage, i, resA_ref[:, i])
    for i in range(13):
        put_pair_row(stage, 5 + i, resB_ref[:, i])
    merged, xhat, rstd = merge_pairs(stage, gain_ref, weight_ref[...])
    xhat_ref[...] = xhat
    rstd_ref[...] = jnp.broadcast_to(rstd, rstd_ref.shape)
    merged_ref[...] = merged


def local_back_kernel(
    grad_ref, d30_ref, xhat_ref, rstd_ref, gain_ref, weight_ref, dA_ref, dB_ref, stage
):
    merge_pairs_back(
        grad_ref[...], xhat_ref[...], rstd_ref[:, 0:1], gain_ref, weight_ref[...], stage
    )
    for i in range(5):
        dA_ref[:, i] = pair_row(stage, i)
    for i in range(13):
        dB_ref[:, i] = pair_row(stage, 5 + i)
    dB_ref[:, 13] = d30_ref[...]


def receive_kernel(got_ref, xhat_ref, rstd_ref, gain_ref, weight_ref, d_ref, stage):
    grad = unfold_merged(got_ref[:, 1:5].astype(F32))
    merge_pairs_back(grad, xhat_ref[...], rstd_ref[:, 0:1], gain_ref, weight_ref[...], stage)
    d_ref[:, 0:1] = got_ref[:, 0:1]
    for i in range(8):
        d_ref[:, 1 + i] = pair_row(stage, i)


def merge_call(kernel, us, shapes, pairs, *operands):
    return pl.pallas_call(
        kernel,
        out_shape=[jax.ShapeDtypeStruct(shape, kind) for shape, kind in shapes],
        scratch_shapes=[pltpu.VMEM((WT, pairs, 2, 40, 128), F32)],
        compiler_params=params(),
        cost_estimate=cost(us),
    )(*operands)


def middle_kernel(
    merged_ref, resB_ref, next_ref, cot_ref, cta_ref, cha_ref, cdg_ref,
    mg1_ref, mg2_ref, g3_ref, row_ref, col_ref, mw1_ref, mw2_ref, p3_ref, biasA_ref, biasB_ref, ow3_ref,
    dm_ref, d30_ref, dN_ref, so_ref, sta_ref, sha_ref,
    stage, stage2, xhat2, rstd2, cotw, k_s, v_s, qT_s, kT_s, vT_s, probs_s, oT_s, inv_s, doT_s, dqkv_s,
):
    cotw[...] = jnp.zeros((4, 7, 8, 512), F32)
    cotw[0:2, 0:4, 0:7, :] = cot_ref[2:4, 3:7].astype(F32)
    cotw[2:4, 0:4, 0:7, :] = unfold(cta_ref[:, 11:15].astype(F32))
    cotw[0:2, 4:7, 0:7, :] = unfold(cha_ref[:, 3:6].astype(F32))
    cotw[2:4, 4:7, 0:7, :] = unfold(cdg_ref[:, 3:6].astype(F32))

    def put_merged(first, count, values):
        for half in range(2):
            block = values[:, 128 * half : 128 * half + 128].reshape(WT, count, 16, 128)
            for i in range(count):
                stage2[half, :, (first + i) // 2, (first + i) % 2, 0:16] = block[:, i]

    def take_merged(first, count):
        halves = [
            jnp.concatenate(
                [
                    stage2[half, :, (first + i) // 2, (first + i) % 2, 0:16].reshape(WT, 1, 16, 128)
                    for i in range(count)
                ],
                1,
            ).reshape(WT * count * 16, 128)
            for half in range(2)
        ]
        return jnp.concatenate(halves, 1)

    put_merged(0, 9, merged_ref[...])
    put_merged(10, 4, unfold_merged(next_ref[:, 1:5].astype(F32)))
    clear_pads(stage)
    put_pair_row(stage, 0, resB_ref[:, 13])
    put_pair_row(stage, 1, next_ref[:, 0])
    merged, xhat_seam, rstd_seam = merge_pairs(stage, mg1_ref, mw1_ref[...])
    put_merged(9, 1, merged)
    pieces = [
        stage2[half, :, :, q % 2, pl.ds(q // 2, 8, stride=2), :].reshape(ROWS, 128)
        for q in range(4)
        for half in range(2)
    ]
    xhat, rstd = normalise(jnp.concatenate(pieces, 1))
    xhat2[...] = xhat
    rstd2[...] = jnp.broadcast_to(rstd, (ROWS, 128))
    merged_two = dot((xhat * mg2_ref[...]).astype(BF), mw2_ref[...]).astype(BF).astype(F32)
    xhat3, rstd3 = normalise(merged_two)
    n3 = (xhat3 * g3_ref[...]).astype(BF)
    packed = [dot(n3, p3_ref[:, 512 * i : 512 * i + 512]) for i in range(3)]
    for g in range(4):
        q, k, v = (part[:, 128 * g : 128 * g + 128] for part in packed)
        q = lengthen((q * (SCALE * LOG2E)).astype(BF))
        k, v = k.astype(BF), v.astype(BF)
        k_s[g] = k
        v_s[g] = v
        qT_s[g] = q.T
        kT_s[g] = lengthen(k).T
        vT_s[g] = lengthen(v).T

    def bias_at(head):
        return jnp.concatenate([biasA_ref[head], biasB_ref[head]], 0)

    mask = region_mask(col_ref[...], row_ref[...])

    operands = []
    for g in range(4):

        def keep(h, probs, g=g):
            probs_s[g * 4 + h] = probs

        operands.append((k_s[g], qT_s[g], vT_s[g], mask, lambda h, g=g: bias_at(g * 4 + h), keep))
    for g, (oT, inverse) in enumerate(attend_four(operands)):
        oT_s[g] = oT
        inv_s[g] = inverse
    att = jnp.concatenate([oT_s[g].astype(BF).T[:ROWS] for g in range(4)], 1)
    mixed = dot(att, ow3_ref[...]).astype(BF).astype(F32)
    section = (merged_two + mixed).reshape(4, 7, 8, 512)
    section = fold(section[:, :, 0:7])
    so_ref[...] = section[0:2, 0:4].astype(BF)
    sta_ref[...] = section[2:4].astype(BF)
    sha_ref[...] = section[0:2, 4:7].astype(BF)

    cot = cotw[...].reshape(ROWS, 512)
    cot_long = lengthen(cot.astype(BF))
    doT = dot_nt(ow3_ref[...], cot_long)
    for g in range(4):
        doT_s[g] = doT[128 * g : 128 * g + 128]

    def group_back(g):
        dqkv_s[g], dqkv_s[4 + g], dqkv_s[8 + g] = yield from attend_four_back(
            v_s[g], qT_s[g], kT_s[g], oT_s[g], doT_s[g], inv_s[g], lambda h: probs_s[g * 4 + h]
        )

    lockstep(group_back(g) for g in range(4))
    dpacked = jnp.concatenate([dqkv_s[i] for i in range(12)], 1)
    dn3 = dot_nt(dpacked, p3_ref[...])
    dm2 = cot + normalise_back(dn3 * g3_ref[...], xhat3, rstd3)
    dn2 = dot_nt(dm2.astype(BF), mw2_ref[...])
    dg2 = normalise_back(dn2 * mg2_ref[...], xhat2[...], rstd2[:, 0:1])
    for q in range(4):
        for half in range(2):
            at = 256 * q + 128 * half
            stage2[half, :, :, q % 2, pl.ds(q // 2, 8, stride=2), :] = dg2[:, at : at + 128].reshape(
                4, 7, 8, 128
            )

    dm_ref[...] = take_merged(0, 9)
    merge_pairs_back(take_merged(9, 1), xhat_seam, rstd_seam, mg1_ref, mw1_ref[...], stage)
    d30_ref[...] = pair_row(stage, 0)
    dN_ref[:, 0] = pair_row(stage, 1)
    dN_ref[:, 1:5] = fold_merged(take_merged(10, 4), 4).astype(BF)


def middle(*operands):
    shapes = [
        (4, 28, 128), (4, 5, 28, 128), (2, 4, 28, 128), (2, 7, 28, 128), (2, 3, 28, 128),
    ]
    return pl.pallas_call(
        middle_kernel,
        out_shape=[jax.ShapeDtypeStruct((576, 256), F32)]
        + [jax.ShapeDtypeStruct(s, BF) for s in shapes],
        scratch_shapes=[
            pltpu.VMEM((4, 1, 2, 40, 128), F32),
            pltpu.VMEM((2, 4, 7, 2, 24, 128), F32),
            pltpu.VMEM((ROWS, 1024), F32),
            pltpu.VMEM((ROWS, 128), F32),
            pltpu.VMEM((4, 7, 8, 512), F32),
            pltpu.VMEM((4, ROWS, 128), BF),
            pltpu.VMEM((4, ROWS, 128), BF),
            pltpu.VMEM((4, 128, LANES), BF),
            pltpu.VMEM((4, 128, LANES), BF),
            pltpu.VMEM((4, 128, LANES), BF),
            pltpu.VMEM((16, ROWS, LANES), BF),
            pltpu.VMEM((4, 128, LANES), F32),
            pltpu.VMEM((4, 8, LANES), F32),
            pltpu.VMEM((4, 128, LANES), F32),
            pltpu.VMEM((12, ROWS, 128), BF),
        ],
        compiler_params=params(24),
        cost_estimate=cost(9),
    )(*operands)


def join_kernel(ta_ref, own_ref, so_ref, grad_ref, section_ref, wide, narrow):
    for t in range(WT):
        wide[:, pl.ds(t, 28, stride=4), :] = (ta_ref if t < 2 else own_ref)[t % 2, 0:11].astype(F32)
        low = (ta_ref[t, 11:15] if t < 2 else so_ref[t - 2]).astype(F32)
        for g in range(4):
            narrow[g, :, pl.ds(t, 7, stride=4), :] = low[:, 7 * g : 7 * g + 7]
    for i in range(11):
        grad_ref[17 + i] = wide[i, 0:112].reshape(28, 4, 128).astype(BF)
    for i in range(4):
        row = jnp.concatenate([narrow[g, i, 0:28] for g in range(4)], 1)
        section_ref[3 + i] = row.reshape(7, 4, 512).astype(BF)


JOINED = [
    jax.ShapeDtypeStruct((28, 28, 4, 128), BF),
    jax.ShapeDtypeStruct((7, 7, 4, 512), BF),
]


def join(ta, own, section_own):
    return pl.pallas_call(
        join_kernel,
        out_shape=JOINED,
        scratch_shapes=[pltpu.VMEM((11, 120, 128), F32), pltpu.VMEM((4, 4, 32, 128), F32)],
        compiler_params=params(),
        cost_estimate=cost(2),
    )(ta, own, section_own)


def last_kernel(
    grad_hbm, section_hbm, ta_ref, own_ref, dg_ref, ha_ref, grad_out, section_out,
    wide, narrow, rows, section_rows, sems,
):
    del grad_hbm, section_hbm
    for t in range(WT):
        corner = dg_ref if t < 2 else ha_ref
        wide[0:3, pl.ds(t, 28, stride=4), :] = corner[t % 2, 0:3].astype(F32)
        wide[3:17, pl.ds(t, 28, stride=4), :] = (ta_ref if t < 2 else own_ref)[t % 2].astype(F32)
        high = corner[t % 2, 3:6].astype(F32)
        for g in range(4):
            narrow[g, :, pl.ds(t, 7, stride=4), :] = high[:, 7 * g : 7 * g + 7]
    for i in range(8):
        rows[i] = wide[i, 0:112].reshape(28, 4, 128).astype(BF)
    start = pltpu.make_async_copy(rows.at[0:8], grad_out.at[0:8], sems.at[2])
    start.start()
    for i in range(8, 17):
        rows[i] = wide[i, 0:112].reshape(28, 4, 128).astype(BF)
    copy = pltpu.make_async_copy(rows.at[8:17], grad_out.at[8:17], sems.at[0])
    copy.start()
    for i in range(3):
        row = jnp.concatenate([narrow[g, i, 0:28] for g in range(4)], 1)
        section_rows[i] = row.reshape(7, 4, 512).astype(BF)
    other = pltpu.make_async_copy(section_rows, section_out.at[0:3], sems.at[1])
    other.start()
    start.wait()
    copy.wait()
    other.wait()


def join_last(grad, section, ta, own, dg, ha):
    return pl.pallas_call(
        last_kernel,
        in_specs=[pl.BlockSpec(memory_space=pl.ANY)] * 2
        + [pl.BlockSpec(memory_space=pltpu.VMEM)] * 4,
        out_specs=[pl.BlockSpec(memory_space=pl.ANY)] * 2,
        out_shape=JOINED,
        scratch_shapes=[
            pltpu.VMEM((17, 120, 128), F32),
            pltpu.VMEM((4, 3, 32, 128), F32),
            pltpu.VMEM((17, 28, 4, 128), BF),
            pltpu.VMEM((3, 7, 4, 512), BF),
            pltpu.SemaphoreType.DMA((3,)),
        ],
        input_output_aliases={0: 0, 1: 1},
        compiler_params=params(),
        cost_estimate=cost(1),
    )(grad, section, ta, own, dg, ha)


IN_ORDER = Layout(major_to_minor=(0, 1, 2, 3))


def inward(values):
    return with_layout_constraint(jnp.transpose(values, (1, 2, 0, 3)), IN_ORDER)


def outward(values):
    return jnp.transpose(with_layout_constraint(values, IN_ORDER), (2, 0, 1, 3))


def send(values, axes, by):
    axes = axes.split()
    sizes = [lax.axis_size(a) for a in axes]
    if len(axes) == 1:
        pairs = [(i, (i + by) % sizes[0]) for i in range(sizes[0])]
    else:
        n, m = sizes
        pairs = [
            (i * m + j, (i + by) % n * m + (j + by) % m) for i in range(n) for j in range(m)
        ]
    return lax.ppermute(values, tuple(axes), pairs)


def per_device(
    tokens,
    regions_one,
    regions_three,
    gain_one,
    projection_one,
    outward_one,
    table_one,
    merge_gain_one,
    merge_weight_one,
    merge_gain_two,
    merge_weight_two,
    gain_three,
    projection_three,
    outward_three,
    table_three,
    cotangent,
):
    (early,) = arrange(early_kernel, (14,), tokens)
    ta_early = send(inward(early), "ta", -1)
    late, ha_late, dg_late = arrange(late_kernel, (15, 6, 6), tokens, cotangent)
    ha_late = send(ha_late, "ha", -1)
    dg_late = send(dg_late, "ha ta", -1)
    ta_late = send(inward(late), "ta", -1)
    bias_one, spread, row_one, row_three, col_one, col_three = prepare(
        table_one, table_three, regions_one, regions_three
    )
    gain, merge_gain, seam = gain_one[None], merge_gain_one[None], merge_weight_one
    args = (gain, projection_one, outward_one, bias_one, spread)
    (res_send, res_a, bias_a), saved_a = front(False, (tokens, outward(ta_early)), *args, row_one, col_one)
    row_send, *early_norm = merge_call(
        send_kernel, 0.5, [((4, 5, 28, 128), BF), ((256, 512), F32), ((256, 128), F32)], 4,
        res_send, merge_gain, seam,
    )
    row_next = send(row_send, "ha", -1)
    ta_late, res_a = lax.optimization_barrier((ta_late, res_a))
    ta_late = outward(ta_late)
    (res_b, bias_b), saved_b = front(True, (tokens, ta_late, ha_late, dg_late), *args, row_one, col_one)
    merged, *local_norm = merge_call(
        local_kernel, 0.1, [((576, 256), F32), ((576, 512), F32), ((576, 128), F32)], 9,
        res_a, res_b, merge_gain, seam,
    )
    row_next, merged = lax.optimization_barrier((row_next, merged))
    d_merged, d_30, d_send, sec_own, sec_ta, sec_ha = middle(
        merged, res_b, row_next, cotangent, ta_late, ha_late, dg_late,
        merge_gain, merge_gain_two[None], gain_three[None], row_three, col_three,
        merge_weight_one, merge_weight_two, projection_three, bias_a, bias_b, outward_three,
    )
    d_prev = send(d_send, "ha", 1)
    d_a, d_b = merge_call(
        local_back_kernel, 1, [((4, 5, 28, 128), BF), ((4, 14, 28, 128), BF)], 9,
        d_merged, d_30, *local_norm, merge_gain, seam,
    )
    own_b, ta_b, ha_b = back(
        True, (d_b, sec_ta, sec_ha), gain, projection_one, outward_one, saved_b
    )
    d_prev, own_b = lax.optimization_barrier((d_prev, own_b))
    ta_b = send(inward(ta_b), "ta", 1)
    ha_b = send(ha_b, "ha", 1)
    (d_first,) = merge_call(
        receive_kernel, 0.5, [((4, 9, 28, 128), BF)], 4, d_prev, *early_norm, merge_gain, seam
    )
    own_a, ta_a = back(False, (d_first, d_a), gain, projection_one, outward_one, saved_a)
    ta_b, ha_b, own_a = lax.optimization_barrier((ta_b, ha_b, own_a))
    ta_a = send(inward(ta_a), "ta", 1)
    dg_b = send(ha_b[2:], "ta", 1)
    grad, section = join(outward(ta_b), own_b, sec_own)
    ta_a, dg_b, grad = lax.optimization_barrier((ta_a, dg_b, grad))
    grad, section = join_last(grad, section, outward(ta_a), own_a, dg_b, ha_b)
    return (jnp.transpose(section, (2, 0, 1, 3)), jnp.transpose(grad, (2, 0, 1, 3)))


def solution(mesh):
    tile = P(("col", "ta"), "ha", None, None)
    ids = P(("col", "ta"), "ha", None)
    in_specs = (tile, ids, ids) + (P(),) * 12 + (tile,)
    return jax.shard_map(
        per_device, mesh=mesh, in_specs=in_specs, out_specs=(tile, tile), check_vma=False
    )
```
